32 devices in a mesh: parts: 2 (over x), tensor: 16 (over z, y, core).
Axes of the slice: x: 2, y: 2, z: 4, core: 2. Of those that a mesh axis runs over, the one named last changes fastest.
Arguments:
- hidden: bfloat16 [320, 8192], P('parts'), parts along dimension 0, may hold values from -6 to 6
- key_value_weight: bfloat16 [2048, 8192], P('tensor'), may hold values from -0.0625 to 0.0625
- adapter_down_weight: bfloat16 [8192, 16, 128], P('tensor'), may hold values from -0.0625 to 0.0625
- adapter_up_weight: bfloat16 [2048, 16, 64], P('tensor'), may hold values from -0.75 to 0.75
- tenant: int32 [32], P('parts'), parts along dimension 0, may hold values from 0 to 7
- tenant_page_table: int32 [8], replicated, may hold values from 0 to 15, as said below
- request_block_count: int32 [32], P('parts'), parts along dimension 0, may hold values from 1 to 2, 20 in all
- last_block_tokens: int32 [32], P('parts'), parts along dimension 0, may hold values from 1 to 8
- placement: int32 [32], P('parts'), parts along dimension 0, may hold values from 0 to 31, as said below
- key_value_cache: bfloat16 [64, 128, 2048], P(('parts', 'tensor')), parts along dimension 0, may hold values from -4 to 4
- context_length: int32 [64], P(('parts', 'tensor')), parts along dimension 0, may hold values from 2 to 128
- decode_step_query: bfloat16 [4, 64, 8192], P(None, ('parts', 'tensor')), parts along dimension 1, may hold values from -40 to 40
- step_key_value: bfloat16 [4, 64, 2048], P(None, ('parts', 'tensor')), parts along dimension 1, may hold values from -6 to 6
Outputs:
- attended: bfloat16 [4, 64, 8192], P(None, ('parts', 'tensor')), parts along dimension 1
The draws below stay inside these ranges and needn't reach their ends.
There are 2 independent parts, one for each index of `parts`. The reference program is written for one: setup_inputs(seed, part) draws one part's arguments, and reference() takes and returns one part's arrays. A program takes and returns all parts, laid end to end along the dimension named above; an argument that names none is the same for every part. Nothing has to cross between parts.
Inputs may be any that keep to these rules, and one draw needn't show every extreme that they name: `tenant_page_table`: different tenants have different pages. `request_block_count`: the counts sum to 20; each request's blocks follow those of the request before it. Requests go to different devices: placement // 2 differs between requests.
All inputs are finite; a program needn't handle non-finite values.
Results may differ from the reference program's by a relative error of at most 0.0051.
Values may be sent and summed in bfloat16 or wider, within the bound.
No kernel may reach another device: no remote copies, remote signals or barrier semaphores. Data moves between devices by JAX's collectives and lax.ppermute only.
A program may use at most 128 MiB of HBM per device.

```python
import math
import jax
import jax.numpy as jnp
import numpy as np
from jax import lax

MODEL_WIDTH = 8192
HEADS = 64
KVH = 8
HD = 128
ADAPTER_RANK = 64
BLK = 8
MOSTB = 2
STEPS = 4
ADAPTER_PAGES = 16
TENANT_COUNT = 8
DEC_DEV = 2
CTX = 128
KEY_VALUE_WIDTH = 2048
TOK = 160
NB = 20
NREQ = 16
ROWS = 32
CAPT = 16


def draw_tenant_page_table(key, part):
    key = jax.random.fold_in(key, 1)
    return jax.random.permutation(key, ADAPTER_PAGES)[:TENANT_COUNT].astype(jnp.int32)


def draw_placement(key, part):
    key = jax.random.fold_in(key, 2)
    key_device, key_order, key_slot = jax.random.split(key, 3)
    device_count = ROWS // DEC_DEV
    middle = (jax.random.permutation(key_device, device_count - 2) + 1).astype(jnp.int32)
    base = jnp.concatenate([jnp.array([0, device_count - 1], jnp.int32), middle[:NREQ - 2]])
    order = jax.random.permutation(key_order, NREQ)
    devices_of = base[order].astype(jnp.int32)
    slots = jax.random.randint(key_slot, (NREQ,), 0, DEC_DEV, dtype=jnp.int32)
    slots = jnp.where(devices_of == 0, 0, slots)
    slots = jnp.where(devices_of == device_count - 1, DEC_DEV - 1, slots)
    return (devices_of * DEC_DEV + slots).astype(jnp.int32)


def draw_context_length(key, part):
    key = jax.random.fold_in(key, 3)
    key_len, key_row = jax.random.split(key)
    lengths = jax.random.randint(key_len, (ROWS,), 2, CTX + 1, dtype=jnp.int32)
    longest = jax.random.randint(key_row, (), 0, ROWS, dtype=jnp.int32)
    return jnp.where(jnp.arange(ROWS, dtype=jnp.int32) == longest, CTX, lengths).astype(jnp.int32)


def draw_key_value_cache(key, part):
    key = jax.random.fold_in(key, 4)
    values = jax.random.truncated_normal(key, -4.0, 4.0, (ROWS, CTX, KEY_VALUE_WIDTH), jnp.float32)
    return values.astype(jnp.bfloat16)


def draw_decode_step_query(key, part):
    key = jax.random.fold_in(key, 6)
    values = jax.random.truncated_normal(key, -4.0, 4.0, (STEPS, ROWS, HEADS * HD), jnp.float32)
    return values.astype(jnp.bfloat16)


def place_ends(result, own_key, smallest, largest):
    place = [jax.random.randint(jax.random.fold_in(own_key, axis), (), 0, length) for axis, length in enumerate(result.shape)]
    main_axis = result.shape.index(max(result.shape))
    next_to = place[:main_axis] + [(place[main_axis] + 1) % result.shape[main_axis]] + place[main_axis + 1:]
    return result.at[tuple(place)].set(smallest).at[tuple(next_to)].set(largest)


def level_of(stream_key, dims, pieces, low, high):
    gain = 1.0
    for axis_at, shards_of in pieces:
        draws = jax.random.uniform(jax.random.fold_in(jax.random.fold_in(stream_key, 6), axis_at), (shards_of,), jnp.float32, low / len(pieces), high / len(pieces))
        gain = gain * jnp.repeat(jnp.exp(draws), dims[axis_at] // shards_of).reshape((-1,) + (1,) * (len(dims) - 1 - axis_at))
    return gain


def split_up(number_of, total, bound, lean):
    loads = [(1 << 20) // math.isqrt(rank ** lean) + 1 for rank in range(2, number_of + 1)]
    surplus, holding = total - bound - (number_of - 1), [1] * (number_of - 1)
    while surplus > 0:
        movable = [i for i in range(number_of - 1) if holding[i] < bound]
        pool, budget = sum([loads[i] for i in movable]), surplus
        for i in movable:
            addition = min(bound - holding[i], max(1, budget * loads[i] // pool), surplus)
            holding[i] = holding[i] + addition
            surplus = surplus - addition
    return np.array([bound] + holding)


def ragged(key, amount, total, most, lean):
    if amount == 2:
        one = jax.random.randint(key, (), max(1, total - most), min(most, total - 1) + 1)
        return jnp.stack([one, total - one])
    sizes = jnp.asarray(split_up(amount, total, most, lean), jnp.int32)
    twos = (amount - 1) // 2
    donor, taker = sizes[1:1 + 2 * twos:2], sizes[2:2 + 2 * twos:2]
    room = jnp.minimum(donor - 1, most - taker)
    passed = jax.random.randint(jax.random.fold_in(key, 1), (twos,), 0, 1 << 20) % (room + 1)
    sizes = sizes.at[1:1 + 2 * twos:2].set(donor - passed).at[2:2 + 2 * twos:2].set(taker + passed)
    return sizes[jax.random.permutation(jax.random.fold_in(key, 2), amount)]


def bell_draw(rng, extent, scale, limit, cuts=(), kind=jnp.bfloat16):
    gain = level_of(rng, extent, cuts, -0.22, 0.18) if cuts else 1.0
    entries = jax.random.normal(rng, extent, jnp.float32) * scale * gain
    return jnp.minimum(jnp.maximum(entries, -limit), limit).astype(kind)


def setup_inputs(seed: int = 0, part: int = 0) -> dict:
    seeds = jax.random.split(jax.random.key(seed), 14)
    part_splits = jax.random.split(jax.random.fold_in(seeds[13], part), 14)
    hidden = bell_draw(part_splits[0], (TOK, MODEL_WIDTH), 1.0, 6.0)
    key_value_weight = bell_draw(seeds[1], (KEY_VALUE_WIDTH, MODEL_WIDTH), MODEL_WIDTH ** -0.5, 0.0625, ((0, 16),))
    adapter_down_weight = bell_draw(seeds[2], (MODEL_WIDTH, ADAPTER_PAGES, 2 * ADAPTER_RANK), MODEL_WIDTH ** -0.5, 0.0625, ((0, 16),))
    adapter_up_weight = bell_draw(seeds[3], (KEY_VALUE_WIDTH, ADAPTER_PAGES, ADAPTER_RANK), ADAPTER_RANK ** -0.5, 0.75, ((0, 16),))
    tenant = place_ends(jax.random.randint(part_splits[4], (NREQ,), 0, TENANT_COUNT), jax.random.fold_in(part_splits[4], 1), 0, TENANT_COUNT - 1).astype(jnp.int32)
    tenant_page_table = draw_tenant_page_table(jax.random.fold_in(seeds[13], 71), part)
    request_block_count = ragged(part_splits[6], NREQ, NB, MOSTB, 1).astype(jnp.int32)
    last_block_tokens = place_ends(jax.random.randint(part_splits[7], (NREQ,), 1, BLK + 1), jax.random.fold_in(part_splits[7], 1), 1, BLK).astype(jnp.int32)
    placement = draw_placement(jax.random.fold_in(jax.random.fold_in(seeds[13], part), 71), part)
    key_value_cache = draw_key_value_cache(jax.random.fold_in(jax.random.fold_in(seeds[13], part), 71), part)
    context_length = draw_context_length(jax.random.fold_in(jax.random.fold_in(seeds[13], part), 71), part)
    decode_step_query = draw_decode_step_query(jax.random.fold_in(jax.random.fold_in(seeds[13], part), 71), part)
    step_key_value = bell_draw(part_splits[12], (STEPS, ROWS, KEY_VALUE_WIDTH), 1.0, 6.0, ((1, 16),))
    return {"hidden": hidden, "key_value_weight": key_value_weight, "adapter_down_weight": adapter_down_weight, "adapter_up_weight": adapter_up_weight, "tenant": tenant, "tenant_page_table": tenant_page_table, "request_block_count": request_block_count, "last_block_tokens": last_block_tokens, "placement": placement, "key_value_cache": key_value_cache, "context_length": context_length, "decode_step_query": decode_step_query, "step_key_value": step_key_value}


ADAPTER_SCALE = 0.5
NEG_LARGE = -1.0e30


def reference(hidden, key_value_weight, adapter_down_weight, adapter_up_weight, tenant, tenant_page_table, request_block_count, last_block_tokens, placement, key_value_cache, context_length, decode_step_query, step_key_value):
    req_end = jnp.cumsum(request_block_count).astype(jnp.int32)
    req_start = (req_end - request_block_count).astype(jnp.int32)
    block_of = jnp.arange(TOK, dtype=jnp.int32) // BLK
    owner_request = jnp.sum((req_end[None, :] <= block_of[:, None]).astype(jnp.int32), axis=1).astype(jnp.int32)
    tok_tenant = tenant[owner_request]
    tenant_hot = tok_tenant[:, None] == jnp.arange(TENANT_COUNT, dtype=jnp.int32)[None, :]
    selected_down_maps = adapter_down_weight[:, tenant_page_table, :].reshape(MODEL_WIDTH, TENANT_COUNT * 2 * ADAPTER_RANK)
    products = jnp.dot(hidden, selected_down_maps, preferred_element_type=jnp.float32).reshape(TOK, TENANT_COUNT, 2 * ADAPTER_RANK)
    shrunk = jnp.sum(jnp.where(tenant_hot[:, :, None], products, jnp.zeros((), jnp.float32)), axis=1).astype(jnp.bfloat16)
    half_width = KEY_VALUE_WIDTH // 2
    selected_up_maps = adapter_up_weight[:, tenant_page_table, :]
    zero_value = jnp.zeros((), jnp.bfloat16)
    masked_keys = jnp.where(tenant_hot[:, :, None], shrunk[:, None, :ADAPTER_RANK], zero_value).reshape(TOK, TENANT_COUNT * ADAPTER_RANK)
    masked_values = jnp.where(tenant_hot[:, :, None], shrunk[:, None, ADAPTER_RANK:], zero_value).reshape(TOK, TENANT_COUNT * ADAPTER_RANK)
    adapter_key_delta = jnp.dot(masked_keys, selected_up_maps[:half_width].reshape(half_width, TENANT_COUNT * ADAPTER_RANK).T, preferred_element_type=jnp.float32)
    adapter_value_delta = jnp.dot(masked_values, selected_up_maps[half_width:].reshape(half_width, TENANT_COUNT * ADAPTER_RANK).T, preferred_element_type=jnp.float32)
    base_key_value = jnp.dot(hidden, key_value_weight.T, preferred_element_type=jnp.float32)
    prefill_key_value = (base_key_value + ADAPTER_SCALE * jnp.concatenate([adapter_key_delta, adapter_value_delta], axis=1)).astype(jnp.bfloat16)

    row_hit = placement[None, :] == jnp.arange(ROWS, dtype=jnp.int32)[:, None]
    new_lengths = ((request_block_count - 1) * BLK + last_block_tokens).astype(jnp.int32)
    row_length = jnp.sum(jnp.where(row_hit, new_lengths[None, :], 0), axis=1).astype(jnp.int32)
    row_start = jnp.sum(jnp.where(row_hit, (req_start * BLK)[None, :], 0), axis=1).astype(jnp.int32)
    offsets = jnp.arange(CAPT, dtype=jnp.int32)
    token_index = jnp.clip(row_start[:, None] + offsets[None, :], 0, TOK - 1).astype(jnp.int32)
    new_rows = prefill_key_value[token_index].astype(jnp.float32)
    new_ok = offsets[None, :] < row_length[:, None]

    cache_keys = key_value_cache[:, :, :half_width].astype(jnp.float32).reshape(ROWS, CTX, KVH, HD)
    cache_values = key_value_cache[:, :, half_width:].astype(jnp.float32).reshape(ROWS, CTX, KVH, HD)
    new_keys = new_rows[:, :, :half_width].reshape(ROWS, CAPT, KVH, HD)
    new_values = new_rows[:, :, half_width:].reshape(ROWS, CAPT, KVH, HD)
    step_keys = step_key_value[:, :, :half_width].astype(jnp.float32).reshape(STEPS, ROWS, KVH, HD)
    step_values = step_key_value[:, :, half_width:].astype(jnp.float32).reshape(STEPS, ROWS, KVH, HD)
    cache_ok = jnp.arange(CTX, dtype=jnp.int32)[None, :] < context_length[:, None]
    outputs = []
    for step in range(STEPS):
        step_ok = jnp.broadcast_to(jnp.arange(STEPS, dtype=jnp.int32)[None, :] <= step, (ROWS, STEPS))
        allowed = jnp.concatenate([cache_ok, new_ok, step_ok], axis=1)[:, None, None, :]
        queries = decode_step_query[step].astype(jnp.float32).reshape(ROWS, KVH, HEADS // KVH, HD)
        scores = jnp.concatenate([
            jnp.einsum("rkgd,rckd->rkgc", queries, cache_keys),
            jnp.einsum("rkgd,rjkd->rkgj", queries, new_keys),
            jnp.einsum("rkgd,srkd->rkgs", queries, step_keys)], axis=3) * (HD ** -0.5)
        scores = jnp.where(allowed, scores, NEG_LARGE)
        highest = jnp.max(scores, axis=3, keepdims=True)
        weights = jnp.exp(scores - highest)
        denominator = jnp.sum(weights, axis=3)
        soft_weights = lax.optimization_barrier(weights.astype(jnp.bfloat16)).astype(jnp.float32)
        combined = jnp.einsum("rkgc,rckd->rkgd", soft_weights[..., :CTX], cache_values)
        combined = combined + jnp.einsum("rkgj,rjkd->rkgd", soft_weights[..., CTX:CTX + CAPT], new_values)
        combined = combined + jnp.einsum("rkgs,srkd->rkgd", soft_weights[..., CTX + CAPT:], step_values)
        outputs.append((combined / denominator[..., None]).reshape(ROWS, HEADS * HD).astype(jnp.bfloat16))
    return jnp.stack(outputs, axis=0)
```

```python
import functools

import jax
import jax.numpy as jnp
from jax import lax
from jax.experimental import pallas as pl
from jax.experimental.pallas import tpu as pltpu
from jax.sharding import PartitionSpec as P

HEADS = 64
KVH = 8
HD = 128
BLK = 8
MOSTB = 2
CAPT = MOSTB * BLK
ADAPTER_SCALE = 0.5
NEG_LARGE = -1e30
VMEM_LIMIT = 60 * 1024 * 1024
WIRE = jnp.float32

SMEM_SPEC = pl.BlockSpec(memory_space=pltpu.SMEM)
VMEM_SPEC = pl.BlockSpec(memory_space=pltpu.VMEM)
ANY_SPEC = pl.BlockSpec(memory_space=pl.ANY)


def up_kernel(dec_rows, tenant, table, placement, up, out, page_of, sems):
    requests = tenant.shape[0]
    devices = out.shape[0]
    for dest in range(devices):
        page_of[dest] = 0
    for r in range(requests):
        page_of[placement[r] // dec_rows] = table[tenant[r]]
    copies = []
    for dest in range(devices):
        copy = pltpu.make_async_copy(up.at[page_of[dest]], out.at[dest], sems.at[dest])
        copy.start()
        copies.append(copy)
    for copy in copies:
        copy.wait()


def project_kernel(
    dec_rows, chunks, tenant, table, counts, placement, hidden, weight, down, out,
    h_s, w_s, d_s, mine_s, sel_s, base_s, part_s, sems,
):
    tokens, width = hidden.shape
    features = weight.shape[0]
    local, pages, rank2 = down.shape
    tenants = table.shape[0]
    requests = tenant.shape[0]
    devices = out.shape[0]
    me = lax.axis_index("tensor")
    step = width // chunks
    dstep = local // chunks

    def my_copy():
        return pltpu.make_async_copy(
            hidden.at[:, pl.ds(pl.multiple_of(me * local, 128), local)], mine_s, sems.at[0, 3]
        )

    my_copy().start()
    d_copies, h_copies, w_copies = [], [], []
    for c in range(chunks):
        d_copies.append(pltpu.make_async_copy(
            down.at[pl.ds(c * dstep, dstep)], d_s.at[pl.ds(c * dstep, dstep)], sems.at[c, 0]))
        h_copies.append(pltpu.make_async_copy(
            hidden.at[:, pl.ds(c * step, step)], h_s.at[c], sems.at[c, 1]))
        w_copies.append(pltpu.make_async_copy(
            weight.at[:, pl.ds(c * step, step)], w_s.at[c], sems.at[c, 2]))
    for c in range(chunks):
        d_copies[c].start()
    for c in range(chunks):
        h_copies[c].start()
        w_copies[c].start()

    rows = lax.broadcasted_iota(jnp.int32, (tenants * 16, 16 * pages), 0)
    cols = lax.broadcasted_iota(jnp.int32, (tenants * 16, 16 * pages), 1)
    page_of_row = jnp.zeros_like(rows)
    for k in range(tenants):
        page_of_row = jnp.where(rows // 16 == k, table[k], page_of_row)
    pick = (rows % 16 == cols // pages) & (cols % pages == page_of_row)
    pick = jnp.where(pick, jnp.float32(1), jnp.float32(0)).astype(jnp.bfloat16)

    for c in range(chunks):
        d_copies[c].wait()
        for b in range(c * dstep // 16, (c + 1) * dstep // 16):
            block = d_s[pl.ds(b * 16, 16)].reshape(16 * pages, rank2)
            chosen = jnp.dot(pick, block, preferred_element_type=jnp.float32)
            sel_s[b] = chosen.astype(jnp.bfloat16)
    my_copy().wait()
    mine = mine_s[...]
    for k in range(tenants):
        maps = sel_s[:, k * 16 : (k + 1) * 16, :].reshape(local, rank2)
        part_s[k, :tokens] = jnp.dot(mine, maps, preferred_element_type=jnp.float32)
        part_s[k, tokens:] = jnp.zeros((BLK, rank2), jnp.float32)

    total = jnp.zeros((tokens, features), jnp.float32)
    for c in range(chunks):
        h_copies[c].wait()
        w_copies[c].wait()
        total = total + lax.dot_general(
            h_s[c], w_s[c], (((1,), (1,)), ((), ())), preferred_element_type=jnp.float32
        )
    base_s[...] = jnp.zeros_like(base_s)
    base_s[:tokens, :features] = total

    if requests < devices:
        out[...] = jnp.zeros_like(out)
    first = jnp.int32(0)
    for r in range(requests):
        dest = placement[r] // dec_rows
        start = pl.multiple_of(first * BLK, BLK)
        out[dest, :, :128] = base_s[pl.ds(start, CAPT), :].astype(out.dtype)
        out[dest, :, 128:] = part_s[tenant[r], pl.ds(start, CAPT), :].astype(out.dtype)
        first = first + counts[r]


def attend_kernel(fused, counts, last, placement, lengths, *refs):
    if fused:
        received, ups, cache, query, steps_kv, out = refs
        base, part = received.at[:, :, :HD], received.at[:, :, HD:]
    else:
        base, part, ups, cache, query, steps_kv, out = refs
    dec_rows, ctx, kv_width = cache.shape
    half_width = kv_width // 2
    step_rows = steps_kv.shape[0]
    steps = step_rows // dec_rows
    rank = ups.shape[1]
    requests = placement.shape[0]
    me = lax.axis_index("tensor")
    group = HEADS // KVH * dec_rows
    q_rows = steps * group

    my_slot = jnp.int32(-1)
    my_length = jnp.int32(0)
    for r in range(requests):
        hit = placement[r] // dec_rows == me
        my_slot = jnp.where(hit, placement[r] % dec_rows, my_slot)
        my_length = jnp.where(hit, (counts[r] - 1) * BLK + last[r], my_length)

    shrunk = part[0].astype(jnp.float32)
    for i in range(1, part.shape[0]):
        shrunk = shrunk + part[i].astype(jnp.float32)
    shrunk = shrunk.astype(jnp.bfloat16)
    halves = (shrunk[:, :rank], shrunk[:, rank:])

    row = lax.broadcasted_iota(jnp.int32, (q_rows, ctx), 0)
    col = lax.broadcasted_iota(jnp.int32, (q_rows, ctx), 1)
    row_slot = row % dec_rows
    cache_ok = [(row_slot == g) & (col < lengths[g]) for g in range(dec_rows)]
    extra = CAPT + 16
    row = lax.broadcasted_iota(jnp.int32, (q_rows, extra), 0)
    col = lax.broadcasted_iota(jnp.int32, (q_rows, extra), 1)
    row_slot = row % dec_rows
    row_step = row // group
    step_col = col - CAPT
    extra_ok = ((col < CAPT) & (row_slot == my_slot) & (col < my_length)) | (
        (step_col >= 0)
        & (step_col < step_rows)
        & (step_col % dec_rows == row_slot)
        & (step_col // dec_rows <= row_step)
    )
    pad = jnp.zeros((16 - step_rows, HD), jnp.bfloat16)

    def fresh(i):
        half = halves[i // KVH]
        delta = jnp.dot(half, ups[i], preferred_element_type=jnp.float32)
        return (base[i].astype(jnp.float32) + ADAPTER_SCALE * delta).astype(jnp.bfloat16)

    nt = (((1,), (1,)), ((), ()))
    scale = HD ** (-0.5)
    for k in range(KVH):
        lanes = pl.ds(k * HD, HD)
        vlanes = pl.ds(half_width + k * HD, HD)
        q = jnp.concatenate(
            [query[pl.ds(s * HEADS * dec_rows + k * group, group), :] for s in range(steps)], axis=0
        )
        extra_keys = jnp.concatenate([fresh(k), steps_kv[:, lanes], pad], axis=0)
        extra_values = jnp.concatenate([fresh(KVH + k), steps_kv[:, vlanes], pad], axis=0)
        scores = []
        for g in range(dec_rows):
            s = lax.dot_general(q, cache[g, :, lanes], nt, preferred_element_type=jnp.float32)
            scores.append(jnp.where(cache_ok[g], s * scale, NEG_LARGE))
        s = lax.dot_general(q, extra_keys, nt, preferred_element_type=jnp.float32)
        scores.append(jnp.where(extra_ok, s * scale, NEG_LARGE))
        top = functools.reduce(
            jnp.maximum, [jnp.max(s, axis=1, keepdims=True) for s in scores]
        )
        weights = [jnp.exp(s - top) for s in scores]
        total = sum(jnp.sum(w, axis=1, keepdims=True) for w in weights)
        values = [cache[g, :, vlanes] for g in range(dec_rows)] + [extra_values]
        mixed = sum(
            jnp.dot(w.astype(jnp.bfloat16), v, preferred_element_type=jnp.float32)
            for w, v in zip(weights, values)
        )
        result = (mixed / total).astype(jnp.bfloat16)
        for s in range(steps):
            out[pl.ds(s * HEADS * dec_rows + k * group, group), :] = result[
                s * group : (s + 1) * group
            ]


def body(
    hidden,
    key_value_weight,
    adapter_down_weight,
    adapter_up_weight,
    tenant,
    tenant_page_table,
    request_block_count,
    last_block_tokens,
    placement,
    key_value_cache,
    context_length,
    decode_step_query,
    step_key_value,
):
    devices = lax.axis_size("tensor")
    tokens, width = hidden.shape
    features = key_value_weight.shape[0]
    local, pages, rank2 = adapter_down_weight.shape
    rank = adapter_up_weight.shape[2]
    tenants = tenant_page_table.shape[0]
    dec_rows, ctx, kv_width = key_value_cache.shape
    steps = step_key_value.shape[0]
    params = pltpu.CompilerParams(vmem_limit_bytes=VMEM_LIMIT)

    up_by_page = jnp.transpose(adapter_up_weight, (1, 2, 0))
    up_out = pl.pallas_call(
        functools.partial(up_kernel, dec_rows),
        out_shape=jax.ShapeDtypeStruct((devices, rank, features), jnp.bfloat16),
        in_specs=[SMEM_SPEC] * 3 + [ANY_SPEC],
        out_specs=ANY_SPEC,
        scratch_shapes=[pltpu.SMEM((devices,), jnp.int32), pltpu.SemaphoreType.DMA((devices,))],
        compiler_params=params,
        name="up_maps",
    )(tenant, tenant_page_table, placement, up_by_page)
    ups = lax.all_to_all(up_out, "tensor", split_axis=0, concat_axis=0, tiled=True)

    chunks = 8
    outgoing = pl.pallas_call(
        functools.partial(project_kernel, dec_rows, chunks),
        out_shape=jax.ShapeDtypeStruct((devices, CAPT, 128 + rank2), WIRE),
        in_specs=[SMEM_SPEC] * 4 + [ANY_SPEC] * 3,
        out_specs=VMEM_SPEC,
        scratch_shapes=[
            pltpu.VMEM((chunks, tokens, width // chunks), jnp.bfloat16),
            pltpu.VMEM((chunks, features, width // chunks), jnp.bfloat16),
            pltpu.VMEM((local, pages, rank2), jnp.bfloat16),
            pltpu.VMEM((tokens, local), jnp.bfloat16),
            pltpu.VMEM((local // 16, tenants * 16, rank2), jnp.bfloat16),
            pltpu.VMEM((tokens + BLK, 128), jnp.float32),
            pltpu.VMEM((tenants, tokens + BLK, rank2), jnp.float32),
            pltpu.SemaphoreType.DMA((chunks, 4)),
        ],
        compiler_params=params,
        name="project",
    )(
        tenant, tenant_page_table, request_block_count, placement,
        hidden, key_value_weight, adapter_down_weight,
    )
    received = lax.all_to_all(outgoing, "tensor", split_axis=0, concat_axis=0, tiled=True)

    heads2 = kv_width // HD
    fused = features == HD
    if fused:
        arrived = (received,)
    else:
        pieces = HD // features
        base = received[:, :, :features].reshape(heads2, pieces, CAPT, features)
        base = base.transpose(0, 2, 1, 3).reshape(heads2, CAPT, HD)
        ups = ups.reshape(heads2, pieces, rank, features)
        ups = ups.transpose(0, 2, 1, 3).reshape(heads2, rank, HD)
        arrived = (base, received[:, :, 128:])

    query = decode_step_query.reshape(steps, dec_rows, HEADS, HD)
    query = query.transpose(0, 2, 1, 3).reshape(steps * HEADS * dec_rows, HD)
    steps_kv = step_key_value.reshape(steps * dec_rows, kv_width)
    attended = pl.pallas_call(
        functools.partial(attend_kernel, fused),
        out_shape=jax.ShapeDtypeStruct((steps * HEADS * dec_rows, HD), jnp.bfloat16),
        in_specs=[SMEM_SPEC] * 4 + [VMEM_SPEC] * (len(arrived) + 4),
        out_specs=VMEM_SPEC,
        compiler_params=params,
        name="attend",
    )(
        request_block_count, last_block_tokens, placement, context_length,
        *arrived, ups, key_value_cache, query, steps_kv,
    )
    attended = attended.reshape(steps, HEADS, dec_rows, HD).transpose(0, 2, 1, 3)
    return attended.reshape(steps, dec_rows, HEADS * HD)


def solution(mesh):
    return jax.shard_map(
        body,
        mesh=mesh,
        in_specs=(
            P("parts", None),
            P("tensor", None),
            P("tensor", None, None),
            P("tensor", None, None),
            P("parts"),
            P(),
            P("parts"),
            P("parts"),
            P("parts"),
            P(("parts", "tensor"), None, None),
            P(("parts", "tensor")),
            P(None, ("parts", "tensor"), None),
            P(None, ("parts", "tensor"), None),
        ),
        out_specs=P(None, ("parts", "tensor"), None),
        check_vma=False,
    )
```

```python
import functools

import jax
import jax.numpy as jnp
from jax import lax
from jax.experimental import pallas as pl
from jax.experimental.pallas import tpu as pltpu
from jax.sharding import PartitionSpec as P

HEADS = 64
KVH = 8
HD = 128
BLK = 8
MOSTB = 2
CAPT = MOSTB * BLK
ADAPTER_SCALE = 0.5
NEG_LARGE = -1e30
VMEM_LIMIT = 24 * 1024 * 1024
WIRE = jnp.bfloat16

SMEM_SPEC = pl.BlockSpec(memory_space=pltpu.SMEM)
VMEM_SPEC = pl.BlockSpec(memory_space=pltpu.VMEM)
ANY_SPEC = pl.BlockSpec(memory_space=pl.ANY)


def div(x, n):
    shift = n.bit_length() - 1
    return lax.shift_right_logical(x, shift) if n == 1 << shift else x // n


def mod(x, n):
    return x & (n - 1) if n & (n - 1) == 0 else x % n


def partial_kernel(
    dec_rows, chunks, tenant, table, counts, placement, hidden, down, up, out,
    d_s, mine_s, sel_s, part_s, sems,
):
    tokens = hidden.shape[0]
    local, pages, rank2 = down.shape
    features = up.shape[2]
    tenants = table.shape[0]
    requests = tenant.shape[0]
    devices = out.shape[0]
    me = lax.axis_index("tensor")
    step = local // chunks

    d_copies = []
    for c in range(chunks):
        d_copies.append(pltpu.make_async_copy(
            down.at[pl.ds(c * step, step)], d_s.at[pl.ds(c * step, step)], sems.at[c]))
        d_copies[c].start()
    my_copy = pltpu.make_async_copy(
        hidden.at[:, pl.ds(pl.multiple_of(me * local, 128), local)], mine_s, sems.at[chunks]
    )
    my_copy.start()

    rows = lax.broadcasted_iota(jnp.int32, (tenants * 16, 16 * pages), 0)
    cols = lax.broadcasted_iota(jnp.int32, (tenants * 16, 16 * pages), 1)
    page_of_row = jnp.zeros_like(rows)
    for k in range(tenants):
        page_of_row = jnp.where(div(rows, 16) == k, table[k], page_of_row)
    pick = (mod(rows, 16) == div(cols, pages)) & (mod(cols, pages) == page_of_row)
    pick = jnp.where(pick, jnp.float32(1), jnp.float32(0)).astype(jnp.bfloat16)

    if requests < devices:
        out[...] = jnp.zeros_like(out)
    for r in range(requests):
        dest = div(placement[r], dec_rows)
        out[dest, CAPT:, :features] = up[table[tenant[r]]]

    for c in range(chunks):
        d_copies[c].wait()
        for b in range(c * step // 16, (c + 1) * step // 16):
            block = d_s[pl.ds(b * 16, 16)].reshape(16 * pages, rank2)
            chosen = jnp.dot(pick, block, preferred_element_type=jnp.float32)
            sel_s[b] = chosen.astype(jnp.bfloat16)
    my_copy.wait()
    mine = mine_s[...]
    for k in range(0, tenants, 2):
        width = min(2, tenants - k)
        maps = jnp.concatenate(
            [sel_s[:, j * 16 : (j + 1) * 16, :].reshape(local, rank2) for j in range(k, k + width)],
            axis=1,
        )
        product = jnp.dot(mine, maps, preferred_element_type=jnp.float32)
        for j in range(width):
            part_s[k + j, :tokens] = product[:, j * rank2 : (j + 1) * rank2]
            part_s[k + j, tokens:] = jnp.zeros((BLK, rank2), jnp.float32)

    first = jnp.int32(0)
    for r in range(requests):
        dest = div(placement[r], dec_rows)
        start = pl.multiple_of(first * BLK, BLK)
        out[dest, :CAPT, :] = part_s[tenant[r], pl.ds(start, CAPT), :].astype(out.dtype)
        first = first + counts[r]


def base_kernel(
    dec_rows, chunks, counts, placement, hidden, weight, out, h_s, w_s, base_s, sems,
):
    tokens, width = hidden.shape
    features = weight.shape[0]
    requests = placement.shape[0]
    devices = out.shape[0]
    step = width // chunks
    h_copies, w_copies = [], []
    for c in range(chunks):
        h_copies.append(pltpu.make_async_copy(
            hidden.at[:, pl.ds(c * step, step)], h_s.at[c], sems.at[c, 0]))
        w_copies.append(pltpu.make_async_copy(
            weight.at[:, pl.ds(c * step, step)], w_s.at[c], sems.at[c, 1]))
        h_copies[c].start()
        w_copies[c].start()
    total = jnp.zeros((tokens, features), jnp.float32)
    for c in range(chunks):
        h_copies[c].wait()
        w_copies[c].wait()
        total = total + lax.dot_general(
            h_s[c], w_s[c], (((1,), (1,)), ((), ())), preferred_element_type=jnp.float32
        )
    base_s[tokens:] = jnp.zeros((BLK, HD), jnp.float32)
    if features < HD:
        base_s[...] = jnp.zeros_like(base_s)
    base_s[:tokens, :features] = total
    if requests < devices:
        out[...] = jnp.zeros_like(out)
    first = jnp.int32(0)
    for r in range(requests):
        dest = div(placement[r], dec_rows)
        start = pl.multiple_of(first * BLK, BLK)
        out[dest] = base_s[pl.ds(start, CAPT), :].astype(out.dtype)
        first = first + counts[r]


NT = (((1,), (1,)), ((), ()))


def gather_queries(query, k, group, steps, stride):
    return jnp.concatenate(
        [query[pl.ds(s * stride + k * group, group), :] for s in range(steps)], axis=0
    )


def cached_kernel(
    lengths, part, ups, cache, query, steps_kv, delta, acc, top_out, total_out,
):
    dec_rows, ctx, kv_width = cache.shape
    half_width = kv_width // 2
    heads2 = delta.shape[0]
    step_rows = KVH * dec_rows
    steps = steps_kv.shape[0] // (2 * step_rows)
    rank = ups.shape[1]
    group = HEADS // KVH * dec_rows
    q_rows = steps * group
    stride = HEADS * dec_rows

    shrunk = part[0].astype(jnp.float32)
    for i in range(1, part.shape[0]):
        shrunk = shrunk + part[i].astype(jnp.float32)
    shrunk = shrunk.astype(jnp.bfloat16)
    halves = (shrunk[:, :rank], shrunk[:, rank:])
    for i in range(heads2):
        delta[i] = ADAPTER_SCALE * jnp.dot(
            halves[i // KVH], ups[i], preferred_element_type=jnp.float32
        )

    row = lax.broadcasted_iota(jnp.int32, (q_rows, ctx), 0)
    col = lax.broadcasted_iota(jnp.int32, (q_rows, ctx), 1)
    row_slot = mod(row, dec_rows)
    cache_ok = [(row_slot == g) & (col < lengths[g]) for g in range(dec_rows)]
    row = lax.broadcasted_iota(jnp.int32, (q_rows, steps * step_rows), 0)
    col = lax.broadcasted_iota(jnp.int32, (q_rows, steps * step_rows), 1)
    step_ok = (mod(row, dec_rows) == mod(col, dec_rows)) & (div(col, step_rows) <= div(row, group))
    step_head = div(mod(col, step_rows), dec_rows)
    step_keys, step_values = (
        jnp.concatenate(
            [steps_kv[pl.ds((2 * s + half) * step_rows, step_rows), :] for s in range(steps)], axis=0
        )
        for half in range(2)
    )

    scale = HD ** (-0.5)
    for k in range(KVH):
        lanes = pl.ds(k * HD, HD)
        vlanes = pl.ds(half_width + k * HD, HD)
        q = gather_queries(query, k, group, steps, stride)
        keys = [cache[g, :, lanes] for g in range(dec_rows)] + [step_keys]
        values = [cache[g, :, vlanes] for g in range(dec_rows)] + [step_values]
        scores = [
            jnp.where(
                ok,
                lax.dot_general(q, key, NT, preferred_element_type=jnp.float32) * scale,
                NEG_LARGE,
            )
            for ok, key in zip(cache_ok + [step_ok & (step_head == k)], keys)
        ]
        top = functools.reduce(jnp.maximum, [jnp.max(s, axis=1, keepdims=True) for s in scores])
        weights = [jnp.exp(s - top) for s in scores]
        total = sum(jnp.sum(w, axis=1, keepdims=True) for w in weights)
        acc[k] = sum(
            jnp.dot(w.astype(jnp.bfloat16), v, preferred_element_type=jnp.float32)
            for w, v in zip(weights, values)
        )
        top_out[k] = jnp.broadcast_to(top, (q_rows, HD))
        total_out[k] = jnp.broadcast_to(total, (q_rows, HD))


def merge_kernel(
    dec_rows, steps, counts, last, placement, base, delta, acc, top_in, total_in, query, out,
):
    requests = placement.shape[0]
    me = lax.axis_index("tensor")
    group = HEADS // KVH * dec_rows
    q_rows = steps * group
    stride = HEADS * dec_rows

    my_slot = jnp.int32(-1)
    my_length = jnp.int32(0)
    for r in range(requests):
        hit = div(placement[r], dec_rows) == me
        my_slot = jnp.where(hit, mod(placement[r], dec_rows), my_slot)
        my_length = jnp.where(hit, (counts[r] - 1) * BLK + last[r], my_length)
    row = lax.broadcasted_iota(jnp.int32, (q_rows, CAPT), 0)
    col = lax.broadcasted_iota(jnp.int32, (q_rows, CAPT), 1)
    ok = (mod(row, dec_rows) == my_slot) & (col < my_length)

    scale = HD ** (-0.5)
    for k in range(KVH):
        q = gather_queries(query, k, group, steps, stride)
        keys = (base[k].astype(jnp.float32) + delta[k]).astype(jnp.bfloat16)
        values = (base[KVH + k].astype(jnp.float32) + delta[KVH + k]).astype(jnp.bfloat16)
        s = lax.dot_general(q, keys, NT, preferred_element_type=jnp.float32)
        s = jnp.where(ok, s * scale, NEG_LARGE)
        old = top_in[k]
        top = jnp.maximum(old, jnp.max(s, axis=1, keepdims=True))
        fade = jnp.exp(old - top)
        w = jnp.exp(s - top[:, :CAPT])
        total = total_in[k] * fade + jnp.sum(w, axis=1, keepdims=True)
        mixed = acc[k] * fade + jnp.dot(
            w.astype(jnp.bfloat16), values, preferred_element_type=jnp.float32
        )
        result = (mixed / total).astype(jnp.bfloat16)
        for s in range(steps):
            out[pl.ds(s * stride + k * group, group), :] = result[s * group : (s + 1) * group]


def body(
    hidden,
    key_value_weight,
    adapter_down_weight,
    adapter_up_weight,
    tenant,
    tenant_page_table,
    request_block_count,
    last_block_tokens,
    placement,
    key_value_cache,
    context_length,
    decode_step_query,
    step_key_value,
):
    devices = lax.axis_size("tensor")
    tokens, width = hidden.shape
    features = key_value_weight.shape[0]
    local, pages, rank2 = adapter_down_weight.shape
    rank = adapter_up_weight.shape[2]
    tenants = tenant_page_table.shape[0]
    dec_rows, ctx, kv_width = key_value_cache.shape
    steps = step_key_value.shape[0]
    params = pltpu.CompilerParams(vmem_limit_bytes=VMEM_LIMIT)

    heads2 = kv_width // HD
    group = HEADS // KVH * dec_rows
    q_rows = steps * group
    chunks = 4
    up_by_page = jnp.transpose(adapter_up_weight, (1, 2, 0))
    first_out = pl.pallas_call(
        functools.partial(partial_kernel, dec_rows, chunks),
        out_shape=jax.ShapeDtypeStruct((devices, CAPT + rank, HD), WIRE),
        in_specs=[SMEM_SPEC] * 4 + [ANY_SPEC] * 2 + [VMEM_SPEC],
        out_specs=VMEM_SPEC,
        scratch_shapes=[
            pltpu.VMEM((local, pages, rank2), jnp.bfloat16),
            pltpu.VMEM((tokens, local), jnp.bfloat16),
            pltpu.VMEM((local // 16, tenants * 16, rank2), jnp.bfloat16),
            pltpu.VMEM((tenants, tokens + BLK, rank2), jnp.float32),
            pltpu.SemaphoreType.DMA((chunks + 1,)),
        ],
        compiler_params=params,
        name="partials",
    )(
        tenant, tenant_page_table, request_block_count, placement,
        hidden, adapter_down_weight, up_by_page,
    )
    first_in = lax.all_to_all(first_out, "tensor", split_axis=0, concat_axis=0, tiled=True)

    chunks = 8
    second_out = pl.pallas_call(
        functools.partial(base_kernel, dec_rows, chunks),
        out_shape=jax.ShapeDtypeStruct((devices, CAPT, HD), WIRE),
        in_specs=[SMEM_SPEC] * 2 + [ANY_SPEC] * 2,
        out_specs=VMEM_SPEC,
        scratch_shapes=[
            pltpu.VMEM((chunks, tokens, width // chunks), jnp.bfloat16),
            pltpu.VMEM((chunks, features, width // chunks), jnp.bfloat16),
            pltpu.VMEM((tokens + BLK, HD), jnp.float32),
            pltpu.SemaphoreType.DMA((chunks, 2)),
        ],
        compiler_params=params,
        name="base",
    )(request_block_count, placement, hidden, key_value_weight)
    second_in = lax.all_to_all(second_out, "tensor", split_axis=0, concat_axis=0, tiled=True)

    query = decode_step_query.reshape(steps, dec_rows, HEADS, HD)
    query = query.transpose(0, 2, 1, 3).reshape(steps * HEADS * dec_rows, HD)
    steps_kv = step_key_value.reshape(steps, dec_rows, heads2, HD)
    steps_kv = steps_kv.transpose(0, 2, 1, 3).reshape(steps * heads2 * dec_rows, HD)
    fused = features == HD
    if fused:
        arrived = (first_in,)
        base = second_in
    else:
        pieces = HD // features
        ups = first_in[:, CAPT:, :features].reshape(heads2, pieces, rank, features)
        ups = ups.transpose(0, 2, 1, 3).reshape(heads2, rank, HD)
        arrived = (first_in[:, :CAPT], ups)
        base = second_in[:, :, :features].reshape(heads2, pieces, CAPT, features)
        base = base.transpose(0, 2, 1, 3).reshape(heads2, CAPT, HD)

    def cached(lengths, *refs):
        if fused:
            both, *rest = refs
            rest = (both.at[:, :CAPT, :], both.at[:, CAPT:, :], *rest)
        else:
            rest = refs
        cached_kernel(lengths, *rest)

    partial_state = jax.ShapeDtypeStruct((KVH, q_rows, HD), jnp.float32)
    delta, acc, top, total = pl.pallas_call(
        cached,
        out_shape=(
            jax.ShapeDtypeStruct((heads2, CAPT, HD), jnp.float32),
            partial_state,
            partial_state,
            partial_state,
        ),
        in_specs=[SMEM_SPEC] + [VMEM_SPEC] * (len(arrived) + 3),
        out_specs=(VMEM_SPEC,) * 4,
        compiler_params=params,
        name="cached",
    )(context_length, *arrived, key_value_cache, query, steps_kv)
    attended = pl.pallas_call(
        functools.partial(merge_kernel, dec_rows, steps),
        out_shape=jax.ShapeDtypeStruct((steps * HEADS * dec_rows, HD), jnp.bfloat16),
        in_specs=[SMEM_SPEC] * 3 + [VMEM_SPEC] * 6,
        out_specs=VMEM_SPEC,
        compiler_params=params,
        name="merge",
    )(
        request_block_count, last_block_tokens, placement,
        base, delta, acc, top, total, query,
    )
    attended = attended.reshape(steps, HEADS, dec_rows, HD).transpose(0, 2, 1, 3)
    return attended.reshape(steps, dec_rows, HEADS * HD)


def solution(mesh):
    return jax.shard_map(
        body,
        mesh=mesh,
        in_specs=(
            P("parts", None),
            P("tensor", None),
            P("tensor", None, None),
            P("tensor", None, None),
            P("parts"),
            P(),
            P("parts"),
            P("parts"),
            P("parts"),
            P(("parts", "tensor"), None, None),
            P(("parts", "tensor")),
            P(None, ("parts", "tensor"), None),
            P(None, ("parts", "tensor"), None),
        ),
        out_specs=P(None, ("parts", "tensor"), None),
        check_vma=False,
    )
```

```python
import functools

import jax
import jax.numpy as jnp
from jax import lax
from jax.experimental import pallas as pl
from jax.experimental.pallas import tpu as pltpu
from jax.sharding import PartitionSpec as P

HEADS = 64
KVH = 8
HD = 128
BLK = 8
MOSTB = 2
CAPT = MOSTB * BLK
ADAPTER_SCALE = 0.5
NEG_LARGE = -1e30
PROJECT_VMEM = 60 * 1024 * 1024
ATTEND_VMEM = 16 * 1024 * 1024
WIRE = jnp.bfloat16

SMEM_SPEC = pl.BlockSpec(memory_space=pltpu.SMEM)
VMEM_SPEC = pl.BlockSpec(memory_space=pltpu.VMEM)
ANY_SPEC = pl.BlockSpec(memory_space=pl.ANY)


def div(x, n):
    shift = n.bit_length() - 1
    return lax.shift_right_logical(x, shift) if n == 1 << shift else x // n


def mod(x, n):
    return x & (n - 1) if n & (n - 1) == 0 else x % n


def project_kernel(
    dec_rows, chunks, devices, tenant, table, counts, placement, hidden, weight, down, up, *refs
):
    outs = refs[:devices]
    h_s, w_s, d_s, mine_s, u_s, sel_s, part_s, base_s, dest_table, sems = refs[devices:]
    tokens, width = hidden.shape
    features = weight.shape[0]
    local, pages, rank2 = down.shape
    tenants = table.shape[0]
    requests = tenant.shape[0]
    me = lax.axis_index("tensor")
    d_step = local // chunks
    step = width // chunks

    d_copies, h_copies, w_copies = [], [], []
    for c in range(chunks):
        d_copies.append(pltpu.make_async_copy(
            down.at[pl.ds(c * d_step, d_step)], d_s.at[pl.ds(c * d_step, d_step)], sems.at[c, 0]))
        h_copies.append(pltpu.make_async_copy(
            hidden.at[:, pl.ds(c * step, step)], h_s.at[c], sems.at[c, 1]))
        w_copies.append(pltpu.make_async_copy(
            weight.at[:, pl.ds(c * step, step)], w_s.at[c], sems.at[c, 2]))
    my_copy = pltpu.make_async_copy(
        hidden.at[:, pl.ds(pl.multiple_of(me * local, 128), local)], mine_s, sems.at[0, 3]
    )
    up_copy = pltpu.make_async_copy(up, u_s, sems.at[1, 3])
    for copy in d_copies + [my_copy, up_copy]:
        copy.start()
    for c in range(chunks):
        h_copies[c].start()
        w_copies[c].start()

    for dest in range(devices):
        dest_table[0, dest] = 0
        dest_table[1, dest] = 0
    first = jnp.int32(0)
    for r in range(requests):
        dest = div(placement[r], dec_rows)
        dest_table[0, dest] = first * BLK
        dest_table[1, dest] = tenant[r]
        first = first + counts[r]

    rows = lax.broadcasted_iota(jnp.int32, (tenants * 16, 16 * pages), 0)
    cols = lax.broadcasted_iota(jnp.int32, (tenants * 16, 16 * pages), 1)
    page_of_row = jnp.zeros_like(rows)
    for k in range(tenants):
        page_of_row = jnp.where(div(rows, 16) == k, table[k], page_of_row)
    pick = (mod(rows, 16) == div(cols, pages)) & (mod(cols, pages) == page_of_row)
    pick = jnp.where(pick, jnp.float32(1), jnp.float32(0)).astype(jnp.bfloat16)

    for c in range(chunks):
        d_copies[c].wait()
        for b in range(c * d_step // 16, (c + 1) * d_step // 16):
            block = d_s[pl.ds(b * 16, 16)].reshape(16 * pages, rank2)
            chosen = jnp.dot(pick, block, preferred_element_type=jnp.float32)
            sel_s[b] = chosen.astype(jnp.bfloat16)
    my_copy.wait()
    mine = mine_s[...]
    for k in range(0, tenants, 2):
        pair = min(2, tenants - k)
        maps = jnp.concatenate(
            [sel_s[:, j * 16 : (j + 1) * 16, :].reshape(local, rank2) for j in range(k, k + pair)],
            axis=1,
        )
        product = jnp.dot(mine, maps, preferred_element_type=jnp.float32)
        for j in range(pair):
            part_s[k + j, :tokens] = product[:, j * rank2 : (j + 1) * rank2]
            part_s[k + j, tokens:] = jnp.zeros((BLK, rank2), jnp.float32)

    total = jnp.zeros((tokens, features), jnp.float32)
    for c in range(chunks):
        h_copies[c].wait()
        w_copies[c].wait()
        total = total + lax.dot_general(
            h_s[c], w_s[c], (((1,), (1,)), ((), ())), preferred_element_type=jnp.float32
        )
    base_s[tokens:] = jnp.zeros((BLK, HD), jnp.float32)
    if features < HD:
        base_s[...] = jnp.zeros_like(base_s)
    base_s[:tokens, :features] = total

    up_copy.wait()
    for s in range(devices):
        dest = partner(me, s, devices)
        start = pl.multiple_of(dest_table[0, dest], BLK)
        who = dest_table[1, dest]
        out = outs[s]
        out[:CAPT, :] = part_s[who, pl.ds(start, CAPT), :].astype(out.dtype)
        out[CAPT : 2 * CAPT, :] = base_s[pl.ds(start, CAPT), :].astype(out.dtype)
        if features < HD:
            out[2 * CAPT :, :] = jnp.zeros_like(out[2 * CAPT :, :])
        out[2 * CAPT :, :features] = u_s[table[who]]


def partner(me, s, devices):
    return me ^ s if devices & (devices - 1) == 0 else (me + s) % devices


def sender(me, s, devices):
    return me ^ s if devices & (devices - 1) == 0 else (me + devices - s) % devices


NT = (((1,), (1,)), ((), ()))


def gather_queries(query, k, group, steps, stride):
    return jnp.concatenate(
        [query[pl.ds(s * stride + k * group, group), :] for s in range(steps)], axis=0
    )


def cached_kernel(
    lengths, cache, query, steps_kv, acc, top_out, total_out,
):
    dec_rows, ctx, kv_width = cache.shape
    half_width = kv_width // 2
    step_rows = KVH * dec_rows
    steps = steps_kv.shape[0] // (2 * step_rows)
    group = HEADS // KVH * dec_rows
    q_rows = steps * group
    stride = HEADS * dec_rows

    row = lax.broadcasted_iota(jnp.int32, (q_rows, ctx), 0)
    col = lax.broadcasted_iota(jnp.int32, (q_rows, ctx), 1)
    row_slot = mod(row, dec_rows)
    cache_ok = [(row_slot == g) & (col < lengths[g]) for g in range(dec_rows)]
    row = lax.broadcasted_iota(jnp.int32, (q_rows, steps * step_rows), 0)
    col = lax.broadcasted_iota(jnp.int32, (q_rows, steps * step_rows), 1)
    step_ok = (mod(row, dec_rows) == mod(col, dec_rows)) & (div(col, step_rows) <= div(row, group))
    step_head = div(mod(col, step_rows), dec_rows)
    step_keys, step_values = (
        jnp.concatenate(
            [steps_kv[pl.ds((2 * s + half) * step_rows, step_rows), :] for s in range(steps)], axis=0
        )
        for half in range(2)
    )

    scale = HD ** (-0.5)
    for k in range(KVH):
        lanes = pl.ds(k * HD, HD)
        vlanes = pl.ds(half_width + k * HD, HD)
        q = gather_queries(query, k, group, steps, stride)
        keys = [cache[g, :, lanes] for g in range(dec_rows)] + [step_keys]
        values = [cache[g, :, vlanes] for g in range(dec_rows)] + [step_values]
        scores = [
            jnp.where(
                ok,
                lax.dot_general(q, key, NT, preferred_element_type=jnp.float32) * scale,
                NEG_LARGE,
            )
            for ok, key in zip(cache_ok + [step_ok & (step_head == k)], keys)
        ]
        top = functools.reduce(jnp.maximum, [jnp.max(s, axis=1, keepdims=True) for s in scores])
        weights = [jnp.exp(s - top) for s in scores]
        total = sum(jnp.sum(w, axis=1, keepdims=True) for w in weights)
        acc[k] = sum(
            jnp.dot(w.astype(jnp.bfloat16), v, preferred_element_type=jnp.float32)
            for w, v in zip(weights, values)
        )
        top_out[k] = jnp.broadcast_to(top, (q_rows, HD))
        total_out[k] = jnp.broadcast_to(total, (q_rows, HD))


def merge_kernel(
    dec_rows, steps, devices, features, counts, last, placement, *refs
):
    arrived = refs[:devices]
    acc, top_in, total_in, query, out, box = refs[devices:]
    requests = placement.shape[0]
    rank = arrived[0].shape[0] - 2 * CAPT
    me = lax.axis_index("tensor")
    group = HEADS // KVH * dec_rows
    q_rows = steps * group
    stride = HEADS * dec_rows

    for s in range(devices):
        box[sender(me, s, devices)] = arrived[s][...]
    my_slot = jnp.int32(-1)
    my_length = jnp.int32(0)
    for r in range(requests):
        hit = div(placement[r], dec_rows) == me
        my_slot = jnp.where(hit, mod(placement[r], dec_rows), my_slot)
        my_length = jnp.where(hit, (counts[r] - 1) * BLK + last[r], my_length)
    row = lax.broadcasted_iota(jnp.int32, (q_rows, CAPT), 0)
    col = lax.broadcasted_iota(jnp.int32, (q_rows, CAPT), 1)
    ok = (mod(row, dec_rows) == my_slot) & (col < my_length)

    shrunk = box[0, :CAPT].astype(jnp.float32)
    for i in range(1, devices):
        shrunk = shrunk + box[i, :CAPT].astype(jnp.float32)
    shrunk = shrunk.astype(jnp.bfloat16)
    halves = (shrunk[:, :rank], shrunk[:, rank:])
    pieces = HD // features

    def fresh(i):
        base = [box[i * pieces + p, CAPT : 2 * CAPT, :features] for p in range(pieces)]
        ups = [box[i * pieces + p, 2 * CAPT :, :features] for p in range(pieces)]
        base = base[0] if pieces == 1 else jnp.concatenate(base, axis=1)
        ups = ups[0] if pieces == 1 else jnp.concatenate(ups, axis=1)
        delta = jnp.dot(halves[i // KVH], ups, preferred_element_type=jnp.float32)
        return (base.astype(jnp.float32) + ADAPTER_SCALE * delta).astype(jnp.bfloat16)

    scale = HD ** (-0.5)
    for k in range(KVH):
        q = gather_queries(query, k, group, steps, stride)
        keys, values = fresh(k), fresh(KVH + k)
        s = lax.dot_general(q, keys, NT, preferred_element_type=jnp.float32)
        s = jnp.where(ok, s * scale, NEG_LARGE)
        old = top_in[k]
        top = jnp.maximum(old, jnp.max(s, axis=1, keepdims=True))
        fade = jnp.exp(old - top)
        w = jnp.exp(s - top[:, :CAPT])
        total = total_in[k] * fade + jnp.sum(w, axis=1, keepdims=True)
        mixed = acc[k] * fade + jnp.dot(
            w.astype(jnp.bfloat16), values, preferred_element_type=jnp.float32
        )
        result = (mixed / total).astype(jnp.bfloat16)
        for s in range(steps):
            out[pl.ds(s * stride + k * group, group), :] = result[s * group : (s + 1) * group]


def body(
    hidden,
    key_value_weight,
    adapter_down_weight,
    adapter_up_weight,
    tenant,
    tenant_page_table,
    request_block_count,
    last_block_tokens,
    placement,
    key_value_cache,
    context_length,
    decode_step_query,
    step_key_value,
):
    devices = lax.axis_size("tensor")
    tokens, width = hidden.shape
    features = key_value_weight.shape[0]
    local, pages, rank2 = adapter_down_weight.shape
    rank = adapter_up_weight.shape[2]
    tenants = tenant_page_table.shape[0]
    dec_rows, ctx, kv_width = key_value_cache.shape
    steps = step_key_value.shape[0]
    heads2 = kv_width // HD
    group = HEADS // KVH * dec_rows
    q_rows = steps * group
    chunks = 4
    up_by_page = jnp.transpose(adapter_up_weight, (1, 2, 0))
    rows = 2 * CAPT + rank
    outgoing = pl.pallas_call(
        functools.partial(project_kernel, dec_rows, chunks, devices),
        out_shape=[jax.ShapeDtypeStruct((rows, HD), WIRE)] * devices,
        in_specs=[SMEM_SPEC] * 4 + [ANY_SPEC] * 4,
        out_specs=[VMEM_SPEC] * devices,
        scratch_shapes=[
            pltpu.VMEM((chunks, tokens, width // chunks), jnp.bfloat16),
            pltpu.VMEM((chunks, features, width // chunks), jnp.bfloat16),
            pltpu.VMEM((local, pages, rank2), jnp.bfloat16),
            pltpu.VMEM((tokens, local), jnp.bfloat16),
            pltpu.VMEM((pages, rank, features), jnp.bfloat16),
            pltpu.VMEM((local // 16, tenants * 16, rank2), jnp.bfloat16),
            pltpu.VMEM((tenants, tokens + BLK, rank2), jnp.float32),
            pltpu.VMEM((tokens + BLK, HD), jnp.float32),
            pltpu.SMEM((2, devices), jnp.int32),
            pltpu.SemaphoreType.DMA((chunks, 4)),
        ],
        compiler_params=pltpu.CompilerParams(vmem_limit_bytes=PROJECT_VMEM),
        name="project",
    )(
        tenant, tenant_page_table, request_block_count, placement,
        hidden, key_value_weight, adapter_down_weight, up_by_page,
    )
    arrived = [outgoing[0]]
    for s in range(1, devices):
        route = [(i, partner(i, s, devices)) for i in range(devices)]
        arrived.append(lax.ppermute(outgoing[s], "tensor", route))

    query = decode_step_query.reshape(steps, dec_rows, HEADS, HD)
    query = query.transpose(0, 2, 1, 3).reshape(steps * HEADS * dec_rows, HD)
    steps_kv = step_key_value.reshape(steps, dec_rows, heads2, HD)
    steps_kv = steps_kv.transpose(0, 2, 1, 3).reshape(steps * heads2 * dec_rows, HD)
    partial_state = jax.ShapeDtypeStruct((KVH, q_rows, HD), jnp.float32)
    acc, top, total = pl.pallas_call(
        cached_kernel,
        out_shape=(partial_state,) * 3,
        in_specs=[SMEM_SPEC] + [VMEM_SPEC] * 3,
        out_specs=(VMEM_SPEC,) * 3,
        compiler_params=pltpu.CompilerParams(vmem_limit_bytes=ATTEND_VMEM),
        name="cached",
    )(context_length, key_value_cache, query, steps_kv)
    attended = pl.pallas_call(
        functools.partial(merge_kernel, dec_rows, steps, devices, features),
        out_shape=jax.ShapeDtypeStruct((steps * HEADS * dec_rows, HD), jnp.bfloat16),
        in_specs=[SMEM_SPEC] * 3 + [VMEM_SPEC] * (devices + 4),
        out_specs=VMEM_SPEC,
        scratch_shapes=[pltpu.VMEM((devices, rows, HD), WIRE)],
        compiler_params=pltpu.CompilerParams(vmem_limit_bytes=ATTEND_VMEM),
        name="merge",
    )(
        request_block_count, last_block_tokens, placement, *arrived, acc, top, total, query,
    )
    attended = attended.reshape(steps, HEADS, dec_rows, HD).transpose(0, 2, 1, 3)
    return attended.reshape(steps, dec_rows, HEADS * HD)


def solution(mesh):
    return jax.shard_map(
        body,
        mesh=mesh,
        in_specs=(
            P("parts", None),
            P("tensor", None),
            P("tensor", None, None),
            P("tensor", None, None),
            P("parts"),
            P(),
            P("parts"),
            P("parts"),
            P("parts"),
            P(("parts", "tensor"), None, None),
            P(("parts", "tensor")),
            P(None, ("parts", "tensor"), None),
            P(None, ("parts", "tensor"), None),
        ),
        out_specs=P(None, ("parts", "tensor"), None),
        check_vma=False,
    )
```

```python
import functools

import jax
import jax.numpy as jnp
from jax import lax
from jax.experimental import pallas as pl
from jax.experimental.pallas import tpu as pltpu
from jax.sharding import PartitionSpec as P

HEADS = 64
KVH = 8
HD = 128
BLK = 8
MOSTB = 2
CAPT = MOSTB * BLK
ADAPTER_SCALE = 0.5
NEG_LARGE = -1e30
PROJECT_VMEM = 60 * 1024 * 1024
ATTEND_VMEM = 16 * 1024 * 1024
WIRE = jnp.bfloat16

SMEM_SPEC = pl.BlockSpec(memory_space=pltpu.SMEM)
VMEM_SPEC = pl.BlockSpec(memory_space=pltpu.VMEM)
ANY_SPEC = pl.BlockSpec(memory_space=pl.ANY)


def div(x, n):
    shift = n.bit_length() - 1
    return lax.shift_right_logical(x, shift) if n == 1 << shift else x // n


def mod(x, n):
    return x & (n - 1) if n & (n - 1) == 0 else x % n


def project_kernel(
    dec_rows, chunks, devices, tenant, table, counts, placement, hidden, weight, down, up, out,
    h_s, w_s, d_s, mine_s, u_s, sel_s, part_s, base_s, dest_table, sems,
):
    tokens, width = hidden.shape
    features = weight.shape[0]
    local, pages, rank2 = down.shape
    tenants = table.shape[0]
    requests = tenant.shape[0]
    me = lax.axis_index("tensor")
    d_step = local // chunks
    step = width // chunks

    d_copies, h_copies, w_copies = [], [], []
    for c in range(chunks):
        d_copies.append(pltpu.make_async_copy(
            down.at[pl.ds(c * d_step, d_step)], d_s.at[pl.ds(c * d_step, d_step)], sems.at[c, 0]))
        h_copies.append(pltpu.make_async_copy(
            hidden.at[:, pl.ds(c * step, step)], h_s.at[c], sems.at[c, 1]))
        w_copies.append(pltpu.make_async_copy(
            weight.at[:, pl.ds(c * step, step)], w_s.at[c], sems.at[c, 2]))
    my_copy = pltpu.make_async_copy(
        hidden.at[:, pl.ds(pl.multiple_of(me * local, 128), local)], mine_s, sems.at[0, 3]
    )
    up_copy = pltpu.make_async_copy(up, u_s, sems.at[1, 3])
    for copy in d_copies + [my_copy, up_copy]:
        copy.start()
    for c in range(chunks):
        h_copies[c].start()
        w_copies[c].start()

    for dest in range(devices):
        dest_table[0, dest] = 0
        dest_table[1, dest] = 0
    first = jnp.int32(0)
    for r in range(requests):
        dest = div(placement[r], dec_rows)
        dest_table[0, dest] = first * BLK
        dest_table[1, dest] = tenant[r]
        first = first + counts[r]

    rows = lax.broadcasted_iota(jnp.int32, (tenants * 16, 16 * pages), 0)
    cols = lax.broadcasted_iota(jnp.int32, (tenants * 16, 16 * pages), 1)
    page_of_row = jnp.zeros_like(rows)
    for k in range(tenants):
        page_of_row = jnp.where(div(rows, 16) == k, table[k], page_of_row)
    pick = (mod(rows, 16) == div(cols, pages)) & (mod(cols, pages) == page_of_row)
    pick = jnp.where(pick, jnp.float32(1), jnp.float32(0)).astype(jnp.bfloat16)

    for c in range(chunks):
        d_copies[c].wait()
        for b in range(c * d_step // 16, (c + 1) * d_step // 16):
            block = d_s[pl.ds(b * 16, 16)].reshape(16 * pages, rank2)
            chosen = jnp.dot(pick, block, preferred_element_type=jnp.float32)
            sel_s[b] = chosen.astype(jnp.bfloat16)
    my_copy.wait()
    mine = mine_s[...]
    for k in range(0, tenants, 2):
        pair = min(2, tenants - k)
        maps = jnp.concatenate(
            [sel_s[:, j * 16 : (j + 1) * 16, :].reshape(local, rank2) for j in range(k, k + pair)],
            axis=1,
        )
        product = jnp.dot(mine, maps, preferred_element_type=jnp.float32)
        for j in range(pair):
            part_s[k + j, :tokens] = product[:, j * rank2 : (j + 1) * rank2]
            part_s[k + j, tokens:] = jnp.zeros((BLK, rank2), jnp.float32)

    total = jnp.zeros((tokens, features), jnp.float32)
    for c in range(chunks):
        h_copies[c].wait()
        w_copies[c].wait()
        total = total + lax.dot_general(
            h_s[c], w_s[c], (((1,), (1,)), ((), ())), preferred_element_type=jnp.float32
        )
    base_s[tokens:] = jnp.zeros((BLK, HD), jnp.float32)
    if features < HD:
        base_s[...] = jnp.zeros_like(base_s)
    base_s[:tokens, :features] = total

    up_copy.wait()
    for dest in range(devices):
        start = pl.multiple_of(dest_table[0, dest], BLK)
        who = dest_table[1, dest]
        out[dest, :CAPT, :] = part_s[who, pl.ds(start, CAPT), :].astype(out.dtype)
        out[dest, CAPT : 2 * CAPT, :] = base_s[pl.ds(start, CAPT), :].astype(out.dtype)
        if features < HD:
            out[dest, 2 * CAPT :, :] = jnp.zeros((out.shape[1] - 2 * CAPT, HD), out.dtype)
        out[dest, 2 * CAPT :, :features] = u_s[table[who]]


NT = (((1,), (1,)), ((), ()))


def gather_queries(query, k, group, steps, stride):
    return jnp.concatenate(
        [query[pl.ds(s * stride + k * group, group), :] for s in range(steps)], axis=0
    )


def cached_kernel(
    lengths, cache, query, steps_kv, acc, top_out, total_out,
):
    dec_rows, ctx, kv_width = cache.shape
    half_width = kv_width // 2
    step_rows = KVH * dec_rows
    steps = steps_kv.shape[0] // (2 * step_rows)
    group = HEADS // KVH * dec_rows
    q_rows = steps * group
    stride = HEADS * dec_rows

    row = lax.broadcasted_iota(jnp.int32, (q_rows, ctx), 0)
    col = lax.broadcasted_iota(jnp.int32, (q_rows, ctx), 1)
    row_slot = mod(row, dec_rows)
    cache_ok = [(row_slot == g) & (col < lengths[g]) for g in range(dec_rows)]
    row = lax.broadcasted_iota(jnp.int32, (q_rows, steps * step_rows), 0)
    col = lax.broadcasted_iota(jnp.int32, (q_rows, steps * step_rows), 1)
    step_ok = (mod(row, dec_rows) == mod(col, dec_rows)) & (div(col, step_rows) <= div(row, group))
    step_head = div(mod(col, step_rows), dec_rows)
    step_keys, step_values = (
        jnp.concatenate(
            [steps_kv[pl.ds((2 * s + half) * step_rows, step_rows), :] for s in range(steps)], axis=0
        )
        for half in range(2)
    )

    scale = HD ** (-0.5)
    for k in range(KVH):
        lanes = pl.ds(k * HD, HD)
        vlanes = pl.ds(half_width + k * HD, HD)
        q = gather_queries(query, k, group, steps, stride)
        keys = [cache[g, :, lanes] for g in range(dec_rows)] + [step_keys]
        values = [cache[g, :, vlanes] for g in range(dec_rows)] + [step_values]
        scores = [
            jnp.where(
                ok,
                lax.dot_general(q, key, NT, preferred_element_type=jnp.float32) * scale,
                NEG_LARGE,
            )
            for ok, key in zip(cache_ok + [step_ok & (step_head == k)], keys)
        ]
        top = functools.reduce(jnp.maximum, [jnp.max(s, axis=1, keepdims=True) for s in scores])
        weights = [jnp.exp(s - top) for s in scores]
        total = sum(jnp.sum(w, axis=1, keepdims=True) for w in weights)
        acc[k] = sum(
            jnp.dot(w.astype(jnp.bfloat16), v, preferred_element_type=jnp.float32)
            for w, v in zip(weights, values)
        )
        top_out[k] = jnp.broadcast_to(top, (q_rows, HD))
        total_out[k] = jnp.broadcast_to(total, (q_rows, HD))


def merge_kernel(
    dec_rows, steps, devices, features, counts, last, placement,
    box, acc, top_in, total_in, query, out,
):
    requests = placement.shape[0]
    rank = box.shape[1] - 2 * CAPT
    me = lax.axis_index("tensor")
    group = HEADS // KVH * dec_rows
    q_rows = steps * group
    stride = HEADS * dec_rows

    my_slot = jnp.int32(-1)
    my_length = jnp.int32(0)
    for r in range(requests):
        hit = div(placement[r], dec_rows) == me
        my_slot = jnp.where(hit, mod(placement[r], dec_rows), my_slot)
        my_length = jnp.where(hit, (counts[r] - 1) * BLK + last[r], my_length)
    row = lax.broadcasted_iota(jnp.int32, (q_rows, CAPT), 0)
    col = lax.broadcasted_iota(jnp.int32, (q_rows, CAPT), 1)
    ok = (mod(row, dec_rows) == my_slot) & (col < my_length)

    shrunk = box[0, :CAPT].astype(jnp.float32)
    for i in range(1, devices):
        shrunk = shrunk + box[i, :CAPT].astype(jnp.float32)
    shrunk = shrunk.astype(jnp.bfloat16)
    halves = (shrunk[:, :rank], shrunk[:, rank:])
    pieces = HD // features

    def fresh(i):
        base = [box[i * pieces + p, CAPT : 2 * CAPT, :features] for p in range(pieces)]
        ups = [box[i * pieces + p, 2 * CAPT :, :features] for p in range(pieces)]
        base = base[0] if pieces == 1 else jnp.concatenate(base, axis=1)
        ups = ups[0] if pieces == 1 else jnp.concatenate(ups, axis=1)
        delta = jnp.dot(halves[i // KVH], ups, preferred_element_type=jnp.float32)
        return (base.astype(jnp.float32) + ADAPTER_SCALE * delta).astype(jnp.bfloat16)

    scale = HD ** (-0.5)
    for k in range(KVH):
        q = gather_queries(query, k, group, steps, stride)
        keys, values = fresh(k), fresh(KVH + k)
        s = lax.dot_general(q, keys, NT, preferred_element_type=jnp.float32)
        s = jnp.where(ok, s * scale, NEG_LARGE)
        old = top_in[k]
        top = jnp.maximum(old, jnp.max(s, axis=1, keepdims=True))
        fade = jnp.exp(old - top)
        w = jnp.exp(s - top[:, :CAPT])
        total = total_in[k] * fade + jnp.sum(w, axis=1, keepdims=True)
        mixed = acc[k] * fade + jnp.dot(
            w.astype(jnp.bfloat16), values, preferred_element_type=jnp.float32
        )
        result = (mixed / total).astype(jnp.bfloat16)
        for s in range(steps):
            out[pl.ds(s * stride + k * group, group), :] = result[s * group : (s + 1) * group]


def body(
    hidden,
    key_value_weight,
    adapter_down_weight,
    adapter_up_weight,
    tenant,
    tenant_page_table,
    request_block_count,
    last_block_tokens,
    placement,
    key_value_cache,
    context_length,
    decode_step_query,
    step_key_value,
):
    devices = lax.axis_size("tensor")
    tokens, width = hidden.shape
    features = key_value_weight.shape[0]
    local, pages, rank2 = adapter_down_weight.shape
    rank = adapter_up_weight.shape[2]
    tenants = tenant_page_table.shape[0]
    dec_rows, ctx, kv_width = key_value_cache.shape
    steps = step_key_value.shape[0]
    heads2 = kv_width // HD
    group = HEADS // KVH * dec_rows
    q_rows = steps * group
    chunks = 4
    up_by_page = jnp.transpose(adapter_up_weight, (1, 2, 0))
    rows = 2 * CAPT + rank
    outgoing = pl.pallas_call(
        functools.partial(project_kernel, dec_rows, chunks, devices),
        out_shape=jax.ShapeDtypeStruct((devices, rows, HD), WIRE),
        in_specs=[SMEM_SPEC] * 4 + [ANY_SPEC] * 4,
        out_specs=VMEM_SPEC,
        scratch_shapes=[
            pltpu.VMEM((chunks, tokens, width // chunks), jnp.bfloat16),
            pltpu.VMEM((chunks, features, width // chunks), jnp.bfloat16),
            pltpu.VMEM((local, pages, rank2), jnp.bfloat16),
            pltpu.VMEM((tokens, local), jnp.bfloat16),
            pltpu.VMEM((pages, rank, features), jnp.bfloat16),
            pltpu.VMEM((local // 16, tenants * 16, rank2), jnp.bfloat16),
            pltpu.VMEM((tenants, tokens + BLK, rank2), jnp.float32),
            pltpu.VMEM((tokens + BLK, HD), jnp.float32),
            pltpu.SMEM((2, devices), jnp.int32),
            pltpu.SemaphoreType.DMA((chunks, 4)),
        ],
        compiler_params=pltpu.CompilerParams(vmem_limit_bytes=PROJECT_VMEM),
        name="project",
    )(
        tenant, tenant_page_table, request_block_count, placement,
        hidden, key_value_weight, adapter_down_weight, up_by_page,
    )
    arrived = lax.all_to_all(outgoing, "tensor", split_axis=0, concat_axis=0, tiled=True)

    query = decode_step_query.reshape(steps, dec_rows, HEADS, HD)
    query = query.transpose(0, 2, 1, 3).reshape(steps * HEADS * dec_rows, HD)
    steps_kv = step_key_value.reshape(steps, dec_rows, heads2, HD)
    steps_kv = steps_kv.transpose(0, 2, 1, 3).reshape(steps * heads2 * dec_rows, HD)
    partial_state = jax.ShapeDtypeStruct((KVH, q_rows, HD), jnp.float32)
    acc, top, total = pl.pallas_call(
        cached_kernel,
        out_shape=(partial_state,) * 3,
        in_specs=[SMEM_SPEC] + [VMEM_SPEC] * 3,
        out_specs=(VMEM_SPEC,) * 3,
        compiler_params=pltpu.CompilerParams(vmem_limit_bytes=ATTEND_VMEM),
        name="cached",
    )(context_length, key_value_cache, query, steps_kv)
    attended = pl.pallas_call(
        functools.partial(merge_kernel, dec_rows, steps, devices, features),
        out_shape=jax.ShapeDtypeStruct((steps * HEADS * dec_rows, HD), jnp.bfloat16),
        in_specs=[SMEM_SPEC] * 3 + [VMEM_SPEC] * 5,
        out_specs=VMEM_SPEC,
        compiler_params=pltpu.CompilerParams(vmem_limit_bytes=ATTEND_VMEM),
        name="merge",
    )(
        request_block_count, last_block_tokens, placement, arrived, acc, top, total, query,
    )
    attended = attended.reshape(steps, HEADS, dec_rows, HD).transpose(0, 2, 1, 3)
    return attended.reshape(steps, dec_rows, HEADS * HD)


def solution(mesh):
    return jax.shard_map(
        body,
        mesh=mesh,
        in_specs=(
            P("parts", None),
            P("tensor", None),
            P("tensor", None, None),
            P("tensor", None, None),
            P("parts"),
            P(),
            P("parts"),
            P("parts"),
            P("parts"),
            P(("parts", "tensor"), None, None),
            P(("parts", "tensor")),
            P(None, ("parts", "tensor"), None),
            P(None, ("parts", "tensor"), None),
        ),
        out_specs=P(None, ("parts", "tensor"), None),
        check_vma=False,
    )
```

```python
import functools

import jax
import jax.numpy as jnp
from jax import lax
from jax.experimental import pallas as pl
from jax.experimental.pallas import tpu as pltpu
from jax.sharding import PartitionSpec as P

HEADS = 64
KVH = 8
HD = 128
BLK = 8
MOSTB = 2
CAPT = MOSTB * BLK
ADAPTER_SCALE = 0.5
NEG_LARGE = -1e30
PROJECT_VMEM = 32 * 1024 * 1024
ATTEND_VMEM = 16 * 1024 * 1024
WIRE = jnp.bfloat16

SMEM_SPEC = pl.BlockSpec(memory_space=pltpu.SMEM)
VMEM_SPEC = pl.BlockSpec(memory_space=pltpu.VMEM)
ANY_SPEC = pl.BlockSpec(memory_space=pl.ANY)


def div(x, n):
    shift = n.bit_length() - 1
    return lax.shift_right_logical(x, shift) if n == 1 << shift else x // n


def mod(x, n):
    return x & (n - 1) if n & (n - 1) == 0 else x % n


def project_kernel(
    dec_rows, chunks, devices, tenant_h, table_h, counts_h, placement_h, hidden, weight, down, up, out,
    tenant, table, counts, placement,
    h_s, w_s, d_s, mine_s, u_s, sel_s, part_s, base_s, dest_table, sems, int_sems,
):
    tokens, width = hidden.shape
    features = weight.shape[0]
    local, pages, rank2 = down.shape
    tenants = table.shape[0]
    requests = tenant.shape[0]
    me = lax.axis_index("tensor")
    d_step = local // chunks
    step = width // chunks

    int_copies = [
        pltpu.make_async_copy(src, dst, int_sems.at[i])
        for i, (src, dst) in enumerate(
            ((table_h, table), (tenant_h, tenant), (counts_h, counts), (placement_h, placement))
        )
    ]
    for copy in int_copies:
        copy.start()
    d_copies, h_copies, w_copies = [], [], []
    for c in range(chunks):
        d_copies.append(pltpu.make_async_copy(
            down.at[pl.ds(c * d_step, d_step)], d_s.at[pl.ds(c * d_step, d_step)], sems.at[c, 0]))
        h_copies.append(pltpu.make_async_copy(
            hidden.at[:, pl.ds(c * step, step)], h_s.at[c], sems.at[c, 1]))
        w_copies.append(pltpu.make_async_copy(
            weight.at[:, pl.ds(c * step, step)], w_s.at[c], sems.at[c, 2]))
    my_copy = pltpu.make_async_copy(
        hidden.at[:, pl.ds(pl.multiple_of(me * local, 128), local)], mine_s, sems.at[0, 3]
    )
    up_copy = pltpu.make_async_copy(up, u_s, sems.at[1, 3])
    for copy in d_copies + [my_copy, up_copy]:
        copy.start()
    for c in range(chunks):
        h_copies[c].start()
        w_copies[c].start()

    int_copies[0].wait()
    rows = lax.broadcasted_iota(jnp.int32, (tenants * 16, 16 * pages), 0)
    cols = lax.broadcasted_iota(jnp.int32, (tenants * 16, 16 * pages), 1)
    page_of_row = jnp.zeros_like(rows)
    for k in range(tenants):
        page_of_row = jnp.where(div(rows, 16) == k, table[k], page_of_row)
    pick = (mod(rows, 16) == div(cols, pages)) & (mod(cols, pages) == page_of_row)
    pick = jnp.where(pick, jnp.float32(1), jnp.float32(0)).astype(jnp.bfloat16)

    for c in range(chunks):
        d_copies[c].wait()
        for b in range(c * d_step // 16, (c + 1) * d_step // 16, 2):
            block = jnp.concatenate(
                [d_s[pl.ds((b + i) * 16, 16)].reshape(16 * pages, rank2) for i in range(2)], axis=1
            )
            chosen = jnp.dot(pick, block, preferred_element_type=jnp.float32)
            for i in range(2):
                sel_s[b + i] = chosen[:, i * rank2 : (i + 1) * rank2].astype(jnp.bfloat16)
    for copy in int_copies[1:]:
        copy.wait()
    for dest in range(devices):
        dest_table[0, dest] = 0
        dest_table[1, dest] = 0
    first = jnp.int32(0)
    for r in range(requests):
        dest = div(placement[r], dec_rows)
        dest_table[0, dest] = first * BLK
        dest_table[1, dest] = tenant[r]
        first = first + counts[r]
    my_copy.wait()
    mine = mine_s[...]
    for k in range(0, tenants, 2):
        pair = min(2, tenants - k)
        maps = jnp.concatenate(
            [sel_s[:, j * 16 : (j + 1) * 16, :].reshape(local, rank2) for j in range(k, k + pair)],
            axis=1,
        )
        product = jnp.dot(mine, maps, preferred_element_type=jnp.float32)
        for j in range(pair):
            part_s[k + j, :tokens] = product[:, j * rank2 : (j + 1) * rank2]
            part_s[k + j, tokens:] = jnp.zeros((BLK, rank2), jnp.float32)

    total = jnp.zeros((tokens, features), jnp.float32)
    for c in range(chunks):
        h_copies[c].wait()
        w_copies[c].wait()
        total = total + lax.dot_general(
            h_s[c], w_s[c], (((1,), (1,)), ((), ())), preferred_element_type=jnp.float32
        )
    base_s[tokens:] = jnp.zeros((BLK, HD), jnp.float32)
    if features < HD:
        base_s[...] = jnp.zeros_like(base_s)
    base_s[:tokens, :features] = total

    up_copy.wait()
    for dest in range(devices):
        start = pl.multiple_of(dest_table[0, dest], BLK)
        who = dest_table[1, dest]
        out[dest, :CAPT, :] = part_s[who, pl.ds(start, CAPT), :].astype(out.dtype)
        out[dest, CAPT : 2 * CAPT, :] = base_s[pl.ds(start, CAPT), :].astype(out.dtype)
        if features < HD:
            out[dest, 2 * CAPT :, :] = jnp.zeros((out.shape[1] - 2 * CAPT, HD), out.dtype)
        out[dest, 2 * CAPT :, :features] = u_s[table[who]]


NT = (((1,), (1,)), ((), ()))


def gather_queries(query, k, group, steps, stride):
    return jnp.concatenate(
        [query[pl.ds(s * stride + k * group, group), :] for s in range(steps)], axis=0
    )


def cached_kernel(
    lengths, counts, last, placement, cache, query, steps_kv, acc, top_out, total_out, fresh_ok,
):
    dec_rows, ctx, kv_width = cache.shape
    half_width = kv_width // 2
    step_rows = KVH * dec_rows
    steps = steps_kv.shape[0] // (2 * step_rows)
    group = HEADS // KVH * dec_rows
    q_rows = steps * group
    stride = HEADS * dec_rows

    row = lax.broadcasted_iota(jnp.int32, (q_rows, ctx), 0)
    col = lax.broadcasted_iota(jnp.int32, (q_rows, ctx), 1)
    row_slot = mod(row, dec_rows)
    cache_ok = [(row_slot == g) & (col < lengths[g]) for g in range(dec_rows)]
    row = lax.broadcasted_iota(jnp.int32, (q_rows, steps * step_rows), 0)
    col = lax.broadcasted_iota(jnp.int32, (q_rows, steps * step_rows), 1)
    step_ok = (mod(row, dec_rows) == mod(col, dec_rows)) & (div(col, step_rows) <= div(row, group))
    step_head = div(mod(col, step_rows), dec_rows)
    step_keys, step_values = (
        jnp.concatenate(
            [steps_kv[pl.ds((2 * s + half) * step_rows, step_rows), :] for s in range(steps)], axis=0
        )
        for half in range(2)
    )

    scale = HD ** (-0.5)
    for k in range(KVH):
        lanes = pl.ds(k * HD, HD)
        vlanes = pl.ds(half_width + k * HD, HD)
        q = gather_queries(query, k, group, steps, stride)
        keys = [cache[g, :, lanes] for g in range(dec_rows)] + [step_keys]
        values = [cache[g, :, vlanes] for g in range(dec_rows)] + [step_values]
        scores = [
            jnp.where(
                ok,
                lax.dot_general(q, key, NT, preferred_element_type=jnp.float32) * scale,
                NEG_LARGE,
            )
            for ok, key in zip(cache_ok + [step_ok & (step_head == k)], keys)
        ]
        top = functools.reduce(jnp.maximum, [jnp.max(s, axis=1, keepdims=True) for s in scores])
        weights = [jnp.exp(s - top) for s in scores]
        total = sum(jnp.sum(w, axis=1, keepdims=True) for w in weights)
        mixed = sum(
            jnp.dot(w.astype(jnp.bfloat16), v, preferred_element_type=jnp.float32)
            for w, v in zip(weights, values)
        )
        for s in range(steps):
            here = pl.ds(s * stride + k * group, group)
            part = slice(s * group, (s + 1) * group)
            acc[here, :] = mixed[part]
            top_out[here, :] = jnp.broadcast_to(top[part], (group, HD))
            total_out[here, :] = jnp.broadcast_to(total[part], (group, HD))

    my_slot = jnp.int32(-1)
    my_length = jnp.int32(0)
    for r in range(placement.shape[0]):
        hit = div(placement[r], dec_rows) == lax.axis_index("tensor")
        my_slot = jnp.where(hit, mod(placement[r], dec_rows), my_slot)
        my_length = jnp.where(hit, (counts[r] - 1) * BLK + last[r], my_length)
    row = lax.broadcasted_iota(jnp.int32, fresh_ok.shape, 0)
    col = lax.broadcasted_iota(jnp.int32, fresh_ok.shape, 1)
    ok = (
        (mod(div(row, group), KVH) == div(col, CAPT))
        & (mod(row, dec_rows) == my_slot)
        & (mod(col, CAPT) < my_length)
    )
    fresh_ok[...] = jnp.where(ok, jnp.float32(1), jnp.float32(0))


def merge_kernel(features, box, acc, top_in, total_in, fresh_ok, query, out):
    devices = box.shape[0]
    rank = box.shape[1] - 2 * CAPT
    shrunk = box[0, :CAPT].astype(jnp.float32)
    for i in range(1, devices):
        shrunk = shrunk + box[i, :CAPT].astype(jnp.float32)
    shrunk = shrunk.astype(jnp.bfloat16)
    halves = (shrunk[:, :rank], shrunk[:, rank:])
    pieces = HD // features

    def fresh(i):
        base = [box[i * pieces + p, CAPT : 2 * CAPT, :features] for p in range(pieces)]
        ups = [box[i * pieces + p, 2 * CAPT :, :features] for p in range(pieces)]
        base = base[0] if pieces == 1 else jnp.concatenate(base, axis=1)
        ups = ups[0] if pieces == 1 else jnp.concatenate(ups, axis=1)
        delta = jnp.dot(halves[i // KVH], ups, preferred_element_type=jnp.float32)
        return (base.astype(jnp.float32) + ADAPTER_SCALE * delta).astype(jnp.bfloat16)

    keys = jnp.concatenate([fresh(k) for k in range(KVH)], axis=0)
    values = jnp.concatenate([fresh(KVH + k) for k in range(KVH)], axis=0)
    scale = HD ** (-0.5)
    part = 128
    for c in range(out.shape[0] // part):
        here = pl.ds(c * part, part)
        s = lax.dot_general(query[here, :], keys, NT, preferred_element_type=jnp.float32)
        s = jnp.where(fresh_ok[here, :] > 0, s * scale, NEG_LARGE)
        old = top_in[here, :]
        top = jnp.maximum(old, jnp.max(s, axis=1, keepdims=True))
        fade = jnp.exp(old - top)
        w = jnp.exp(s - top)
        total = total_in[here, :] * fade + jnp.sum(w, axis=1, keepdims=True)
        mixed = acc[here, :] * fade + jnp.dot(
            w.astype(jnp.bfloat16), values, preferred_element_type=jnp.float32
        )
        out[here, :] = (mixed / total).astype(jnp.bfloat16)


def body(
    hidden,
    key_value_weight,
    adapter_down_weight,
    adapter_up_weight,
    tenant,
    tenant_page_table,
    request_block_count,
    last_block_tokens,
    placement,
    key_value_cache,
    context_length,
    decode_step_query,
    step_key_value,
):
    devices = lax.axis_size("tensor")
    tokens, width = hidden.shape
    features = key_value_weight.shape[0]
    local, pages, rank2 = adapter_down_weight.shape
    rank = adapter_up_weight.shape[2]
    tenants = tenant_page_table.shape[0]
    dec_rows, ctx, kv_width = key_value_cache.shape
    steps = step_key_value.shape[0]
    heads2 = kv_width // HD
    chunks = 4
    up_by_page = jnp.transpose(adapter_up_weight, (1, 2, 0))
    rows = 2 * CAPT + rank
    outgoing = pl.pallas_call(
        functools.partial(project_kernel, dec_rows, chunks, devices),
        out_shape=pltpu.VMEM((devices, rows, HD), WIRE),
        in_specs=[ANY_SPEC] * 8,
        out_specs=VMEM_SPEC,
        scratch_shapes=[
            pltpu.SMEM(tenant.shape, jnp.int32),
            pltpu.SMEM(tenant_page_table.shape, jnp.int32),
            pltpu.SMEM(request_block_count.shape, jnp.int32),
            pltpu.SMEM(placement.shape, jnp.int32),
            pltpu.VMEM((chunks, tokens, width // chunks), jnp.bfloat16),
            pltpu.VMEM((chunks, features, width // chunks), jnp.bfloat16),
            pltpu.VMEM((local, pages, rank2), jnp.bfloat16),
            pltpu.VMEM((tokens, local), jnp.bfloat16),
            pltpu.VMEM((pages, rank, features), jnp.bfloat16),
            pltpu.VMEM((local // 16, tenants * 16, rank2), jnp.bfloat16),
            pltpu.VMEM((tenants, tokens + BLK, rank2), jnp.float32),
            pltpu.VMEM((tokens + BLK, HD), jnp.float32),
            pltpu.SMEM((2, devices), jnp.int32),
            pltpu.SemaphoreType.DMA((chunks, 4)),
            pltpu.SemaphoreType.DMA((4,)),
        ],
        compiler_params=pltpu.CompilerParams(vmem_limit_bytes=PROJECT_VMEM),
        name="project",
    )(
        *(
            pltpu.with_memory_space_constraint(x, pltpu.HBM)
            for x in (
                tenant, tenant_page_table, request_block_count, placement,
                hidden, key_value_weight, adapter_down_weight, up_by_page,
            )
        )
    )
    arrived = lax.all_to_all(outgoing, "tensor", split_axis=0, concat_axis=0, tiled=True)

    query = decode_step_query.reshape(steps, dec_rows, HEADS, HD)
    query = query.transpose(0, 2, 1, 3).reshape(steps * HEADS * dec_rows, HD)
    steps_kv = step_key_value.reshape(steps, dec_rows, heads2, HD)
    steps_kv = steps_kv.transpose(0, 2, 1, 3).reshape(steps * heads2 * dec_rows, HD)
    state = jax.ShapeDtypeStruct((steps * HEADS * dec_rows, HD), jnp.float32)
    acc, top, total, fresh_ok = pl.pallas_call(
        cached_kernel,
        out_shape=(state,) * 4,
        in_specs=[SMEM_SPEC] * 4 + [VMEM_SPEC] * 3,
        out_specs=(VMEM_SPEC,) * 4,
        compiler_params=pltpu.CompilerParams(vmem_limit_bytes=ATTEND_VMEM),
        name="cached",
    )(
        context_length, request_block_count, last_block_tokens, placement,
        key_value_cache, query, steps_kv,
    )
    attended = pl.pallas_call(
        functools.partial(merge_kernel, features),
        out_shape=jax.ShapeDtypeStruct((steps * HEADS * dec_rows, HD), jnp.bfloat16),
        in_specs=[VMEM_SPEC] * 6,
        out_specs=VMEM_SPEC,
        compiler_params=pltpu.CompilerParams(vmem_limit_bytes=ATTEND_VMEM),
        name="merge",
    )(arrived, acc, top, total, fresh_ok, query)
    attended = attended.reshape(steps, HEADS, dec_rows, HD).transpose(0, 2, 1, 3)
    return attended.reshape(steps, dec_rows, HEADS * HD)


def solution(mesh):
    return jax.shard_map(
        body,
        mesh=mesh,
        in_specs=(
            P("parts", None),
            P("tensor", None),
            P("tensor", None, None),
            P("tensor", None, None),
            P("parts"),
            P(),
            P("parts"),
            P("parts"),
            P("parts"),
            P(("parts", "tensor"), None, None),
            P(("parts", "tensor")),
            P(None, ("parts", "tensor"), None),
            P(None, ("parts", "tensor"), None),
        ),
        out_specs=P(None, ("parts", "tensor"), None),
        check_vma=False,
    )
```

```python
import functools

import jax
import jax.numpy as jnp
from jax import lax
from jax.experimental import pallas as pl
from jax.experimental.pallas import tpu as pltpu
from jax.sharding import PartitionSpec as P

HEADS = 64
KVH = 8
HD = 128
BLK = 8
MOSTB = 2
CAPT = MOSTB * BLK
ADAPTER_SCALE = 0.5
NEG_LARGE = -1e30
PROJECT_VMEM = 32 * 1024 * 1024
ATTEND_VMEM = 16 * 1024 * 1024
WIRE = jnp.bfloat16

SMEM_SPEC = pl.BlockSpec(memory_space=pltpu.SMEM)
VMEM_SPEC = pl.BlockSpec(memory_space=pltpu.VMEM)
ANY_SPEC = pl.BlockSpec(memory_space=pl.ANY)


def div(x, n):
    shift = n.bit_length() - 1
    return lax.shift_right_logical(x, shift) if n == 1 << shift else x // n


def mod(x, n):
    return x & (n - 1) if n & (n - 1) == 0 else x % n


def project_kernel(
    dec_rows, d_chunks, chunks, devices, tenant_h, table_h, counts_h, placement_h, hidden, weight, down, up, out,
    tenant, table, counts, placement,
    h_s, w_s, d_s, mine_s, u_s, sel_s, part_s, base_s, dest_table, sems, d_sems, int_sems,
):
    tokens, width = hidden.shape
    features = weight.shape[0]
    local, pages, rank2 = down.shape
    tenants = table.shape[0]
    requests = tenant.shape[0]
    me = lax.axis_index("tensor")
    d_step = local // d_chunks
    step = width // chunks

    int_copies = [
        pltpu.make_async_copy(src, dst, int_sems.at[i])
        for i, (src, dst) in enumerate(
            ((table_h, table), (tenant_h, tenant), (counts_h, counts), (placement_h, placement))
        )
    ]
    for copy in int_copies:
        copy.start()
    d_copies = [
        pltpu.make_async_copy(
            down.at[pl.ds(c * d_step, d_step)], d_s.at[pl.ds(c * d_step, d_step)], d_sems.at[c])
        for c in range(d_chunks)
    ]
    h_copies = [
        pltpu.make_async_copy(hidden.at[:, pl.ds(c * step, step)], h_s.at[c], sems.at[c, 0])
        for c in range(chunks)
    ]
    w_copies = [
        pltpu.make_async_copy(weight.at[:, pl.ds(c * step, step)], w_s.at[c], sems.at[c, 1])
        for c in range(chunks)
    ]
    my_copy = pltpu.make_async_copy(
        hidden.at[:, pl.ds(pl.multiple_of(me * local, 128), local)], mine_s, d_sems.at[d_chunks]
    )
    up_copy = pltpu.make_async_copy(up, u_s, d_sems.at[d_chunks + 1])
    for copy in d_copies + [my_copy, up_copy]:
        copy.start()
    for c in range(chunks):
        h_copies[c].start()
        w_copies[c].start()

    int_copies[0].wait()
    rows = lax.broadcasted_iota(jnp.int32, (tenants * 16, 16 * pages), 0)
    cols = lax.broadcasted_iota(jnp.int32, (tenants * 16, 16 * pages), 1)
    page_of_row = jnp.zeros_like(rows)
    for k in range(tenants):
        page_of_row = jnp.where(div(rows, 16) == k, table[k], page_of_row)
    pick = (mod(rows, 16) == div(cols, pages)) & (mod(cols, pages) == page_of_row)
    pick = jnp.where(pick, jnp.float32(1), jnp.float32(0)).astype(jnp.bfloat16)

    for c in range(d_chunks):
        d_copies[c].wait()
        for b in range(c * d_step // 16, (c + 1) * d_step // 16, 2):
            block = jnp.concatenate(
                [d_s[pl.ds((b + i) * 16, 16)].reshape(16 * pages, rank2) for i in range(2)], axis=1
            )
            chosen = jnp.dot(pick, block, preferred_element_type=jnp.float32)
            for i in range(2):
                sel_s[b + i] = chosen[:, i * rank2 : (i + 1) * rank2].astype(jnp.bfloat16)
    for copy in int_copies[1:]:
        copy.wait()
    for dest in range(devices):
        dest_table[0, dest] = 0
        dest_table[1, dest] = 0
    first = jnp.int32(0)
    for r in range(requests):
        dest = div(placement[r], dec_rows)
        dest_table[0, dest] = first * BLK
        dest_table[1, dest] = tenant[r]
        first = first + counts[r]
    my_copy.wait()
    mine = mine_s[...]
    for k in range(0, tenants, 2):
        pair = min(2, tenants - k)
        maps = jnp.concatenate(
            [sel_s[:, j * 16 : (j + 1) * 16, :].reshape(local, rank2) for j in range(k, k + pair)],
            axis=1,
        )
        product = jnp.dot(mine, maps, preferred_element_type=jnp.float32)
        for j in range(pair):
            part_s[k + j, :tokens] = product[:, j * rank2 : (j + 1) * rank2]
            part_s[k + j, tokens:] = jnp.zeros((BLK, rank2), jnp.float32)

    up_copy.wait()
    for dest in range(devices):
        start = pl.multiple_of(dest_table[0, dest], BLK)
        who = dest_table[1, dest]
        out[dest, :CAPT, :] = part_s[who, pl.ds(start, CAPT), :].astype(out.dtype)
        if features < HD:
            out[dest, 2 * CAPT :, :] = jnp.zeros((out.shape[1] - 2 * CAPT, HD), out.dtype)
        out[dest, 2 * CAPT :, :features] = u_s[table[who]]

    total = jnp.zeros((tokens, features), jnp.float32)
    for c in range(chunks):
        h_copies[c].wait()
        w_copies[c].wait()
        total = total + lax.dot_general(h_s[c], w_s[c], NT, preferred_element_type=jnp.float32)
    base_s[tokens:] = jnp.zeros((BLK, HD), jnp.float32)
    if features < HD:
        base_s[...] = jnp.zeros_like(base_s)
    base_s[:tokens, :features] = total
    for dest in range(devices):
        start = pl.multiple_of(dest_table[0, dest], BLK)
        out[dest, CAPT : 2 * CAPT, :] = base_s[pl.ds(start, CAPT), :].astype(out.dtype)


NT = (((1,), (1,)), ((), ()))


def gather_queries(query, k, group, steps, stride):
    return jnp.concatenate(
        [query[pl.ds(s * stride + k * group, group), :] for s in range(steps)], axis=0
    )


def cached_kernel(
    lengths, counts, last, placement, cache, query, steps_kv, acc, top_out, total_out, fresh_ok,
):
    dec_rows, ctx, kv_width = cache.shape
    half_width = kv_width // 2
    step_rows = KVH * dec_rows
    steps = steps_kv.shape[0] // (2 * step_rows)
    group = HEADS // KVH * dec_rows
    q_rows = steps * group
    stride = HEADS * dec_rows

    row = lax.broadcasted_iota(jnp.int32, (q_rows, ctx), 0)
    col = lax.broadcasted_iota(jnp.int32, (q_rows, ctx), 1)
    row_slot = mod(row, dec_rows)
    cache_ok = [(row_slot == g) & (col < lengths[g]) for g in range(dec_rows)]
    row = lax.broadcasted_iota(jnp.int32, (q_rows, steps * step_rows), 0)
    col = lax.broadcasted_iota(jnp.int32, (q_rows, steps * step_rows), 1)
    step_ok = (mod(row, dec_rows) == mod(col, dec_rows)) & (div(col, step_rows) <= div(row, group))
    step_head = div(mod(col, step_rows), dec_rows)
    step_keys, step_values = (
        jnp.concatenate(
            [steps_kv[pl.ds((2 * s + half) * step_rows, step_rows), :] for s in range(steps)], axis=0
        )
        for half in range(2)
    )

    scale = HD ** (-0.5)
    for k in range(KVH):
        lanes = pl.ds(k * HD, HD)
        vlanes = pl.ds(half_width + k * HD, HD)
        q = gather_queries(query, k, group, steps, stride)
        keys = [cache[g, :, lanes] for g in range(dec_rows)] + [step_keys]
        values = [cache[g, :, vlanes] for g in range(dec_rows)] + [step_values]
        scores = [
            jnp.where(
                ok,
                lax.dot_general(q, key, NT, preferred_element_type=jnp.float32) * scale,
                NEG_LARGE,
            )
            for ok, key in zip(cache_ok + [step_ok & (step_head == k)], keys)
        ]
        top = functools.reduce(jnp.maximum, [jnp.max(s, axis=1, keepdims=True) for s in scores])
        weights = [jnp.exp(s - top) for s in scores]
        total = sum(jnp.sum(w, axis=1, keepdims=True) for w in weights)
        mixed = sum(
            jnp.dot(w.astype(jnp.bfloat16), v, preferred_element_type=jnp.float32)
            for w, v in zip(weights, values)
        )
        for s in range(steps):
            here = pl.ds(s * stride + k * group, group)
            part = slice(s * group, (s + 1) * group)
            acc[here, :] = mixed[part]
            top_out[here, :] = jnp.broadcast_to(top[part], (group, HD))
            total_out[here, :] = jnp.broadcast_to(total[part], (group, HD))

    my_slot = jnp.int32(-1)
    my_length = jnp.int32(0)
    for r in range(placement.shape[0]):
        hit = div(placement[r], dec_rows) == lax.axis_index("tensor")
        my_slot = jnp.where(hit, mod(placement[r], dec_rows), my_slot)
        my_length = jnp.where(hit, (counts[r] - 1) * BLK + last[r], my_length)
    row = lax.broadcasted_iota(jnp.int32, fresh_ok.shape, 0)
    col = lax.broadcasted_iota(jnp.int32, fresh_ok.shape, 1)
    ok = (
        (mod(div(row, group), KVH) == div(col, CAPT))
        & (mod(row, dec_rows) == my_slot)
        & (mod(col, CAPT) < my_length)
    )
    fresh_ok[...] = jnp.where(ok, jnp.float32(1), jnp.float32(0))


def merge_kernel(features, box, acc, top_in, total_in, fresh_ok, query, out, result, sems):
    devices = box.shape[0]
    rank = box.shape[1] - 2 * CAPT
    terms = [box[i, :CAPT].astype(jnp.float32) for i in range(devices)]
    while len(terms) > 1:
        pairs = [a + b for a, b in zip(terms[::2], terms[1::2])]
        terms = pairs + terms[2 * len(pairs) :]
    shrunk = terms[0].astype(jnp.bfloat16)
    halves = (shrunk[:, :rank], shrunk[:, rank:])
    pieces = HD // features

    def rows(i, first, count):
        parts = [box[i * pieces + p, first : first + count, :features] for p in range(pieces)]
        return parts[0] if pieces == 1 else jnp.concatenate(parts, axis=1)

    def fresh(first):
        made = []
        for i in range(first, first + KVH, 2):
            ups = jnp.concatenate([rows(i + j, 2 * CAPT, rank) for j in range(2)], axis=1)
            delta = jnp.dot(halves[first // KVH], ups, preferred_element_type=jnp.float32)
            for j in range(2):
                base = rows(i + j, CAPT, CAPT).astype(jnp.float32)
                both = base + ADAPTER_SCALE * delta[:, j * HD : (j + 1) * HD]
                made.append(both.astype(jnp.bfloat16))
        return jnp.concatenate(made, axis=0)

    keys, values = fresh(0), fresh(KVH)
    scale = HD ** (-0.5)
    part = out.shape[0] // sems.shape[0]
    copies = []
    for c in range(sems.shape[0]):
        here = pl.ds(c * part, part)
        s = lax.dot_general(query[here, :], keys, NT, preferred_element_type=jnp.float32)
        s = jnp.where(fresh_ok[here, :] > 0, s * scale, NEG_LARGE)
        old = top_in[here, :]
        top = jnp.maximum(old, jnp.max(s, axis=1, keepdims=True))
        fade = jnp.exp(old - top)
        w = jnp.exp(s - top)
        total = total_in[here, :] * fade + jnp.sum(w, axis=1, keepdims=True)
        mixed = acc[here, :] * fade + jnp.dot(
            w.astype(jnp.bfloat16), values, preferred_element_type=jnp.float32
        )
        result[here, :] = (mixed / total).astype(jnp.bfloat16)
        copies.append(pltpu.make_async_copy(result.at[here, :], out.at[here, :], sems.at[c]))
        copies[c].start()
    for copy in copies:
        copy.wait()


def body(
    hidden,
    key_value_weight,
    adapter_down_weight,
    adapter_up_weight,
    tenant,
    tenant_page_table,
    request_block_count,
    last_block_tokens,
    placement,
    key_value_cache,
    context_length,
    decode_step_query,
    step_key_value,
):
    devices = lax.axis_size("tensor")
    tokens, width = hidden.shape
    features = key_value_weight.shape[0]
    local, pages, rank2 = adapter_down_weight.shape
    rank = adapter_up_weight.shape[2]
    tenants = tenant_page_table.shape[0]
    dec_rows, ctx, kv_width = key_value_cache.shape
    steps = step_key_value.shape[0]
    heads2 = kv_width // HD
    d_chunks, chunks = 4, 8
    up_by_page = jnp.transpose(adapter_up_weight, (1, 2, 0))
    rows = 2 * CAPT + rank
    outgoing = pl.pallas_call(
        functools.partial(project_kernel, dec_rows, d_chunks, chunks, devices),
        out_shape=pltpu.VMEM((devices, rows, HD), WIRE),
        in_specs=[ANY_SPEC] * 8,
        out_specs=VMEM_SPEC,
        scratch_shapes=[
            pltpu.SMEM(tenant.shape, jnp.int32),
            pltpu.SMEM(tenant_page_table.shape, jnp.int32),
            pltpu.SMEM(request_block_count.shape, jnp.int32),
            pltpu.SMEM(placement.shape, jnp.int32),
            pltpu.VMEM((chunks, tokens, width // chunks), jnp.bfloat16),
            pltpu.VMEM((chunks, features, width // chunks), jnp.bfloat16),
            pltpu.VMEM((local, pages, rank2), jnp.bfloat16),
            pltpu.VMEM((tokens, local), jnp.bfloat16),
            pltpu.VMEM((pages, rank, features), jnp.bfloat16),
            pltpu.VMEM((local // 16, tenants * 16, rank2), jnp.bfloat16),
            pltpu.VMEM((tenants, tokens + BLK, rank2), jnp.float32),
            pltpu.VMEM((tokens + BLK, HD), jnp.float32),
            pltpu.SMEM((2, devices), jnp.int32),
            pltpu.SemaphoreType.DMA((chunks, 2)),
            pltpu.SemaphoreType.DMA((d_chunks + 2,)),
            pltpu.SemaphoreType.DMA((4,)),
        ],
        compiler_params=pltpu.CompilerParams(vmem_limit_bytes=PROJECT_VMEM),
        name="project",
    )(
        *(
            pltpu.with_memory_space_constraint(x, pltpu.HBM)
            for x in (
                tenant, tenant_page_table, request_block_count, placement,
                hidden, key_value_weight, adapter_down_weight, up_by_page,
            )
        )
    )
    arrived = lax.all_to_all(outgoing, "tensor", split_axis=0, concat_axis=0, tiled=True)

    query = decode_step_query.reshape(steps, dec_rows, HEADS, HD)
    query = query.transpose(0, 2, 1, 3).reshape(steps * HEADS * dec_rows, HD)
    steps_kv = step_key_value.reshape(steps, dec_rows, heads2, HD)
    steps_kv = steps_kv.transpose(0, 2, 1, 3).reshape(steps * heads2 * dec_rows, HD)
    state = jax.ShapeDtypeStruct((steps * HEADS * dec_rows, HD), jnp.float32)
    acc, top, total, fresh_ok = pl.pallas_call(
        cached_kernel,
        out_shape=(state,) * 4,
        in_specs=[SMEM_SPEC] * 4 + [VMEM_SPEC] * 3,
        out_specs=(VMEM_SPEC,) * 4,
        compiler_params=pltpu.CompilerParams(vmem_limit_bytes=ATTEND_VMEM),
        name="cached",
    )(
        context_length, request_block_count, last_block_tokens, placement,
        key_value_cache, query, steps_kv,
    )
    attended = pl.pallas_call(
        functools.partial(merge_kernel, features),
        out_shape=jax.ShapeDtypeStruct((steps * HEADS * dec_rows, HD), jnp.bfloat16),
        in_specs=[VMEM_SPEC] * 6,
        out_specs=ANY_SPEC,
        scratch_shapes=[
            pltpu.VMEM((steps * HEADS * dec_rows, HD), jnp.bfloat16),
            pltpu.SemaphoreType.DMA((steps,)),
        ],
        compiler_params=pltpu.CompilerParams(vmem_limit_bytes=ATTEND_VMEM),
        name="merge",
    )(arrived, acc, top, total, fresh_ok, query)
    attended = attended.reshape(steps, HEADS, dec_rows, HD).transpose(0, 2, 1, 3)
    return attended.reshape(steps, dec_rows, HEADS * HD)


def solution(mesh):
    return jax.shard_map(
        body,
        mesh=mesh,
        in_specs=(
            P("parts", None),
            P("tensor", None),
            P("tensor", None, None),
            P("tensor", None, None),
            P("parts"),
            P(),
            P("parts"),
            P("parts"),
            P("parts"),
            P(("parts", "tensor"), None, None),
            P(("parts", "tensor")),
            P(None, ("parts", "tensor"), None),
            P(None, ("parts", "tensor"), None),
        ),
        out_specs=P(None, ("parts", "tensor"), None),
        check_vma=False,
    )
```

```python
import functools

import jax
import jax.numpy as jnp
from jax import lax
from jax.experimental import pallas as pl
from jax.experimental.pallas import tpu as pltpu
from jax.sharding import PartitionSpec as P

HEADS = 64
KVH = 8
HD = 128
BLK = 8
MOSTB = 2
CAPT = MOSTB * BLK
ADAPTER_SCALE = 0.5
NEG_LARGE = -1e30
PROJECT_VMEM = 32 * 1024 * 1024
ATTEND_VMEM = 16 * 1024 * 1024
WIRE = jnp.bfloat16

SMEM_SPEC = pl.BlockSpec(memory_space=pltpu.SMEM)
VMEM_SPEC = pl.BlockSpec(memory_space=pltpu.VMEM)
ANY_SPEC = pl.BlockSpec(memory_space=pl.ANY)


def div(x, n):
    shift = n.bit_length() - 1
    return lax.shift_right_logical(x, shift) if n == 1 << shift else x // n


def mod(x, n):
    return x & (n - 1) if n & (n - 1) == 0 else x % n


def project_kernel(
    dec_rows, d_chunks, chunks, devices, tenant_h, table_h, counts_h, placement_h, hidden, weight, down, up, out,
    tenant, table, counts, placement,
    h_s, w_s, d_s, mine_s, u_s, sel_s, part_s, base_s, dest_table, sems, d_sems, int_sems,
):
    tokens, width = hidden.shape
    features = weight.shape[0]
    local, pages, rank2 = down.shape
    tenants = table.shape[0]
    requests = tenant.shape[0]
    me = lax.axis_index("tensor")
    d_step = local // d_chunks
    step = width // chunks

    int_copies = [
        pltpu.make_async_copy(src, dst, int_sems.at[i])
        for i, (src, dst) in enumerate(
            ((table_h, table), (tenant_h, tenant), (counts_h, counts), (placement_h, placement))
        )
    ]
    for copy in int_copies:
        copy.start()
    d_copies = [
        pltpu.make_async_copy(
            down.at[pl.ds(c * d_step, d_step)], d_s.at[pl.ds(c * d_step, d_step)], d_sems.at[c])
        for c in range(d_chunks)
    ]
    h_copies = [
        pltpu.make_async_copy(hidden.at[:, pl.ds(c * step, step)], h_s.at[c], sems.at[c, 0])
        for c in range(chunks)
    ]
    w_copies = [
        pltpu.make_async_copy(weight.at[:, pl.ds(c * step, step)], w_s.at[c], sems.at[c, 1])
        for c in range(chunks)
    ]
    my_copy = pltpu.make_async_copy(
        hidden.at[:, pl.ds(pl.multiple_of(me * local, 128), local)], mine_s, d_sems.at[d_chunks]
    )
    up_copy = pltpu.make_async_copy(up, u_s, d_sems.at[d_chunks + 1])
    for copy in d_copies + [my_copy, up_copy]:
        copy.start()
    for c in range(chunks):
        h_copies[c].start()
        w_copies[c].start()

    int_copies[0].wait()
    rows = lax.broadcasted_iota(jnp.int32, (tenants * 16, 16 * pages), 0)
    cols = lax.broadcasted_iota(jnp.int32, (tenants * 16, 16 * pages), 1)
    page_of_row = jnp.zeros_like(rows)
    for k in range(tenants):
        page_of_row = jnp.where(div(rows, 16) == k, table[k], page_of_row)
    pick = (mod(rows, 16) == div(cols, pages)) & (mod(cols, pages) == page_of_row)
    pick = jnp.where(pick, jnp.float32(1), jnp.float32(0)).astype(jnp.bfloat16)

    for c in range(d_chunks):
        d_copies[c].wait()
        for b in range(c * d_step // 16, (c + 1) * d_step // 16, 2):
            block = jnp.concatenate(
                [d_s[pl.ds((b + i) * 16, 16)].reshape(16 * pages, rank2) for i in range(2)], axis=1
            )
            chosen = jnp.dot(pick, block, preferred_element_type=jnp.float32)
            for i in range(2):
                sel_s[b + i] = chosen[:, i * rank2 : (i + 1) * rank2].astype(jnp.bfloat16)
    for copy in int_copies[1:]:
        copy.wait()
    for dest in range(devices):
        dest_table[0, dest] = 0
        dest_table[1, dest] = 0
    first = jnp.int32(0)
    for r in range(requests):
        dest = div(placement[r], dec_rows)
        dest_table[0, dest] = first * BLK
        dest_table[1, dest] = tenant[r]
        first = first + counts[r]
    my_copy.wait()
    mine = mine_s[...]
    for k in range(0, tenants, 2):
        pair = min(2, tenants - k)
        maps = jnp.concatenate(
            [sel_s[:, j * 16 : (j + 1) * 16, :].reshape(local, rank2) for j in range(k, k + pair)],
            axis=1,
        )
        product = jnp.dot(mine, maps, preferred_element_type=jnp.float32)
        for j in range(pair):
            part_s[k + j, :tokens] = product[:, j * rank2 : (j + 1) * rank2]
            part_s[k + j, tokens:] = jnp.zeros((BLK, rank2), jnp.float32)

    total = jnp.zeros((tokens, features), jnp.float32)
    for c in range(chunks):
        h_copies[c].wait()
        w_copies[c].wait()
        total = total + lax.dot_general(h_s[c], w_s[c], NT, preferred_element_type=jnp.float32)
    base_s[tokens:] = jnp.zeros((BLK, HD), jnp.float32)
    if features < HD:
        base_s[...] = jnp.zeros_like(base_s)
    base_s[:tokens, :features] = total
    up_copy.wait()
    for dest in range(devices):
        start = pl.multiple_of(dest_table[0, dest], BLK)
        who = dest_table[1, dest]
        out[dest, :CAPT, :] = part_s[who, pl.ds(start, CAPT), :].astype(out.dtype)
        out[dest, CAPT : 2 * CAPT, :] = base_s[pl.ds(start, CAPT), :].astype(out.dtype)
        if features < HD:
            out[dest, 2 * CAPT :, :] = jnp.zeros((out.shape[1] - 2 * CAPT, HD), out.dtype)
        out[dest, 2 * CAPT :, :features] = u_s[table[who]]


NT = (((1,), (1,)), ((), ()))


def gather_queries(query, k, group, steps, stride):
    return jnp.concatenate(
        [query[pl.ds(s * stride + k * group, group), :] for s in range(steps)], axis=0
    )


def cached_kernel(
    lengths, counts, last, placement, cache, query, steps_kv, acc, top_out, total_out, fresh_ok,
):
    dec_rows, ctx, kv_width = cache.shape
    half_width = kv_width // 2
    step_rows = KVH * dec_rows
    steps = steps_kv.shape[0] // (2 * step_rows)
    group = HEADS // KVH * dec_rows
    q_rows = steps * group
    stride = HEADS * dec_rows

    row = lax.broadcasted_iota(jnp.int32, (q_rows, ctx), 0)
    col = lax.broadcasted_iota(jnp.int32, (q_rows, ctx), 1)
    row_slot = mod(row, dec_rows)
    cache_ok = [(row_slot == g) & (col < lengths[g]) for g in range(dec_rows)]
    row = lax.broadcasted_iota(jnp.int32, (q_rows, steps * step_rows), 0)
    col = lax.broadcasted_iota(jnp.int32, (q_rows, steps * step_rows), 1)
    step_ok = (mod(row, dec_rows) == mod(col, dec_rows)) & (div(col, step_rows) <= div(row, group))
    step_head = div(mod(col, step_rows), dec_rows)
    step_keys, step_values = (
        jnp.concatenate(
            [steps_kv[pl.ds((2 * s + half) * step_rows, step_rows), :] for s in range(steps)], axis=0
        )
        for half in range(2)
    )

    scale = HD ** (-0.5)
    for k in range(KVH):
        lanes = pl.ds(k * HD, HD)
        vlanes = pl.ds(half_width + k * HD, HD)
        q = gather_queries(query, k, group, steps, stride)
        keys = [cache[g, :, lanes] for g in range(dec_rows)] + [step_keys]
        values = [cache[g, :, vlanes] for g in range(dec_rows)] + [step_values]
        scores = [
            jnp.where(
                ok,
                lax.dot_general(q, key, NT, preferred_element_type=jnp.float32) * scale,
                NEG_LARGE,
            )
            for ok, key in zip(cache_ok + [step_ok & (step_head == k)], keys)
        ]
        top = functools.reduce(jnp.maximum, [jnp.max(s, axis=1, keepdims=True) for s in scores])
        weights = [jnp.exp(s - top) for s in scores]
        total = sum(jnp.sum(w, axis=1, keepdims=True) for w in weights)
        mixed = sum(
            jnp.dot(w.astype(jnp.bfloat16), v, preferred_element_type=jnp.float32)
            for w, v in zip(weights, values)
        )
        for s in range(steps):
            here = pl.ds(s * stride + k * group, group)
            part = slice(s * group, (s + 1) * group)
            acc[here, :] = mixed[part]
            top_out[here, :] = jnp.broadcast_to(top[part], (group, HD))
            total_out[here, :] = jnp.broadcast_to(total[part], (group, HD))

    my_slot = jnp.int32(-1)
    my_length = jnp.int32(0)
    for r in range(placement.shape[0]):
        hit = div(placement[r], dec_rows) == lax.axis_index("tensor")
        my_slot = jnp.where(hit, mod(placement[r], dec_rows), my_slot)
        my_length = jnp.where(hit, (counts[r] - 1) * BLK + last[r], my_length)
    row = lax.broadcasted_iota(jnp.int32, fresh_ok.shape, 0)
    col = lax.broadcasted_iota(jnp.int32, fresh_ok.shape, 1)
    ok = (
        (mod(div(row, group), KVH) == div(col, CAPT))
        & (mod(row, dec_rows) == my_slot)
        & (mod(col, CAPT) < my_length)
    )
    fresh_ok[...] = jnp.where(ok, jnp.float32(1), jnp.float32(0))


def merge_kernel(features, box, acc, top_in, total_in, fresh_ok, query, out, result, sems):
    devices = box.shape[0]
    rank = box.shape[1] - 2 * CAPT
    terms = [box[i, :CAPT].astype(jnp.float32) for i in range(devices)]
    while len(terms) > 1:
        pairs = [a + b for a, b in zip(terms[::2], terms[1::2])]
        terms = pairs + terms[2 * len(pairs) :]
    shrunk = terms[0].astype(jnp.bfloat16)
    halves = (shrunk[:, :rank], shrunk[:, rank:])
    pieces = HD // features

    def rows(i, first, count):
        parts = [box[i * pieces + p, first : first + count, :features] for p in range(pieces)]
        return parts[0] if pieces == 1 else jnp.concatenate(parts, axis=1)

    def fresh(first):
        made = []
        for i in range(first, first + KVH, 2):
            ups = jnp.concatenate([rows(i + j, 2 * CAPT, rank) for j in range(2)], axis=1)
            delta = jnp.dot(halves[first // KVH], ups, preferred_element_type=jnp.float32)
            for j in range(2):
                base = rows(i + j, CAPT, CAPT).astype(jnp.float32)
                both = base + ADAPTER_SCALE * delta[:, j * HD : (j + 1) * HD]
                made.append(both.astype(jnp.bfloat16))
        return jnp.concatenate(made, axis=0)

    keys, values = fresh(0), fresh(KVH)
    scale = HD ** (-0.5)
    part = out.shape[0] // sems.shape[0]
    copies = []
    for c in range(sems.shape[0]):
        here = pl.ds(c * part, part)
        s = lax.dot_general(query[here, :], keys, NT, preferred_element_type=jnp.float32)
        s = jnp.where(fresh_ok[here, :] > 0, s * scale, NEG_LARGE)
        old = top_in[here, :]
        top = jnp.maximum(old, jnp.max(s, axis=1, keepdims=True))
        fade = jnp.exp(old - top)
        w = jnp.exp(s - top)
        total = total_in[here, :] * fade + jnp.sum(w, axis=1, keepdims=True)
        mixed = acc[here, :] * fade + jnp.dot(
            w.astype(jnp.bfloat16), values, preferred_element_type=jnp.float32
        )
        result[here, :] = (mixed / total).astype(jnp.bfloat16)
        copies.append(pltpu.make_async_copy(result.at[here, :], out.at[here, :], sems.at[c]))
        copies[c].start()
    for copy in copies:
        copy.wait()


def body(
    hidden,
    key_value_weight,
    adapter_down_weight,
    adapter_up_weight,
    tenant,
    tenant_page_table,
    request_block_count,
    last_block_tokens,
    placement,
    key_value_cache,
    context_length,
    decode_step_query,
    step_key_value,
):
    devices = lax.axis_size("tensor")
    tokens, width = hidden.shape
    features = key_value_weight.shape[0]
    local, pages, rank2 = adapter_down_weight.shape
    rank = adapter_up_weight.shape[2]
    tenants = tenant_page_table.shape[0]
    dec_rows, ctx, kv_width = key_value_cache.shape
    steps = step_key_value.shape[0]
    heads2 = kv_width // HD
    d_chunks, chunks = 2, 2
    up_by_page = jnp.transpose(adapter_up_weight, (1, 2, 0))
    rows = 2 * CAPT + rank
    outgoing = pl.pallas_call(
        functools.partial(project_kernel, dec_rows, d_chunks, chunks, devices),
        out_shape=pltpu.VMEM((devices, rows, HD), WIRE),
        in_specs=[ANY_SPEC] * 8,
        out_specs=VMEM_SPEC,
        scratch_shapes=[
            pltpu.SMEM(tenant.shape, jnp.int32),
            pltpu.SMEM(tenant_page_table.shape, jnp.int32),
            pltpu.SMEM(request_block_count.shape, jnp.int32),
            pltpu.SMEM(placement.shape, jnp.int32),
            pltpu.VMEM((chunks, tokens, width // chunks), jnp.bfloat16),
            pltpu.VMEM((chunks, features, width // chunks), jnp.bfloat16),
            pltpu.VMEM((local, pages, rank2), jnp.bfloat16),
            pltpu.VMEM((tokens, local), jnp.bfloat16),
            pltpu.VMEM((pages, rank, features), jnp.bfloat16),
            pltpu.VMEM((local // 16, tenants * 16, rank2), jnp.bfloat16),
            pltpu.VMEM((tenants, tokens + BLK, rank2), jnp.float32),
            pltpu.VMEM((tokens + BLK, HD), jnp.float32),
            pltpu.SMEM((2, devices), jnp.int32),
            pltpu.SemaphoreType.DMA((chunks, 2)),
            pltpu.SemaphoreType.DMA((d_chunks + 2,)),
            pltpu.SemaphoreType.DMA((4,)),
        ],
        compiler_params=pltpu.CompilerParams(vmem_limit_bytes=PROJECT_VMEM),
        name="project",
    )(
        *(
            pltpu.with_memory_space_constraint(x, pltpu.HBM)
            for x in (
                tenant, tenant_page_table, request_block_count, placement,
                hidden, key_value_weight, adapter_down_weight, up_by_page,
            )
        )
    )
    arrived = lax.all_to_all(outgoing, "tensor", split_axis=0, concat_axis=0, tiled=True)

    query = decode_step_query.reshape(steps, dec_rows, HEADS, HD)
    query = query.transpose(0, 2, 1, 3).reshape(steps * HEADS * dec_rows, HD)
    steps_kv = step_key_value.reshape(steps, dec_rows, heads2, HD)
    steps_kv = steps_kv.transpose(0, 2, 1, 3).reshape(steps * heads2 * dec_rows, HD)
    state = jax.ShapeDtypeStruct((steps * HEADS * dec_rows, HD), jnp.float32)
    acc, top, total, fresh_ok = pl.pallas_call(
        cached_kernel,
        out_shape=(state,) * 4,
        in_specs=[SMEM_SPEC] * 4 + [VMEM_SPEC] * 3,
        out_specs=(VMEM_SPEC,) * 4,
        compiler_params=pltpu.CompilerParams(vmem_limit_bytes=ATTEND_VMEM),
        name="cached",
    )(
        context_length, request_block_count, last_block_tokens, placement,
        key_value_cache, query, steps_kv,
    )
    attended = pl.pallas_call(
        functools.partial(merge_kernel, features),
        out_shape=jax.ShapeDtypeStruct((steps * HEADS * dec_rows, HD), jnp.bfloat16),
        in_specs=[VMEM_SPEC] * 6,
        out_specs=ANY_SPEC,
        scratch_shapes=[
            pltpu.VMEM((steps * HEADS * dec_rows, HD), jnp.bfloat16),
            pltpu.SemaphoreType.DMA((steps,)),
        ],
        compiler_params=pltpu.CompilerParams(vmem_limit_bytes=ATTEND_VMEM),
        name="merge",
    )(arrived, acc, top, total, fresh_ok, query)
    attended = attended.reshape(steps, HEADS, dec_rows, HD).transpose(0, 2, 1, 3)
    return attended.reshape(steps, dec_rows, HEADS * HD)


def solution(mesh):
    return jax.shard_map(
        body,
        mesh=mesh,
        in_specs=(
            P("parts", None),
            P("tensor", None),
            P("tensor", None, None),
            P("tensor", None, None),
            P("parts"),
            P(),
            P("parts"),
            P("parts"),
            P("parts"),
            P(("parts", "tensor"), None, None),
            P(("parts", "tensor")),
            P(None, ("parts", "tensor"), None),
            P(None, ("parts", "tensor"), None),
        ),
        out_specs=P(None, ("parts", "tensor"), None),
        check_vma=False,
    )
```

```python
import functools

import jax
import jax.numpy as jnp
from jax import lax
from jax.experimental import pallas as pl
from jax.experimental.pallas import tpu as pltpu
from jax.sharding import PartitionSpec as P

HEADS = 64
KVH = 8
HD = 128
BLK = 8
MOSTB = 2
CAPT = MOSTB * BLK
ADAPTER_SCALE = 0.5
NEG_LARGE = -1e30
PROJECT_VMEM = 32 * 1024 * 1024
ATTEND_VMEM = 16 * 1024 * 1024
WIRE = jnp.bfloat16

SMEM_SPEC = pl.BlockSpec(memory_space=pltpu.SMEM)
VMEM_SPEC = pl.BlockSpec(memory_space=pltpu.VMEM)
ANY_SPEC = pl.BlockSpec(memory_space=pl.ANY)


def div(x, n):
    shift = n.bit_length() - 1
    return lax.shift_right_logical(x, shift) if n == 1 << shift else x // n


def mod(x, n):
    return x & (n - 1) if n & (n - 1) == 0 else x % n


def project_kernel(
    dec_rows, cuts, tenant_h, table_h, counts_h, placement_h, hidden, weight, down, up, out,
    tenant, table, counts, placement,
    h_s, w_s, d_s, mine_s, u_s, spread_s, part_s, base_s, dest_table, hw_sems, sems,
):
    tokens, width = hidden.shape
    features = weight.shape[0]
    local, pages, rank2 = down.shape
    requests = tenant.shape[0]
    devices = out.shape[0]
    me = lax.axis_index("tensor")

    my_copy = pltpu.make_async_copy(
        hidden.at[:, pl.ds(pl.multiple_of(me * local, 128), local)], mine_s, sems.at[0]
    )
    int_copies = [
        pltpu.make_async_copy(src, dst, sems.at[3 + i])
        for i, (src, dst) in enumerate(
            ((table_h, table), (tenant_h, tenant), (counts_h, counts), (placement_h, placement))
        )
    ]
    d_copy = pltpu.make_async_copy(down, d_s, sems.at[1])
    up_copy = pltpu.make_async_copy(up, u_s, sems.at[2])
    for copy in [my_copy] + int_copies + [d_copy]:
        copy.start()
    hw_copies = []
    for c, (first, last) in enumerate(zip(cuts[:-1], cuts[1:])):
        lanes = pl.ds(first, last - first)
        pair = (
            pltpu.make_async_copy(hidden.at[:, lanes], h_s.at[:, lanes], hw_sems.at[c, 0]),
            pltpu.make_async_copy(weight.at[:, lanes], w_s.at[:, lanes], hw_sems.at[c, 1]),
        )
        for copy in pair:
            copy.start()
        hw_copies.append(pair)
    up_copy.start()

    per_tile = 256 // pages
    tiles = 128 // per_tile
    row = lax.broadcasted_iota(jnp.int32, (128, 256), 0)
    col = lax.broadcasted_iota(jnp.int32, (128, 256), 1)
    spreads = [
        jnp.where(row == div(col, pages) + j * per_tile, jnp.float32(1), jnp.float32(0)).astype(
            jnp.bfloat16
        )
        for j in range(tiles)
    ]
    for copy in int_copies:
        copy.wait()
    for dest in range(devices):
        dest_table[0, dest] = 0
        dest_table[1, dest] = 0
    row = lax.broadcasted_iota(jnp.int32, (tokens, 128), 0)
    page_of_token = jnp.zeros_like(row)
    first = jnp.int32(0)
    for r in range(requests):
        dest = div(placement[r], dec_rows)
        page = table[tenant[r]]
        dest_table[0, dest] = first * BLK
        dest_table[1, dest] = page
        page_of_token = jnp.where(row >= first * BLK, page, page_of_token)
        first = first + counts[r]
    own_page = mod(lax.broadcasted_iota(jnp.int32, (tokens, 128), 1), pages) == page_of_token
    own_page = jnp.concatenate([own_page, own_page], axis=1)

    my_copy.wait()
    for g in range(local // 128):
        mine = mine_s[:, g * 128 : (g + 1) * 128]
        for j in range(tiles):
            wide = jnp.dot(mine, spreads[j], preferred_element_type=jnp.float32)
            wide = jnp.where(own_page, wide, jnp.float32(0)).astype(jnp.bfloat16)
            spread_s[:, pl.ds((g * tiles + j) * 256, 256)] = wide
    d_copy.wait()
    part_s[tokens:] = jnp.zeros((BLK, rank2), jnp.float32)
    part_s[:tokens] = jnp.dot(
        spread_s[...], d_s[...].reshape(local * pages, rank2), preferred_element_type=jnp.float32
    )

    total = jnp.zeros((tokens, features), jnp.float32)
    for c, (first, last) in enumerate(zip(cuts[:-1], cuts[1:])):
        for copy in hw_copies[c]:
            copy.wait()
        total = total + lax.dot_general(
            h_s[:, first:last], w_s[:, first:last], NT, preferred_element_type=jnp.float32
        )
    base_s[tokens:] = jnp.zeros((BLK, HD), jnp.float32)
    if features < HD:
        base_s[...] = jnp.zeros_like(base_s)
    base_s[:tokens, :features] = total
    up_copy.wait()
    for dest in range(devices):
        start = pl.multiple_of(dest_table[0, dest], BLK)
        out[dest, :CAPT, :] = part_s[pl.ds(start, CAPT), :].astype(out.dtype)
        out[dest, CAPT : 2 * CAPT, :] = base_s[pl.ds(start, CAPT), :].astype(out.dtype)
        if features < HD:
            out[dest, 2 * CAPT :, :] = jnp.zeros((out.shape[1] - 2 * CAPT, HD), out.dtype)
        out[dest, 2 * CAPT :, :features] = u_s[dest_table[1, dest]]


NT = (((1,), (1,)), ((), ()))


def gather_queries(query, k, group, steps, stride):
    return jnp.concatenate(
        [query[pl.ds(s * stride + k * group, group), :] for s in range(steps)], axis=0
    )


def cached_kernel(
    lengths, counts, last, placement, cache, query, steps_kv, acc, top_out, total_out, fresh_ok,
):
    dec_rows, ctx, kv_width = cache.shape
    half_width = kv_width // 2
    step_rows = KVH * dec_rows
    steps = steps_kv.shape[0] // (2 * step_rows)
    group = HEADS // KVH * dec_rows
    q_rows = steps * group
    stride = HEADS * dec_rows

    row = lax.broadcasted_iota(jnp.int32, (q_rows, ctx), 0)
    col = lax.broadcasted_iota(jnp.int32, (q_rows, ctx), 1)
    row_slot = mod(row, dec_rows)
    cache_ok = [(row_slot == g) & (col < lengths[g]) for g in range(dec_rows)]
    row = lax.broadcasted_iota(jnp.int32, (q_rows, steps * step_rows), 0)
    col = lax.broadcasted_iota(jnp.int32, (q_rows, steps * step_rows), 1)
    step_ok = (mod(row, dec_rows) == mod(col, dec_rows)) & (div(col, step_rows) <= div(row, group))
    step_head = div(mod(col, step_rows), dec_rows)
    step_keys, step_values = (
        jnp.concatenate(
            [steps_kv[pl.ds((2 * s + half) * step_rows, step_rows), :] for s in range(steps)], axis=0
        )
        for half in range(2)
    )

    scale = HD ** (-0.5)
    for k in range(KVH):
        lanes = pl.ds(k * HD, HD)
        vlanes = pl.ds(half_width + k * HD, HD)
        q = gather_queries(query, k, group, steps, stride)
        keys = [cache[g, :, lanes] for g in range(dec_rows)] + [step_keys]
        values = [cache[g, :, vlanes] for g in range(dec_rows)] + [step_values]
        scores = [
            jnp.where(
                ok,
                lax.dot_general(q, key, NT, preferred_element_type=jnp.float32) * scale,
                NEG_LARGE,
            )
            for ok, key in zip(cache_ok + [step_ok & (step_head == k)], keys)
        ]
        top = functools.reduce(jnp.maximum, [jnp.max(s, axis=1, keepdims=True) for s in scores])
        weights = [jnp.exp(s - top) for s in scores]
        total = sum(jnp.sum(w, axis=1, keepdims=True) for w in weights)
        mixed = sum(
            jnp.dot(w.astype(jnp.bfloat16), v, preferred_element_type=jnp.float32)
            for w, v in zip(weights, values)
        )
        for s in range(steps):
            here = pl.ds(s * stride + k * group, group)
            part = slice(s * group, (s + 1) * group)
            acc[here, :] = mixed[part]
            top_out[here, :] = jnp.broadcast_to(top[part], (group, HD))
            total_out[here, :] = jnp.broadcast_to(total[part], (group, HD))

    my_slot = jnp.int32(-1)
    my_length = jnp.int32(0)
    for r in range(placement.shape[0]):
        hit = div(placement[r], dec_rows) == lax.axis_index("tensor")
        my_slot = jnp.where(hit, mod(placement[r], dec_rows), my_slot)
        my_length = jnp.where(hit, (counts[r] - 1) * BLK + last[r], my_length)
    row = lax.broadcasted_iota(jnp.int32, fresh_ok.shape, 0)
    col = lax.broadcasted_iota(jnp.int32, fresh_ok.shape, 1)
    ok = (
        (mod(div(row, group), KVH) == div(col, CAPT))
        & (mod(row, dec_rows) == my_slot)
        & (mod(col, CAPT) < my_length)
    )
    fresh_ok[...] = jnp.where(ok, jnp.float32(1), jnp.float32(0))


def merge_kernel(features, box, acc, top_in, total_in, fresh_ok, query, out, result, sems):
    devices = box.shape[0]
    rank = box.shape[1] - 2 * CAPT
    terms = [box[i, :CAPT].astype(jnp.float32) for i in range(devices)]
    while len(terms) > 1:
        pairs = [a + b for a, b in zip(terms[::2], terms[1::2])]
        terms = pairs + terms[2 * len(pairs) :]
    shrunk = terms[0].astype(jnp.bfloat16)
    halves = (shrunk[:, :rank], shrunk[:, rank:])
    pieces = HD // features

    def rows(i, first, count):
        parts = [box[i * pieces + p, first : first + count, :features] for p in range(pieces)]
        return parts[0] if pieces == 1 else jnp.concatenate(parts, axis=1)

    def fresh(first):
        made = []
        for i in range(first, first + KVH, 2):
            ups = jnp.concatenate([rows(i + j, 2 * CAPT, rank) for j in range(2)], axis=1)
            delta = jnp.dot(halves[first // KVH], ups, preferred_element_type=jnp.float32)
            for j in range(2):
                base = rows(i + j, CAPT, CAPT).astype(jnp.float32)
                both = base + ADAPTER_SCALE * delta[:, j * HD : (j + 1) * HD]
                made.append(both.astype(jnp.bfloat16))
        return jnp.concatenate(made, axis=0)

    keys, values = fresh(0), fresh(KVH)
    scale = HD ** (-0.5)
    part = out.shape[0] // sems.shape[0]
    copies = []
    for c in range(sems.shape[0]):
        here = pl.ds(c * part, part)
        s = lax.dot_general(query[here, :], keys, NT, preferred_element_type=jnp.float32)
        s = jnp.where(fresh_ok[here, :] > 0, s * scale, NEG_LARGE)
        old = top_in[here, :]
        top = jnp.maximum(old, jnp.max(s, axis=1, keepdims=True))
        fade = jnp.exp(old - top)
        w = jnp.exp(s - top)
        total = total_in[here, :] * fade + jnp.sum(w, axis=1, keepdims=True)
        mixed = acc[here, :] * fade + jnp.dot(
            w.astype(jnp.bfloat16), values, preferred_element_type=jnp.float32
        )
        result[here, :] = (mixed / total).astype(jnp.bfloat16)
        copies.append(pltpu.make_async_copy(result.at[here, :], out.at[here, :], sems.at[c]))
        copies[c].start()
    for copy in copies:
        copy.wait()


def body(
    hidden,
    key_value_weight,
    adapter_down_weight,
    adapter_up_weight,
    tenant,
    tenant_page_table,
    request_block_count,
    last_block_tokens,
    placement,
    key_value_cache,
    context_length,
    decode_step_query,
    step_key_value,
):
    devices = lax.axis_size("tensor")
    tokens, width = hidden.shape
    features = key_value_weight.shape[0]
    local, pages, rank2 = adapter_down_weight.shape
    rank = adapter_up_weight.shape[2]
    tenants = tenant_page_table.shape[0]
    dec_rows, ctx, kv_width = key_value_cache.shape
    steps = step_key_value.shape[0]
    heads2 = kv_width // HD
    cuts = (0, width * 3 // 8, width * 6 // 8, width)
    up_by_page = jnp.transpose(adapter_up_weight, (1, 2, 0))
    rows = 2 * CAPT + rank
    outgoing = pl.pallas_call(
        functools.partial(project_kernel, dec_rows, cuts),
        out_shape=pltpu.VMEM((devices, rows, HD), WIRE),
        in_specs=[ANY_SPEC] * 8,
        out_specs=VMEM_SPEC,
        scratch_shapes=[
            pltpu.SMEM(tenant.shape, jnp.int32),
            pltpu.SMEM(tenant_page_table.shape, jnp.int32),
            pltpu.SMEM(request_block_count.shape, jnp.int32),
            pltpu.SMEM(placement.shape, jnp.int32),
            pltpu.VMEM((tokens, width), jnp.bfloat16),
            pltpu.VMEM((features, width), jnp.bfloat16),
            pltpu.VMEM((local, pages, rank2), jnp.bfloat16),
            pltpu.VMEM((tokens, local), jnp.bfloat16),
            pltpu.VMEM((pages, rank, features), jnp.bfloat16),
            pltpu.VMEM((tokens, local * pages), jnp.bfloat16),
            pltpu.VMEM((tokens + BLK, rank2), jnp.float32),
            pltpu.VMEM((tokens + BLK, HD), jnp.float32),
            pltpu.SMEM((2, devices), jnp.int32),
            pltpu.SemaphoreType.DMA((len(cuts) - 1, 2)),
            pltpu.SemaphoreType.DMA((7,)),
        ],
        compiler_params=pltpu.CompilerParams(vmem_limit_bytes=PROJECT_VMEM),
        name="project",
    )(
        *(
            pltpu.with_memory_space_constraint(x, pltpu.HBM)
            for x in (
                tenant, tenant_page_table, request_block_count, placement,
                hidden, key_value_weight, adapter_down_weight, up_by_page,
            )
        )
    )
    arrived = lax.all_to_all(outgoing, "tensor", split_axis=0, concat_axis=0, tiled=True)

    query = decode_step_query.reshape(steps, dec_rows, HEADS, HD)
    query = query.transpose(0, 2, 1, 3).reshape(steps * HEADS * dec_rows, HD)
    steps_kv = step_key_value.reshape(steps, dec_rows, heads2, HD)
    steps_kv = steps_kv.transpose(0, 2, 1, 3).reshape(steps * heads2 * dec_rows, HD)
    state = jax.ShapeDtypeStruct((steps * HEADS * dec_rows, HD), jnp.float32)
    acc, top, total, fresh_ok = pl.pallas_call(
        cached_kernel,
        out_shape=(state,) * 4,
        in_specs=[SMEM_SPEC] * 4 + [VMEM_SPEC] * 3,
        out_specs=(VMEM_SPEC,) * 4,
        compiler_params=pltpu.CompilerParams(vmem_limit_bytes=ATTEND_VMEM),
        name="cached",
    )(
        context_length, request_block_count, last_block_tokens, placement,
        key_value_cache, query, steps_kv,
    )
    attended = pl.pallas_call(
        functools.partial(merge_kernel, features),
        out_shape=jax.ShapeDtypeStruct((steps * HEADS * dec_rows, HD), jnp.bfloat16),
        in_specs=[VMEM_SPEC] * 6,
        out_specs=ANY_SPEC,
        scratch_shapes=[
            pltpu.VMEM((steps * HEADS * dec_rows, HD), jnp.bfloat16),
            pltpu.SemaphoreType.DMA((steps,)),
        ],
        compiler_params=pltpu.CompilerParams(vmem_limit_bytes=ATTEND_VMEM),
        name="merge",
    )(arrived, acc, top, total, fresh_ok, query)
    attended = attended.reshape(steps, HEADS, dec_rows, HD).transpose(0, 2, 1, 3)
    return attended.reshape(steps, dec_rows, HEADS * HD)


def solution(mesh):
    return jax.shard_map(
        body,
        mesh=mesh,
        in_specs=(
            P("parts", None),
            P("tensor", None),
            P("tensor", None, None),
            P("tensor", None, None),
            P("parts"),
            P(),
            P("parts"),
            P("parts"),
            P("parts"),
            P(("parts", "tensor"), None, None),
            P(("parts", "tensor")),
            P(None, ("parts", "tensor"), None),
            P(None, ("parts", "tensor"), None),
        ),
        out_specs=P(None, ("parts", "tensor"), None),
        check_vma=False,
    )
```

```python
import functools

import jax
import jax.numpy as jnp
from jax import lax
from jax.experimental import pallas as pl
from jax.experimental.pallas import tpu as pltpu
from jax.sharding import PartitionSpec as P

HEADS = 64
KVH = 8
HD = 128
BLK = 8
MOSTB = 2
CAPT = MOSTB * BLK
ADAPTER_SCALE = 0.5
NEG_LARGE = -1e30
PROJECT_VMEM = 32 * 1024 * 1024
ATTEND_VMEM = 16 * 1024 * 1024
WIRE = jnp.bfloat16

SMEM_SPEC = pl.BlockSpec(memory_space=pltpu.SMEM)
VMEM_SPEC = pl.BlockSpec(memory_space=pltpu.VMEM)
ANY_SPEC = pl.BlockSpec(memory_space=pl.ANY)


def div(x, n):
    shift = n.bit_length() - 1
    return lax.shift_right_logical(x, shift) if n == 1 << shift else x // n


def mod(x, n):
    return x & (n - 1) if n & (n - 1) == 0 else x % n


def project_kernel(
    dec_rows, d_chunks, cuts, tenant_h, table_h, counts_h, placement_h, hidden, weight, down, up, out,
    tenant, table, counts, placement,
    h_s, w_s, d_s, mine_s, u_s, sel_s, part_s, base_s, dest_table, hw_sems, d_sems, sems,
):
    tokens, width = hidden.shape
    features = weight.shape[0]
    local, pages, rank2 = down.shape
    tenants = table.shape[0]
    requests = tenant.shape[0]
    devices = out.shape[0]
    me = lax.axis_index("tensor")
    d_step = local // d_chunks

    int_copies = [
        pltpu.make_async_copy(src, dst, sems.at[2 + i])
        for i, (src, dst) in enumerate(
            ((table_h, table), (tenant_h, tenant), (counts_h, counts), (placement_h, placement))
        )
    ]
    d_copies = [
        pltpu.make_async_copy(
            down.at[pl.ds(c * d_step, d_step)], d_s.at[pl.ds(c * d_step, d_step)], d_sems.at[c])
        for c in range(d_chunks)
    ]
    my_copy = pltpu.make_async_copy(
        hidden.at[:, pl.ds(pl.multiple_of(me * local, 128), local)], mine_s, sems.at[0]
    )
    up_copy = pltpu.make_async_copy(up, u_s, sems.at[1])
    for copy in int_copies + d_copies + [my_copy]:
        copy.start()
    spans = list(zip(cuts[:-1], cuts[1:]))
    hw_copies = []
    for c, (first, last) in enumerate(spans):
        lanes = pl.ds(first, last - first)
        pair = (
            pltpu.make_async_copy(hidden.at[:, lanes], h_s.at[:, lanes], hw_sems.at[c, 0]),
            pltpu.make_async_copy(weight.at[:, lanes], w_s.at[:, lanes], hw_sems.at[c, 1]),
        )
        for copy in pair:
            copy.start()
        hw_copies.append(pair)
        if c == 0:
            up_copy.start()

    for copy in int_copies:
        copy.wait()
    rows = lax.broadcasted_iota(jnp.int32, (tenants * 16, 16 * pages), 0)
    cols = lax.broadcasted_iota(jnp.int32, (tenants * 16, 16 * pages), 1)
    page_of_row = jnp.zeros_like(rows)
    for k in range(tenants):
        page_of_row = jnp.where(div(rows, 16) == k, table[k], page_of_row)
    pick = (mod(rows, 16) == div(cols, pages)) & (mod(cols, pages) == page_of_row)
    pick = jnp.where(pick, jnp.float32(1), jnp.float32(0)).astype(jnp.bfloat16)
    if requests < devices:
        for dest in range(devices):
            dest_table[0, dest] = 0
            dest_table[1, dest] = 0
    first = jnp.int32(0)
    for r in range(requests):
        dest = div(placement[r], dec_rows)
        dest_table[0, dest] = first * BLK
        dest_table[1, dest] = tenant[r]
        first = first + counts[r]

    for c in range(d_chunks):
        d_copies[c].wait()
        for b in range(c * d_step // 16, (c + 1) * d_step // 16, 2):
            block = jnp.concatenate(
                [d_s[pl.ds((b + i) * 16, 16)].reshape(16 * pages, rank2) for i in range(2)], axis=1
            )
            chosen = jnp.dot(pick, block, preferred_element_type=jnp.float32)
            for i in range(2):
                sel_s[b + i] = chosen[:, i * rank2 : (i + 1) * rank2].astype(jnp.bfloat16)
    my_copy.wait()
    mine = mine_s[...]
    for k in range(0, tenants, 2):
        pair = min(2, tenants - k)
        maps = jnp.concatenate(
            [sel_s[:, j * 16 : (j + 1) * 16, :].reshape(local, rank2) for j in range(k, k + pair)],
            axis=1,
        )
        product = jnp.dot(mine, maps, preferred_element_type=jnp.float32)
        for j in range(pair):
            part_s[k + j, :tokens] = product[:, j * rank2 : (j + 1) * rank2]
            part_s[k + j, tokens:] = jnp.zeros((BLK, rank2), jnp.float32)

    base_s[tokens:] = jnp.zeros((BLK, HD), jnp.float32)
    if features < HD:
        base_s[...] = jnp.zeros_like(base_s)
    total = jnp.zeros((tokens, features), jnp.float32)
    for c, (first, last) in enumerate(spans):
        for copy in hw_copies[c]:
            copy.wait()
        if c == 1:
            up_copy.wait()
            for dest in range(devices):
                start = pl.multiple_of(dest_table[0, dest], BLK)
                who = dest_table[1, dest]
                out[dest, :CAPT, :] = part_s[who, pl.ds(start, CAPT), :].astype(out.dtype)
                if features < HD:
                    out[dest, 2 * CAPT :, :] = jnp.zeros((out.shape[1] - 2 * CAPT, HD), out.dtype)
                out[dest, 2 * CAPT :, :features] = u_s[table[who]]
        total = total + lax.dot_general(
            h_s[:, first:last], w_s[:, first:last], NT, preferred_element_type=jnp.float32
        )
    base_s[:tokens, :features] = total
    for dest in range(devices):
        start = pl.multiple_of(dest_table[0, dest], BLK)
        out[dest, CAPT : 2 * CAPT, :] = base_s[pl.ds(start, CAPT), :].astype(out.dtype)


NT = (((1,), (1,)), ((), ()))


def gather_queries(query, k, group, steps, stride):
    return jnp.concatenate(
        [query[pl.ds(s * stride + k * group, group), :] for s in range(steps)], axis=0
    )


def cached_kernel(
    lengths, counts, last, placement, cache, query, steps_kv, acc, top_out, total_out, fresh_ok,
):
    dec_rows, ctx, kv_width = cache.shape
    half_width = kv_width // 2
    step_rows = KVH * dec_rows
    steps = steps_kv.shape[0] // (2 * step_rows)
    group = HEADS // KVH * dec_rows
    q_rows = steps * group
    stride = HEADS * dec_rows

    row = lax.broadcasted_iota(jnp.int32, (q_rows, ctx), 0)
    col = lax.broadcasted_iota(jnp.int32, (q_rows, ctx), 1)
    row_slot = mod(row, dec_rows)
    cache_ok = [(row_slot == g) & (col < lengths[g]) for g in range(dec_rows)]
    row = lax.broadcasted_iota(jnp.int32, (q_rows, steps * step_rows), 0)
    col = lax.broadcasted_iota(jnp.int32, (q_rows, steps * step_rows), 1)
    step_ok = (mod(row, dec_rows) == mod(col, dec_rows)) & (div(col, step_rows) <= div(row, group))
    step_head = div(mod(col, step_rows), dec_rows)
    step_keys, step_values = (
        jnp.concatenate(
            [steps_kv[pl.ds((2 * s + half) * step_rows, step_rows), :] for s in range(steps)], axis=0
        )
        for half in range(2)
    )

    scale = HD ** (-0.5)
    for k in range(KVH):
        lanes = pl.ds(k * HD, HD)
        vlanes = pl.ds(half_width + k * HD, HD)
        q = gather_queries(query, k, group, steps, stride)
        keys = [cache[g, :, lanes] for g in range(dec_rows)] + [step_keys]
        values = [cache[g, :, vlanes] for g in range(dec_rows)] + [step_values]
        scores = [
            jnp.where(
                ok,
                lax.dot_general(q, key, NT, preferred_element_type=jnp.float32) * scale,
                NEG_LARGE,
            )
            for ok, key in zip(cache_ok + [step_ok & (step_head == k)], keys)
        ]
        top = functools.reduce(jnp.maximum, [jnp.max(s, axis=1, keepdims=True) for s in scores])
        weights = [jnp.exp(s - top) for s in scores]
        total = sum(jnp.sum(w, axis=1, keepdims=True) for w in weights)
        mixed = sum(
            jnp.dot(w.astype(jnp.bfloat16), v, preferred_element_type=jnp.float32)
            for w, v in zip(weights, values)
        )
        for s in range(steps):
            here = pl.ds(s * stride + k * group, group)
            part = slice(s * group, (s + 1) * group)
            acc[here, :] = mixed[part]
            top_out[here, :] = jnp.broadcast_to(top[part], (group, HD))
            total_out[here, :] = jnp.broadcast_to(total[part], (group, HD))

    my_slot = jnp.int32(-1)
    my_length = jnp.int32(0)
    for r in range(placement.shape[0]):
        hit = div(placement[r], dec_rows) == lax.axis_index("tensor")
        my_slot = jnp.where(hit, mod(placement[r], dec_rows), my_slot)
        my_length = jnp.where(hit, (counts[r] - 1) * BLK + last[r], my_length)
    row = lax.broadcasted_iota(jnp.int32, fresh_ok.shape, 0)
    col = lax.broadcasted_iota(jnp.int32, fresh_ok.shape, 1)
    ok = (
        (mod(div(row, group), KVH) == div(col, CAPT))
        & (mod(row, dec_rows) == my_slot)
        & (mod(col, CAPT) < my_length)
    )
    fresh_ok[...] = jnp.where(ok, jnp.float32(1), jnp.float32(0))


def merge_kernel(features, box, acc, top_in, total_in, fresh_ok, query, out, result, sems):
    devices = box.shape[0]
    rank = box.shape[1] - 2 * CAPT
    terms = [box[i, :CAPT].astype(jnp.float32) for i in range(devices)]
    while len(terms) > 1:
        pairs = [a + b for a, b in zip(terms[::2], terms[1::2])]
        terms = pairs + terms[2 * len(pairs) :]
    shrunk = terms[0].astype(jnp.bfloat16)
    halves = (shrunk[:, :rank], shrunk[:, rank:])
    pieces = HD // features

    def rows(i, first, count):
        parts = [box[i * pieces + p, first : first + count, :features] for p in range(pieces)]
        return parts[0] if pieces == 1 else jnp.concatenate(parts, axis=1)

    def fresh(first):
        made = []
        for i in range(first, first + KVH, 2):
            ups = jnp.concatenate([rows(i + j, 2 * CAPT, rank) for j in range(2)], axis=1)
            delta = jnp.dot(halves[first // KVH], ups, preferred_element_type=jnp.float32)
            for j in range(2):
                base = rows(i + j, CAPT, CAPT).astype(jnp.float32)
                both = base + ADAPTER_SCALE * delta[:, j * HD : (j + 1) * HD]
                made.append(both.astype(jnp.bfloat16))
        return jnp.concatenate(made, axis=0)

    keys, values = fresh(0), fresh(KVH)
    scale = HD ** (-0.5)
    part = out.shape[0] // sems.shape[0]
    copies = []
    for c in range(sems.shape[0]):
        here = pl.ds(c * part, part)
        s = lax.dot_general(query[here, :], keys, NT, preferred_element_type=jnp.float32)
        s = jnp.where(fresh_ok[here, :] > 0, s * scale, NEG_LARGE)
        old = top_in[here, :]
        top = jnp.maximum(old, jnp.max(s, axis=1, keepdims=True))
        fade = jnp.exp(old - top)
        w = jnp.exp(s - top)
        total = total_in[here, :] * fade + jnp.sum(w, axis=1, keepdims=True)
        mixed = acc[here, :] * fade + jnp.dot(
            w.astype(jnp.bfloat16), values, preferred_element_type=jnp.float32
        )
        result[here, :] = (mixed / total).astype(jnp.bfloat16)
        copies.append(pltpu.make_async_copy(result.at[here, :], out.at[here, :], sems.at[c]))
        copies[c].start()
    for copy in copies:
        copy.wait()


def body(
    hidden,
    key_value_weight,
    adapter_down_weight,
    adapter_up_weight,
    tenant,
    tenant_page_table,
    request_block_count,
    last_block_tokens,
    placement,
    key_value_cache,
    context_length,
    decode_step_query,
    step_key_value,
):
    devices = lax.axis_size("tensor")
    tokens, width = hidden.shape
    features = key_value_weight.shape[0]
    local, pages, rank2 = adapter_down_weight.shape
    rank = adapter_up_weight.shape[2]
    tenants = tenant_page_table.shape[0]
    dec_rows, ctx, kv_width = key_value_cache.shape
    steps = step_key_value.shape[0]
    heads2 = kv_width // HD
    d_chunks = 2
    cuts = (0, width * 3 // 8, width * 6 // 8, width)
    up_by_page = jnp.transpose(adapter_up_weight, (1, 2, 0))
    rows = 2 * CAPT + rank
    outgoing = pl.pallas_call(
        functools.partial(project_kernel, dec_rows, d_chunks, cuts),
        out_shape=pltpu.VMEM((devices, rows, HD), WIRE),
        in_specs=[ANY_SPEC] * 8,
        out_specs=VMEM_SPEC,
        scratch_shapes=[
            pltpu.SMEM(tenant.shape, jnp.int32),
            pltpu.SMEM(tenant_page_table.shape, jnp.int32),
            pltpu.SMEM(request_block_count.shape, jnp.int32),
            pltpu.SMEM(placement.shape, jnp.int32),
            pltpu.VMEM((tokens, width), jnp.bfloat16),
            pltpu.VMEM((features, width), jnp.bfloat16),
            pltpu.VMEM((local, pages, rank2), jnp.bfloat16),
            pltpu.VMEM((tokens, local), jnp.bfloat16),
            pltpu.VMEM((pages, rank, features), jnp.bfloat16),
            pltpu.VMEM((local // 16, tenants * 16, rank2), jnp.bfloat16),
            pltpu.VMEM((tenants, tokens + BLK, rank2), jnp.float32),
            pltpu.VMEM((tokens + BLK, HD), jnp.float32),
            pltpu.SMEM((2, devices), jnp.int32),
            pltpu.SemaphoreType.DMA((len(cuts) - 1, 2)),
            pltpu.SemaphoreType.DMA((d_chunks,)),
            pltpu.SemaphoreType.DMA((6,)),
        ],
        compiler_params=pltpu.CompilerParams(vmem_limit_bytes=PROJECT_VMEM),
        name="project",
    )(
        *(
            pltpu.with_memory_space_constraint(x, pltpu.HBM)
            for x in (
                tenant, tenant_page_table, request_block_count, placement,
                hidden, key_value_weight, adapter_down_weight, up_by_page,
            )
        )
    )
    arrived = lax.all_to_all(outgoing, "tensor", split_axis=0, concat_axis=0, tiled=True)

    query = decode_step_query.reshape(steps, dec_rows, HEADS, HD)
    query = query.transpose(0, 2, 1, 3).reshape(steps * HEADS * dec_rows, HD)
    steps_kv = step_key_value.reshape(steps, dec_rows, heads2, HD)
    steps_kv = steps_kv.transpose(0, 2, 1, 3).reshape(steps * heads2 * dec_rows, HD)
    state = jax.ShapeDtypeStruct((steps * HEADS * dec_rows, HD), jnp.float32)
    acc, top, total, fresh_ok = pl.pallas_call(
        cached_kernel,
        out_shape=(state,) * 4,
        in_specs=[SMEM_SPEC] * 4 + [VMEM_SPEC] * 3,
        out_specs=(VMEM_SPEC,) * 4,
        compiler_params=pltpu.CompilerParams(vmem_limit_bytes=ATTEND_VMEM),
        name="cached",
    )(
        context_length, request_block_count, last_block_tokens, placement,
        key_value_cache, query, steps_kv,
    )
    attended = pl.pallas_call(
        functools.partial(merge_kernel, features),
        out_shape=jax.ShapeDtypeStruct((steps * HEADS * dec_rows, HD), jnp.bfloat16),
        in_specs=[VMEM_SPEC] * 6,
        out_specs=ANY_SPEC,
        scratch_shapes=[
            pltpu.VMEM((steps * HEADS * dec_rows, HD), jnp.bfloat16),
            pltpu.SemaphoreType.DMA((steps,)),
        ],
        compiler_params=pltpu.CompilerParams(vmem_limit_bytes=ATTEND_VMEM),
        name="merge",
    )(arrived, acc, top, total, fresh_ok, query)
    attended = attended.reshape(steps, HEADS, dec_rows, HD).transpose(0, 2, 1, 3)
    return attended.reshape(steps, dec_rows, HEADS * HD)


def solution(mesh):
    return jax.shard_map(
        body,
        mesh=mesh,
        in_specs=(
            P("parts", None),
            P("tensor", None),
            P("tensor", None, None),
            P("tensor", None, None),
            P("parts"),
            P(),
            P("parts"),
            P("parts"),
            P("parts"),
            P(("parts", "tensor"), None, None),
            P(("parts", "tensor")),
            P(None, ("parts", "tensor"), None),
            P(None, ("parts", "tensor"), None),
        ),
        out_specs=P(None, ("parts", "tensor"), None),
        check_vma=False,
    )
```

```python
import functools

import jax
import jax.numpy as jnp
from jax import lax
from jax.experimental import pallas as pl
from jax.experimental.pallas import tpu as pltpu
from jax.sharding import PartitionSpec as P

HEADS = 64
KVH = 8
HD = 128
BLK = 8
MOSTB = 2
CAPT = MOSTB * BLK
ADAPTER_SCALE = 0.5
NEG_LARGE = -1e30
PROJECT_VMEM = 32 * 1024 * 1024
ATTEND_VMEM = 16 * 1024 * 1024
WIRE = jnp.bfloat16

SMEM_SPEC = pl.BlockSpec(memory_space=pltpu.SMEM)
VMEM_SPEC = pl.BlockSpec(memory_space=pltpu.VMEM)
ANY_SPEC = pl.BlockSpec(memory_space=pl.ANY)


def div(x, n):
    shift = n.bit_length() - 1
    return lax.shift_right_logical(x, shift) if n == 1 << shift else x // n


def mod(x, n):
    return x & (n - 1) if n & (n - 1) == 0 else x % n


def project_kernel(
    dec_rows, d_chunks, chunks, tenant_h, table_h, counts_h, placement_h, hidden, weight, down, up, out,
    tenant, table, counts, placement,
    h_s, w_s, wt_s, d_s, mine_s, u_s, sel_s, part_s, base_s, dest_table, h_sems, d_sems, sems,
):
    tokens, width = hidden.shape
    features = weight.shape[0]
    local, pages, rank2 = down.shape
    tenants = table.shape[0]
    requests = tenant.shape[0]
    devices = out.shape[0]
    me = lax.axis_index("tensor")
    d_step = local // d_chunks
    step = width // chunks

    int_copies = [
        pltpu.make_async_copy(src, dst, sems.at[3 + i])
        for i, (src, dst) in enumerate(
            ((table_h, table), (tenant_h, tenant), (counts_h, counts), (placement_h, placement))
        )
    ]
    d_copies = [
        pltpu.make_async_copy(
            down.at[pl.ds(c * d_step, d_step)], d_s.at[pl.ds(c * d_step, d_step)], d_sems.at[c])
        for c in range(d_chunks)
    ]
    my_copy = pltpu.make_async_copy(
        hidden.at[:, pl.ds(pl.multiple_of(me * local, 128), local)], mine_s, sems.at[0]
    )
    up_copy = pltpu.make_async_copy(up, u_s, sems.at[1])
    w_copy = pltpu.make_async_copy(weight, w_s, sems.at[2])
    h_copies = [
        pltpu.make_async_copy(
            hidden.at[:, pl.ds(c * step, step)], h_s.at[:, pl.ds(c * step, step)], h_sems.at[c])
        for c in range(chunks)
    ]
    for copy in int_copies + d_copies + [my_copy, w_copy, up_copy] + h_copies:
        copy.start()

    int_copies[0].wait()
    rows = lax.broadcasted_iota(jnp.int32, (tenants * 16, 16 * pages), 0)
    cols = lax.broadcasted_iota(jnp.int32, (tenants * 16, 16 * pages), 1)
    page_of_row = jnp.zeros_like(rows)
    for k in range(tenants):
        page_of_row = jnp.where(div(rows, 16) == k, table[k], page_of_row)
    pick = (mod(rows, 16) == div(cols, pages)) & (mod(cols, pages) == page_of_row)
    pick = jnp.where(pick, jnp.float32(1), jnp.float32(0)).astype(jnp.bfloat16)

    for c in range(d_chunks):
        d_copies[c].wait()
        for b in range(c * d_step // 16, (c + 1) * d_step // 16, 2):
            block = jnp.concatenate(
                [d_s[pl.ds((b + i) * 16, 16)].reshape(16 * pages, rank2) for i in range(2)], axis=1
            )
            chosen = jnp.dot(pick, block, preferred_element_type=jnp.float32)
            for i in range(2):
                sel_s[b + i] = chosen[:, i * rank2 : (i + 1) * rank2].astype(jnp.bfloat16)
    my_copy.wait()
    w_copy.wait()
    if features == HD:
        wt_s[...] = w_s[...].T
    mine = mine_s[...]
    for k in range(0, tenants, 2):
        pair = min(2, tenants - k)
        maps = jnp.concatenate(
            [sel_s[:, j * 16 : (j + 1) * 16, :].reshape(local, rank2) for j in range(k, k + pair)],
            axis=1,
        )
        product = jnp.dot(mine, maps, preferred_element_type=jnp.float32)
        for j in range(pair):
            part_s[k + j, :tokens] = product[:, j * rank2 : (j + 1) * rank2]
            part_s[k + j, tokens:] = jnp.zeros((BLK, rank2), jnp.float32)
    for copy in int_copies[1:]:
        copy.wait()
    if requests < devices:
        for dest in range(devices):
            dest_table[0, dest] = 0
            dest_table[1, dest] = 0
    first = jnp.int32(0)
    for r in range(requests):
        dest = div(placement[r], dec_rows)
        dest_table[0, dest] = first * BLK
        dest_table[1, dest] = tenant[r]
        first = first + counts[r]

    total = jnp.zeros((tokens, features), jnp.float32)
    for c in range(chunks):
        h_copies[c].wait()
        lanes = slice(c * step, (c + 1) * step)
        if features == HD:
            total = total + jnp.dot(
                h_s[:, lanes], wt_s[lanes, :], preferred_element_type=jnp.float32
            )
        else:
            total = total + lax.dot_general(
                h_s[:, lanes], w_s[:, lanes], NT, preferred_element_type=jnp.float32
            )
    base_s[tokens:] = jnp.zeros((BLK, HD), jnp.float32)
    if features < HD:
        base_s[...] = jnp.zeros_like(base_s)
    base_s[:tokens, :features] = total
    up_copy.wait()
    for dest in range(devices):
        start = pl.multiple_of(dest_table[0, dest], BLK)
        who = dest_table[1, dest]
        out[dest, :CAPT, :] = part_s[who, pl.ds(start, CAPT), :].astype(out.dtype)
        out[dest, CAPT : 2 * CAPT, :] = base_s[pl.ds(start, CAPT), :].astype(out.dtype)
        if features < HD:
            out[dest, 2 * CAPT :, :] = jnp.zeros((out.shape[1] - 2 * CAPT, HD), out.dtype)
        out[dest, 2 * CAPT :, :features] = u_s[table[who]]


NT = (((1,), (1,)), ((), ()))


def gather_queries(query, k, group, steps, stride):
    return jnp.concatenate(
        [query[pl.ds(s * stride + k * group, group), :] for s in range(steps)], axis=0
    )


def cached_kernel(
    lengths, counts, last, placement, cache, query, steps_kv, acc, top_out, total_out, fresh_ok,
):
    dec_rows, ctx, kv_width = cache.shape
    half_width = kv_width // 2
    step_rows = KVH * dec_rows
    steps = steps_kv.shape[0] // (2 * step_rows)
    group = HEADS // KVH * dec_rows
    q_rows = steps * group
    stride = HEADS * dec_rows

    row = lax.broadcasted_iota(jnp.int32, (q_rows, ctx), 0)
    col = lax.broadcasted_iota(jnp.int32, (q_rows, ctx), 1)
    row_slot = mod(row, dec_rows)
    cache_ok = [(row_slot == g) & (col < lengths[g]) for g in range(dec_rows)]
    row = lax.broadcasted_iota(jnp.int32, (q_rows, steps * step_rows), 0)
    col = lax.broadcasted_iota(jnp.int32, (q_rows, steps * step_rows), 1)
    step_ok = (mod(row, dec_rows) == mod(col, dec_rows)) & (div(col, step_rows) <= div(row, group))
    step_head = div(mod(col, step_rows), dec_rows)
    step_keys, step_values = (
        jnp.concatenate(
            [steps_kv[pl.ds((2 * s + half) * step_rows, step_rows), :] for s in range(steps)], axis=0
        )
        for half in range(2)
    )

    scale = HD ** (-0.5)
    for k in range(KVH):
        lanes = pl.ds(k * HD, HD)
        vlanes = pl.ds(half_width + k * HD, HD)
        q = gather_queries(query, k, group, steps, stride)
        keys = [cache[g, :, lanes] for g in range(dec_rows)] + [step_keys]
        values = [cache[g, :, vlanes] for g in range(dec_rows)] + [step_values]
        scores = [
            jnp.where(
                ok,
                lax.dot_general(q, key, NT, preferred_element_type=jnp.float32) * scale,
                NEG_LARGE,
            )
            for ok, key in zip(cache_ok + [step_ok & (step_head == k)], keys)
        ]
        top = functools.reduce(jnp.maximum, [jnp.max(s, axis=1, keepdims=True) for s in scores])
        weights = [jnp.exp(s - top) for s in scores]
        total = sum(jnp.sum(w, axis=1, keepdims=True) for w in weights)
        mixed = sum(
            jnp.dot(w.astype(jnp.bfloat16), v, preferred_element_type=jnp.float32)
            for w, v in zip(weights, values)
        )
        for s in range(steps):
            here = pl.ds(s * stride + k * group, group)
            part = slice(s * group, (s + 1) * group)
            acc[here, :] = mixed[part]
            top_out[here, :] = jnp.broadcast_to(top[part], (group, HD))
            total_out[here, :] = jnp.broadcast_to(total[part], (group, HD))

    my_slot = jnp.int32(-1)
    my_length = jnp.int32(0)
    for r in range(placement.shape[0]):
        hit = div(placement[r], dec_rows) == lax.axis_index("tensor")
        my_slot = jnp.where(hit, mod(placement[r], dec_rows), my_slot)
        my_length = jnp.where(hit, (counts[r] - 1) * BLK + last[r], my_length)
    row = lax.broadcasted_iota(jnp.int32, fresh_ok.shape, 0)
    col = lax.broadcasted_iota(jnp.int32, fresh_ok.shape, 1)
    ok = (
        (mod(div(row, group), KVH) == div(col, CAPT))
        & (mod(row, dec_rows) == my_slot)
        & (mod(col, CAPT) < my_length)
    )
    fresh_ok[...] = jnp.where(ok, jnp.float32(1), jnp.float32(0))


def merge_kernel(features, box, acc, top_in, total_in, fresh_ok, query, out, result, sems):
    devices = box.shape[0]
    rank = box.shape[1] - 2 * CAPT
    terms = [box[i, :CAPT].astype(jnp.float32) for i in range(devices)]
    while len(terms) > 1:
        pairs = [a + b for a, b in zip(terms[::2], terms[1::2])]
        terms = pairs + terms[2 * len(pairs) :]
    shrunk = terms[0].astype(jnp.bfloat16)
    halves = (shrunk[:, :rank], shrunk[:, rank:])
    pieces = HD // features

    def rows(i, first, count):
        parts = [box[i * pieces + p, first : first + count, :features] for p in range(pieces)]
        return parts[0] if pieces == 1 else jnp.concatenate(parts, axis=1)

    def fresh(first):
        made = []
        for i in range(first, first + KVH, 2):
            ups = jnp.concatenate([rows(i + j, 2 * CAPT, rank) for j in range(2)], axis=1)
            delta = jnp.dot(halves[first // KVH], ups, preferred_element_type=jnp.float32)
            for j in range(2):
                base = rows(i + j, CAPT, CAPT).astype(jnp.float32)
                both = base + ADAPTER_SCALE * delta[:, j * HD : (j + 1) * HD]
                made.append(both.astype(jnp.bfloat16))
        return jnp.concatenate(made, axis=0)

    keys, values = fresh(0), fresh(KVH)
    scale = HD ** (-0.5)
    part = out.shape[0] // sems.shape[0]
    copies = []
    for c in range(sems.shape[0]):
        here = pl.ds(c * part, part)
        s = lax.dot_general(query[here, :], keys, NT, preferred_element_type=jnp.float32)
        s = jnp.where(fresh_ok[here, :] > 0, s * scale, NEG_LARGE)
        old = top_in[here, :]
        top = jnp.maximum(old, jnp.max(s, axis=1, keepdims=True))
        fade = jnp.exp(old - top)
        w = jnp.exp(s - top)
        total = total_in[here, :] * fade + jnp.sum(w, axis=1, keepdims=True)
        mixed = acc[here, :] * fade + jnp.dot(
            w.astype(jnp.bfloat16), values, preferred_element_type=jnp.float32
        )
        result[here, :] = (mixed / total).astype(jnp.bfloat16)
        copies.append(pltpu.make_async_copy(result.at[here, :], out.at[here, :], sems.at[c]))
        copies[c].start()
    for copy in copies:
        copy.wait()


def body(
    hidden,
    key_value_weight,
    adapter_down_weight,
    adapter_up_weight,
    tenant,
    tenant_page_table,
    request_block_count,
    last_block_tokens,
    placement,
    key_value_cache,
    context_length,
    decode_step_query,
    step_key_value,
):
    devices = lax.axis_size("tensor")
    tokens, width = hidden.shape
    features = key_value_weight.shape[0]
    local, pages, rank2 = adapter_down_weight.shape
    rank = adapter_up_weight.shape[2]
    tenants = tenant_page_table.shape[0]
    dec_rows, ctx, kv_width = key_value_cache.shape
    steps = step_key_value.shape[0]
    heads2 = kv_width // HD
    d_chunks, chunks = 2, 2
    up_by_page = jnp.transpose(adapter_up_weight, (1, 2, 0))
    rows = 2 * CAPT + rank
    outgoing = pl.pallas_call(
        functools.partial(project_kernel, dec_rows, d_chunks, chunks),
        out_shape=pltpu.VMEM((devices, rows, HD), WIRE),
        in_specs=[ANY_SPEC] * 8,
        out_specs=VMEM_SPEC,
        scratch_shapes=[
            pltpu.SMEM(tenant.shape, jnp.int32),
            pltpu.SMEM(tenant_page_table.shape, jnp.int32),
            pltpu.SMEM(request_block_count.shape, jnp.int32),
            pltpu.SMEM(placement.shape, jnp.int32),
            pltpu.VMEM((tokens, width), jnp.bfloat16),
            pltpu.VMEM((features, width), jnp.bfloat16),
            pltpu.VMEM((width, HD), jnp.bfloat16),
            pltpu.VMEM((local, pages, rank2), jnp.bfloat16),
            pltpu.VMEM((tokens, local), jnp.bfloat16),
            pltpu.VMEM((pages, rank, features), jnp.bfloat16),
            pltpu.VMEM((local // 16, tenants * 16, rank2), jnp.bfloat16),
            pltpu.VMEM((tenants, tokens + BLK, rank2), jnp.float32),
            pltpu.VMEM((tokens + BLK, HD), jnp.float32),
            pltpu.SMEM((2, devices), jnp.int32),
            pltpu.SemaphoreType.DMA((chunks,)),
            pltpu.SemaphoreType.DMA((d_chunks,)),
            pltpu.SemaphoreType.DMA((7,)),
        ],
        compiler_params=pltpu.CompilerParams(vmem_limit_bytes=PROJECT_VMEM),
        name="project",
    )(
        *(
            pltpu.with_memory_space_constraint(x, pltpu.HBM)
            for x in (
                tenant, tenant_page_table, request_block_count, placement,
                hidden, key_value_weight, adapter_down_weight, up_by_page,
            )
        )
    )
    arrived = lax.all_to_all(outgoing, "tensor", split_axis=0, concat_axis=0, tiled=True)

    query = decode_step_query.reshape(steps, dec_rows, HEADS, HD)
    query = query.transpose(0, 2, 1, 3).reshape(steps * HEADS * dec_rows, HD)
    steps_kv = step_key_value.reshape(steps, dec_rows, heads2, HD)
    steps_kv = steps_kv.transpose(0, 2, 1, 3).reshape(steps * heads2 * dec_rows, HD)
    state = jax.ShapeDtypeStruct((steps * HEADS * dec_rows, HD), jnp.float32)
    acc, top, total, fresh_ok = pl.pallas_call(
        cached_kernel,
        out_shape=(state,) * 4,
        in_specs=[SMEM_SPEC] * 4 + [VMEM_SPEC] * 3,
        out_specs=(VMEM_SPEC,) * 4,
        compiler_params=pltpu.CompilerParams(vmem_limit_bytes=ATTEND_VMEM),
        name="cached",
    )(
        context_length, request_block_count, last_block_tokens, placement,
        key_value_cache, query, steps_kv,
    )
    attended = pl.pallas_call(
        functools.partial(merge_kernel, features),
        out_shape=jax.ShapeDtypeStruct((steps * HEADS * dec_rows, HD), jnp.bfloat16),
        in_specs=[VMEM_SPEC] * 6,
        out_specs=ANY_SPEC,
        scratch_shapes=[
            pltpu.VMEM((steps * HEADS * dec_rows, HD), jnp.bfloat16),
            pltpu.SemaphoreType.DMA((steps,)),
        ],
        compiler_params=pltpu.CompilerParams(vmem_limit_bytes=ATTEND_VMEM),
        name="merge",
    )(arrived, acc, top, total, fresh_ok, query)
    attended = attended.reshape(steps, HEADS, dec_rows, HD).transpose(0, 2, 1, 3)
    return attended.reshape(steps, dec_rows, HEADS * HD)


def solution(mesh):
    return jax.shard_map(
        body,
        mesh=mesh,
        in_specs=(
            P("parts", None),
            P("tensor", None),
            P("tensor", None, None),
            P("tensor", None, None),
            P("parts"),
            P(),
            P("parts"),
            P("parts"),
            P("parts"),
            P(("parts", "tensor"), None, None),
            P(("parts", "tensor")),
            P(None, ("parts", "tensor"), None),
            P(None, ("parts", "tensor"), None),
        ),
        out_specs=P(None, ("parts", "tensor"), None),
        check_vma=False,
    )
```

```python
import functools

import jax
import jax.numpy as jnp
from jax import lax
from jax.experimental import pallas as pl
from jax.experimental.pallas import tpu as pltpu
from jax.sharding import PartitionSpec as P

HEADS = 64
KVH = 8
HD = 128
BLK = 8
MOSTB = 2
CAPT = MOSTB * BLK
ADAPTER_SCALE = 0.5
NEG_LARGE = -1e30
PROJECT_VMEM = 32 * 1024 * 1024
ATTEND_VMEM = 16 * 1024 * 1024
WIRE = jnp.bfloat16

SMEM_SPEC = pl.BlockSpec(memory_space=pltpu.SMEM)
VMEM_SPEC = pl.BlockSpec(memory_space=pltpu.VMEM)
ANY_SPEC = pl.BlockSpec(memory_space=pl.ANY)


def div(x, n):
    shift = n.bit_length() - 1
    return lax.shift_right_logical(x, shift) if n == 1 << shift else x // n


def mod(x, n):
    return x & (n - 1) if n & (n - 1) == 0 else x % n


def project_kernel(
    dec_rows, d_chunks, chunks, devices, tenant_h, table_h, counts_h, placement_h, hidden, weight, down, up, out,
    tenant, table, counts, placement,
    h_s, w_s, d_s, mine_s, u_s, sel_s, part_s, base_s, dest_table, sems, d_sems, int_sems,
):
    tokens, width = hidden.shape
    features = weight.shape[0]
    local, pages, rank2 = down.shape
    tenants = table.shape[0]
    requests = tenant.shape[0]
    me = lax.axis_index("tensor")
    d_step = local // d_chunks
    step = width // chunks

    int_copies = [
        pltpu.make_async_copy(src, dst, int_sems.at[i])
        for i, (src, dst) in enumerate(
            ((table_h, table), (tenant_h, tenant), (counts_h, counts), (placement_h, placement))
        )
    ]
    for copy in int_copies:
        copy.start()
    d_copies = [
        pltpu.make_async_copy(
            down.at[pl.ds(c * d_step, d_step)], d_s.at[pl.ds(c * d_step, d_step)], d_sems.at[c])
        for c in range(d_chunks)
    ]
    h_copies = [
        pltpu.make_async_copy(hidden.at[:, pl.ds(c * step, step)], h_s.at[c], sems.at[c, 0])
        for c in range(chunks)
    ]
    w_copies = [
        pltpu.make_async_copy(weight.at[:, pl.ds(c * step, step)], w_s.at[c], sems.at[c, 1])
        for c in range(chunks)
    ]
    my_copy = pltpu.make_async_copy(
        hidden.at[:, pl.ds(pl.multiple_of(me * local, 128), local)], mine_s, d_sems.at[d_chunks]
    )
    up_copy = pltpu.make_async_copy(up, u_s, d_sems.at[d_chunks + 1])
    for copy in d_copies + [my_copy, up_copy]:
        copy.start()
    for c in range(chunks):
        h_copies[c].start()
        w_copies[c].start()

    int_copies[0].wait()
    rows = lax.broadcasted_iota(jnp.int32, (tenants * 16, 16 * pages), 0)
    cols = lax.broadcasted_iota(jnp.int32, (tenants * 16, 16 * pages), 1)
    page_of_row = jnp.zeros_like(rows)
    for k in range(tenants):
        page_of_row = jnp.where(div(rows, 16) == k, table[k], page_of_row)
    pick = (mod(rows, 16) == div(cols, pages)) & (mod(cols, pages) == page_of_row)
    pick = jnp.where(pick, jnp.float32(1), jnp.float32(0)).astype(jnp.bfloat16)

    for c in range(d_chunks):
        d_copies[c].wait()
        for b in range(c * d_step // 16, (c + 1) * d_step // 16, 2):
            block = jnp.concatenate(
                [d_s[pl.ds((b + i) * 16, 16)].reshape(16 * pages, rank2) for i in range(2)], axis=1
            )
            chosen = jnp.dot(pick, block, preferred_element_type=jnp.float32)
            for i in range(2):
                sel_s[b + i] = chosen[:, i * rank2 : (i + 1) * rank2].astype(jnp.bfloat16)
    for copy in int_copies[1:]:
        copy.wait()
    for dest in range(devices):
        dest_table[0, dest] = 0
        dest_table[1, dest] = 0
    first = jnp.int32(0)
    for r in range(requests):
        dest = div(placement[r], dec_rows)
        dest_table[0, dest] = first * BLK
        dest_table[1, dest] = tenant[r]
        first = first + counts[r]
    my_copy.wait()
    mine = mine_s[...]
    for k in range(0, tenants, 2):
        pair = min(2, tenants - k)
        maps = jnp.concatenate(
            [sel_s[:, j * 16 : (j + 1) * 16, :].reshape(local, rank2) for j in range(k, k + pair)],
            axis=1,
        )
        product = jnp.dot(mine, maps, preferred_element_type=jnp.float32)
        for j in range(pair):
            part_s[k + j, :tokens] = product[:, j * rank2 : (j + 1) * rank2]
            part_s[k + j, tokens:] = jnp.zeros((BLK, rank2), jnp.float32)

    total = jnp.zeros((tokens, features), jnp.float32)
    for c in range(chunks):
        h_copies[c].wait()
        w_copies[c].wait()
        total = total + lax.dot_general(h_s[c], w_s[c], NT, preferred_element_type=jnp.float32)
    base_s[tokens:] = jnp.zeros((BLK, HD), jnp.float32)
    if features < HD:
        base_s[...] = jnp.zeros_like(base_s)
    base_s[:tokens, :features] = total
    up_copy.wait()
    for dest in range(devices):
        start = pl.multiple_of(dest_table[0, dest], BLK)
        who = dest_table[1, dest]
        out[dest, :CAPT, :] = part_s[who, pl.ds(start, CAPT), :].astype(out.dtype)
        out[dest, CAPT : 2 * CAPT, :] = base_s[pl.ds(start, CAPT), :].astype(out.dtype)
        if features < HD:
            out[dest, 2 * CAPT :, :] = jnp.zeros((out.shape[1] - 2 * CAPT, HD), out.dtype)
        out[dest, 2 * CAPT :, :features] = u_s[table[who]]


NT = (((1,), (1,)), ((), ()))


def gather_queries(query, k, group, steps, stride):
    return jnp.concatenate(
        [query[pl.ds(s * stride + k * group, group), :] for s in range(steps)], axis=0
    )


def cached_kernel(
    lengths, counts, last, placement, cache, query, steps_kv, acc, top_out, total_out, fresh_ok,
):
    dec_rows, ctx, kv_width = cache.shape
    half_width = kv_width // 2
    step_rows = KVH * dec_rows
    steps = steps_kv.shape[0] // (2 * step_rows)
    group = HEADS // KVH * dec_rows
    q_rows = steps * group
    stride = HEADS * dec_rows

    row = lax.broadcasted_iota(jnp.int32, (q_rows, ctx), 0)
    col = lax.broadcasted_iota(jnp.int32, (q_rows, ctx), 1)
    row_slot = mod(row, dec_rows)
    cache_ok = [(row_slot == g) & (col < lengths[g]) for g in range(dec_rows)]
    row = lax.broadcasted_iota(jnp.int32, (q_rows, steps * step_rows), 0)
    col = lax.broadcasted_iota(jnp.int32, (q_rows, steps * step_rows), 1)
    step_ok = (mod(row, dec_rows) == mod(col, dec_rows)) & (div(col, step_rows) <= div(row, group))
    step_head = div(mod(col, step_rows), dec_rows)
    step_keys, step_values = (
        jnp.concatenate(
            [steps_kv[pl.ds((2 * s + half) * step_rows, step_rows), :] for s in range(steps)], axis=0
        )
        for half in range(2)
    )

    scale = HD ** (-0.5)
    for k in range(KVH):
        lanes = pl.ds(k * HD, HD)
        vlanes = pl.ds(half_width + k * HD, HD)
        q = gather_queries(query, k, group, steps, stride)
        keys = [cache[g, :, lanes] for g in range(dec_rows)] + [step_keys]
        values = [cache[g, :, vlanes] for g in range(dec_rows)] + [step_values]
        scores = [
            jnp.where(
                ok,
                lax.dot_general(q, key, NT, preferred_element_type=jnp.float32) * scale,
                NEG_LARGE,
            )
            for ok, key in zip(cache_ok + [step_ok & (step_head == k)], keys)
        ]
        top = functools.reduce(jnp.maximum, [jnp.max(s, axis=1, keepdims=True) for s in scores])
        weights = [jnp.exp(s - top) for s in scores]
        total = sum(jnp.sum(w, axis=1, keepdims=True) for w in weights)
        mixed = sum(
            jnp.dot(w.astype(jnp.bfloat16), v, preferred_element_type=jnp.float32)
            for w, v in zip(weights, values)
        )
        for s in range(steps):
            here = pl.ds(s * stride + k * group, group)
            part = slice(s * group, (s + 1) * group)
            acc[here, :] = mixed[part]
            top_out[here, :] = jnp.broadcast_to(top[part], (group, HD))
            total_out[here, :] = jnp.broadcast_to(total[part], (group, HD))

    my_slot = jnp.int32(-1)
    my_length = jnp.int32(0)
    for r in range(placement.shape[0]):
        hit = div(placement[r], dec_rows) == lax.axis_index("tensor")
        my_slot = jnp.where(hit, mod(placement[r], dec_rows), my_slot)
        my_length = jnp.where(hit, (counts[r] - 1) * BLK + last[r], my_length)
    row = lax.broadcasted_iota(jnp.int32, fresh_ok.shape, 0)
    col = lax.broadcasted_iota(jnp.int32, fresh_ok.shape, 1)
    ok = (
        (mod(div(row, group), KVH) == div(col, CAPT))
        & (mod(row, dec_rows) == my_slot)
        & (mod(col, CAPT) < my_length)
    )
    fresh_ok[...] = jnp.where(ok, jnp.float32(1), jnp.float32(0))


def merge_kernel(features, box, acc, top_in, total_in, fresh_ok, query, out, result, sems):
    devices = box.shape[0]
    rank = box.shape[1] - 2 * CAPT
    terms = [box[i, :CAPT].astype(jnp.float32) for i in range(devices)]
    while len(terms) > 1:
        pairs = [a + b for a, b in zip(terms[::2], terms[1::2])]
        terms = pairs + terms[2 * len(pairs) :]
    shrunk = terms[0].astype(jnp.bfloat16)
    halves = (shrunk[:, :rank], shrunk[:, rank:])
    pieces = HD // features

    def rows(i, first, count):
        parts = [box[i * pieces + p, first : first + count, :features] for p in range(pieces)]
        return parts[0] if pieces == 1 else jnp.concatenate(parts, axis=1)

    def fresh(first):
        made = []
        for i in range(first, first + KVH, 2):
            ups = jnp.concatenate([rows(i + j, 2 * CAPT, rank) for j in range(2)], axis=1)
            delta = jnp.dot(halves[first // KVH], ups, preferred_element_type=jnp.float32)
            for j in range(2):
                base = rows(i + j, CAPT, CAPT).astype(jnp.float32)
                both = base + ADAPTER_SCALE * delta[:, j * HD : (j + 1) * HD]
                made.append(both.astype(jnp.bfloat16))
        return jnp.concatenate(made, axis=0)

    keys, values = fresh(0), fresh(KVH)
    scale = HD ** (-0.5)
    part = out.shape[0] // sems.shape[0]
    copies = []
    for c in range(sems.shape[0]):
        here = pl.ds(c * part, part)
        s = lax.dot_general(query[here, :], keys, NT, preferred_element_type=jnp.float32)
        s = jnp.where(fresh_ok[here, :] > 0, s * scale, NEG_LARGE)
        old = top_in[here, :]
        top = jnp.maximum(old, jnp.max(s, axis=1, keepdims=True))
        fade = jnp.exp(old - top)
        w = jnp.exp(s - top)
        total = total_in[here, :] * fade + jnp.sum(w, axis=1, keepdims=True)
        mixed = acc[here, :] * fade + jnp.dot(
            w.astype(jnp.bfloat16), values, preferred_element_type=jnp.float32
        )
        result[here, :] = (mixed / total).astype(jnp.bfloat16)
        copies.append(pltpu.make_async_copy(result.at[here, :], out.at[here, :], sems.at[c]))
        copies[c].start()
    for copy in copies:
        copy.wait()


def in_hbm(*arrays):
    return [pltpu.with_memory_space_constraint(x, pltpu.HBM) for x in arrays]


def body(
    hidden,
    key_value_weight,
    adapter_down_weight,
    adapter_up_weight,
    tenant,
    tenant_page_table,
    request_block_count,
    last_block_tokens,
    placement,
    key_value_cache,
    context_length,
    decode_step_query,
    step_key_value,
):
    devices = lax.axis_size("tensor")
    tokens, width = hidden.shape
    features = key_value_weight.shape[0]
    local, pages, rank2 = adapter_down_weight.shape
    rank = adapter_up_weight.shape[2]
    tenants = tenant_page_table.shape[0]
    dec_rows, ctx, kv_width = key_value_cache.shape
    steps = step_key_value.shape[0]
    heads2 = kv_width // HD
    d_chunks, chunks = 2, 4
    up_by_page = jnp.transpose(adapter_up_weight, (1, 2, 0))
    rows = 2 * CAPT + rank
    outgoing = pl.pallas_call(
        functools.partial(project_kernel, dec_rows, d_chunks, chunks, devices),
        out_shape=pltpu.VMEM((devices, rows, HD), WIRE),
        in_specs=[ANY_SPEC] * 8,
        out_specs=VMEM_SPEC,
        scratch_shapes=[
            pltpu.SMEM(tenant.shape, jnp.int32),
            pltpu.SMEM(tenant_page_table.shape, jnp.int32),
            pltpu.SMEM(request_block_count.shape, jnp.int32),
            pltpu.SMEM(placement.shape, jnp.int32),
            pltpu.VMEM((chunks, tokens, width // chunks), jnp.bfloat16),
            pltpu.VMEM((chunks, features, width // chunks), jnp.bfloat16),
            pltpu.VMEM((local, pages, rank2), jnp.bfloat16),
            pltpu.VMEM((tokens, local), jnp.bfloat16),
            pltpu.VMEM((pages, rank, features), jnp.bfloat16),
            pltpu.VMEM((local // 16, tenants * 16, rank2), jnp.bfloat16),
            pltpu.VMEM((tenants, tokens + BLK, rank2), jnp.float32),
            pltpu.VMEM((tokens + BLK, HD), jnp.float32),
            pltpu.SMEM((2, devices), jnp.int32),
            pltpu.SemaphoreType.DMA((chunks, 2)),
            pltpu.SemaphoreType.DMA((d_chunks + 2,)),
            pltpu.SemaphoreType.DMA((4,)),
        ],
        compiler_params=pltpu.CompilerParams(vmem_limit_bytes=PROJECT_VMEM),
        name="project",
    )(
        *in_hbm(
            tenant, tenant_page_table, request_block_count, placement,
            hidden, key_value_weight, adapter_down_weight, up_by_page,
        )
    )
    arrived = lax.all_to_all(outgoing, "tensor", split_axis=0, concat_axis=0, tiled=True)

    query = decode_step_query.reshape(steps, dec_rows, HEADS, HD)
    query = query.transpose(0, 2, 1, 3).reshape(steps * HEADS * dec_rows, HD)
    steps_kv = step_key_value.reshape(steps, dec_rows, heads2, HD)
    steps_kv = steps_kv.transpose(0, 2, 1, 3).reshape(steps * heads2 * dec_rows, HD)
    state = jax.ShapeDtypeStruct((steps * HEADS * dec_rows, HD), jnp.float32)
    acc, top, total, fresh_ok = pl.pallas_call(
        cached_kernel,
        out_shape=(state,) * 4,
        in_specs=[SMEM_SPEC] * 4 + [VMEM_SPEC] * 3,
        out_specs=(VMEM_SPEC,) * 4,
        compiler_params=pltpu.CompilerParams(vmem_limit_bytes=ATTEND_VMEM),
        name="cached",
    )(
        *in_hbm(
            context_length, request_block_count, last_block_tokens, placement,
            key_value_cache, query, steps_kv,
        )
    )
    attended = pl.pallas_call(
        functools.partial(merge_kernel, features),
        out_shape=jax.ShapeDtypeStruct((steps * HEADS * dec_rows, HD), jnp.bfloat16),
        in_specs=[VMEM_SPEC] * 6,
        out_specs=ANY_SPEC,
        scratch_shapes=[
            pltpu.VMEM((steps * HEADS * dec_rows, HD), jnp.bfloat16),
            pltpu.SemaphoreType.DMA((steps,)),
        ],
        compiler_params=pltpu.CompilerParams(vmem_limit_bytes=ATTEND_VMEM),
        name="merge",
    )(arrived, acc, top, total, fresh_ok, query)
    attended = attended.reshape(steps, HEADS, dec_rows, HD).transpose(0, 2, 1, 3)
    return attended.reshape(steps, dec_rows, HEADS * HD)


def solution(mesh):
    return jax.shard_map(
        body,
        mesh=mesh,
        in_specs=(
            P("parts", None),
            P("tensor", None),
            P("tensor", None, None),
            P("tensor", None, None),
            P("parts"),
            P(),
            P("parts"),
            P("parts"),
            P("parts"),
            P(("parts", "tensor"), None, None),
            P(("parts", "tensor")),
            P(None, ("parts", "tensor"), None),
            P(None, ("parts", "tensor"), None),
        ),
        out_specs=P(None, ("parts", "tensor"), None),
        check_vma=False,
    )
```

```python
import functools

import jax
import jax.numpy as jnp
from jax import lax
from jax.experimental import pallas as pl
from jax.experimental.pallas import tpu as pltpu
from jax.sharding import PartitionSpec as P

HEADS = 64
KVH = 8
HD = 128
BLK = 8
MOSTB = 2
CAPT = MOSTB * BLK
ADAPTER_SCALE = 0.5
NEG_LARGE = -1e30
PROJECT_VMEM = 32 * 1024 * 1024
ATTEND_VMEM = 16 * 1024 * 1024
WIRE = jnp.bfloat16

SMEM_SPEC = pl.BlockSpec(memory_space=pltpu.SMEM)
VMEM_SPEC = pl.BlockSpec(memory_space=pltpu.VMEM)
ANY_SPEC = pl.BlockSpec(memory_space=pl.ANY)


def div(x, n):
    shift = n.bit_length() - 1
    return lax.shift_right_logical(x, shift) if n == 1 << shift else x // n


def mod(x, n):
    return x & (n - 1) if n & (n - 1) == 0 else x % n


def project_kernel(
    dec_rows, d_chunks, chunks, devices, tenant_h, table_h, counts_h, placement_h, hidden, weight, down, up, out,
    tenant, table, counts, placement,
    h_s, w_s, d_s, mine_s, u_s, sel_s, part_s, base_s, dest_table, sems, d_sems, int_sems,
):
    tokens, width = hidden.shape
    features = weight.shape[0]
    local, pages, rank2 = down.shape
    tenants = table.shape[0]
    requests = tenant.shape[0]
    me = lax.axis_index("tensor")
    d_step = local // d_chunks
    step = width // chunks

    int_copies = [
        pltpu.make_async_copy(src, dst, int_sems.at[i])
        for i, (src, dst) in enumerate(
            ((table_h, table), (tenant_h, tenant), (counts_h, counts), (placement_h, placement))
        )
    ]
    for copy in int_copies:
        copy.start()
    d_copies = [
        pltpu.make_async_copy(
            down.at[pl.ds(c * d_step, d_step)], d_s.at[pl.ds(c * d_step, d_step)], d_sems.at[c])
        for c in range(d_chunks)
    ]
    h_copies = [
        pltpu.make_async_copy(hidden.at[:, pl.ds(c * step, step)], h_s.at[c], sems.at[c, 0])
        for c in range(chunks)
    ]
    w_copies = [
        pltpu.make_async_copy(weight.at[:, pl.ds(c * step, step)], w_s.at[c], sems.at[c, 1])
        for c in range(chunks)
    ]
    my_copy = pltpu.make_async_copy(
        hidden.at[:, pl.ds(pl.multiple_of(me * local, 128), local)], mine_s, d_sems.at[d_chunks]
    )
    up_copy = pltpu.make_async_copy(up, u_s, d_sems.at[d_chunks + 1])
    for copy in d_copies + [my_copy, up_copy]:
        copy.start()
    for c in range(chunks):
        h_copies[c].start()
        w_copies[c].start()

    int_copies[0].wait()
    rows = lax.broadcasted_iota(jnp.int32, (tenants * 16, 16 * pages), 0)
    cols = lax.broadcasted_iota(jnp.int32, (tenants * 16, 16 * pages), 1)
    page_of_row = jnp.zeros_like(rows)
    for k in range(tenants):
        page_of_row = jnp.where(div(rows, 16) == k, table[k], page_of_row)
    pick = (mod(rows, 16) == div(cols, pages)) & (mod(cols, pages) == page_of_row)
    pick = jnp.where(pick, jnp.float32(1), jnp.float32(0)).astype(jnp.bfloat16)

    for c in range(d_chunks):
        d_copies[c].wait()
        for b in range(c * d_step // 16, (c + 1) * d_step // 16, 2):
            block = jnp.concatenate(
                [d_s[pl.ds((b + i) * 16, 16)].reshape(16 * pages, rank2) for i in range(2)], axis=1
            )
            chosen = jnp.dot(pick, block, preferred_element_type=jnp.float32)
            for i in range(2):
                sel_s[b + i] = chosen[:, i * rank2 : (i + 1) * rank2].astype(jnp.bfloat16)
    for copy in int_copies[1:]:
        copy.wait()
    for dest in range(devices):
        dest_table[0, dest] = 0
        dest_table[1, dest] = 0
    first = jnp.int32(0)
    for r in range(requests):
        dest = div(placement[r], dec_rows)
        dest_table[0, dest] = first * BLK
        dest_table[1, dest] = tenant[r]
        first = first + counts[r]
    my_copy.wait()
    mine = mine_s[...]
    for k in range(0, tenants, 2):
        pair = min(2, tenants - k)
        maps = jnp.concatenate(
            [sel_s[:, j * 16 : (j + 1) * 16, :].reshape(local, rank2) for j in range(k, k + pair)],
            axis=1,
        )
        product = jnp.dot(mine, maps, preferred_element_type=jnp.float32)
        for j in range(pair):
            part_s[k + j, :tokens] = product[:, j * rank2 : (j + 1) * rank2]
            part_s[k + j, tokens:] = jnp.zeros((BLK, rank2), jnp.float32)

    total = jnp.zeros((tokens, features), jnp.float32)
    for c in range(chunks):
        h_copies[c].wait()
        w_copies[c].wait()
        total = total + lax.dot_general(h_s[c], w_s[c], NT, preferred_element_type=jnp.float32)
    base_s[tokens:] = jnp.zeros((BLK, HD), jnp.float32)
    if features < HD:
        base_s[...] = jnp.zeros_like(base_s)
    base_s[:tokens, :features] = total
    up_copy.wait()
    for dest in range(devices):
        start = pl.multiple_of(dest_table[0, dest], BLK)
        who = dest_table[1, dest]
        out[dest, :CAPT, :] = part_s[who, pl.ds(start, CAPT), :].astype(out.dtype)
        out[dest, CAPT : 2 * CAPT, :] = base_s[pl.ds(start, CAPT), :].astype(out.dtype)
        if features < HD:
            out[dest, 2 * CAPT :, :] = jnp.zeros((out.shape[1] - 2 * CAPT, HD), out.dtype)
        out[dest, 2 * CAPT :, :features] = u_s[table[who]]


NT = (((1,), (1,)), ((), ()))


def gather_queries(query, k, group, steps, stride):
    return jnp.concatenate(
        [query[pl.ds(s * stride + k * group, group), :] for s in range(steps)], axis=0
    )


def cached_kernel(
    lengths, counts, last, placement, cache, query, steps_kv, acc, top_out, total_out, fresh_ok,
):
    dec_rows, ctx, kv_width = cache.shape
    half_width = kv_width // 2
    step_rows = KVH * dec_rows
    steps = steps_kv.shape[0] // (2 * step_rows)
    group = HEADS // KVH * dec_rows
    q_rows = steps * group
    stride = HEADS * dec_rows

    row = lax.broadcasted_iota(jnp.int32, (q_rows, ctx), 0)
    col = lax.broadcasted_iota(jnp.int32, (q_rows, ctx), 1)
    row_slot = mod(row, dec_rows)
    cache_ok = [(row_slot == g) & (col < lengths[g]) for g in range(dec_rows)]
    row = lax.broadcasted_iota(jnp.int32, (q_rows, steps * step_rows), 0)
    col = lax.broadcasted_iota(jnp.int32, (q_rows, steps * step_rows), 1)
    step_ok = (mod(row, dec_rows) == mod(col, dec_rows)) & (div(col, step_rows) <= div(row, group))
    step_head = div(mod(col, step_rows), dec_rows)
    step_keys, step_values = (
        jnp.concatenate(
            [steps_kv[pl.ds((2 * s + half) * step_rows, step_rows), :] for s in range(steps)], axis=0
        )
        for half in range(2)
    )

    scale = HD ** (-0.5)
    for k in range(KVH):
        lanes = pl.ds(k * HD, HD)
        vlanes = pl.ds(half_width + k * HD, HD)
        q = gather_queries(query, k, group, steps, stride)
        keys = [cache[g, :, lanes] for g in range(dec_rows)] + [step_keys]
        values = [cache[g, :, vlanes] for g in range(dec_rows)] + [step_values]
        scores = [
            jnp.where(
                ok,
                lax.dot_general(q, key, NT, preferred_element_type=jnp.float32) * scale,
                NEG_LARGE,
            )
            for ok, key in zip(cache_ok + [step_ok & (step_head == k)], keys)
        ]
        top = functools.reduce(jnp.maximum, [jnp.max(s, axis=1, keepdims=True) for s in scores])
        weights = [jnp.exp(s - top) for s in scores]
        total = sum(jnp.sum(w, axis=1, keepdims=True) for w in weights)
        mixed = sum(
            jnp.dot(w.astype(jnp.bfloat16), v, preferred_element_type=jnp.float32)
            for w, v in zip(weights, values)
        )
        for s in range(steps):
            here = pl.ds(s * stride + k * group, group)
            part = slice(s * group, (s + 1) * group)
            acc[here, :] = mixed[part]
            top_out[here, :] = jnp.broadcast_to(top[part], (group, HD))
            total_out[here, :] = jnp.broadcast_to(total[part], (group, HD))

    my_slot = jnp.int32(-1)
    my_length = jnp.int32(0)
    for r in range(placement.shape[0]):
        hit = div(placement[r], dec_rows) == lax.axis_index("tensor")
        my_slot = jnp.where(hit, mod(placement[r], dec_rows), my_slot)
        my_length = jnp.where(hit, (counts[r] - 1) * BLK + last[r], my_length)
    row = lax.broadcasted_iota(jnp.int32, fresh_ok.shape, 0)
    col = lax.broadcasted_iota(jnp.int32, fresh_ok.shape, 1)
    ok = (
        (mod(div(row, group), KVH) == div(col, CAPT))
        & (mod(row, dec_rows) == my_slot)
        & (mod(col, CAPT) < my_length)
    )
    fresh_ok[...] = jnp.where(ok, jnp.float32(1), jnp.float32(0))


def merge_kernel(features, box, acc, top_in, total_in, fresh_ok, query, out, result, sems):
    devices = box.shape[0]
    rank = box.shape[1] - 2 * CAPT
    terms = [box[i, :CAPT].astype(jnp.float32) for i in range(devices)]
    while len(terms) > 1:
        pairs = [a + b for a, b in zip(terms[::2], terms[1::2])]
        terms = pairs + terms[2 * len(pairs) :]
    shrunk = terms[0].astype(jnp.bfloat16)
    halves = (shrunk[:, :rank], shrunk[:, rank:])
    pieces = HD // features

    def rows(i, first, count):
        parts = [box[i * pieces + p, first : first + count, :features] for p in range(pieces)]
        return parts[0] if pieces == 1 else jnp.concatenate(parts, axis=1)

    def fresh(first):
        made = []
        for i in range(first, first + KVH, 2):
            ups = jnp.concatenate([rows(i + j, 2 * CAPT, rank) for j in range(2)], axis=1)
            delta = jnp.dot(halves[first // KVH], ups, preferred_element_type=jnp.float32)
            for j in range(2):
                base = rows(i + j, CAPT, CAPT).astype(jnp.float32)
                both = base + ADAPTER_SCALE * delta[:, j * HD : (j + 1) * HD]
                made.append(both.astype(jnp.bfloat16))
        return jnp.concatenate(made, axis=0)

    keys, values = fresh(0), fresh(KVH)
    scale = HD ** (-0.5)
    part = out.shape[0] // sems.shape[0]
    copies = []
    for c in range(sems.shape[0]):
        here = pl.ds(c * part, part)
        s = lax.dot_general(query[here, :], keys, NT, preferred_element_type=jnp.float32)
        s = jnp.where(fresh_ok[here, :] > 0, s * scale, NEG_LARGE)
        old = top_in[here, :]
        top = jnp.maximum(old, jnp.max(s, axis=1, keepdims=True))
        fade = jnp.exp(old - top)
        w = jnp.exp(s - top)
        total = total_in[here, :] * fade + jnp.sum(w, axis=1, keepdims=True)
        mixed = acc[here, :] * fade + jnp.dot(
            w.astype(jnp.bfloat16), values, preferred_element_type=jnp.float32
        )
        result[here, :] = (mixed / total).astype(jnp.bfloat16)
        copies.append(pltpu.make_async_copy(result.at[here, :], out.at[here, :], sems.at[c]))
        copies[c].start()
    for copy in copies:
        copy.wait()


def body(
    hidden,
    key_value_weight,
    adapter_down_weight,
    adapter_up_weight,
    tenant,
    tenant_page_table,
    request_block_count,
    last_block_tokens,
    placement,
    key_value_cache,
    context_length,
    decode_step_query,
    step_key_value,
):
    devices = lax.axis_size("tensor")
    tokens, width = hidden.shape
    features = key_value_weight.shape[0]
    local, pages, rank2 = adapter_down_weight.shape
    rank = adapter_up_weight.shape[2]
    tenants = tenant_page_table.shape[0]
    dec_rows, ctx, kv_width = key_value_cache.shape
    steps = step_key_value.shape[0]
    heads2 = kv_width // HD
    d_chunks, chunks = 4, 2
    up_by_page = jnp.transpose(adapter_up_weight, (1, 2, 0))
    rows = 2 * CAPT + rank
    outgoing = pl.pallas_call(
        functools.partial(project_kernel, dec_rows, d_chunks, chunks, devices),
        out_shape=pltpu.VMEM((devices, rows, HD), WIRE),
        in_specs=[ANY_SPEC] * 8,
        out_specs=VMEM_SPEC,
        scratch_shapes=[
            pltpu.SMEM(tenant.shape, jnp.int32),
            pltpu.SMEM(tenant_page_table.shape, jnp.int32),
            pltpu.SMEM(request_block_count.shape, jnp.int32),
            pltpu.SMEM(placement.shape, jnp.int32),
            pltpu.VMEM((chunks, tokens, width // chunks), jnp.bfloat16),
            pltpu.VMEM((chunks, features, width // chunks), jnp.bfloat16),
            pltpu.VMEM((local, pages, rank2), jnp.bfloat16),
            pltpu.VMEM((tokens, local), jnp.bfloat16),
            pltpu.VMEM((pages, rank, features), jnp.bfloat16),
            pltpu.VMEM((local // 16, tenants * 16, rank2), jnp.bfloat16),
            pltpu.VMEM((tenants, tokens + BLK, rank2), jnp.float32),
            pltpu.VMEM((tokens + BLK, HD), jnp.float32),
            pltpu.SMEM((2, devices), jnp.int32),
            pltpu.SemaphoreType.DMA((chunks, 2)),
            pltpu.SemaphoreType.DMA((d_chunks + 2,)),
            pltpu.SemaphoreType.DMA((4,)),
        ],
        compiler_params=pltpu.CompilerParams(vmem_limit_bytes=PROJECT_VMEM),
        name="project",
    )(
        *(
            pltpu.with_memory_space_constraint(x, pltpu.HBM)
            for x in (
                tenant, tenant_page_table, request_block_count, placement,
                hidden, key_value_weight, adapter_down_weight, up_by_page,
            )
        )
    )
    arrived = lax.all_to_all(outgoing, "tensor", split_axis=0, concat_axis=0, tiled=True)

    query = decode_step_query.reshape(steps, dec_rows, HEADS, HD)
    query = query.transpose(0, 2, 1, 3).reshape(steps * HEADS * dec_rows, HD)
    steps_kv = step_key_value.reshape(steps, dec_rows, heads2, HD)
    steps_kv = steps_kv.transpose(0, 2, 1, 3).reshape(steps * heads2 * dec_rows, HD)
    state = jax.ShapeDtypeStruct((steps * HEADS * dec_rows, HD), jnp.float32)
    acc, top, total, fresh_ok = pl.pallas_call(
        cached_kernel,
        out_shape=(state,) * 4,
        in_specs=[SMEM_SPEC] * 4 + [VMEM_SPEC] * 3,
        out_specs=(VMEM_SPEC,) * 4,
        compiler_params=pltpu.CompilerParams(vmem_limit_bytes=ATTEND_VMEM),
        name="cached",
    )(
        context_length, request_block_count, last_block_tokens, placement,
        key_value_cache, query, steps_kv,
    )
    attended = pl.pallas_call(
        functools.partial(merge_kernel, features),
        out_shape=jax.ShapeDtypeStruct((steps * HEADS * dec_rows, HD), jnp.bfloat16),
        in_specs=[VMEM_SPEC] * 6,
        out_specs=ANY_SPEC,
        scratch_shapes=[
            pltpu.VMEM((steps * HEADS * dec_rows, HD), jnp.bfloat16),
            pltpu.SemaphoreType.DMA((steps,)),
        ],
        compiler_params=pltpu.CompilerParams(vmem_limit_bytes=ATTEND_VMEM),
        name="merge",
    )(arrived, acc, top, total, fresh_ok, query)
    attended = attended.reshape(steps, HEADS, dec_rows, HD).transpose(0, 2, 1, 3)
    return attended.reshape(steps, dec_rows, HEADS * HD)


def solution(mesh):
    return jax.shard_map(
        body,
        mesh=mesh,
        in_specs=(
            P("parts", None),
            P("tensor", None),
            P("tensor", None, None),
            P("tensor", None, None),
            P("parts"),
            P(),
            P("parts"),
            P("parts"),
            P("parts"),
            P(("parts", "tensor"), None, None),
            P(("parts", "tensor")),
            P(None, ("parts", "tensor"), None),
            P(None, ("parts", "tensor"), None),
        ),
        out_specs=P(None, ("parts", "tensor"), None),
        check_vma=False,
    )
```

```python
import functools

import jax
import jax.numpy as jnp
from jax import lax
from jax.experimental import pallas as pl
from jax.experimental.pallas import tpu as pltpu
from jax.sharding import PartitionSpec as P

HEADS = 64
KVH = 8
HD = 128
BLK = 8
MOSTB = 2
CAPT = MOSTB * BLK
ADAPTER_SCALE = 0.5
NEG_LARGE = -1e30
PROJECT_VMEM = 32 * 1024 * 1024
ATTEND_VMEM = 16 * 1024 * 1024
WIRE = jnp.bfloat16

SMEM_SPEC = pl.BlockSpec(memory_space=pltpu.SMEM)
VMEM_SPEC = pl.BlockSpec(memory_space=pltpu.VMEM)
ANY_SPEC = pl.BlockSpec(memory_space=pl.ANY)


def div(x, n):
    shift = n.bit_length() - 1
    return lax.shift_right_logical(x, shift) if n == 1 << shift else x // n


def mod(x, n):
    return x & (n - 1) if n & (n - 1) == 0 else x % n


def project_kernel(
    dec_rows, d_chunks, chunks, devices, tenant_h, table_h, counts_h, placement_h, hidden, weight, down, up, out,
    tenant, table, counts, placement,
    h_s, w_s, d_s, mine_s, u_s, sel_s, part_s, base_s, dest_table, sems, d_sems, int_sems,
):
    tokens, width = hidden.shape
    features = weight.shape[0]
    local, pages, rank2 = down.shape
    tenants = table.shape[0]
    requests = tenant.shape[0]
    me = lax.axis_index("tensor")
    d_step = local // d_chunks
    step = width // chunks

    int_copies = [
        pltpu.make_async_copy(src, dst, int_sems.at[i])
        for i, (src, dst) in enumerate(
            ((table_h, table), (tenant_h, tenant), (counts_h, counts), (placement_h, placement))
        )
    ]
    d_copies = [
        pltpu.make_async_copy(
            down.at[pl.ds(c * d_step, d_step)], d_s.at[pl.ds(c * d_step, d_step)], d_sems.at[c])
        for c in range(d_chunks)
    ]
    h_copies = [
        pltpu.make_async_copy(hidden.at[:, pl.ds(c * step, step)], h_s.at[c], sems.at[c, 0])
        for c in range(chunks)
    ]
    w_copies = [
        pltpu.make_async_copy(weight.at[:, pl.ds(c * step, step)], w_s.at[c], sems.at[c, 1])
        for c in range(chunks)
    ]
    my_copy = pltpu.make_async_copy(
        hidden.at[:, pl.ds(pl.multiple_of(me * local, 128), local)], mine_s, d_sems.at[d_chunks]
    )
    up_copy = pltpu.make_async_copy(up, u_s, d_sems.at[d_chunks + 1])
    for copy in d_copies + int_copies[:1] + [my_copy]:
        copy.start()
    for c in range(chunks):
        h_copies[c].start()
        w_copies[c].start()
    for copy in int_copies[1:] + [up_copy]:
        copy.start()

    int_copies[0].wait()
    rows = lax.broadcasted_iota(jnp.int32, (tenants * 16, 16 * pages), 0)
    cols = lax.broadcasted_iota(jnp.int32, (tenants * 16, 16 * pages), 1)
    page_of_row = jnp.zeros_like(rows)
    for k in range(tenants):
        page_of_row = jnp.where(div(rows, 16) == k, table[k], page_of_row)
    pick = (mod(rows, 16) == div(cols, pages)) & (mod(cols, pages) == page_of_row)
    pick = jnp.where(pick, jnp.float32(1), jnp.float32(0)).astype(jnp.bfloat16)

    for c in range(d_chunks):
        d_copies[c].wait()
        for b in range(c * d_step // 16, (c + 1) * d_step // 16, 2):
            block = jnp.concatenate(
                [d_s[pl.ds((b + i) * 16, 16)].reshape(16 * pages, rank2) for i in range(2)], axis=1
            )
            chosen = jnp.dot(pick, block, preferred_element_type=jnp.float32)
            for i in range(2):
                sel_s[b + i] = chosen[:, i * rank2 : (i + 1) * rank2].astype(jnp.bfloat16)
    for copy in int_copies[1:]:
        copy.wait()
    for dest in range(devices):
        dest_table[0, dest] = 0
        dest_table[1, dest] = 0
    first = jnp.int32(0)
    for r in range(requests):
        dest = div(placement[r], dec_rows)
        dest_table[0, dest] = first * BLK
        dest_table[1, dest] = tenant[r]
        first = first + counts[r]
    my_copy.wait()
    mine = mine_s[...]
    for k in range(0, tenants, 2):
        pair = min(2, tenants - k)
        maps = jnp.concatenate(
            [sel_s[:, j * 16 : (j + 1) * 16, :].reshape(local, rank2) for j in range(k, k + pair)],
            axis=1,
        )
        product = jnp.dot(mine, maps, preferred_element_type=jnp.float32)
        for j in range(pair):
            part_s[k + j, :tokens] = product[:, j * rank2 : (j + 1) * rank2]
            part_s[k + j, tokens:] = jnp.zeros((BLK, rank2), jnp.float32)

    total = jnp.zeros((tokens, features), jnp.float32)
    for c in range(chunks):
        h_copies[c].wait()
        w_copies[c].wait()
        total = total + lax.dot_general(h_s[c], w_s[c], NT, preferred_element_type=jnp.float32)
    base_s[tokens:] = jnp.zeros((BLK, HD), jnp.float32)
    if features < HD:
        base_s[...] = jnp.zeros_like(base_s)
    base_s[:tokens, :features] = total
    up_copy.wait()
    for dest in range(devices):
        start = pl.multiple_of(dest_table[0, dest], BLK)
        who = dest_table[1, dest]
        out[dest, :CAPT, :] = part_s[who, pl.ds(start, CAPT), :].astype(out.dtype)
        out[dest, CAPT : 2 * CAPT, :] = base_s[pl.ds(start, CAPT), :].astype(out.dtype)
        if features < HD:
            out[dest, 2 * CAPT :, :] = jnp.zeros((out.shape[1] - 2 * CAPT, HD), out.dtype)
        out[dest, 2 * CAPT :, :features] = u_s[table[who]]


NT = (((1,), (1,)), ((), ()))


def gather_queries(query, k, group, steps, stride):
    return jnp.concatenate(
        [query[pl.ds(s * stride + k * group, group), :] for s in range(steps)], axis=0
    )


def cached_kernel(
    lengths, counts, last, placement, cache, query, steps_kv, acc, top_out, total_out, fresh_ok,
):
    dec_rows, ctx, kv_width = cache.shape
    half_width = kv_width // 2
    step_rows = KVH * dec_rows
    steps = steps_kv.shape[0] // (2 * step_rows)
    group = HEADS // KVH * dec_rows
    q_rows = steps * group
    stride = HEADS * dec_rows

    row = lax.broadcasted_iota(jnp.int32, (q_rows, ctx), 0)
    col = lax.broadcasted_iota(jnp.int32, (q_rows, ctx), 1)
    row_slot = mod(row, dec_rows)
    cache_ok = [(row_slot == g) & (col < lengths[g]) for g in range(dec_rows)]
    row = lax.broadcasted_iota(jnp.int32, (q_rows, steps * step_rows), 0)
    col = lax.broadcasted_iota(jnp.int32, (q_rows, steps * step_rows), 1)
    step_ok = (mod(row, dec_rows) == mod(col, dec_rows)) & (div(col, step_rows) <= div(row, group))
    step_head = div(mod(col, step_rows), dec_rows)
    step_keys, step_values = (
        jnp.concatenate(
            [steps_kv[pl.ds((2 * s + half) * step_rows, step_rows), :] for s in range(steps)], axis=0
        )
        for half in range(2)
    )

    scale = HD ** (-0.5)
    for k in range(KVH):
        lanes = pl.ds(k * HD, HD)
        vlanes = pl.ds(half_width + k * HD, HD)
        q = gather_queries(query, k, group, steps, stride)
        keys = [cache[g, :, lanes] for g in range(dec_rows)] + [step_keys]
        values = [cache[g, :, vlanes] for g in range(dec_rows)] + [step_values]
        scores = [
            jnp.where(
                ok,
                lax.dot_general(q, key, NT, preferred_element_type=jnp.float32) * scale,
                NEG_LARGE,
            )
            for ok, key in zip(cache_ok + [step_ok & (step_head == k)], keys)
        ]
        top = functools.reduce(jnp.maximum, [jnp.max(s, axis=1, keepdims=True) for s in scores])
        weights = [jnp.exp(s - top) for s in scores]
        total = sum(jnp.sum(w, axis=1, keepdims=True) for w in weights)
        mixed = sum(
            jnp.dot(w.astype(jnp.bfloat16), v, preferred_element_type=jnp.float32)
            for w, v in zip(weights, values)
        )
        for s in range(steps):
            here = pl.ds(s * stride + k * group, group)
            part = slice(s * group, (s + 1) * group)
            acc[here, :] = mixed[part]
            top_out[here, :] = jnp.broadcast_to(top[part], (group, HD))
            total_out[here, :] = jnp.broadcast_to(total[part], (group, HD))

    my_slot = jnp.int32(-1)
    my_length = jnp.int32(0)
    for r in range(placement.shape[0]):
        hit = div(placement[r], dec_rows) == lax.axis_index("tensor")
        my_slot = jnp.where(hit, mod(placement[r], dec_rows), my_slot)
        my_length = jnp.where(hit, (counts[r] - 1) * BLK + last[r], my_length)
    row = lax.broadcasted_iota(jnp.int32, fresh_ok.shape, 0)
    col = lax.broadcasted_iota(jnp.int32, fresh_ok.shape, 1)
    ok = (
        (mod(div(row, group), KVH) == div(col, CAPT))
        & (mod(row, dec_rows) == my_slot)
        & (mod(col, CAPT) < my_length)
    )
    fresh_ok[...] = jnp.where(ok, jnp.float32(1), jnp.float32(0))


def merge_kernel(features, box, acc, top_in, total_in, fresh_ok, query, out, result, sems):
    devices = box.shape[0]
    rank = box.shape[1] - 2 * CAPT
    terms = [box[i, :CAPT].astype(jnp.float32) for i in range(devices)]
    while len(terms) > 1:
        pairs = [a + b for a, b in zip(terms[::2], terms[1::2])]
        terms = pairs + terms[2 * len(pairs) :]
    shrunk = terms[0].astype(jnp.bfloat16)
    halves = (shrunk[:, :rank], shrunk[:, rank:])
    pieces = HD // features

    def rows(i, first, count):
        parts = [box[i * pieces + p, first : first + count, :features] for p in range(pieces)]
        return parts[0] if pieces == 1 else jnp.concatenate(parts, axis=1)

    def fresh(first):
        made = []
        for i in range(first, first + KVH, 2):
            ups = jnp.concatenate([rows(i + j, 2 * CAPT, rank) for j in range(2)], axis=1)
            delta = jnp.dot(halves[first // KVH], ups, preferred_element_type=jnp.float32)
            for j in range(2):
                base = rows(i + j, CAPT, CAPT).astype(jnp.float32)
                both = base + ADAPTER_SCALE * delta[:, j * HD : (j + 1) * HD]
                made.append(both.astype(jnp.bfloat16))
        return jnp.concatenate(made, axis=0)

    keys, values = fresh(0), fresh(KVH)
    scale = HD ** (-0.5)
    part = out.shape[0] // sems.shape[0]
    copies = []
    for c in range(sems.shape[0]):
        here = pl.ds(c * part, part)
        s = lax.dot_general(query[here, :], keys, NT, preferred_element_type=jnp.float32)
        s = jnp.where(fresh_ok[here, :] > 0, s * scale, NEG_LARGE)
        old = top_in[here, :]
        top = jnp.maximum(old, jnp.max(s, axis=1, keepdims=True))
        fade = jnp.exp(old - top)
        w = jnp.exp(s - top)
        total = total_in[here, :] * fade + jnp.sum(w, axis=1, keepdims=True)
        mixed = acc[here, :] * fade + jnp.dot(
            w.astype(jnp.bfloat16), values, preferred_element_type=jnp.float32
        )
        result[here, :] = (mixed / total).astype(jnp.bfloat16)
        copies.append(pltpu.make_async_copy(result.at[here, :], out.at[here, :], sems.at[c]))
        copies[c].start()
    for copy in copies:
        copy.wait()


def body(
    hidden,
    key_value_weight,
    adapter_down_weight,
    adapter_up_weight,
    tenant,
    tenant_page_table,
    request_block_count,
    last_block_tokens,
    placement,
    key_value_cache,
    context_length,
    decode_step_query,
    step_key_value,
):
    devices = lax.axis_size("tensor")
    tokens, width = hidden.shape
    features = key_value_weight.shape[0]
    local, pages, rank2 = adapter_down_weight.shape
    rank = adapter_up_weight.shape[2]
    tenants = tenant_page_table.shape[0]
    dec_rows, ctx, kv_width = key_value_cache.shape
    steps = step_key_value.shape[0]
    heads2 = kv_width // HD
    d_chunks, chunks = 4, 2
    up_by_page = jnp.transpose(adapter_up_weight, (1, 2, 0))
    rows = 2 * CAPT + rank
    outgoing = pl.pallas_call(
        functools.partial(project_kernel, dec_rows, d_chunks, chunks, devices),
        out_shape=pltpu.VMEM((devices, rows, HD), WIRE),
        in_specs=[ANY_SPEC] * 8,
        out_specs=VMEM_SPEC,
        scratch_shapes=[
            pltpu.SMEM(tenant.shape, jnp.int32),
            pltpu.SMEM(tenant_page_table.shape, jnp.int32),
            pltpu.SMEM(request_block_count.shape, jnp.int32),
            pltpu.SMEM(placement.shape, jnp.int32),
            pltpu.VMEM((chunks, tokens, width // chunks), jnp.bfloat16),
            pltpu.VMEM((chunks, features, width // chunks), jnp.bfloat16),
            pltpu.VMEM((local, pages, rank2), jnp.bfloat16),
            pltpu.VMEM((tokens, local), jnp.bfloat16),
            pltpu.VMEM((pages, rank, features), jnp.bfloat16),
            pltpu.VMEM((local // 16, tenants * 16, rank2), jnp.bfloat16),
            pltpu.VMEM((tenants, tokens + BLK, rank2), jnp.float32),
            pltpu.VMEM((tokens + BLK, HD), jnp.float32),
            pltpu.SMEM((2, devices), jnp.int32),
            pltpu.SemaphoreType.DMA((chunks, 2)),
            pltpu.SemaphoreType.DMA((d_chunks + 2,)),
            pltpu.SemaphoreType.DMA((4,)),
        ],
        compiler_params=pltpu.CompilerParams(vmem_limit_bytes=PROJECT_VMEM),
        name="project",
    )(
        *(
            pltpu.with_memory_space_constraint(x, pltpu.HBM)
            for x in (
                tenant, tenant_page_table, request_block_count, placement,
                hidden, key_value_weight, adapter_down_weight, up_by_page,
            )
        )
    )
    arrived = lax.all_to_all(outgoing, "tensor", split_axis=0, concat_axis=0, tiled=True)

    query = decode_step_query.reshape(steps, dec_rows, HEADS, HD)
    query = query.transpose(0, 2, 1, 3).reshape(steps * HEADS * dec_rows, HD)
    steps_kv = step_key_value.reshape(steps, dec_rows, heads2, HD)
    steps_kv = steps_kv.transpose(0, 2, 1, 3).reshape(steps * heads2 * dec_rows, HD)
    state = jax.ShapeDtypeStruct((steps * HEADS * dec_rows, HD), jnp.float32)
    acc, top, total, fresh_ok = pl.pallas_call(
        cached_kernel,
        out_shape=(state,) * 4,
        in_specs=[SMEM_SPEC] * 4 + [VMEM_SPEC] * 3,
        out_specs=(VMEM_SPEC,) * 4,
        compiler_params=pltpu.CompilerParams(vmem_limit_bytes=ATTEND_VMEM),
        name="cached",
    )(
        context_length, request_block_count, last_block_tokens, placement,
        key_value_cache, query, steps_kv,
    )
    attended = pl.pallas_call(
        functools.partial(merge_kernel, features),
        out_shape=jax.ShapeDtypeStruct((steps * HEADS * dec_rows, HD), jnp.bfloat16),
        in_specs=[VMEM_SPEC] * 6,
        out_specs=ANY_SPEC,
        scratch_shapes=[
            pltpu.VMEM((steps * HEADS * dec_rows, HD), jnp.bfloat16),
            pltpu.SemaphoreType.DMA((steps,)),
        ],
        compiler_params=pltpu.CompilerParams(vmem_limit_bytes=ATTEND_VMEM),
        name="merge",
    )(arrived, acc, top, total, fresh_ok, query)
    attended = attended.reshape(steps, HEADS, dec_rows, HD).transpose(0, 2, 1, 3)
    return attended.reshape(steps, dec_rows, HEADS * HD)


def solution(mesh):
    return jax.shard_map(
        body,
        mesh=mesh,
        in_specs=(
            P("parts", None),
            P("tensor", None),
            P("tensor", None, None),
            P("tensor", None, None),
            P("parts"),
            P(),
            P("parts"),
            P("parts"),
            P("parts"),
            P(("parts", "tensor"), None, None),
            P(("parts", "tensor")),
            P(None, ("parts", "tensor"), None),
            P(None, ("parts", "tensor"), None),
        ),
        out_specs=P(None, ("parts", "tensor"), None),
        check_vma=False,
    )
```

```python
import functools

import jax
import jax.numpy as jnp
from jax import lax
from jax.experimental import pallas as pl
from jax.experimental.pallas import tpu as pltpu
from jax.sharding import PartitionSpec as P

HEADS = 64
KVH = 8
HD = 128
BLK = 8
MOSTB = 2
CAPT = MOSTB * BLK
ADAPTER_SCALE = 0.5
NEG_LARGE = -1e30
PROJECT_VMEM = 32 * 1024 * 1024
ATTEND_VMEM = 16 * 1024 * 1024
WIRE = jnp.bfloat16

SMEM_SPEC = pl.BlockSpec(memory_space=pltpu.SMEM)
VMEM_SPEC = pl.BlockSpec(memory_space=pltpu.VMEM)
ANY_SPEC = pl.BlockSpec(memory_space=pl.ANY)


def div(x, n):
    shift = n.bit_length() - 1
    return lax.shift_right_logical(x, shift) if n == 1 << shift else x // n


def mod(x, n):
    return x & (n - 1) if n & (n - 1) == 0 else x % n


def project_kernel(
    dec_rows, d_chunks, chunks, devices, tenant_h, table_h, counts_h, placement_h, hidden, weight, down, up, out,
    tenant, table, counts, placement,
    h_s, w_s, d_s, mine_s, u_s, sel_s, part_s, base_s, dest_table, sems, d_sems, int_sems,
):
    tokens, width = hidden.shape
    features = weight.shape[0]
    local, pages, rank2 = down.shape
    tenants = table.shape[0]
    requests = tenant.shape[0]
    me = lax.axis_index("tensor")
    d_step = local // d_chunks
    step = width // chunks

    int_copies = [
        pltpu.make_async_copy(src, dst, int_sems.at[i])
        for i, (src, dst) in enumerate(
            ((table_h, table), (tenant_h, tenant), (counts_h, counts), (placement_h, placement))
        )
    ]
    d_copies = [
        pltpu.make_async_copy(
            down.at[pl.ds(c * d_step, d_step)], d_s.at[pl.ds(c * d_step, d_step)], d_sems.at[c])
        for c in range(d_chunks)
    ]
    h_copies = [
        pltpu.make_async_copy(hidden.at[:, pl.ds(c * step, step)], h_s.at[c], sems.at[c, 0])
        for c in range(chunks)
    ]
    w_copies = [
        pltpu.make_async_copy(weight.at[:, pl.ds(c * step, step)], w_s.at[c], sems.at[c, 1])
        for c in range(chunks)
    ]
    my_copy = pltpu.make_async_copy(
        hidden.at[:, pl.ds(pl.multiple_of(me * local, 128), local)], mine_s, d_sems.at[d_chunks]
    )
    up_copy = pltpu.make_async_copy(up, u_s, d_sems.at[d_chunks + 1])
    for copy in d_copies + int_copies[:1] + [my_copy]:
        copy.start()
    for c in range(chunks):
        h_copies[c].start()
        w_copies[c].start()
    for copy in int_copies[1:] + [up_copy]:
        copy.start()

    int_copies[0].wait()
    rows = lax.broadcasted_iota(jnp.int32, (tenants * 16, 16 * pages), 0)
    cols = lax.broadcasted_iota(jnp.int32, (tenants * 16, 16 * pages), 1)
    page_of_row = jnp.zeros_like(rows)
    for k in range(tenants):
        page_of_row = jnp.where(div(rows, 16) == k, table[k], page_of_row)
    pick = (mod(rows, 16) == div(cols, pages)) & (mod(cols, pages) == page_of_row)
    pick = jnp.where(pick, jnp.float32(1), jnp.float32(0)).astype(jnp.bfloat16)

    for c in range(d_chunks):
        d_copies[c].wait()
        for b in range(c * d_step // 16, (c + 1) * d_step // 16, 2):
            block = jnp.concatenate(
                [d_s[pl.ds((b + i) * 16, 16)].reshape(16 * pages, rank2) for i in range(2)], axis=1
            )
            chosen = jnp.dot(pick, block, preferred_element_type=jnp.float32)
            for i in range(2):
                sel_s[b + i] = chosen[:, i * rank2 : (i + 1) * rank2].astype(jnp.bfloat16)
    for copy in int_copies[1:]:
        copy.wait()
    for dest in range(devices):
        dest_table[0, dest] = 0
        dest_table[1, dest] = 0
    first = jnp.int32(0)
    for r in range(requests):
        dest = div(placement[r], dec_rows)
        dest_table[0, dest] = first * BLK
        dest_table[1, dest] = tenant[r]
        first = first + counts[r]
    my_copy.wait()
    mine = mine_s[...]
    for k in range(0, tenants, 2):
        pair = min(2, tenants - k)
        maps = jnp.concatenate(
            [sel_s[:, j * 16 : (j + 1) * 16, :].reshape(local, rank2) for j in range(k, k + pair)],
            axis=1,
        )
        product = jnp.dot(mine, maps, preferred_element_type=jnp.float32)
        for j in range(pair):
            part_s[k + j, :tokens] = product[:, j * rank2 : (j + 1) * rank2]
            part_s[k + j, tokens:] = jnp.zeros((BLK, rank2), jnp.float32)

    total = jnp.zeros((tokens, features), jnp.float32)
    for c in range(chunks):
        h_copies[c].wait()
        w_copies[c].wait()
        quarter = width // chunks // 4
        sums = [
            lax.dot_general(
                h_s[c, :, i * quarter : (i + 1) * quarter],
                w_s[c, :, i * quarter : (i + 1) * quarter],
                NT,
                preferred_element_type=jnp.float32,
            )
            for i in range(4)
        ]
        total = total + ((sums[0] + sums[1]) + (sums[2] + sums[3]))
    base_s[tokens:] = jnp.zeros((BLK, HD), jnp.float32)
    if features < HD:
        base_s[...] = jnp.zeros_like(base_s)
    base_s[:tokens, :features] = total
    up_copy.wait()
    for dest in range(devices):
        start = pl.multiple_of(dest_table[0, dest], BLK)
        who = dest_table[1, dest]
        out[dest, :CAPT, :] = part_s[who, pl.ds(start, CAPT), :].astype(out.dtype)
        out[dest, CAPT : 2 * CAPT, :] = base_s[pl.ds(start, CAPT), :].astype(out.dtype)
        if features < HD:
            out[dest, 2 * CAPT :, :] = jnp.zeros((out.shape[1] - 2 * CAPT, HD), out.dtype)
        out[dest, 2 * CAPT :, :features] = u_s[table[who]]


NT = (((1,), (1,)), ((), ()))


def gather_queries(query, k, group, steps, stride):
    return jnp.concatenate(
        [query[pl.ds(s * stride + k * group, group), :] for s in range(steps)], axis=0
    )


def cached_kernel(
    lengths, counts, last, placement, cache, query, steps_kv, acc, top_out, total_out, fresh_ok,
):
    dec_rows, ctx, kv_width = cache.shape
    half_width = kv_width // 2
    step_rows = KVH * dec_rows
    steps = steps_kv.shape[0] // (2 * step_rows)
    group = HEADS // KVH * dec_rows
    q_rows = steps * group
    stride = HEADS * dec_rows

    row = lax.broadcasted_iota(jnp.int32, (q_rows, ctx), 0)
    col = lax.broadcasted_iota(jnp.int32, (q_rows, ctx), 1)
    row_slot = mod(row, dec_rows)
    cache_ok = [(row_slot == g) & (col < lengths[g]) for g in range(dec_rows)]
    row = lax.broadcasted_iota(jnp.int32, (q_rows, steps * step_rows), 0)
    col = lax.broadcasted_iota(jnp.int32, (q_rows, steps * step_rows), 1)
    step_ok = (mod(row, dec_rows) == mod(col, dec_rows)) & (div(col, step_rows) <= div(row, group))
    step_head = div(mod(col, step_rows), dec_rows)
    step_keys, step_values = (
        jnp.concatenate(
            [steps_kv[pl.ds((2 * s + half) * step_rows, step_rows), :] for s in range(steps)], axis=0
        )
        for half in range(2)
    )

    scale = HD ** (-0.5)
    for k in range(KVH):
        lanes = pl.ds(k * HD, HD)
        vlanes = pl.ds(half_width + k * HD, HD)
        q = gather_queries(query, k, group, steps, stride)
        keys = [cache[g, :, lanes] for g in range(dec_rows)] + [step_keys]
        values = [cache[g, :, vlanes] for g in range(dec_rows)] + [step_values]
        scores = [
            jnp.where(
                ok,
                lax.dot_general(q, key, NT, preferred_element_type=jnp.float32) * scale,
                NEG_LARGE,
            )
            for ok, key in zip(cache_ok + [step_ok & (step_head == k)], keys)
        ]
        top = functools.reduce(jnp.maximum, [jnp.max(s, axis=1, keepdims=True) for s in scores])
        weights = [jnp.exp(s - top) for s in scores]
        total = sum(jnp.sum(w, axis=1, keepdims=True) for w in weights)
        mixed = sum(
            jnp.dot(w.astype(jnp.bfloat16), v, preferred_element_type=jnp.float32)
            for w, v in zip(weights, values)
        )
        for s in range(steps):
            here = pl.ds(s * stride + k * group, group)
            part = slice(s * group, (s + 1) * group)
            acc[here, :] = mixed[part]
            top_out[here, :] = jnp.broadcast_to(top[part], (group, HD))
            total_out[here, :] = jnp.broadcast_to(total[part], (group, HD))

    my_slot = jnp.int32(-1)
    my_length = jnp.int32(0)
    for r in range(placement.shape[0]):
        hit = div(placement[r], dec_rows) == lax.axis_index("tensor")
        my_slot = jnp.where(hit, mod(placement[r], dec_rows), my_slot)
        my_length = jnp.where(hit, (counts[r] - 1) * BLK + last[r], my_length)
    row = lax.broadcasted_iota(jnp.int32, fresh_ok.shape, 0)
    col = lax.broadcasted_iota(jnp.int32, fresh_ok.shape, 1)
    ok = (
        (mod(div(row, group), KVH) == div(col, CAPT))
        & (mod(row, dec_rows) == my_slot)
        & (mod(col, CAPT) < my_length)
    )
    fresh_ok[...] = jnp.where(ok, jnp.float32(1), jnp.float32(0))


def merge_kernel(features, box, acc, top_in, total_in, fresh_ok, query, out, result, sems):
    devices = box.shape[0]
    rank = box.shape[1] - 2 * CAPT
    terms = [box[i, :CAPT].astype(jnp.float32) for i in range(devices)]
    while len(terms) > 1:
        pairs = [a + b for a, b in zip(terms[::2], terms[1::2])]
        terms = pairs + terms[2 * len(pairs) :]
    shrunk = terms[0].astype(jnp.bfloat16)
    halves = (shrunk[:, :rank], shrunk[:, rank:])
    pieces = HD // features

    def rows(i, first, count):
        parts = [box[i * pieces + p, first : first + count, :features] for p in range(pieces)]
        return parts[0] if pieces == 1 else jnp.concatenate(parts, axis=1)

    def fresh(first):
        made = []
        for i in range(first, first + KVH, 2):
            ups = jnp.concatenate([rows(i + j, 2 * CAPT, rank) for j in range(2)], axis=1)
            delta = jnp.dot(halves[first // KVH], ups, preferred_element_type=jnp.float32)
            for j in range(2):
                base = rows(i + j, CAPT, CAPT).astype(jnp.float32)
                both = base + ADAPTER_SCALE * delta[:, j * HD : (j + 1) * HD]
                made.append(both.astype(jnp.bfloat16))
        return jnp.concatenate(made, axis=0)

    keys, values = fresh(0), fresh(KVH)
    scale = HD ** (-0.5)
    part = out.shape[0] // sems.shape[0]
    copies = []
    for c in range(sems.shape[0]):
        here = pl.ds(c * part, part)
        s = lax.dot_general(query[here, :], keys, NT, preferred_element_type=jnp.float32)
        s = jnp.where(fresh_ok[here, :] > 0, s * scale, NEG_LARGE)
        old = top_in[here, :]
        top = jnp.maximum(old, jnp.max(s, axis=1, keepdims=True))
        fade = jnp.exp(old - top)
        w = jnp.exp(s - top)
        total = total_in[here, :] * fade + jnp.sum(w, axis=1, keepdims=True)
        mixed = acc[here, :] * fade + jnp.dot(
            w.astype(jnp.bfloat16), values, preferred_element_type=jnp.float32
        )
        result[here, :] = (mixed / total).astype(jnp.bfloat16)
        copies.append(pltpu.make_async_copy(result.at[here, :], out.at[here, :], sems.at[c]))
        copies[c].start()
    for copy in copies:
        copy.wait()


def body(
    hidden,
    key_value_weight,
    adapter_down_weight,
    adapter_up_weight,
    tenant,
    tenant_page_table,
    request_block_count,
    last_block_tokens,
    placement,
    key_value_cache,
    context_length,
    decode_step_query,
    step_key_value,
):
    devices = lax.axis_size("tensor")
    tokens, width = hidden.shape
    features = key_value_weight.shape[0]
    local, pages, rank2 = adapter_down_weight.shape
    rank = adapter_up_weight.shape[2]
    tenants = tenant_page_table.shape[0]
    dec_rows, ctx, kv_width = key_value_cache.shape
    steps = step_key_value.shape[0]
    heads2 = kv_width // HD
    d_chunks, chunks = 4, 2
    up_by_page = jnp.transpose(adapter_up_weight, (1, 2, 0))
    rows = 2 * CAPT + rank
    outgoing = pl.pallas_call(
        functools.partial(project_kernel, dec_rows, d_chunks, chunks, devices),
        out_shape=pltpu.VMEM((devices, rows, HD), WIRE),
        in_specs=[ANY_SPEC] * 8,
        out_specs=VMEM_SPEC,
        scratch_shapes=[
            pltpu.SMEM(tenant.shape, jnp.int32),
            pltpu.SMEM(tenant_page_table.shape, jnp.int32),
            pltpu.SMEM(request_block_count.shape, jnp.int32),
            pltpu.SMEM(placement.shape, jnp.int32),
            pltpu.VMEM((chunks, tokens, width // chunks), jnp.bfloat16),
            pltpu.VMEM((chunks, features, width // chunks), jnp.bfloat16),
            pltpu.VMEM((local, pages, rank2), jnp.bfloat16),
            pltpu.VMEM((tokens, local), jnp.bfloat16),
            pltpu.VMEM((pages, rank, features), jnp.bfloat16),
            pltpu.VMEM((local // 16, tenants * 16, rank2), jnp.bfloat16),
            pltpu.VMEM((tenants, tokens + BLK, rank2), jnp.float32),
            pltpu.VMEM((tokens + BLK, HD), jnp.float32),
            pltpu.SMEM((2, devices), jnp.int32),
            pltpu.SemaphoreType.DMA((chunks, 2)),
            pltpu.SemaphoreType.DMA((d_chunks + 2,)),
            pltpu.SemaphoreType.DMA((4,)),
        ],
        compiler_params=pltpu.CompilerParams(vmem_limit_bytes=PROJECT_VMEM),
        name="project",
    )(
        *(
            pltpu.with_memory_space_constraint(x, pltpu.HBM)
            for x in (
                tenant, tenant_page_table, request_block_count, placement,
                hidden, key_value_weight, adapter_down_weight, up_by_page,
            )
        )
    )
    arrived = lax.all_to_all(outgoing, "tensor", split_axis=0, concat_axis=0, tiled=True)

    query = decode_step_query.reshape(steps, dec_rows, HEADS, HD)
    query = query.transpose(0, 2, 1, 3).reshape(steps * HEADS * dec_rows, HD)
    steps_kv = step_key_value.reshape(steps, dec_rows, heads2, HD)
    steps_kv = steps_kv.transpose(0, 2, 1, 3).reshape(steps * heads2 * dec_rows, HD)
    state = jax.ShapeDtypeStruct((steps * HEADS * dec_rows, HD), jnp.float32)
    acc, top, total, fresh_ok = pl.pallas_call(
        cached_kernel,
        out_shape=(state,) * 4,
        in_specs=[SMEM_SPEC] * 4 + [VMEM_SPEC] * 3,
        out_specs=(VMEM_SPEC,) * 4,
        compiler_params=pltpu.CompilerParams(vmem_limit_bytes=ATTEND_VMEM),
        name="cached",
    )(
        context_length, request_block_count, last_block_tokens, placement,
        key_value_cache, query, steps_kv,
    )
    attended = pl.pallas_call(
        functools.partial(merge_kernel, features),
        out_shape=jax.ShapeDtypeStruct((steps * HEADS * dec_rows, HD), jnp.bfloat16),
        in_specs=[VMEM_SPEC] * 6,
        out_specs=ANY_SPEC,
        scratch_shapes=[
            pltpu.VMEM((steps * HEADS * dec_rows, HD), jnp.bfloat16),
            pltpu.SemaphoreType.DMA((steps,)),
        ],
        compiler_params=pltpu.CompilerParams(vmem_limit_bytes=ATTEND_VMEM),
        name="merge",
    )(arrived, acc, top, total, fresh_ok, query)
    attended = attended.reshape(steps, HEADS, dec_rows, HD).transpose(0, 2, 1, 3)
    return attended.reshape(steps, dec_rows, HEADS * HD)


def solution(mesh):
    return jax.shard_map(
        body,
        mesh=mesh,
        in_specs=(
            P("parts", None),
            P("tensor", None),
            P("tensor", None, None),
            P("tensor", None, None),
            P("parts"),
            P(),
            P("parts"),
            P("parts"),
            P("parts"),
            P(("parts", "tensor"), None, None),
            P(("parts", "tensor")),
            P(None, ("parts", "tensor"), None),
            P(None, ("parts", "tensor"), None),
        ),
        out_specs=P(None, ("parts", "tensor"), None),
        check_vma=False,
    )
```

```python
import functools

import jax
import jax.numpy as jnp
from jax import lax
from jax.experimental import pallas as pl
from jax.experimental.pallas import tpu as pltpu
from jax.sharding import PartitionSpec as P

HEADS = 64
KVH = 8
HD = 128
BLK = 8
MOSTB = 2
CAPT = MOSTB * BLK
ADAPTER_SCALE = 0.5
NEG_LARGE = -1e30
PROJECT_VMEM = 32 * 1024 * 1024
ATTEND_VMEM = 16 * 1024 * 1024
WIRE = jnp.bfloat16

SMEM_SPEC = pl.BlockSpec(memory_space=pltpu.SMEM)
VMEM_SPEC = pl.BlockSpec(memory_space=pltpu.VMEM)
ANY_SPEC = pl.BlockSpec(memory_space=pl.ANY)


def div(x, n):
    shift = n.bit_length() - 1
    return lax.shift_right_logical(x, shift) if n == 1 << shift else x // n


def mod(x, n):
    return x & (n - 1) if n & (n - 1) == 0 else x % n


def project_kernel(
    dec_rows, parts, tenant_h, table_h, counts_h, placement_h, hidden, weight, down, up, out,
    tenant, table, counts, placement,
    h_s, w_s, wt_s, d_s, mine_s, u_s, sel_s, part_s, base_s, dest_table, w_sems, sems,
):
    tokens, width = hidden.shape
    features = weight.shape[0]
    local, pages, rank2 = down.shape
    tenants = table.shape[0]
    requests = tenant.shape[0]
    devices = out.shape[0]
    me = lax.axis_index("tensor")
    step = width // parts

    int_copies = [
        pltpu.make_async_copy(src, dst, sems.at[3 + i])
        for i, (src, dst) in enumerate(
            ((table_h, table), (tenant_h, tenant), (counts_h, counts), (placement_h, placement))
        )
    ]
    w_copies = [
        pltpu.make_async_copy(
            weight.at[:, pl.ds(c * step, step)], w_s.at[:, pl.ds(c * step, step)], w_sems.at[c])
        for c in range(parts)
    ]
    d_copy = pltpu.make_async_copy(down, d_s, sems.at[0])
    my_copy = pltpu.make_async_copy(
        hidden.at[:, pl.ds(pl.multiple_of(me * local, 128), local)], mine_s, sems.at[1]
    )
    h_copy = pltpu.make_async_copy(hidden, h_s, sems.at[2])
    up_copy = pltpu.make_async_copy(up, u_s, sems.at[7])
    for copy in w_copies + int_copies + [d_copy, my_copy, h_copy, up_copy]:
        copy.start()

    int_copies[0].wait()
    rows = lax.broadcasted_iota(jnp.int32, (tenants * 16, 16 * pages), 0)
    cols = lax.broadcasted_iota(jnp.int32, (tenants * 16, 16 * pages), 1)
    page_of_row = jnp.zeros_like(rows)
    for k in range(tenants):
        page_of_row = jnp.where(div(rows, 16) == k, table[k], page_of_row)
    pick = (mod(rows, 16) == div(cols, pages)) & (mod(cols, pages) == page_of_row)
    pick = jnp.where(pick, jnp.float32(1), jnp.float32(0)).astype(jnp.bfloat16)

    def turn(c):
        if features == HD:
            wt_s[pl.ds(c * step, step), :] = w_s[:, pl.ds(c * step, step)].T

    early = parts // 2
    for c in range(early):
        w_copies[c].wait()
        turn(c)
    for c in range(early, parts):
        w_copies[c].wait()
    d_copy.wait()
    for c in range(early, parts):
        turn(c)
    for b in range(0, local // 16, 2):
        block = jnp.concatenate(
            [d_s[pl.ds((b + i) * 16, 16)].reshape(16 * pages, rank2) for i in range(2)], axis=1
        )
        chosen = jnp.dot(pick, block, preferred_element_type=jnp.float32)
        for i in range(2):
            sel_s[b + i] = chosen[:, i * rank2 : (i + 1) * rank2].astype(jnp.bfloat16)
    for copy in int_copies[1:] + [my_copy, h_copy, up_copy]:
        copy.wait()
    mine = mine_s[...]
    for k in range(0, tenants, 2):
        pair = min(2, tenants - k)
        maps = jnp.concatenate(
            [sel_s[:, j * 16 : (j + 1) * 16, :].reshape(local, rank2) for j in range(k, k + pair)],
            axis=1,
        )
        product = jnp.dot(mine, maps, preferred_element_type=jnp.float32)
        for j in range(pair):
            part_s[k + j, :tokens] = product[:, j * rank2 : (j + 1) * rank2]
            part_s[k + j, tokens:] = jnp.zeros((BLK, rank2), jnp.float32)
    if requests < devices:
        for dest in range(devices):
            dest_table[0, dest] = 0
            dest_table[1, dest] = 0
    first = jnp.int32(0)
    for r in range(requests):
        dest = div(placement[r], dec_rows)
        dest_table[0, dest] = first * BLK
        dest_table[1, dest] = tenant[r]
        first = first + counts[r]

    if features == HD:
        total = jnp.dot(h_s[...], wt_s[...], preferred_element_type=jnp.float32)
    else:
        total = lax.dot_general(h_s[...], w_s[...], NT, preferred_element_type=jnp.float32)
    base_s[tokens:] = jnp.zeros((BLK, HD), jnp.float32)
    if features < HD:
        base_s[...] = jnp.zeros_like(base_s)
    base_s[:tokens, :features] = total
    for dest in range(devices):
        start = pl.multiple_of(dest_table[0, dest], BLK)
        who = dest_table[1, dest]
        out[dest, :CAPT, :] = part_s[who, pl.ds(start, CAPT), :].astype(out.dtype)
        out[dest, CAPT : 2 * CAPT, :] = base_s[pl.ds(start, CAPT), :].astype(out.dtype)
        if features < HD:
            out[dest, 2 * CAPT :, :] = jnp.zeros((out.shape[1] - 2 * CAPT, HD), out.dtype)
        out[dest, 2 * CAPT :, :features] = u_s[table[who]]


NT = (((1,), (1,)), ((), ()))


def gather_queries(query, k, group, steps, stride):
    return jnp.concatenate(
        [query[pl.ds(s * stride + k * group, group), :] for s in range(steps)], axis=0
    )


def cached_kernel(
    lengths, counts, last, placement, cache, query, steps_kv, acc, top_out, total_out, fresh_ok,
):
    dec_rows, ctx, kv_width = cache.shape
    half_width = kv_width // 2
    step_rows = KVH * dec_rows
    steps = steps_kv.shape[0] // (2 * step_rows)
    group = HEADS // KVH * dec_rows
    q_rows = steps * group
    stride = HEADS * dec_rows

    row = lax.broadcasted_iota(jnp.int32, (q_rows, ctx), 0)
    col = lax.broadcasted_iota(jnp.int32, (q_rows, ctx), 1)
    row_slot = mod(row, dec_rows)
    cache_ok = [(row_slot == g) & (col < lengths[g]) for g in range(dec_rows)]
    row = lax.broadcasted_iota(jnp.int32, (q_rows, steps * step_rows), 0)
    col = lax.broadcasted_iota(jnp.int32, (q_rows, steps * step_rows), 1)
    step_ok = (mod(row, dec_rows) == mod(col, dec_rows)) & (div(col, step_rows) <= div(row, group))
    step_head = div(mod(col, step_rows), dec_rows)
    step_keys, step_values = (
        jnp.concatenate(
            [steps_kv[pl.ds((2 * s + half) * step_rows, step_rows), :] for s in range(steps)], axis=0
        )
        for half in range(2)
    )

    scale = HD ** (-0.5)
    for k in range(KVH):
        lanes = pl.ds(k * HD, HD)
        vlanes = pl.ds(half_width + k * HD, HD)
        q = gather_queries(query, k, group, steps, stride)
        keys = [cache[g, :, lanes] for g in range(dec_rows)] + [step_keys]
        values = [cache[g, :, vlanes] for g in range(dec_rows)] + [step_values]
        scores = [
            jnp.where(
                ok,
                lax.dot_general(q, key, NT, preferred_element_type=jnp.float32) * scale,
                NEG_LARGE,
            )
            for ok, key in zip(cache_ok + [step_ok & (step_head == k)], keys)
        ]
        top = functools.reduce(jnp.maximum, [jnp.max(s, axis=1, keepdims=True) for s in scores])
        weights = [jnp.exp(s - top) for s in scores]
        total = sum(jnp.sum(w, axis=1, keepdims=True) for w in weights)
        mixed = sum(
            jnp.dot(w.astype(jnp.bfloat16), v, preferred_element_type=jnp.float32)
            for w, v in zip(weights, values)
        )
        for s in range(steps):
            here = pl.ds(s * stride + k * group, group)
            part = slice(s * group, (s + 1) * group)
            acc[here, :] = mixed[part]
            top_out[here, :] = jnp.broadcast_to(top[part], (group, HD))
            total_out[here, :] = jnp.broadcast_to(total[part], (group, HD))

    my_slot = jnp.int32(-1)
    my_length = jnp.int32(0)
    for r in range(placement.shape[0]):
        hit = div(placement[r], dec_rows) == lax.axis_index("tensor")
        my_slot = jnp.where(hit, mod(placement[r], dec_rows), my_slot)
        my_length = jnp.where(hit, (counts[r] - 1) * BLK + last[r], my_length)
    row = lax.broadcasted_iota(jnp.int32, fresh_ok.shape, 0)
    col = lax.broadcasted_iota(jnp.int32, fresh_ok.shape, 1)
    ok = (
        (mod(div(row, group), KVH) == div(col, CAPT))
        & (mod(row, dec_rows) == my_slot)
        & (mod(col, CAPT) < my_length)
    )
    fresh_ok[...] = jnp.where(ok, jnp.float32(1), jnp.float32(0))


def merge_kernel(features, box, acc, top_in, total_in, fresh_ok, query, out, result, sems):
    devices = box.shape[0]
    rank = box.shape[1] - 2 * CAPT
    terms = [box[i, :CAPT].astype(jnp.float32) for i in range(devices)]
    while len(terms) > 1:
        pairs = [a + b for a, b in zip(terms[::2], terms[1::2])]
        terms = pairs + terms[2 * len(pairs) :]
    shrunk = terms[0].astype(jnp.bfloat16)
    halves = (shrunk[:, :rank], shrunk[:, rank:])
    pieces = HD // features

    def rows(i, first, count):
        parts = [box[i * pieces + p, first : first + count, :features] for p in range(pieces)]
        return parts[0] if pieces == 1 else jnp.concatenate(parts, axis=1)

    def fresh(first):
        made = []
        for i in range(first, first + KVH, 2):
            ups = jnp.concatenate([rows(i + j, 2 * CAPT, rank) for j in range(2)], axis=1)
            delta = jnp.dot(halves[first // KVH], ups, preferred_element_type=jnp.float32)
            for j in range(2):
                base = rows(i + j, CAPT, CAPT).astype(jnp.float32)
                both = base + ADAPTER_SCALE * delta[:, j * HD : (j + 1) * HD]
                made.append(both.astype(jnp.bfloat16))
        return jnp.concatenate(made, axis=0)

    keys, values = fresh(0), fresh(KVH)
    scale = HD ** (-0.5)
    part = out.shape[0] // sems.shape[0]
    copies = []
    for c in range(sems.shape[0]):
        here = pl.ds(c * part, part)
        s = lax.dot_general(query[here, :], keys, NT, preferred_element_type=jnp.float32)
        s = jnp.where(fresh_ok[here, :] > 0, s * scale, NEG_LARGE)
        old = top_in[here, :]
        top = jnp.maximum(old, jnp.max(s, axis=1, keepdims=True))
        fade = jnp.exp(old - top)
        w = jnp.exp(s - top)
        total = total_in[here, :] * fade + jnp.sum(w, axis=1, keepdims=True)
        mixed = acc[here, :] * fade + jnp.dot(
            w.astype(jnp.bfloat16), values, preferred_element_type=jnp.float32
        )
        result[here, :] = (mixed / total).astype(jnp.bfloat16)
        copies.append(pltpu.make_async_copy(result.at[here, :], out.at[here, :], sems.at[c]))
        copies[c].start()
    for copy in copies:
        copy.wait()


def body(
    hidden,
    key_value_weight,
    adapter_down_weight,
    adapter_up_weight,
    tenant,
    tenant_page_table,
    request_block_count,
    last_block_tokens,
    placement,
    key_value_cache,
    context_length,
    decode_step_query,
    step_key_value,
):
    devices = lax.axis_size("tensor")
    tokens, width = hidden.shape
    features = key_value_weight.shape[0]
    local, pages, rank2 = adapter_down_weight.shape
    rank = adapter_up_weight.shape[2]
    tenants = tenant_page_table.shape[0]
    dec_rows, ctx, kv_width = key_value_cache.shape
    steps = step_key_value.shape[0]
    heads2 = kv_width // HD
    parts = 4
    up_by_page = jnp.transpose(adapter_up_weight, (1, 2, 0))
    rows = 2 * CAPT + rank
    outgoing = pl.pallas_call(
        functools.partial(project_kernel, dec_rows, parts),
        out_shape=pltpu.VMEM((devices, rows, HD), WIRE),
        in_specs=[ANY_SPEC] * 8,
        out_specs=VMEM_SPEC,
        scratch_shapes=[
            pltpu.SMEM(tenant.shape, jnp.int32),
            pltpu.SMEM(tenant_page_table.shape, jnp.int32),
            pltpu.SMEM(request_block_count.shape, jnp.int32),
            pltpu.SMEM(placement.shape, jnp.int32),
            pltpu.VMEM((tokens, width), jnp.bfloat16),
            pltpu.VMEM((features, width), jnp.bfloat16),
            pltpu.VMEM((width, HD), jnp.bfloat16),
            pltpu.VMEM((local, pages, rank2), jnp.bfloat16),
            pltpu.VMEM((tokens, local), jnp.bfloat16),
            pltpu.VMEM((pages, rank, features), jnp.bfloat16),
            pltpu.VMEM((local // 16, tenants * 16, rank2), jnp.bfloat16),
            pltpu.VMEM((tenants, tokens + BLK, rank2), jnp.float32),
            pltpu.VMEM((tokens + BLK, HD), jnp.float32),
            pltpu.SMEM((2, devices), jnp.int32),
            pltpu.SemaphoreType.DMA((parts,)),
            pltpu.SemaphoreType.DMA((8,)),
        ],
        compiler_params=pltpu.CompilerParams(vmem_limit_bytes=PROJECT_VMEM),
        name="project",
    )(
        *(
            pltpu.with_memory_space_constraint(x, pltpu.HBM)
            for x in (
                tenant, tenant_page_table, request_block_count, placement,
                hidden, key_value_weight, adapter_down_weight, up_by_page,
            )
        )
    )
    arrived = lax.all_to_all(outgoing, "tensor", split_axis=0, concat_axis=0, tiled=True)

    query = decode_step_query.reshape(steps, dec_rows, HEADS, HD)
    query = query.transpose(0, 2, 1, 3).reshape(steps * HEADS * dec_rows, HD)
    steps_kv = step_key_value.reshape(steps, dec_rows, heads2, HD)
    steps_kv = steps_kv.transpose(0, 2, 1, 3).reshape(steps * heads2 * dec_rows, HD)
    state = jax.ShapeDtypeStruct((steps * HEADS * dec_rows, HD), jnp.float32)
    acc, top, total, fresh_ok = pl.pallas_call(
        cached_kernel,
        out_shape=(state,) * 4,
        in_specs=[SMEM_SPEC] * 4 + [VMEM_SPEC] * 3,
        out_specs=(VMEM_SPEC,) * 4,
        compiler_params=pltpu.CompilerParams(vmem_limit_bytes=ATTEND_VMEM),
        name="cached",
    )(
        context_length, request_block_count, last_block_tokens, placement,
        key_value_cache, query, steps_kv,
    )
    attended = pl.pallas_call(
        functools.partial(merge_kernel, features),
        out_shape=jax.ShapeDtypeStruct((steps * HEADS * dec_rows, HD), jnp.bfloat16),
        in_specs=[VMEM_SPEC] * 6,
        out_specs=ANY_SPEC,
        scratch_shapes=[
            pltpu.VMEM((steps * HEADS * dec_rows, HD), jnp.bfloat16),
            pltpu.SemaphoreType.DMA((steps,)),
        ],
        compiler_params=pltpu.CompilerParams(vmem_limit_bytes=ATTEND_VMEM),
        name="merge",
    )(arrived, acc, top, total, fresh_ok, query)
    attended = attended.reshape(steps, HEADS, dec_rows, HD).transpose(0, 2, 1, 3)
    return attended.reshape(steps, dec_rows, HEADS * HD)


def solution(mesh):
    return jax.shard_map(
        body,
        mesh=mesh,
        in_specs=(
            P("parts", None),
            P("tensor", None),
            P("tensor", None, None),
            P("tensor", None, None),
            P("parts"),
            P(),
            P("parts"),
            P("parts"),
            P("parts"),
            P(("parts", "tensor"), None, None),
            P(("parts", "tensor")),
            P(None, ("parts", "tensor"), None),
            P(None, ("parts", "tensor"), None),
        ),
        out_specs=P(None, ("parts", "tensor"), None),
        check_vma=False,
    )
```

```python
import functools

import jax
import jax.numpy as jnp
from jax import lax
from jax.experimental import pallas as pl
from jax.experimental.pallas import tpu as pltpu
from jax.sharding import PartitionSpec as P

HEADS = 64
KVH = 8
HD = 128
BLK = 8
MOSTB = 2
CAPT = MOSTB * BLK
ADAPTER_SCALE = 0.5
NEG_LARGE = -1e30
PROJECT_VMEM = 32 * 1024 * 1024
ATTEND_VMEM = 16 * 1024 * 1024
WIRE = jnp.bfloat16

SMEM_SPEC = pl.BlockSpec(memory_space=pltpu.SMEM)
VMEM_SPEC = pl.BlockSpec(memory_space=pltpu.VMEM)
ANY_SPEC = pl.BlockSpec(memory_space=pl.ANY)


def div(x, n):
    shift = n.bit_length() - 1
    return lax.shift_right_logical(x, shift) if n == 1 << shift else x // n


def mod(x, n):
    return x & (n - 1) if n & (n - 1) == 0 else x % n


def project_kernel(
    dec_rows, d_chunks, chunks, devices, tenant_h, table_h, counts_h, placement_h, hidden, weight, down, up, out,
    tenant, table, counts, placement,
    h_s, w_s, d_s, mine_s, u_s, sel_s, part_s, base_s, dest_table, sems, d_sems, int_sems,
):
    tokens, width = hidden.shape
    features = weight.shape[0]
    local, pages, rank2 = down.shape
    tenants = table.shape[0]
    requests = tenant.shape[0]
    me = lax.axis_index("tensor")
    d_step = local // d_chunks
    step = width // chunks

    int_copies = [
        pltpu.make_async_copy(src, dst, int_sems.at[i])
        for i, (src, dst) in enumerate(
            ((table_h, table), (tenant_h, tenant), (counts_h, counts), (placement_h, placement))
        )
    ]
    for copy in int_copies:
        copy.start()
    d_copies = [
        pltpu.make_async_copy(
            down.at[pl.ds(c * d_step, d_step)], d_s.at[pl.ds(c * d_step, d_step)], d_sems.at[c])
        for c in range(d_chunks)
    ]
    h_copies = [
        pltpu.make_async_copy(hidden.at[:, pl.ds(c * step, step)], h_s.at[c], sems.at[c, 0])
        for c in range(chunks)
    ]
    w_copies = [
        pltpu.make_async_copy(weight.at[:, pl.ds(c * step, step)], w_s.at[c], sems.at[c, 1])
        for c in range(chunks)
    ]
    my_copy = pltpu.make_async_copy(
        hidden.at[:, pl.ds(pl.multiple_of(me * local, 128), local)], mine_s, d_sems.at[d_chunks]
    )
    up_copy = pltpu.make_async_copy(up, u_s, d_sems.at[d_chunks + 1])
    for copy in d_copies + [my_copy, up_copy]:
        copy.start()
    for c in range(chunks):
        h_copies[c].start()
        w_copies[c].start()

    int_copies[0].wait()
    rows = lax.broadcasted_iota(jnp.int32, (tenants * 16, 16 * pages), 0)
    cols = lax.broadcasted_iota(jnp.int32, (tenants * 16, 16 * pages), 1)
    page_of_row = jnp.zeros_like(rows)
    for k in range(tenants):
        page_of_row = jnp.where(div(rows, 16) == k, table[k], page_of_row)
    pick = (mod(rows, 16) == div(cols, pages)) & (mod(cols, pages) == page_of_row)
    pick = jnp.where(pick, jnp.float32(1), jnp.float32(0)).astype(jnp.bfloat16)

    for c in range(d_chunks):
        d_copies[c].wait()
        for b in range(c * d_step // 16, (c + 1) * d_step // 16, 2):
            block = jnp.concatenate(
                [d_s[pl.ds((b + i) * 16, 16)].reshape(16 * pages, rank2) for i in range(2)], axis=1
            )
            chosen = jnp.dot(pick, block, preferred_element_type=jnp.float32)
            for i in range(2):
                sel_s[b + i] = chosen[:, i * rank2 : (i + 1) * rank2].astype(jnp.bfloat16)
    for copy in int_copies[1:]:
        copy.wait()
    for dest in range(devices):
        dest_table[0, dest] = 0
        dest_table[1, dest] = 0
    first = jnp.int32(0)
    for r in range(requests):
        dest = div(placement[r], dec_rows)
        dest_table[0, dest] = first * BLK
        dest_table[1, dest] = tenant[r]
        first = first + counts[r]
    my_copy.wait()
    mine = mine_s[...]
    for k in range(0, tenants, 2):
        pair = min(2, tenants - k)
        maps = jnp.concatenate(
            [sel_s[:, j * 16 : (j + 1) * 16, :].reshape(local, rank2) for j in range(k, k + pair)],
            axis=1,
        )
        product = jnp.dot(mine, maps, preferred_element_type=jnp.float32)
        for j in range(pair):
            part_s[k + j, :tokens] = product[:, j * rank2 : (j + 1) * rank2]
            part_s[k + j, tokens:] = jnp.zeros((BLK, rank2), jnp.float32)

    total = jnp.zeros((tokens, features), jnp.float32)
    for c in range(chunks):
        h_copies[c].wait()
        w_copies[c].wait()
        total = total + lax.dot_general(h_s[c], w_s[c], NT, preferred_element_type=jnp.float32)
    base_s[tokens:] = jnp.zeros((BLK, HD), jnp.float32)
    if features < HD:
        base_s[...] = jnp.zeros_like(base_s)
    base_s[:tokens, :features] = total
    up_copy.wait()
    for dest in range(devices):
        start = pl.multiple_of(dest_table[0, dest], BLK)
        who = dest_table[1, dest]
        out[dest, :CAPT, :] = part_s[who, pl.ds(start, CAPT), :].astype(out.dtype)
        out[dest, CAPT : 2 * CAPT, :] = base_s[pl.ds(start, CAPT), :].astype(out.dtype)
        if features < HD:
            out[dest, 2 * CAPT :, :] = jnp.zeros((out.shape[1] - 2 * CAPT, HD), out.dtype)
        out[dest, 2 * CAPT :, :features] = u_s[table[who]]


NT = (((1,), (1,)), ((), ()))


def gather_queries(query, k, group, steps, stride):
    return jnp.concatenate(
        [query[pl.ds(s * stride + k * group, group), :] for s in range(steps)], axis=0
    )


def cached_kernel(
    lengths, counts, last, placement, cache, query, steps_kv, acc, top_out, total_out, fresh_ok,
):
    dec_rows, ctx, kv_width = cache.shape
    half_width = kv_width // 2
    step_rows = KVH * dec_rows
    steps = steps_kv.shape[0] // (2 * step_rows)
    group = HEADS // KVH * dec_rows
    q_rows = steps * group
    stride = HEADS * dec_rows

    row = lax.broadcasted_iota(jnp.int32, (q_rows, ctx), 0)
    col = lax.broadcasted_iota(jnp.int32, (q_rows, ctx), 1)
    row_slot = mod(row, dec_rows)
    cache_ok = [(row_slot == g) & (col < lengths[g]) for g in range(dec_rows)]
    row = lax.broadcasted_iota(jnp.int32, (q_rows, steps * step_rows), 0)
    col = lax.broadcasted_iota(jnp.int32, (q_rows, steps * step_rows), 1)
    step_ok = (mod(row, dec_rows) == mod(col, dec_rows)) & (div(col, step_rows) <= div(row, group))
    step_head = div(mod(col, step_rows), dec_rows)
    step_keys, step_values = (
        jnp.concatenate(
            [steps_kv[pl.ds((2 * s + half) * step_rows, step_rows), :] for s in range(steps)], axis=0
        )
        for half in range(2)
    )

    scale = HD ** (-0.5)
    for k in range(KVH):
        lanes = pl.ds(k * HD, HD)
        vlanes = pl.ds(half_width + k * HD, HD)
        q = gather_queries(query, k, group, steps, stride)
        keys = [cache[g, :, lanes] for g in range(dec_rows)] + [step_keys]
        values = [cache[g, :, vlanes] for g in range(dec_rows)] + [step_values]
        scores = [
            jnp.where(
                ok,
                lax.dot_general(q, key, NT, preferred_element_type=jnp.float32) * scale,
                NEG_LARGE,
            )
            for ok, key in zip(cache_ok + [step_ok & (step_head == k)], keys)
        ]
        top = functools.reduce(jnp.maximum, [jnp.max(s, axis=1, keepdims=True) for s in scores])
        weights = [jnp.exp(s - top) for s in scores]
        total = sum(jnp.sum(w, axis=1, keepdims=True) for w in weights)
        mixed = sum(
            jnp.dot(w.astype(jnp.bfloat16), v, preferred_element_type=jnp.float32)
            for w, v in zip(weights, values)
        )
        for s in range(steps):
            here = pl.ds(s * stride + k * group, group)
            part = slice(s * group, (s + 1) * group)
            acc[here, :] = mixed[part]
            top_out[here, :] = jnp.broadcast_to(top[part], (group, HD))
            total_out[here, :] = jnp.broadcast_to(total[part], (group, HD))

    my_slot = jnp.int32(-1)
    my_length = jnp.int32(0)
    for r in range(placement.shape[0]):
        hit = div(placement[r], dec_rows) == lax.axis_index("tensor")
        my_slot = jnp.where(hit, mod(placement[r], dec_rows), my_slot)
        my_length = jnp.where(hit, (counts[r] - 1) * BLK + last[r], my_length)
    row = lax.broadcasted_iota(jnp.int32, fresh_ok.shape, 0)
    col = lax.broadcasted_iota(jnp.int32, fresh_ok.shape, 1)
    ok = (
        (mod(div(row, group), KVH) == div(col, CAPT))
        & (mod(row, dec_rows) == my_slot)
        & (mod(col, CAPT) < my_length)
    )
    fresh_ok[...] = jnp.where(ok, jnp.float32(1), jnp.float32(0))


def merge_kernel(features, box, acc, top_in, total_in, fresh_ok, query, out, result, sems):
    devices = box.shape[0]
    rank = box.shape[1] - 2 * CAPT
    terms = [box[i, :CAPT].astype(jnp.float32) for i in range(devices)]
    while len(terms) > 1:
        pairs = [a + b for a, b in zip(terms[::2], terms[1::2])]
        terms = pairs + terms[2 * len(pairs) :]
    shrunk = terms[0].astype(jnp.bfloat16)
    halves = (shrunk[:, :rank], shrunk[:, rank:])
    pieces = HD // features

    def rows(i, first, count):
        parts = [box[i * pieces + p, first : first + count, :features] for p in range(pieces)]
        return parts[0] if pieces == 1 else jnp.concatenate(parts, axis=1)

    def fresh(first):
        made = []
        for i in range(first, first + KVH, 2):
            ups = jnp.concatenate([rows(i + j, 2 * CAPT, rank) for j in range(2)], axis=1)
            delta = jnp.dot(halves[first // KVH], ups, preferred_element_type=jnp.float32)
            for j in range(2):
                base = rows(i + j, CAPT, CAPT).astype(jnp.float32)
                both = base + ADAPTER_SCALE * delta[:, j * HD : (j + 1) * HD]
                made.append(both.astype(jnp.bfloat16))
        return jnp.concatenate(made, axis=0)

    keys, values = fresh(0), fresh(KVH)
    scale = HD ** (-0.5)
    part = out.shape[0] // sems.shape[0]
    copies = []
    for c in range(sems.shape[0]):
        here = pl.ds(c * part, part)
        s = lax.dot_general(query[here, :], keys, NT, preferred_element_type=jnp.float32)
        s = jnp.where(fresh_ok[here, :] > 0, s * scale, NEG_LARGE)
        old = top_in[here, :]
        top = jnp.maximum(old, jnp.max(s, axis=1, keepdims=True))
        fade = jnp.exp(old - top)
        w = jnp.exp(s - top)
        total = total_in[here, :] * fade + jnp.sum(w, axis=1, keepdims=True)
        mixed = acc[here, :] * fade + jnp.dot(
            w.astype(jnp.bfloat16), values, preferred_element_type=jnp.float32
        )
        result[here, :] = (mixed / total).astype(jnp.bfloat16)
        copies.append(pltpu.make_async_copy(result.at[here, :], out.at[here, :], sems.at[c]))
        copies[c].start()
    for copy in copies:
        copy.wait()


def body(
    hidden,
    key_value_weight,
    adapter_down_weight,
    adapter_up_weight,
    tenant,
    tenant_page_table,
    request_block_count,
    last_block_tokens,
    placement,
    key_value_cache,
    context_length,
    decode_step_query,
    step_key_value,
):
    devices = lax.axis_size("tensor")
    tokens, width = hidden.shape
    features = key_value_weight.shape[0]
    local, pages, rank2 = adapter_down_weight.shape
    rank = adapter_up_weight.shape[2]
    tenants = tenant_page_table.shape[0]
    dec_rows, ctx, kv_width = key_value_cache.shape
    steps = step_key_value.shape[0]
    heads2 = kv_width // HD
    d_chunks, chunks = 4, 2
    up_by_page = jnp.transpose(adapter_up_weight, (1, 2, 0))
    rows = 2 * CAPT + rank
    outgoing = pl.pallas_call(
        functools.partial(project_kernel, dec_rows, d_chunks, chunks, devices),
        out_shape=pltpu.VMEM((devices, rows, HD), WIRE),
        in_specs=[ANY_SPEC] * 8,
        out_specs=VMEM_SPEC,
        scratch_shapes=[
            pltpu.SMEM(tenant.shape, jnp.int32),
            pltpu.SMEM(tenant_page_table.shape, jnp.int32),
            pltpu.SMEM(request_block_count.shape, jnp.int32),
            pltpu.SMEM(placement.shape, jnp.int32),
            pltpu.VMEM((chunks, tokens, width // chunks), jnp.bfloat16),
            pltpu.VMEM((chunks, features, width // chunks), jnp.bfloat16),
            pltpu.VMEM((local, pages, rank2), jnp.bfloat16),
            pltpu.VMEM((tokens, local), jnp.bfloat16),
            pltpu.VMEM((pages, rank, features), jnp.bfloat16),
            pltpu.VMEM((local // 16, tenants * 16, rank2), jnp.bfloat16),
            pltpu.VMEM((tenants, tokens + BLK, rank2), jnp.float32),
            pltpu.VMEM((tokens + BLK, HD), jnp.float32),
            pltpu.SMEM((2, devices), jnp.int32),
            pltpu.SemaphoreType.DMA((chunks, 2)),
            pltpu.SemaphoreType.DMA((d_chunks + 2,)),
            pltpu.SemaphoreType.DMA((4,)),
        ],
        compiler_params=pltpu.CompilerParams(vmem_limit_bytes=PROJECT_VMEM),
        name="project",
    )(
        *(
            pltpu.with_memory_space_constraint(x, pltpu.HBM)
            for x in (
                tenant, tenant_page_table, request_block_count, placement,
                hidden, key_value_weight, adapter_down_weight, up_by_page,
            )
        )
    )
    arrived = lax.all_to_all(outgoing, "tensor", split_axis=0, concat_axis=0, tiled=True)

    query = decode_step_query.reshape(steps, dec_rows, HEADS, HD)
    query = query.transpose(0, 2, 1, 3).reshape(steps * HEADS * dec_rows, HD)
    steps_kv = step_key_value.reshape(steps, dec_rows, heads2, HD)
    steps_kv = steps_kv.transpose(0, 2, 1, 3).reshape(steps * heads2 * dec_rows, HD)
    state = jax.ShapeDtypeStruct((steps * HEADS * dec_rows, HD), jnp.float32)
    acc, top, total, fresh_ok = pl.pallas_call(
        cached_kernel,
        out_shape=(state,) * 4,
        in_specs=[SMEM_SPEC] * 4 + [VMEM_SPEC] * 3,
        out_specs=(VMEM_SPEC,) * 4,
        compiler_params=pltpu.CompilerParams(vmem_limit_bytes=ATTEND_VMEM),
        name="cached",
    )(
        context_length, request_block_count, last_block_tokens, placement,
        pltpu.with_memory_space_constraint(key_value_cache, pltpu.HBM), query, steps_kv,
    )
    attended = pl.pallas_call(
        functools.partial(merge_kernel, features),
        out_shape=jax.ShapeDtypeStruct((steps * HEADS * dec_rows, HD), jnp.bfloat16),
        in_specs=[VMEM_SPEC] * 6,
        out_specs=ANY_SPEC,
        scratch_shapes=[
            pltpu.VMEM((steps * HEADS * dec_rows, HD), jnp.bfloat16),
            pltpu.SemaphoreType.DMA((steps,)),
        ],
        compiler_params=pltpu.CompilerParams(vmem_limit_bytes=ATTEND_VMEM),
        name="merge",
    )(arrived, acc, top, total, fresh_ok, query)
    attended = attended.reshape(steps, HEADS, dec_rows, HD).transpose(0, 2, 1, 3)
    return attended.reshape(steps, dec_rows, HEADS * HD)


def solution(mesh):
    return jax.shard_map(
        body,
        mesh=mesh,
        in_specs=(
            P("parts", None),
            P("tensor", None),
            P("tensor", None, None),
            P("tensor", None, None),
            P("parts"),
            P(),
            P("parts"),
            P("parts"),
            P("parts"),
            P(("parts", "tensor"), None, None),
            P(("parts", "tensor")),
            P(None, ("parts", "tensor"), None),
            P(None, ("parts", "tensor"), None),
        ),
        out_specs=P(None, ("parts", "tensor"), None),
        check_vma=False,
    )
```

```python
import functools

import jax
import jax.numpy as jnp
from jax import lax
from jax.experimental import pallas as pl
from jax.experimental.pallas import tpu as pltpu
from jax.sharding import PartitionSpec as P

HEADS = 64
KVH = 8
HD = 128
BLK = 8
MOSTB = 2
CAPT = MOSTB * BLK
ADAPTER_SCALE = 0.5
NEG_LARGE = -1e30
PROJECT_VMEM = 32 * 1024 * 1024
ATTEND_VMEM = 16 * 1024 * 1024
WIRE = jnp.bfloat16

SMEM_SPEC = pl.BlockSpec(memory_space=pltpu.SMEM)
VMEM_SPEC = pl.BlockSpec(memory_space=pltpu.VMEM)
ANY_SPEC = pl.BlockSpec(memory_space=pl.ANY)


def div(x, n):
    shift = n.bit_length() - 1
    return lax.shift_right_logical(x, shift) if n == 1 << shift else x // n


def mod(x, n):
    return x & (n - 1) if n & (n - 1) == 0 else x % n


def project_kernel(
    dec_rows, d_chunks, chunks, devices, tenant_h, table_h, counts_h, placement_h, hidden, weight, down, up, out,
    tenant, table, counts, placement,
    h_s, w_s, d_s, mine_s, u_s, sel_s, part_s, base_s, dest_table, sems, d_sems, int_sems,
):
    tokens, width = hidden.shape
    features = weight.shape[0]
    local, pages, rank2 = down.shape
    tenants = table.shape[0]
    requests = tenant.shape[0]
    me = lax.axis_index("tensor")
    d_step = local // d_chunks
    step = width // chunks

    int_copies = [
        pltpu.make_async_copy(src, dst, int_sems.at[i])
        for i, (src, dst) in enumerate(
            ((table_h, table), (tenant_h, tenant), (counts_h, counts), (placement_h, placement))
        )
    ]
    for copy in int_copies:
        copy.start()
    d_copies = [
        pltpu.make_async_copy(
            down.at[pl.ds(c * d_step, d_step)], d_s.at[pl.ds(c * d_step, d_step)], d_sems.at[c])
        for c in range(d_chunks)
    ]
    h_copies = [
        pltpu.make_async_copy(hidden.at[:, pl.ds(c * step, step)], h_s.at[c], sems.at[c, 0])
        for c in range(chunks)
    ]
    w_copies = [
        pltpu.make_async_copy(weight.at[:, pl.ds(c * step, step)], w_s.at[c], sems.at[c, 1])
        for c in range(chunks)
    ]
    my_copy = pltpu.make_async_copy(
        hidden.at[:, pl.ds(pl.multiple_of(me * local, 128), local)], mine_s, d_sems.at[d_chunks]
    )
    up_copy = pltpu.make_async_copy(up, u_s, d_sems.at[d_chunks + 1])
    for copy in d_copies + [my_copy, up_copy]:
        copy.start()
    for c in range(chunks):
        h_copies[c].start()
        w_copies[c].start()

    rows = lax.broadcasted_iota(jnp.int32, (pages * 16, 16 * pages), 0)
    cols = lax.broadcasted_iota(jnp.int32, (pages * 16, 16 * pages), 1)
    pick = (mod(rows, 16) == div(cols, pages)) & (mod(cols, pages) == div(rows, 16))
    pick = jnp.where(pick, jnp.float32(1), jnp.float32(0)).astype(jnp.bfloat16)

    for c in range(d_chunks):
        d_copies[c].wait()
        for b in range(c * d_step // 16, (c + 1) * d_step // 16, 2):
            block = jnp.concatenate(
                [d_s[pl.ds((b + i) * 16, 16)].reshape(16 * pages, rank2) for i in range(2)], axis=1
            )
            chosen = jnp.dot(pick, block, preferred_element_type=jnp.float32)
            for i in range(2):
                sel_s[b + i] = chosen[:, i * rank2 : (i + 1) * rank2].astype(jnp.bfloat16)
    for copy in int_copies:
        copy.wait()
    for dest in range(devices):
        dest_table[0, dest] = 0
        dest_table[1, dest] = 0
    first = jnp.int32(0)
    for r in range(requests):
        dest = div(placement[r], dec_rows)
        dest_table[0, dest] = first * BLK
        dest_table[1, dest] = tenant[r]
        first = first + counts[r]
    my_copy.wait()
    mine = mine_s[...]
    for k in range(0, tenants, 2):
        pair = min(2, tenants - k)
        maps = jnp.concatenate(
            [
                sel_s[:, pl.ds(pl.multiple_of(table[j] * 16, 16), 16), :].reshape(local, rank2)
                for j in range(k, k + pair)
            ],
            axis=1,
        )
        product = jnp.dot(mine, maps, preferred_element_type=jnp.float32)
        for j in range(pair):
            part_s[k + j, :tokens] = product[:, j * rank2 : (j + 1) * rank2]
            part_s[k + j, tokens:] = jnp.zeros((BLK, rank2), jnp.float32)

    total = jnp.zeros((tokens, features), jnp.float32)
    for c in range(chunks):
        h_copies[c].wait()
        w_copies[c].wait()
        total = total + lax.dot_general(h_s[c], w_s[c], NT, preferred_element_type=jnp.float32)
    base_s[tokens:] = jnp.zeros((BLK, HD), jnp.float32)
    if features < HD:
        base_s[...] = jnp.zeros_like(base_s)
    base_s[:tokens, :features] = total
    up_copy.wait()
    for dest in range(devices):
        start = pl.multiple_of(dest_table[0, dest], BLK)
        who = dest_table[1, dest]
        out[dest, :CAPT, :] = part_s[who, pl.ds(start, CAPT), :].astype(out.dtype)
        out[dest, CAPT : 2 * CAPT, :] = base_s[pl.ds(start, CAPT), :].astype(out.dtype)
        if features < HD:
            out[dest, 2 * CAPT :, :] = jnp.zeros((out.shape[1] - 2 * CAPT, HD), out.dtype)
        out[dest, 2 * CAPT :, :features] = u_s[table[who]]


NT = (((1,), (1,)), ((), ()))


def gather_queries(query, k, group, steps, stride):
    return jnp.concatenate(
        [query[pl.ds(s * stride + k * group, group), :] for s in range(steps)], axis=0
    )


def cached_kernel(
    lengths, counts, last, placement, cache, query, steps_kv, acc, top_out, total_out, fresh_ok,
):
    dec_rows, ctx, kv_width = cache.shape
    half_width = kv_width // 2
    step_rows = KVH * dec_rows
    steps = steps_kv.shape[0] // (2 * step_rows)
    group = HEADS // KVH * dec_rows
    q_rows = steps * group
    stride = HEADS * dec_rows

    row = lax.broadcasted_iota(jnp.int32, (q_rows, ctx), 0)
    col = lax.broadcasted_iota(jnp.int32, (q_rows, ctx), 1)
    row_slot = mod(row, dec_rows)
    cache_ok = [(row_slot == g) & (col < lengths[g]) for g in range(dec_rows)]
    row = lax.broadcasted_iota(jnp.int32, (q_rows, steps * step_rows), 0)
    col = lax.broadcasted_iota(jnp.int32, (q_rows, steps * step_rows), 1)
    step_ok = (mod(row, dec_rows) == mod(col, dec_rows)) & (div(col, step_rows) <= div(row, group))
    step_head = div(mod(col, step_rows), dec_rows)
    step_keys, step_values = (
        jnp.concatenate(
            [steps_kv[pl.ds((2 * s + half) * step_rows, step_rows), :] for s in range(steps)], axis=0
        )
        for half in range(2)
    )

    scale = HD ** (-0.5)
    for k in range(KVH):
        lanes = pl.ds(k * HD, HD)
        vlanes = pl.ds(half_width + k * HD, HD)
        q = gather_queries(query, k, group, steps, stride)
        keys = [cache[g, :, lanes] for g in range(dec_rows)] + [step_keys]
        values = [cache[g, :, vlanes] for g in range(dec_rows)] + [step_values]
        scores = [
            jnp.where(
                ok,
                lax.dot_general(q, key, NT, preferred_element_type=jnp.float32) * scale,
                NEG_LARGE,
            )
            for ok, key in zip(cache_ok + [step_ok & (step_head == k)], keys)
        ]
        top = functools.reduce(jnp.maximum, [jnp.max(s, axis=1, keepdims=True) for s in scores])
        weights = [jnp.exp(s - top) for s in scores]
        total = sum(jnp.sum(w, axis=1, keepdims=True) for w in weights)
        mixed = sum(
            jnp.dot(w.astype(jnp.bfloat16), v, preferred_element_type=jnp.float32)
            for w, v in zip(weights, values)
        )
        for s in range(steps):
            here = pl.ds(s * stride + k * group, group)
            part = slice(s * group, (s + 1) * group)
            acc[here, :] = mixed[part]
            top_out[here, :] = jnp.broadcast_to(top[part], (group, HD))
            total_out[here, :] = jnp.broadcast_to(total[part], (group, HD))

    my_slot = jnp.int32(-1)
    my_length = jnp.int32(0)
    for r in range(placement.shape[0]):
        hit = div(placement[r], dec_rows) == lax.axis_index("tensor")
        my_slot = jnp.where(hit, mod(placement[r], dec_rows), my_slot)
        my_length = jnp.where(hit, (counts[r] - 1) * BLK + last[r], my_length)
    row = lax.broadcasted_iota(jnp.int32, fresh_ok.shape, 0)
    col = lax.broadcasted_iota(jnp.int32, fresh_ok.shape, 1)
    ok = (
        (mod(div(row, group), KVH) == div(col, CAPT))
        & (mod(row, dec_rows) == my_slot)
        & (mod(col, CAPT) < my_length)
    )
    fresh_ok[...] = jnp.where(ok, jnp.float32(1), jnp.float32(0))


def merge_kernel(features, box, acc, top_in, total_in, fresh_ok, query, out, result, sems):
    devices = box.shape[0]
    rank = box.shape[1] - 2 * CAPT
    terms = [box[i, :CAPT].astype(jnp.float32) for i in range(devices)]
    while len(terms) > 1:
        pairs = [a + b for a, b in zip(terms[::2], terms[1::2])]
        terms = pairs + terms[2 * len(pairs) :]
    shrunk = terms[0].astype(jnp.bfloat16)
    halves = (shrunk[:, :rank], shrunk[:, rank:])
    pieces = HD // features

    def rows(i, first, count):
        parts = [box[i * pieces + p, first : first + count, :features] for p in range(pieces)]
        return parts[0] if pieces == 1 else jnp.concatenate(parts, axis=1)

    def fresh(first):
        made = []
        for i in range(first, first + KVH, 2):
            ups = jnp.concatenate([rows(i + j, 2 * CAPT, rank) for j in range(2)], axis=1)
            delta = jnp.dot(halves[first // KVH], ups, preferred_element_type=jnp.float32)
            for j in range(2):
                base = rows(i + j, CAPT, CAPT).astype(jnp.float32)
                both = base + ADAPTER_SCALE * delta[:, j * HD : (j + 1) * HD]
                made.append(both.astype(jnp.bfloat16))
        return jnp.concatenate(made, axis=0)

    keys, values = fresh(0), fresh(KVH)
    scale = HD ** (-0.5)
    part = out.shape[0] // sems.shape[0]
    copies = []
    for c in range(sems.shape[0]):
        here = pl.ds(c * part, part)
        s = lax.dot_general(query[here, :], keys, NT, preferred_element_type=jnp.float32)
        s = jnp.where(fresh_ok[here, :] > 0, s * scale, NEG_LARGE)
        old = top_in[here, :]
        top = jnp.maximum(old, jnp.max(s, axis=1, keepdims=True))
        fade = jnp.exp(old - top)
        w = jnp.exp(s - top)
        total = total_in[here, :] * fade + jnp.sum(w, axis=1, keepdims=True)
        mixed = acc[here, :] * fade + jnp.dot(
            w.astype(jnp.bfloat16), values, preferred_element_type=jnp.float32
        )
        result[here, :] = (mixed / total).astype(jnp.bfloat16)
        copies.append(pltpu.make_async_copy(result.at[here, :], out.at[here, :], sems.at[c]))
        copies[c].start()
    for copy in copies:
        copy.wait()


def body(
    hidden,
    key_value_weight,
    adapter_down_weight,
    adapter_up_weight,
    tenant,
    tenant_page_table,
    request_block_count,
    last_block_tokens,
    placement,
    key_value_cache,
    context_length,
    decode_step_query,
    step_key_value,
):
    devices = lax.axis_size("tensor")
    tokens, width = hidden.shape
    features = key_value_weight.shape[0]
    local, pages, rank2 = adapter_down_weight.shape
    rank = adapter_up_weight.shape[2]
    tenants = tenant_page_table.shape[0]
    dec_rows, ctx, kv_width = key_value_cache.shape
    steps = step_key_value.shape[0]
    heads2 = kv_width // HD
    d_chunks, chunks = 4, 2
    up_by_page = jnp.transpose(adapter_up_weight, (1, 2, 0))
    rows = 2 * CAPT + rank
    outgoing = pl.pallas_call(
        functools.partial(project_kernel, dec_rows, d_chunks, chunks, devices),
        out_shape=pltpu.VMEM((devices, rows, HD), WIRE),
        in_specs=[ANY_SPEC] * 8,
        out_specs=VMEM_SPEC,
        scratch_shapes=[
            pltpu.SMEM(tenant.shape, jnp.int32),
            pltpu.SMEM(tenant_page_table.shape, jnp.int32),
            pltpu.SMEM(request_block_count.shape, jnp.int32),
            pltpu.SMEM(placement.shape, jnp.int32),
            pltpu.VMEM((chunks, tokens, width // chunks), jnp.bfloat16),
            pltpu.VMEM((chunks, features, width // chunks), jnp.bfloat16),
            pltpu.VMEM((local, pages, rank2), jnp.bfloat16),
            pltpu.VMEM((tokens, local), jnp.bfloat16),
            pltpu.VMEM((pages, rank, features), jnp.bfloat16),
            pltpu.VMEM((local // 16, pages * 16, rank2), jnp.bfloat16),
            pltpu.VMEM((tenants, tokens + BLK, rank2), jnp.float32),
            pltpu.VMEM((tokens + BLK, HD), jnp.float32),
            pltpu.SMEM((2, devices), jnp.int32),
            pltpu.SemaphoreType.DMA((chunks, 2)),
            pltpu.SemaphoreType.DMA((d_chunks + 2,)),
            pltpu.SemaphoreType.DMA((4,)),
        ],
        compiler_params=pltpu.CompilerParams(vmem_limit_bytes=PROJECT_VMEM),
        name="project",
    )(
        *(
            pltpu.with_memory_space_constraint(x, pltpu.HBM)
            for x in (
                tenant, tenant_page_table, request_block_count, placement,
                hidden, key_value_weight, adapter_down_weight, up_by_page,
            )
        )
    )
    arrived = lax.all_to_all(outgoing, "tensor", split_axis=0, concat_axis=0, tiled=True)

    query = decode_step_query.reshape(steps, dec_rows, HEADS, HD)
    query = query.transpose(0, 2, 1, 3).reshape(steps * HEADS * dec_rows, HD)
    steps_kv = step_key_value.reshape(steps, dec_rows, heads2, HD)
    steps_kv = steps_kv.transpose(0, 2, 1, 3).reshape(steps * heads2 * dec_rows, HD)
    state = jax.ShapeDtypeStruct((steps * HEADS * dec_rows, HD), jnp.float32)
    acc, top, total, fresh_ok = pl.pallas_call(
        cached_kernel,
        out_shape=(state,) * 4,
        in_specs=[SMEM_SPEC] * 4 + [VMEM_SPEC] * 3,
        out_specs=(VMEM_SPEC,) * 4,
        compiler_params=pltpu.CompilerParams(vmem_limit_bytes=ATTEND_VMEM),
        name="cached",
    )(
        context_length, request_block_count, last_block_tokens, placement,
        key_value_cache, query, steps_kv,
    )
    attended = pl.pallas_call(
        functools.partial(merge_kernel, features),
        out_shape=jax.ShapeDtypeStruct((steps * HEADS * dec_rows, HD), jnp.bfloat16),
        in_specs=[VMEM_SPEC] * 6,
        out_specs=ANY_SPEC,
        scratch_shapes=[
            pltpu.VMEM((steps * HEADS * dec_rows, HD), jnp.bfloat16),
            pltpu.SemaphoreType.DMA((steps,)),
        ],
        compiler_params=pltpu.CompilerParams(vmem_limit_bytes=ATTEND_VMEM),
        name="merge",
    )(arrived, acc, top, total, fresh_ok, query)
    attended = attended.reshape(steps, HEADS, dec_rows, HD).transpose(0, 2, 1, 3)
    return attended.reshape(steps, dec_rows, HEADS * HD)


def solution(mesh):
    return jax.shard_map(
        body,
        mesh=mesh,
        in_specs=(
            P("parts", None),
            P("tensor", None),
            P("tensor", None, None),
            P("tensor", None, None),
            P("parts"),
            P(),
            P("parts"),
            P("parts"),
            P("parts"),
            P(("parts", "tensor"), None, None),
            P(("parts", "tensor")),
            P(None, ("parts", "tensor"), None),
            P(None, ("parts", "tensor"), None),
        ),
        out_specs=P(None, ("parts", "tensor"), None),
        check_vma=False,
    )
```

```python
import functools

import jax
import jax.numpy as jnp
from jax import lax
from jax.experimental import pallas as pl
from jax.experimental.pallas import tpu as pltpu
from jax.sharding import PartitionSpec as P

HEADS = 64
KVH = 8
HD = 128
BLK = 8
MOSTB = 2
CAPT = MOSTB * BLK
ADAPTER_SCALE = 0.5
NEG_LARGE = -1e30
PROJECT_VMEM = 32 * 1024 * 1024
ATTEND_VMEM = 16 * 1024 * 1024
WIRE = jnp.bfloat16

SMEM_SPEC = pl.BlockSpec(memory_space=pltpu.SMEM)
VMEM_SPEC = pl.BlockSpec(memory_space=pltpu.VMEM)
ANY_SPEC = pl.BlockSpec(memory_space=pl.ANY)


def div(x, n):
    shift = n.bit_length() - 1
    return lax.shift_right_logical(x, shift) if n == 1 << shift else x // n


def mod(x, n):
    return x & (n - 1) if n & (n - 1) == 0 else x % n


def project_kernel(
    dec_rows, parts, tenant_h, table_h, counts_h, placement_h, hidden, weight, down, up, out,
    tenant, table, counts, placement,
    h_s, w_s, wt_s, d_s, mine_s, u_s, sel_s, part_s, base_s, dest_table, w_sems, sems,
):
    tokens, width = hidden.shape
    features = weight.shape[0]
    local, pages, rank2 = down.shape
    tenants = table.shape[0]
    requests = tenant.shape[0]
    devices = out.shape[0]
    me = lax.axis_index("tensor")
    step = width // parts

    int_copies = [
        pltpu.make_async_copy(src, dst, sems.at[3 + i])
        for i, (src, dst) in enumerate(
            ((table_h, table), (tenant_h, tenant), (counts_h, counts), (placement_h, placement))
        )
    ]
    w_copies = [
        pltpu.make_async_copy(
            weight.at[:, pl.ds(c * step, step)], w_s.at[:, pl.ds(c * step, step)], w_sems.at[c])
        for c in range(parts)
    ]
    d_copy = pltpu.make_async_copy(down, d_s, sems.at[0])
    my_copy = pltpu.make_async_copy(
        hidden.at[:, pl.ds(pl.multiple_of(me * local, 128), local)], mine_s, sems.at[1]
    )
    h_copy = pltpu.make_async_copy(hidden, h_s, sems.at[2])
    up_copy = pltpu.make_async_copy(up, u_s, sems.at[7])
    for copy in w_copies + int_copies + [d_copy, my_copy, h_copy, up_copy]:
        copy.start()

    int_copies[0].wait()
    rows = lax.broadcasted_iota(jnp.int32, (tenants * 16, 16 * pages), 0)
    cols = lax.broadcasted_iota(jnp.int32, (tenants * 16, 16 * pages), 1)
    page_of_row = jnp.zeros_like(rows)
    for k in range(tenants):
        page_of_row = jnp.where(div(rows, 16) == k, table[k], page_of_row)
    pick = (mod(rows, 16) == div(cols, pages)) & (mod(cols, pages) == page_of_row)
    pick = jnp.where(pick, jnp.float32(1), jnp.float32(0)).astype(jnp.bfloat16)

    def turn(c):
        if features == HD:
            wt_s[pl.ds(c * step, step), :] = w_s[:, pl.ds(c * step, step)].T

    early = parts // 2
    for c in range(early):
        w_copies[c].wait()
        turn(c)
    for c in range(early, parts):
        w_copies[c].wait()
    d_copy.wait()
    for c in range(early, parts):
        turn(c)
    for b in range(0, local // 16, 2):
        block = jnp.concatenate(
            [d_s[pl.ds((b + i) * 16, 16)].reshape(16 * pages, rank2) for i in range(2)], axis=1
        )
        chosen = jnp.dot(pick, block, preferred_element_type=jnp.float32)
        for i in range(2):
            sel_s[b + i] = chosen[:, i * rank2 : (i + 1) * rank2].astype(jnp.bfloat16)
    for copy in int_copies[1:] + [my_copy, h_copy, up_copy]:
        copy.wait()
    mine = mine_s[...]
    for k in range(0, tenants, 2):
        pair = min(2, tenants - k)
        maps = jnp.concatenate(
            [sel_s[:, j * 16 : (j + 1) * 16, :].reshape(local, rank2) for j in range(k, k + pair)],
            axis=1,
        )
        product = jnp.dot(mine, maps, preferred_element_type=jnp.float32)
        for j in range(pair):
            part_s[k + j, :tokens] = product[:, j * rank2 : (j + 1) * rank2]
            part_s[k + j, tokens:] = jnp.zeros((BLK, rank2), jnp.float32)
    if requests < devices:
        for dest in range(devices):
            dest_table[0, dest] = 0
            dest_table[1, dest] = 0
    first = jnp.int32(0)
    for r in range(requests):
        dest = div(placement[r], dec_rows)
        dest_table[0, dest] = first * BLK
        dest_table[1, dest] = tenant[r]
        first = first + counts[r]

    if features == HD:
        sums = [
            jnp.dot(
                h_s[:, c * step : (c + 1) * step],
                wt_s[c * step : (c + 1) * step, :],
                preferred_element_type=jnp.float32,
            )
            for c in range(parts)
        ]
        total = (sums[0] + sums[1]) + (sums[2] + sums[3])
    else:
        total = lax.dot_general(h_s[...], w_s[...], NT, preferred_element_type=jnp.float32)
    base_s[tokens:] = jnp.zeros((BLK, HD), jnp.float32)
    if features < HD:
        base_s[...] = jnp.zeros_like(base_s)
    base_s[:tokens, :features] = total
    for dest in range(devices):
        start = pl.multiple_of(dest_table[0, dest], BLK)
        who = dest_table[1, dest]
        out[dest, :CAPT, :] = part_s[who, pl.ds(start, CAPT), :].astype(out.dtype)
        out[dest, CAPT : 2 * CAPT, :] = base_s[pl.ds(start, CAPT), :].astype(out.dtype)
        if features < HD:
            out[dest, 2 * CAPT :, :] = jnp.zeros((out.shape[1] - 2 * CAPT, HD), out.dtype)
        out[dest, 2 * CAPT :, :features] = u_s[table[who]]


NT = (((1,), (1,)), ((), ()))


def gather_queries(query, k, group, steps, stride):
    return jnp.concatenate(
        [query[pl.ds(s * stride + k * group, group), :] for s in range(steps)], axis=0
    )


def cached_kernel(
    lengths, counts, last, placement, cache, query, steps_kv, acc, top_out, total_out, fresh_ok,
):
    dec_rows, ctx, kv_width = cache.shape
    half_width = kv_width // 2
    step_rows = KVH * dec_rows
    steps = steps_kv.shape[0] // (2 * step_rows)
    group = HEADS // KVH * dec_rows
    q_rows = steps * group
    stride = HEADS * dec_rows

    row = lax.broadcasted_iota(jnp.int32, (q_rows, ctx), 0)
    col = lax.broadcasted_iota(jnp.int32, (q_rows, ctx), 1)
    row_slot = mod(row, dec_rows)
    cache_ok = [(row_slot == g) & (col < lengths[g]) for g in range(dec_rows)]
    row = lax.broadcasted_iota(jnp.int32, (q_rows, steps * step_rows), 0)
    col = lax.broadcasted_iota(jnp.int32, (q_rows, steps * step_rows), 1)
    step_ok = (mod(row, dec_rows) == mod(col, dec_rows)) & (div(col, step_rows) <= div(row, group))
    step_head = div(mod(col, step_rows), dec_rows)
    step_keys, step_values = (
        jnp.concatenate(
            [steps_kv[pl.ds((2 * s + half) * step_rows, step_rows), :] for s in range(steps)], axis=0
        )
        for half in range(2)
    )

    scale = HD ** (-0.5)
    for k in range(KVH):
        lanes = pl.ds(k * HD, HD)
        vlanes = pl.ds(half_width + k * HD, HD)
        q = gather_queries(query, k, group, steps, stride)
        keys = [cache[g, :, lanes] for g in range(dec_rows)] + [step_keys]
        values = [cache[g, :, vlanes] for g in range(dec_rows)] + [step_values]
        scores = [
            jnp.where(
                ok,
                lax.dot_general(q, key, NT, preferred_element_type=jnp.float32) * scale,
                NEG_LARGE,
            )
            for ok, key in zip(cache_ok + [step_ok & (step_head == k)], keys)
        ]
        top = functools.reduce(jnp.maximum, [jnp.max(s, axis=1, keepdims=True) for s in scores])
        weights = [jnp.exp(s - top) for s in scores]
        total = sum(jnp.sum(w, axis=1, keepdims=True) for w in weights)
        mixed = sum(
            jnp.dot(w.astype(jnp.bfloat16), v, preferred_element_type=jnp.float32)
            for w, v in zip(weights, values)
        )
        for s in range(steps):
            here = pl.ds(s * stride + k * group, group)
            part = slice(s * group, (s + 1) * group)
            acc[here, :] = mixed[part]
            top_out[here, :] = jnp.broadcast_to(top[part], (group, HD))
            total_out[here, :] = jnp.broadcast_to(total[part], (group, HD))

    my_slot = jnp.int32(-1)
    my_length = jnp.int32(0)
    for r in range(placement.shape[0]):
        hit = div(placement[r], dec_rows) == lax.axis_index("tensor")
        my_slot = jnp.where(hit, mod(placement[r], dec_rows), my_slot)
        my_length = jnp.where(hit, (counts[r] - 1) * BLK + last[r], my_length)
    row = lax.broadcasted_iota(jnp.int32, fresh_ok.shape, 0)
    col = lax.broadcasted_iota(jnp.int32, fresh_ok.shape, 1)
    ok = (
        (mod(div(row, group), KVH) == div(col, CAPT))
        & (mod(row, dec_rows) == my_slot)
        & (mod(col, CAPT) < my_length)
    )
    fresh_ok[...] = jnp.where(ok, jnp.float32(1), jnp.float32(0))


def merge_kernel(features, box, acc, top_in, total_in, fresh_ok, query, out, result, sems):
    devices = box.shape[0]
    rank = box.shape[1] - 2 * CAPT
    terms = [box[i, :CAPT].astype(jnp.float32) for i in range(devices)]
    while len(terms) > 1:
        pairs = [a + b for a, b in zip(terms[::2], terms[1::2])]
        terms = pairs + terms[2 * len(pairs) :]
    shrunk = terms[0].astype(jnp.bfloat16)
    halves = (shrunk[:, :rank], shrunk[:, rank:])
    pieces = HD // features

    def rows(i, first, count):
        parts = [box[i * pieces + p, first : first + count, :features] for p in range(pieces)]
        return parts[0] if pieces == 1 else jnp.concatenate(parts, axis=1)

    def fresh(first):
        made = []
        for i in range(first, first + KVH, 2):
            ups = jnp.concatenate([rows(i + j, 2 * CAPT, rank) for j in range(2)], axis=1)
            delta = jnp.dot(halves[first // KVH], ups, preferred_element_type=jnp.float32)
            for j in range(2):
                base = rows(i + j, CAPT, CAPT).astype(jnp.float32)
                both = base + ADAPTER_SCALE * delta[:, j * HD : (j + 1) * HD]
                made.append(both.astype(jnp.bfloat16))
        return jnp.concatenate(made, axis=0)

    keys, values = fresh(0), fresh(KVH)
    scale = HD ** (-0.5)
    part = out.shape[0] // sems.shape[0]
    copies = []
    for c in range(sems.shape[0]):
        here = pl.ds(c * part, part)
        s = lax.dot_general(query[here, :], keys, NT, preferred_element_type=jnp.float32)
        s = jnp.where(fresh_ok[here, :] > 0, s * scale, NEG_LARGE)
        old = top_in[here, :]
        top = jnp.maximum(old, jnp.max(s, axis=1, keepdims=True))
        fade = jnp.exp(old - top)
        w = jnp.exp(s - top)
        total = total_in[here, :] * fade + jnp.sum(w, axis=1, keepdims=True)
        mixed = acc[here, :] * fade + jnp.dot(
            w.astype(jnp.bfloat16), values, preferred_element_type=jnp.float32
        )
        result[here, :] = (mixed / total).astype(jnp.bfloat16)
        copies.append(pltpu.make_async_copy(result.at[here, :], out.at[here, :], sems.at[c]))
        copies[c].start()
    for copy in copies:
        copy.wait()


def body(
    hidden,
    key_value_weight,
    adapter_down_weight,
    adapter_up_weight,
    tenant,
    tenant_page_table,
    request_block_count,
    last_block_tokens,
    placement,
    key_value_cache,
    context_length,
    decode_step_query,
    step_key_value,
):
    devices = lax.axis_size("tensor")
    tokens, width = hidden.shape
    features = key_value_weight.shape[0]
    local, pages, rank2 = adapter_down_weight.shape
    rank = adapter_up_weight.shape[2]
    tenants = tenant_page_table.shape[0]
    dec_rows, ctx, kv_width = key_value_cache.shape
    steps = step_key_value.shape[0]
    heads2 = kv_width // HD
    parts = 4
    up_by_page = jnp.transpose(adapter_up_weight, (1, 2, 0))
    rows = 2 * CAPT + rank
    outgoing = pl.pallas_call(
        functools.partial(project_kernel, dec_rows, parts),
        out_shape=pltpu.VMEM((devices, rows, HD), WIRE),
        in_specs=[ANY_SPEC] * 8,
        out_specs=VMEM_SPEC,
        scratch_shapes=[
            pltpu.SMEM(tenant.shape, jnp.int32),
            pltpu.SMEM(tenant_page_table.shape, jnp.int32),
            pltpu.SMEM(request_block_count.shape, jnp.int32),
            pltpu.SMEM(placement.shape, jnp.int32),
            pltpu.VMEM((tokens, width), jnp.bfloat16),
            pltpu.VMEM((features, width), jnp.bfloat16),
            pltpu.VMEM((width, HD), jnp.bfloat16),
            pltpu.VMEM((local, pages, rank2), jnp.bfloat16),
            pltpu.VMEM((tokens, local), jnp.bfloat16),
            pltpu.VMEM((pages, rank, features), jnp.bfloat16),
            pltpu.VMEM((local // 16, tenants * 16, rank2), jnp.bfloat16),
            pltpu.VMEM((tenants, tokens + BLK, rank2), jnp.float32),
            pltpu.VMEM((tokens + BLK, HD), jnp.float32),
            pltpu.SMEM((2, devices), jnp.int32),
            pltpu.SemaphoreType.DMA((parts,)),
            pltpu.SemaphoreType.DMA((8,)),
        ],
        compiler_params=pltpu.CompilerParams(vmem_limit_bytes=PROJECT_VMEM),
        name="project",
    )(
        *(
            pltpu.with_memory_space_constraint(x, pltpu.HBM)
            for x in (
                tenant, tenant_page_table, request_block_count, placement,
                hidden, key_value_weight, adapter_down_weight, up_by_page,
            )
        )
    )
    arrived = lax.all_to_all(outgoing, "tensor", split_axis=0, concat_axis=0, tiled=True)

    query = decode_step_query.reshape(steps, dec_rows, HEADS, HD)
    query = query.transpose(0, 2, 1, 3).reshape(steps * HEADS * dec_rows, HD)
    steps_kv = step_key_value.reshape(steps, dec_rows, heads2, HD)
    steps_kv = steps_kv.transpose(0, 2, 1, 3).reshape(steps * heads2 * dec_rows, HD)
    state = jax.ShapeDtypeStruct((steps * HEADS * dec_rows, HD), jnp.float32)
    acc, top, total, fresh_ok = pl.pallas_call(
        cached_kernel,
        out_shape=(state,) * 4,
        in_specs=[SMEM_SPEC] * 4 + [VMEM_SPEC] * 3,
        out_specs=(VMEM_SPEC,) * 4,
        compiler_params=pltpu.CompilerParams(vmem_limit_bytes=ATTEND_VMEM),
        name="cached",
    )(
        context_length, request_block_count, last_block_tokens, placement,
        key_value_cache, query, steps_kv,
    )
    attended = pl.pallas_call(
        functools.partial(merge_kernel, features),
        out_shape=jax.ShapeDtypeStruct((steps * HEADS * dec_rows, HD), jnp.bfloat16),
        in_specs=[VMEM_SPEC] * 6,
        out_specs=ANY_SPEC,
        scratch_shapes=[
            pltpu.VMEM((steps * HEADS * dec_rows, HD), jnp.bfloat16),
            pltpu.SemaphoreType.DMA((steps,)),
        ],
        compiler_params=pltpu.CompilerParams(vmem_limit_bytes=ATTEND_VMEM),
        name="merge",
    )(arrived, acc, top, total, fresh_ok, query)
    attended = attended.reshape(steps, HEADS, dec_rows, HD).transpose(0, 2, 1, 3)
    return attended.reshape(steps, dec_rows, HEADS * HD)


def solution(mesh):
    return jax.shard_map(
        body,
        mesh=mesh,
        in_specs=(
            P("parts", None),
            P("tensor", None),
            P("tensor", None, None),
            P("tensor", None, None),
            P("parts"),
            P(),
            P("parts"),
            P("parts"),
            P("parts"),
            P(("parts", "tensor"), None, None),
            P(("parts", "tensor")),
            P(None, ("parts", "tensor"), None),
            P(None, ("parts", "tensor"), None),
        ),
        out_specs=P(None, ("parts", "tensor"), None),
        check_vma=False,
    )
```

```python
import functools

import jax
import jax.numpy as jnp
from jax import lax
from jax.experimental import pallas as pl
from jax.experimental.pallas import tpu as pltpu
from jax.sharding import PartitionSpec as P

HEADS = 64
KVH = 8
HD = 128
BLK = 8
MOSTB = 2
CAPT = MOSTB * BLK
ADAPTER_SCALE = 0.5
NEG_LARGE = -1e30
PROJECT_VMEM = 32 * 1024 * 1024
ATTEND_VMEM = 16 * 1024 * 1024
WIRE = jnp.bfloat16

SMEM_SPEC = pl.BlockSpec(memory_space=pltpu.SMEM)
VMEM_SPEC = pl.BlockSpec(memory_space=pltpu.VMEM)
ANY_SPEC = pl.BlockSpec(memory_space=pl.ANY)


def div(x, n):
    shift = n.bit_length() - 1
    return lax.shift_right_logical(x, shift) if n == 1 << shift else x // n


def mod(x, n):
    return x & (n - 1) if n & (n - 1) == 0 else x % n


def project_kernel(
    dec_rows, d_chunks, chunks, devices, tenant_h, table_h, counts_h, placement_h, hidden, weight, down, up, out,
    tenant, table, counts, placement,
    h_s, w_s, d_s, mine_s, u_s, sel_s, part_s, base_s, dest_table, sems, d_sems, int_sems,
):
    tokens, width = hidden.shape
    features = weight.shape[0]
    local, pages, rank2 = down.shape
    tenants = table.shape[0]
    requests = tenant.shape[0]
    me = lax.axis_index("tensor")
    d_step = local // d_chunks
    step = width // chunks

    int_copies = [
        pltpu.make_async_copy(src, dst, int_sems.at[i])
        for i, (src, dst) in enumerate(
            ((table_h, table), (tenant_h, tenant), (counts_h, counts), (placement_h, placement))
        )
    ]
    for copy in int_copies:
        copy.start()
    d_copies = [
        pltpu.make_async_copy(
            down.at[pl.ds(c * d_step, d_step)], d_s.at[pl.ds(c * d_step, d_step)], d_sems.at[c])
        for c in range(d_chunks)
    ]
    h_copies = [
        pltpu.make_async_copy(hidden.at[:, pl.ds(c * step, step)], h_s.at[c], sems.at[c, 0])
        for c in range(chunks)
    ]
    w_copies = [
        pltpu.make_async_copy(weight.at[:, pl.ds(c * step, step)], w_s.at[c], sems.at[c, 1])
        for c in range(chunks)
    ]
    my_copy = pltpu.make_async_copy(
        hidden.at[:, pl.ds(pl.multiple_of(me * local, 128), local)], mine_s, d_sems.at[d_chunks]
    )
    up_copy = pltpu.make_async_copy(up, u_s, d_sems.at[d_chunks + 1])
    for copy in d_copies + [my_copy, up_copy]:
        copy.start()
    for c in range(chunks):
        h_copies[c].start()
        w_copies[c].start()

    int_copies[0].wait()
    rows = lax.broadcasted_iota(jnp.int32, (tenants * 16, 16 * pages), 0)
    cols = lax.broadcasted_iota(jnp.int32, (tenants * 16, 16 * pages), 1)
    page_of_row = jnp.zeros_like(rows)
    for k in range(tenants):
        page_of_row = jnp.where(div(rows, 16) == k, table[k], page_of_row)
    pick = (mod(rows, 16) == div(cols, pages)) & (mod(cols, pages) == page_of_row)
    pick = jnp.where(pick, jnp.float32(1), jnp.float32(0)).astype(jnp.bfloat16)

    for c in range(d_chunks):
        d_copies[c].wait()
        for b in range(c * d_step // 16, (c + 1) * d_step // 16, 2):
            block = jnp.concatenate(
                [d_s[pl.ds((b + i) * 16, 16)].reshape(16 * pages, rank2) for i in range(2)], axis=1
            )
            chosen = jnp.dot(pick, block, preferred_element_type=jnp.float32)
            for i in range(2):
                sel_s[b + i] = chosen[:, i * rank2 : (i + 1) * rank2].astype(jnp.bfloat16)
    for copy in int_copies[1:]:
        copy.wait()
    for dest in range(devices):
        dest_table[0, dest] = 0
        dest_table[1, dest] = 0
    first = jnp.int32(0)
    for r in range(requests):
        dest = div(placement[r], dec_rows)
        dest_table[0, dest] = first * BLK
        dest_table[1, dest] = tenant[r]
        first = first + counts[r]
    my_copy.wait()
    mine = mine_s[...]
    for k in range(0, tenants, 2):
        pair = min(2, tenants - k)
        maps = jnp.concatenate(
            [sel_s[:, j * 16 : (j + 1) * 16, :].reshape(local, rank2) for j in range(k, k + pair)],
            axis=1,
        )
        product = jnp.dot(mine, maps, preferred_element_type=jnp.float32)
        for j in range(pair):
            part_s[k + j, :tokens] = product[:, j * rank2 : (j + 1) * rank2]
            part_s[k + j, tokens:] = jnp.zeros((BLK, rank2), jnp.float32)

    total = jnp.zeros((features, tokens), jnp.float32)
    for c in range(chunks):
        h_copies[c].wait()
        w_copies[c].wait()
        total = total + lax.dot_general(w_s[c], h_s[c], NT, preferred_element_type=jnp.float32)
    base_s[tokens:] = jnp.zeros((BLK, HD), jnp.float32)
    if features < HD:
        base_s[...] = jnp.zeros_like(base_s)
    base_s[:tokens, :features] = total.T
    up_copy.wait()
    for dest in range(devices):
        start = pl.multiple_of(dest_table[0, dest], BLK)
        who = dest_table[1, dest]
        out[dest, :CAPT, :] = part_s[who, pl.ds(start, CAPT), :].astype(out.dtype)
        out[dest, CAPT : 2 * CAPT, :] = base_s[pl.ds(start, CAPT), :].astype(out.dtype)
        if features < HD:
            out[dest, 2 * CAPT :, :] = jnp.zeros((out.shape[1] - 2 * CAPT, HD), out.dtype)
        out[dest, 2 * CAPT :, :features] = u_s[table[who]]


NT = (((1,), (1,)), ((), ()))


def gather_queries(query, k, group, steps, stride):
    return jnp.concatenate(
        [query[pl.ds(s * stride + k * group, group), :] for s in range(steps)], axis=0
    )


def cached_kernel(
    lengths, counts, last, placement, cache, query, steps_kv, acc, top_out, total_out, fresh_ok,
):
    dec_rows, ctx, kv_width = cache.shape
    half_width = kv_width // 2
    step_rows = KVH * dec_rows
    steps = steps_kv.shape[0] // (2 * step_rows)
    group = HEADS // KVH * dec_rows
    q_rows = steps * group
    stride = HEADS * dec_rows

    row = lax.broadcasted_iota(jnp.int32, (q_rows, ctx), 0)
    col = lax.broadcasted_iota(jnp.int32, (q_rows, ctx), 1)
    row_slot = mod(row, dec_rows)
    cache_ok = [(row_slot == g) & (col < lengths[g]) for g in range(dec_rows)]
    row = lax.broadcasted_iota(jnp.int32, (q_rows, steps * step_rows), 0)
    col = lax.broadcasted_iota(jnp.int32, (q_rows, steps * step_rows), 1)
    step_ok = (mod(row, dec_rows) == mod(col, dec_rows)) & (div(col, step_rows) <= div(row, group))
    step_head = div(mod(col, step_rows), dec_rows)
    step_keys, step_values = (
        jnp.concatenate(
            [steps_kv[pl.ds((2 * s + half) * step_rows, step_rows), :] for s in range(steps)], axis=0
        )
        for half in range(2)
    )

    scale = HD ** (-0.5)
    for k in range(KVH):
        lanes = pl.ds(k * HD, HD)
        vlanes = pl.ds(half_width + k * HD, HD)
        q = gather_queries(query, k, group, steps, stride)
        keys = [cache[g, :, lanes] for g in range(dec_rows)] + [step_keys]
        values = [cache[g, :, vlanes] for g in range(dec_rows)] + [step_values]
        scores = [
            jnp.where(
                ok,
                lax.dot_general(q, key, NT, preferred_element_type=jnp.float32) * scale,
                NEG_LARGE,
            )
            for ok, key in zip(cache_ok + [step_ok & (step_head == k)], keys)
        ]
        top = functools.reduce(jnp.maximum, [jnp.max(s, axis=1, keepdims=True) for s in scores])
        weights = [jnp.exp(s - top) for s in scores]
        total = sum(jnp.sum(w, axis=1, keepdims=True) for w in weights)
        mixed = sum(
            jnp.dot(w.astype(jnp.bfloat16), v, preferred_element_type=jnp.float32)
            for w, v in zip(weights, values)
        )
        for s in range(steps):
            here = pl.ds(s * stride + k * group, group)
            part = slice(s * group, (s + 1) * group)
            acc[here, :] = mixed[part]
            top_out[here, :] = jnp.broadcast_to(top[part], (group, HD))
            total_out[here, :] = jnp.broadcast_to(total[part], (group, HD))

    my_slot = jnp.int32(-1)
    my_length = jnp.int32(0)
    for r in range(placement.shape[0]):
        hit = div(placement[r], dec_rows) == lax.axis_index("tensor")
        my_slot = jnp.where(hit, mod(placement[r], dec_rows), my_slot)
        my_length = jnp.where(hit, (counts[r] - 1) * BLK + last[r], my_length)
    row = lax.broadcasted_iota(jnp.int32, fresh_ok.shape, 0)
    col = lax.broadcasted_iota(jnp.int32, fresh_ok.shape, 1)
    ok = (
        (mod(div(row, group), KVH) == div(col, CAPT))
        & (mod(row, dec_rows) == my_slot)
        & (mod(col, CAPT) < my_length)
    )
    fresh_ok[...] = jnp.where(ok, jnp.float32(1), jnp.float32(0))


def merge_kernel(features, box, acc, top_in, total_in, fresh_ok, query, out, result, sems):
    devices = box.shape[0]
    rank = box.shape[1] - 2 * CAPT
    terms = [box[i, :CAPT].astype(jnp.float32) for i in range(devices)]
    while len(terms) > 1:
        pairs = [a + b for a, b in zip(terms[::2], terms[1::2])]
        terms = pairs + terms[2 * len(pairs) :]
    shrunk = terms[0].astype(jnp.bfloat16)
    halves = (shrunk[:, :rank], shrunk[:, rank:])
    pieces = HD // features

    def rows(i, first, count):
        parts = [box[i * pieces + p, first : first + count, :features] for p in range(pieces)]
        return parts[0] if pieces == 1 else jnp.concatenate(parts, axis=1)

    def fresh(first):
        made = []
        for i in range(first, first + KVH, 2):
            ups = jnp.concatenate([rows(i + j, 2 * CAPT, rank) for j in range(2)], axis=1)
            delta = jnp.dot(halves[first // KVH], ups, preferred_element_type=jnp.float32)
            for j in range(2):
                base = rows(i + j, CAPT, CAPT).astype(jnp.float32)
                both = base + ADAPTER_SCALE * delta[:, j * HD : (j + 1) * HD]
                made.append(both.astype(jnp.bfloat16))
        return jnp.concatenate(made, axis=0)

    keys, values = fresh(0), fresh(KVH)
    scale = HD ** (-0.5)
    part = out.shape[0] // sems.shape[0]
    copies = []
    for c in range(sems.shape[0]):
        here = pl.ds(c * part, part)
        s = lax.dot_general(query[here, :], keys, NT, preferred_element_type=jnp.float32)
        s = jnp.where(fresh_ok[here, :] > 0, s * scale, NEG_LARGE)
        old = top_in[here, :]
        top = jnp.maximum(old, jnp.max(s, axis=1, keepdims=True))
        fade = jnp.exp(old - top)
        w = jnp.exp(s - top)
        total = total_in[here, :] * fade + jnp.sum(w, axis=1, keepdims=True)
        mixed = acc[here, :] * fade + jnp.dot(
            w.astype(jnp.bfloat16), values, preferred_element_type=jnp.float32
        )
        result[here, :] = (mixed / total).astype(jnp.bfloat16)
        copies.append(pltpu.make_async_copy(result.at[here, :], out.at[here, :], sems.at[c]))
        copies[c].start()
    for copy in copies:
        copy.wait()


def body(
    hidden,
    key_value_weight,
    adapter_down_weight,
    adapter_up_weight,
    tenant,
    tenant_page_table,
    request_block_count,
    last_block_tokens,
    placement,
    key_value_cache,
    context_length,
    decode_step_query,
    step_key_value,
):
    devices = lax.axis_size("tensor")
    tokens, width = hidden.shape
    features = key_value_weight.shape[0]
    local, pages, rank2 = adapter_down_weight.shape
    rank = adapter_up_weight.shape[2]
    tenants = tenant_page_table.shape[0]
    dec_rows, ctx, kv_width = key_value_cache.shape
    steps = step_key_value.shape[0]
    heads2 = kv_width // HD
    d_chunks, chunks = 4, 2
    up_by_page = jnp.transpose(adapter_up_weight, (1, 2, 0))
    rows = 2 * CAPT + rank
    outgoing = pl.pallas_call(
        functools.partial(project_kernel, dec_rows, d_chunks, chunks, devices),
        out_shape=pltpu.VMEM((devices, rows, HD), WIRE),
        in_specs=[ANY_SPEC] * 8,
        out_specs=VMEM_SPEC,
        scratch_shapes=[
            pltpu.SMEM(tenant.shape, jnp.int32),
            pltpu.SMEM(tenant_page_table.shape, jnp.int32),
            pltpu.SMEM(request_block_count.shape, jnp.int32),
            pltpu.SMEM(placement.shape, jnp.int32),
            pltpu.VMEM((chunks, tokens, width // chunks), jnp.bfloat16),
            pltpu.VMEM((chunks, features, width // chunks), jnp.bfloat16),
            pltpu.VMEM((local, pages, rank2), jnp.bfloat16),
            pltpu.VMEM((tokens, local), jnp.bfloat16),
            pltpu.VMEM((pages, rank, features), jnp.bfloat16),
            pltpu.VMEM((local // 16, tenants * 16, rank2), jnp.bfloat16),
            pltpu.VMEM((tenants, tokens + BLK, rank2), jnp.float32),
            pltpu.VMEM((tokens + BLK, HD), jnp.float32),
            pltpu.SMEM((2, devices), jnp.int32),
            pltpu.SemaphoreType.DMA((chunks, 2)),
            pltpu.SemaphoreType.DMA((d_chunks + 2,)),
            pltpu.SemaphoreType.DMA((4,)),
        ],
        compiler_params=pltpu.CompilerParams(vmem_limit_bytes=PROJECT_VMEM),
        name="project",
    )(
        *(
            pltpu.with_memory_space_constraint(x, pltpu.HBM)
            for x in (
                tenant, tenant_page_table, request_block_count, placement,
                hidden, key_value_weight, adapter_down_weight, up_by_page,
            )
        )
    )
    arrived = lax.all_to_all(outgoing, "tensor", split_axis=0, concat_axis=0, tiled=True)

    query = decode_step_query.reshape(steps, dec_rows, HEADS, HD)
    query = query.transpose(0, 2, 1, 3).reshape(steps * HEADS * dec_rows, HD)
    steps_kv = step_key_value.reshape(steps, dec_rows, heads2, HD)
    steps_kv = steps_kv.transpose(0, 2, 1, 3).reshape(steps * heads2 * dec_rows, HD)
    state = jax.ShapeDtypeStruct((steps * HEADS * dec_rows, HD), jnp.float32)
    acc, top, total, fresh_ok = pl.pallas_call(
        cached_kernel,
        out_shape=(state,) * 4,
        in_specs=[SMEM_SPEC] * 4 + [VMEM_SPEC] * 3,
        out_specs=(VMEM_SPEC,) * 4,
        compiler_params=pltpu.CompilerParams(vmem_limit_bytes=ATTEND_VMEM),
        name="cached",
    )(
        context_length, request_block_count, last_block_tokens, placement,
        key_value_cache, query, steps_kv,
    )
    attended = pl.pallas_call(
        functools.partial(merge_kernel, features),
        out_shape=jax.ShapeDtypeStruct((steps * HEADS * dec_rows, HD), jnp.bfloat16),
        in_specs=[VMEM_SPEC] * 6,
        out_specs=ANY_SPEC,
        scratch_shapes=[
            pltpu.VMEM((steps * HEADS * dec_rows, HD), jnp.bfloat16),
            pltpu.SemaphoreType.DMA((steps,)),
        ],
        compiler_params=pltpu.CompilerParams(vmem_limit_bytes=ATTEND_VMEM),
        name="merge",
    )(arrived, acc, top, total, fresh_ok, query)
    attended = attended.reshape(steps, HEADS, dec_rows, HD).transpose(0, 2, 1, 3)
    return attended.reshape(steps, dec_rows, HEADS * HD)


def solution(mesh):
    return jax.shard_map(
        body,
        mesh=mesh,
        in_specs=(
            P("parts", None),
            P("tensor", None),
            P("tensor", None, None),
            P("tensor", None, None),
            P("parts"),
            P(),
            P("parts"),
            P("parts"),
            P("parts"),
            P(("parts", "tensor"), None, None),
            P(("parts", "tensor")),
            P(None, ("parts", "tensor"), None),
            P(None, ("parts", "tensor"), None),
        ),
        out_specs=P(None, ("parts", "tensor"), None),
        check_vma=False,
    )
```

```python
import functools

import jax
import jax.numpy as jnp
from jax import lax
from jax.experimental import pallas as pl
from jax.experimental.pallas import tpu as pltpu
from jax.sharding import PartitionSpec as P

HEADS = 64
KVH = 8
HD = 128
BLK = 8
MOSTB = 2
CAPT = MOSTB * BLK
ADAPTER_SCALE = 0.5
NEG_LARGE = -1e30
PROJECT_VMEM = 32 * 1024 * 1024
ATTEND_VMEM = 16 * 1024 * 1024
WIRE = jnp.bfloat16

SMEM_SPEC = pl.BlockSpec(memory_space=pltpu.SMEM)
VMEM_SPEC = pl.BlockSpec(memory_space=pltpu.VMEM)
ANY_SPEC = pl.BlockSpec(memory_space=pl.ANY)


def div(x, n):
    shift = n.bit_length() - 1
    return lax.shift_right_logical(x, shift) if n == 1 << shift else x // n


def mod(x, n):
    return x & (n - 1) if n & (n - 1) == 0 else x % n


def project_kernel(
    dec_rows, d_chunks, chunks, devices, tenant_h, table_h, counts_h, placement_h, hidden, weight, down, up, out,
    tenant, table, counts, placement,
    h_s, w_s, d_s, mine_s, u_s, sel_s, part_s, base_s, dest_table, sems, d_sems, int_sems,
):
    tokens, width = hidden.shape
    features = weight.shape[0]
    local, pages, rank2 = down.shape
    tenants = table.shape[0]
    requests = tenant.shape[0]
    me = lax.axis_index("tensor")
    d_step = local // d_chunks
    step = width // chunks

    int_copies = [
        pltpu.make_async_copy(src, dst, int_sems.at[i])
        for i, (src, dst) in enumerate(
            ((table_h, table), (tenant_h, tenant), (counts_h, counts), (placement_h, placement))
        )
    ]
    for copy in int_copies:
        copy.start()
    d_copies = [
        pltpu.make_async_copy(
            down.at[pl.ds(c * d_step, d_step)], d_s.at[pl.ds(c * d_step, d_step)], d_sems.at[c])
        for c in range(d_chunks)
    ]
    h_copies = [
        pltpu.make_async_copy(hidden.at[:, pl.ds(c * step, step)], h_s.at[c], sems.at[c, 0])
        for c in range(chunks)
    ]
    w_copies = [
        pltpu.make_async_copy(weight.at[:, pl.ds(c * step, step)], w_s.at[c], sems.at[c, 1])
        for c in range(chunks)
    ]
    my_copy = pltpu.make_async_copy(
        hidden.at[:, pl.ds(pl.multiple_of(me * local, 128), local)], mine_s, d_sems.at[d_chunks]
    )
    up_copy = pltpu.make_async_copy(up, u_s, d_sems.at[d_chunks + 1])
    for copy in d_copies + [my_copy, up_copy]:
        copy.start()
    for c in range(chunks):
        h_copies[c].start()
        w_copies[c].start()

    int_copies[0].wait()
    rows = lax.broadcasted_iota(jnp.int32, (tenants * 16, 16 * pages), 0)
    cols = lax.broadcasted_iota(jnp.int32, (tenants * 16, 16 * pages), 1)
    page_of_row = jnp.zeros_like(rows)
    for k in range(tenants):
        page_of_row = jnp.where(div(rows, 16) == k, table[k], page_of_row)
    pick = (mod(rows, 16) == div(cols, pages)) & (mod(cols, pages) == page_of_row)
    pick = jnp.where(pick, jnp.float32(1), jnp.float32(0)).astype(jnp.bfloat16)

    for c in range(d_chunks):
        d_copies[c].wait()
        for b in range(c * d_step // 16, (c + 1) * d_step // 16, 2):
            block = jnp.concatenate(
                [d_s[pl.ds((b + i) * 16, 16)].reshape(16 * pages, rank2) for i in range(2)], axis=1
            )
            chosen = jnp.dot(pick, block, preferred_element_type=jnp.float32)
            for i in range(2):
                sel_s[b + i] = chosen[:, i * rank2 : (i + 1) * rank2].astype(jnp.bfloat16)
    for copy in int_copies[1:]:
        copy.wait()
    for dest in range(devices):
        dest_table[0, dest] = 0
        dest_table[1, dest] = 0
    first = jnp.int32(0)
    for r in range(requests):
        dest = div(placement[r], dec_rows)
        dest_table[0, dest] = first * BLK
        dest_table[1, dest] = tenant[r]
        first = first + counts[r]
    my_copy.wait()
    mine = mine_s[...]
    for k in range(0, tenants, 2):
        pair = min(2, tenants - k)
        maps = jnp.concatenate(
            [sel_s[:, j * 16 : (j + 1) * 16, :].reshape(local, rank2) for j in range(k, k + pair)],
            axis=1,
        )
        product = jnp.dot(mine, maps, preferred_element_type=jnp.float32)
        for j in range(pair):
            part_s[k + j, :tokens] = product[:, j * rank2 : (j + 1) * rank2]
            part_s[k + j, tokens:] = jnp.zeros((BLK, rank2), jnp.float32)

    total = jnp.zeros((tokens, features), jnp.float32)
    for c in range(chunks):
        h_copies[c].wait()
        w_copies[c].wait()
        total = total + lax.dot_general(h_s[c], w_s[c], NT, preferred_element_type=jnp.float32)
    base_s[tokens:] = jnp.zeros((BLK, HD), jnp.float32)
    if features < HD:
        base_s[...] = jnp.zeros_like(base_s)
    base_s[:tokens, :features] = total
    up_copy.wait()
    for dest in range(devices):
        start = pl.multiple_of(dest_table[0, dest], BLK)
        who = dest_table[1, dest]
        out[dest, :CAPT, :] = part_s[who, pl.ds(start, CAPT), :].astype(out.dtype)
        out[dest, CAPT : 2 * CAPT, :] = base_s[pl.ds(start, CAPT), :].astype(out.dtype)
        if features < HD:
            out[dest, 2 * CAPT :, :] = jnp.zeros((out.shape[1] - 2 * CAPT, HD), out.dtype)
        out[dest, 2 * CAPT :, :features] = u_s[table[who]]


NT = (((1,), (1,)), ((), ()))


def gather_queries(query, k, group, steps, stride):
    return jnp.concatenate(
        [query[pl.ds(s * stride + k * group, group), :] for s in range(steps)], axis=0
    )


def cached_kernel(
    lengths, counts, last, placement, cache, query, steps_kv,
    query_t, acc_t, top_t, total_t, fresh_ok, acc, top_out, total_out,
):
    dec_rows, ctx, kv_width = cache.shape
    half_width = kv_width // 2
    step_rows = KVH * dec_rows
    steps = steps_kv.shape[0] // (2 * step_rows)
    group = HEADS // KVH * dec_rows
    q_rows = steps * group
    stride = HEADS * dec_rows

    row = lax.broadcasted_iota(jnp.int32, (q_rows, ctx), 0)
    col = lax.broadcasted_iota(jnp.int32, (q_rows, ctx), 1)
    row_slot = mod(row, dec_rows)
    cache_ok = [(row_slot == g) & (col < lengths[g]) for g in range(dec_rows)]
    row = lax.broadcasted_iota(jnp.int32, (q_rows, steps * step_rows), 0)
    col = lax.broadcasted_iota(jnp.int32, (q_rows, steps * step_rows), 1)
    step_ok = (mod(row, dec_rows) == mod(col, dec_rows)) & (div(col, step_rows) <= div(row, group))
    step_head = div(mod(col, step_rows), dec_rows)
    step_keys, step_values = (
        jnp.concatenate(
            [steps_kv[pl.ds((2 * s + half) * step_rows, step_rows), :] for s in range(steps)], axis=0
        )
        for half in range(2)
    )

    scale = HD ** (-0.5)
    for k in range(KVH):
        lanes = pl.ds(k * HD, HD)
        vlanes = pl.ds(half_width + k * HD, HD)
        q = gather_queries(query, k, group, steps, stride)
        keys = [cache[g, :, lanes] for g in range(dec_rows)] + [step_keys]
        values = [cache[g, :, vlanes] for g in range(dec_rows)] + [step_values]
        scores = [
            jnp.where(
                ok,
                lax.dot_general(q, key, NT, preferred_element_type=jnp.float32) * scale,
                NEG_LARGE,
            )
            for ok, key in zip(cache_ok + [step_ok & (step_head == k)], keys)
        ]
        top = functools.reduce(jnp.maximum, [jnp.max(s, axis=1, keepdims=True) for s in scores])
        weights = [jnp.exp(s - top) for s in scores]
        total = sum(jnp.sum(w, axis=1, keepdims=True) for w in weights)
        mixed = sum(
            jnp.dot(w.astype(jnp.bfloat16), v, preferred_element_type=jnp.float32)
            for w, v in zip(weights, values)
        )
        for s in range(steps):
            here = pl.ds(s * stride + k * group, group)
            part = slice(s * group, (s + 1) * group)
            acc[here, :] = mixed[part]
            top_out[here, :] = jnp.broadcast_to(top[part], (group, HD))
            total_out[here, :] = jnp.broadcast_to(total[part], (group, HD))

    my_slot = jnp.int32(-1)
    my_length = jnp.int32(0)
    for r in range(placement.shape[0]):
        hit = div(placement[r], dec_rows) == lax.axis_index("tensor")
        my_slot = jnp.where(hit, mod(placement[r], dec_rows), my_slot)
        my_length = jnp.where(hit, (counts[r] - 1) * BLK + last[r], my_length)
    col = lax.broadcasted_iota(jnp.int32, fresh_ok.shape, 0)
    row = lax.broadcasted_iota(jnp.int32, fresh_ok.shape, 1)
    ok = (
        (mod(div(row, group), KVH) == div(col, CAPT))
        & (mod(row, dec_rows) == my_slot)
        & (mod(col, CAPT) < my_length)
    )
    fresh_ok[...] = jnp.where(ok, jnp.float32(1), jnp.float32(0))
    query_t[...] = query[...].T
    acc_t[...] = acc[...].T
    top_t[...] = top_out[...].T[: top_t.shape[0]]
    total_t[...] = total_out[...].T[: total_t.shape[0]]


def merge_kernel(features, box, query_t, acc_t, top_t, total_t, fresh_ok, out, result, sems):
    devices = box.shape[0]
    rank = box.shape[1] - 2 * CAPT
    terms = [box[i, :CAPT].astype(jnp.float32) for i in range(devices)]
    while len(terms) > 1:
        pairs = [a + b for a, b in zip(terms[::2], terms[1::2])]
        terms = pairs + terms[2 * len(pairs) :]
    shrunk = terms[0].astype(jnp.bfloat16)
    halves = (shrunk[:, :rank], shrunk[:, rank:])
    pieces = HD // features

    def rows(i, first, count):
        parts = [box[i * pieces + p, first : first + count, :features] for p in range(pieces)]
        return parts[0] if pieces == 1 else jnp.concatenate(parts, axis=1)

    def fresh(first):
        made = []
        for i in range(first, first + KVH, 2):
            ups = jnp.concatenate([rows(i + j, 2 * CAPT, rank) for j in range(2)], axis=1)
            delta = jnp.dot(halves[first // KVH], ups, preferred_element_type=jnp.float32)
            for j in range(2):
                base = rows(i + j, CAPT, CAPT).astype(jnp.float32)
                both = base + ADAPTER_SCALE * delta[:, j * HD : (j + 1) * HD]
                made.append(both.astype(jnp.bfloat16))
        return jnp.concatenate(made, axis=0)

    keys = fresh(0)
    values_t = fresh(KVH).T
    scale = HD ** (-0.5)
    part = out.shape[0] // sems.shape[0]
    copies = []
    for c in range(sems.shape[0]):
        here = pl.ds(c * part, part)
        s = jnp.dot(keys, query_t[:, here], preferred_element_type=jnp.float32)
        s = jnp.where(fresh_ok[:, here] > 0, s * scale, NEG_LARGE)
        old = top_t[:1, here]
        top = jnp.maximum(old, jnp.max(s, axis=0, keepdims=True))
        fade = jnp.exp(old - top)
        w = jnp.exp(s - top)
        total = total_t[:1, here] * fade + jnp.sum(w, axis=0, keepdims=True)
        mixed = acc_t[:, here] * fade + jnp.dot(
            values_t, w.astype(jnp.bfloat16), preferred_element_type=jnp.float32
        )
        result[here, :] = (mixed / total).T.astype(jnp.bfloat16)
        copies.append(pltpu.make_async_copy(result.at[here, :], out.at[here, :], sems.at[c]))
        copies[c].start()
    for copy in copies:
        copy.wait()


def body(
    hidden,
    key_value_weight,
    adapter_down_weight,
    adapter_up_weight,
    tenant,
    tenant_page_table,
    request_block_count,
    last_block_tokens,
    placement,
    key_value_cache,
    context_length,
    decode_step_query,
    step_key_value,
):
    devices = lax.axis_size("tensor")
    tokens, width = hidden.shape
    features = key_value_weight.shape[0]
    local, pages, rank2 = adapter_down_weight.shape
    rank = adapter_up_weight.shape[2]
    tenants = tenant_page_table.shape[0]
    dec_rows, ctx, kv_width = key_value_cache.shape
    steps = step_key_value.shape[0]
    heads2 = kv_width // HD
    d_chunks, chunks = 4, 2
    up_by_page = jnp.transpose(adapter_up_weight, (1, 2, 0))
    rows = 2 * CAPT + rank
    outgoing = pl.pallas_call(
        functools.partial(project_kernel, dec_rows, d_chunks, chunks, devices),
        out_shape=pltpu.VMEM((devices, rows, HD), WIRE),
        in_specs=[ANY_SPEC] * 8,
        out_specs=VMEM_SPEC,
        scratch_shapes=[
            pltpu.SMEM(tenant.shape, jnp.int32),
            pltpu.SMEM(tenant_page_table.shape, jnp.int32),
            pltpu.SMEM(request_block_count.shape, jnp.int32),
            pltpu.SMEM(placement.shape, jnp.int32),
            pltpu.VMEM((chunks, tokens, width // chunks), jnp.bfloat16),
            pltpu.VMEM((chunks, features, width // chunks), jnp.bfloat16),
            pltpu.VMEM((local, pages, rank2), jnp.bfloat16),
            pltpu.VMEM((tokens, local), jnp.bfloat16),
            pltpu.VMEM((pages, rank, features), jnp.bfloat16),
            pltpu.VMEM((local // 16, tenants * 16, rank2), jnp.bfloat16),
            pltpu.VMEM((tenants, tokens + BLK, rank2), jnp.float32),
            pltpu.VMEM((tokens + BLK, HD), jnp.float32),
            pltpu.SMEM((2, devices), jnp.int32),
            pltpu.SemaphoreType.DMA((chunks, 2)),
            pltpu.SemaphoreType.DMA((d_chunks + 2,)),
            pltpu.SemaphoreType.DMA((4,)),
        ],
        compiler_params=pltpu.CompilerParams(vmem_limit_bytes=PROJECT_VMEM),
        name="project",
    )(
        *(
            pltpu.with_memory_space_constraint(x, pltpu.HBM)
            for x in (
                tenant, tenant_page_table, request_block_count, placement,
                hidden, key_value_weight, adapter_down_weight, up_by_page,
            )
        )
    )
    arrived = lax.all_to_all(outgoing, "tensor", split_axis=0, concat_axis=0, tiled=True)

    query = decode_step_query.reshape(steps, dec_rows, HEADS, HD)
    query = query.transpose(0, 2, 1, 3).reshape(steps * HEADS * dec_rows, HD)
    steps_kv = step_key_value.reshape(steps, dec_rows, heads2, HD)
    steps_kv = steps_kv.transpose(0, 2, 1, 3).reshape(steps * heads2 * dec_rows, HD)
    q_rows = steps * HEADS * dec_rows
    state = jax.ShapeDtypeStruct((HD, q_rows), jnp.float32)
    line = jax.ShapeDtypeStruct((8, q_rows), jnp.float32)
    handed = pl.pallas_call(
        cached_kernel,
        out_shape=(
            jax.ShapeDtypeStruct((HD, q_rows), jnp.bfloat16),
            state,
            line,
            line,
            jax.ShapeDtypeStruct((KVH * CAPT, q_rows), jnp.float32),
        ),
        in_specs=[SMEM_SPEC] * 4 + [VMEM_SPEC] * 3,
        out_specs=(VMEM_SPEC,) * 5,
        scratch_shapes=[pltpu.VMEM((q_rows, HD), jnp.float32)] * 3,
        compiler_params=pltpu.CompilerParams(vmem_limit_bytes=ATTEND_VMEM),
        name="cached",
    )(
        context_length, request_block_count, last_block_tokens, placement,
        key_value_cache, query, steps_kv,
    )
    attended = pl.pallas_call(
        functools.partial(merge_kernel, features),
        out_shape=jax.ShapeDtypeStruct((q_rows, HD), jnp.bfloat16),
        in_specs=[VMEM_SPEC] * 6,
        out_specs=ANY_SPEC,
        scratch_shapes=[
            pltpu.VMEM((q_rows, HD), jnp.bfloat16),
            pltpu.SemaphoreType.DMA((steps,)),
        ],
        compiler_params=pltpu.CompilerParams(vmem_limit_bytes=ATTEND_VMEM),
        name="merge",
    )(arrived, *handed)
    attended = attended.reshape(steps, HEADS, dec_rows, HD).transpose(0, 2, 1, 3)
    return attended.reshape(steps, dec_rows, HEADS * HD)


def solution(mesh):
    return jax.shard_map(
        body,
        mesh=mesh,
        in_specs=(
            P("parts", None),
            P("tensor", None),
            P("tensor", None, None),
            P("tensor", None, None),
            P("parts"),
            P(),
            P("parts"),
            P("parts"),
            P("parts"),
            P(("parts", "tensor"), None, None),
            P(("parts", "tensor")),
            P(None, ("parts", "tensor"), None),
            P(None, ("parts", "tensor"), None),
        ),
        out_specs=P(None, ("parts", "tensor"), None),
        check_vma=False,
    )
```

```python
import functools

import jax
import jax.numpy as jnp
from jax import lax
from jax.experimental import pallas as pl
from jax.experimental.pallas import tpu as pltpu
from jax.sharding import PartitionSpec as P

HEADS = 64
KVH = 8
HD = 128
BLK = 8
MOSTB = 2
CAPT = MOSTB * BLK
ADAPTER_SCALE = 0.5
NEG_LARGE = -1e30
PROJECT_VMEM = 32 * 1024 * 1024
ATTEND_VMEM = 16 * 1024 * 1024
WIRE = jnp.bfloat16

SMEM_SPEC = pl.BlockSpec(memory_space=pltpu.SMEM)
VMEM_SPEC = pl.BlockSpec(memory_space=pltpu.VMEM)
ANY_SPEC = pl.BlockSpec(memory_space=pl.ANY)


def div(x, n):
    shift = n.bit_length() - 1
    return lax.shift_right_logical(x, shift) if n == 1 << shift else x // n


def mod(x, n):
    return x & (n - 1) if n & (n - 1) == 0 else x % n


def project_kernel(
    dec_rows, d_chunks, chunks, devices, tenant_h, table_h, counts_h, placement_h, hidden, weight, down, up, out,
    tenant, table, counts, placement,
    h_s, w_s, d_s, mine_s, u_s, sel_s, part_s, base_s, dest_table, sems, d_sems, int_sems,
):
    tokens, width = hidden.shape
    features = weight.shape[0]
    local, pages, rank2 = down.shape
    tenants = table.shape[0]
    requests = tenant.shape[0]
    me = lax.axis_index("tensor")
    d_step = local // d_chunks
    step = width // chunks

    int_copies = [
        pltpu.make_async_copy(src, dst, int_sems.at[i])
        for i, (src, dst) in enumerate(
            ((table_h, table), (tenant_h, tenant), (counts_h, counts), (placement_h, placement))
        )
    ]
    for copy in int_copies:
        copy.start()
    d_copies = [
        pltpu.make_async_copy(
            down.at[pl.ds(c * d_step, d_step)], d_s.at[pl.ds(c * d_step, d_step)], d_sems.at[c])
        for c in range(d_chunks)
    ]
    h_copies = [
        pltpu.make_async_copy(hidden.at[:, pl.ds(c * step, step)], h_s.at[c], sems.at[c, 0])
        for c in range(chunks)
    ]
    w_copies = [
        pltpu.make_async_copy(weight.at[:, pl.ds(c * step, step)], w_s.at[c], sems.at[c, 1])
        for c in range(chunks)
    ]
    my_copy = pltpu.make_async_copy(
        hidden.at[:, pl.ds(pl.multiple_of(me * local, 128), local)], mine_s, d_sems.at[d_chunks]
    )
    up_copy = pltpu.make_async_copy(up, u_s, d_sems.at[d_chunks + 1])
    for copy in d_copies + [my_copy, up_copy]:
        copy.start()
    for c in range(chunks):
        h_copies[c].start()
        w_copies[c].start()

    int_copies[0].wait()
    rows = lax.broadcasted_iota(jnp.int32, (tenants * 16, 16 * pages), 0)
    cols = lax.broadcasted_iota(jnp.int32, (tenants * 16, 16 * pages), 1)
    page_of_row = jnp.zeros_like(rows)
    for k in range(tenants):
        page_of_row = jnp.where(div(rows, 16) == k, table[k], page_of_row)
    pick = (mod(rows, 16) == div(cols, pages)) & (mod(cols, pages) == page_of_row)
    pick = jnp.where(pick, jnp.float32(1), jnp.float32(0)).astype(jnp.bfloat16)

    for c in range(d_chunks):
        d_copies[c].wait()
        for b in range(c * d_step // 16, (c + 1) * d_step // 16, 2):
            block = jnp.concatenate(
                [d_s[pl.ds((b + i) * 16, 16)].reshape(16 * pages, rank2) for i in range(2)], axis=1
            )
            chosen = jnp.dot(pick, block, preferred_element_type=jnp.float32)
            for i in range(2):
                sel_s[b + i] = chosen[:, i * rank2 : (i + 1) * rank2].astype(jnp.bfloat16)
    for copy in int_copies[1:]:
        copy.wait()
    for dest in range(devices):
        dest_table[0, dest] = 0
        dest_table[1, dest] = 0
    first = jnp.int32(0)
    for r in range(requests):
        dest = div(placement[r], dec_rows)
        dest_table[0, dest] = first * BLK
        dest_table[1, dest] = tenant[r]
        first = first + counts[r]
    my_copy.wait()
    mine = mine_s[...]
    for k in range(0, tenants, 2):
        pair = min(2, tenants - k)
        maps = jnp.concatenate(
            [sel_s[:, j * 16 : (j + 1) * 16, :].reshape(local, rank2) for j in range(k, k + pair)],
            axis=1,
        )
        product = jnp.dot(mine, maps, preferred_element_type=jnp.float32)
        for j in range(pair):
            part_s[k + j, :tokens] = product[:, j * rank2 : (j + 1) * rank2]
            part_s[k + j, tokens:] = jnp.zeros((BLK, rank2), jnp.float32)

    total = jnp.zeros((tokens, features), jnp.float32)
    for c in range(chunks):
        h_copies[c].wait()
        w_copies[c].wait()
        total = total + lax.dot_general(h_s[c], w_s[c], NT, preferred_element_type=jnp.float32)
    base_s[tokens:] = jnp.zeros((BLK, HD), jnp.float32)
    if features < HD:
        base_s[...] = jnp.zeros_like(base_s)
    base_s[:tokens, :features] = total
    up_copy.wait()
    places = [
        (pl.multiple_of(dest_table[0, dest], BLK), dest_table[1, dest], table[dest_table[1, dest]])
        for dest in range(devices)
    ]
    for first in range(0, devices, 4):
        group = places[first : first + 4]
        parts = [part_s[who, pl.ds(start, CAPT), :].astype(out.dtype) for start, who, _ in group]
        bases = [base_s[pl.ds(start, CAPT), :].astype(out.dtype) for start, _, _ in group]
        slabs = [u_s[page] for _, _, page in group]
        for i in range(len(group)):
            out[first + i, :CAPT, :] = parts[i]
            out[first + i, CAPT : 2 * CAPT, :] = bases[i]
            if features < HD:
                out[first + i, 2 * CAPT :, :] = jnp.zeros((out.shape[1] - 2 * CAPT, HD), out.dtype)
            out[first + i, 2 * CAPT :, :features] = slabs[i]


NT = (((1,), (1,)), ((), ()))


def gather_queries(query, k, group, steps, stride):
    return jnp.concatenate(
        [query[pl.ds(s * stride + k * group, group), :] for s in range(steps)], axis=0
    )


def cached_kernel(
    lengths, counts, last, placement, cache, query, steps_kv,
    query_t, acc_t, top_t, total_t, fresh_ok, acc, top_out, total_out,
):
    dec_rows, ctx, kv_width = cache.shape
    half_width = kv_width // 2
    step_rows = KVH * dec_rows
    steps = steps_kv.shape[0] // (2 * step_rows)
    group = HEADS // KVH * dec_rows
    q_rows = steps * group
    stride = HEADS * dec_rows

    row = lax.broadcasted_iota(jnp.int32, (q_rows, ctx), 0)
    col = lax.broadcasted_iota(jnp.int32, (q_rows, ctx), 1)
    row_slot = mod(row, dec_rows)
    cache_ok = [(row_slot == g) & (col < lengths[g]) for g in range(dec_rows)]
    row = lax.broadcasted_iota(jnp.int32, (q_rows, steps * step_rows), 0)
    col = lax.broadcasted_iota(jnp.int32, (q_rows, steps * step_rows), 1)
    step_ok = (mod(row, dec_rows) == mod(col, dec_rows)) & (div(col, step_rows) <= div(row, group))
    step_head = div(mod(col, step_rows), dec_rows)
    step_keys, step_values = (
        jnp.concatenate(
            [steps_kv[pl.ds((2 * s + half) * step_rows, step_rows), :] for s in range(steps)], axis=0
        )
        for half in range(2)
    )

    scale = HD ** (-0.5)
    for k in range(KVH):
        lanes = pl.ds(k * HD, HD)
        vlanes = pl.ds(half_width + k * HD, HD)
        q = gather_queries(query, k, group, steps, stride)
        keys = [cache[g, :, lanes] for g in range(dec_rows)] + [step_keys]
        values = [cache[g, :, vlanes] for g in range(dec_rows)] + [step_values]
        scores = [
            jnp.where(
                ok,
                lax.dot_general(q, key, NT, preferred_element_type=jnp.float32) * scale,
                NEG_LARGE,
            )
            for ok, key in zip(cache_ok + [step_ok & (step_head == k)], keys)
        ]
        top = functools.reduce(jnp.maximum, [jnp.max(s, axis=1, keepdims=True) for s in scores])
        weights = [jnp.exp(s - top) for s in scores]
        total = sum(jnp.sum(w, axis=1, keepdims=True) for w in weights)
        mixed = sum(
            jnp.dot(w.astype(jnp.bfloat16), v, preferred_element_type=jnp.float32)
            for w, v in zip(weights, values)
        )
        for s in range(steps):
            here = pl.ds(s * stride + k * group, group)
            part = slice(s * group, (s + 1) * group)
            acc[here, :] = mixed[part]
            top_out[here, :] = jnp.broadcast_to(top[part], (group, HD))
            total_out[here, :] = jnp.broadcast_to(total[part], (group, HD))

    my_slot = jnp.int32(-1)
    my_length = jnp.int32(0)
    for r in range(placement.shape[0]):
        hit = div(placement[r], dec_rows) == lax.axis_index("tensor")
        my_slot = jnp.where(hit, mod(placement[r], dec_rows), my_slot)
        my_length = jnp.where(hit, (counts[r] - 1) * BLK + last[r], my_length)
    col = lax.broadcasted_iota(jnp.int32, fresh_ok.shape, 0)
    row = lax.broadcasted_iota(jnp.int32, fresh_ok.shape, 1)
    ok = (
        (mod(div(row, group), KVH) == div(col, CAPT))
        & (mod(row, dec_rows) == my_slot)
        & (mod(col, CAPT) < my_length)
    )
    fresh_ok[...] = jnp.where(ok, jnp.float32(1), jnp.float32(0))
    query_t[...] = query[...].T
    acc_t[...] = acc[...].T
    top_t[...] = top_out[...].T[: top_t.shape[0]]
    total_t[...] = total_out[...].T[: total_t.shape[0]]


def merge_kernel(features, box, query_t, acc_t, top_t, total_t, fresh_ok, out, result, sems):
    devices = box.shape[0]
    rank = box.shape[1] - 2 * CAPT
    terms = [box[i, :CAPT].astype(jnp.float32) for i in range(devices)]
    while len(terms) > 1:
        pairs = [a + b for a, b in zip(terms[::2], terms[1::2])]
        terms = pairs + terms[2 * len(pairs) :]
    shrunk = terms[0].astype(jnp.bfloat16)
    halves = (shrunk[:, :rank], shrunk[:, rank:])
    pieces = HD // features

    def rows(i, first, count):
        parts = [box[i * pieces + p, first : first + count, :features] for p in range(pieces)]
        return parts[0] if pieces == 1 else jnp.concatenate(parts, axis=1)

    def fresh(first):
        made = []
        for i in range(first, first + KVH, 2):
            ups = jnp.concatenate([rows(i + j, 2 * CAPT, rank) for j in range(2)], axis=1)
            delta = jnp.dot(halves[first // KVH], ups, preferred_element_type=jnp.float32)
            for j in range(2):
                base = rows(i + j, CAPT, CAPT).astype(jnp.float32)
                both = base + ADAPTER_SCALE * delta[:, j * HD : (j + 1) * HD]
                made.append(both.astype(jnp.bfloat16))
        return jnp.concatenate(made, axis=0)

    keys = fresh(0)
    values_t = fresh(KVH).T
    scale = HD ** (-0.5)
    part = out.shape[0] // sems.shape[0]
    copies = []
    for c in range(sems.shape[0]):
        here = pl.ds(c * part, part)
        s = jnp.dot(keys, query_t[:, here], preferred_element_type=jnp.float32)
        s = jnp.where(fresh_ok[:, here] > 0, s * scale, NEG_LARGE)
        old = top_t[:1, here]
        top = jnp.maximum(old, jnp.max(s, axis=0, keepdims=True))
        fade = jnp.exp(old - top)
        w = jnp.exp(s - top)
        total = total_t[:1, here] * fade + jnp.sum(w, axis=0, keepdims=True)
        mixed = acc_t[:, here] * fade + jnp.dot(
            values_t, w.astype(jnp.bfloat16), preferred_element_type=jnp.float32
        )
        result[here, :] = (mixed / total).T.astype(jnp.bfloat16)
        copies.append(pltpu.make_async_copy(result.at[here, :], out.at[here, :], sems.at[c]))
        copies[c].start()
    for copy in copies:
        copy.wait()


def body(
    hidden,
    key_value_weight,
    adapter_down_weight,
    adapter_up_weight,
    tenant,
    tenant_page_table,
    request_block_count,
    last_block_tokens,
    placement,
    key_value_cache,
    context_length,
    decode_step_query,
    step_key_value,
):
    devices = lax.axis_size("tensor")
    tokens, width = hidden.shape
    features = key_value_weight.shape[0]
    local, pages, rank2 = adapter_down_weight.shape
    rank = adapter_up_weight.shape[2]
    tenants = tenant_page_table.shape[0]
    dec_rows, ctx, kv_width = key_value_cache.shape
    steps = step_key_value.shape[0]
    heads2 = kv_width // HD
    d_chunks, chunks = 4, 2
    up_by_page = jnp.transpose(adapter_up_weight, (1, 2, 0))
    rows = 2 * CAPT + rank
    outgoing = pl.pallas_call(
        functools.partial(project_kernel, dec_rows, d_chunks, chunks, devices),
        out_shape=pltpu.VMEM((devices, rows, HD), WIRE),
        in_specs=[ANY_SPEC] * 8,
        out_specs=VMEM_SPEC,
        scratch_shapes=[
            pltpu.SMEM(tenant.shape, jnp.int32),
            pltpu.SMEM(tenant_page_table.shape, jnp.int32),
            pltpu.SMEM(request_block_count.shape, jnp.int32),
            pltpu.SMEM(placement.shape, jnp.int32),
            pltpu.VMEM((chunks, tokens, width // chunks), jnp.bfloat16),
            pltpu.VMEM((chunks, features, width // chunks), jnp.bfloat16),
            pltpu.VMEM((local, pages, rank2), jnp.bfloat16),
            pltpu.VMEM((tokens, local), jnp.bfloat16),
            pltpu.VMEM((pages, rank, features), jnp.bfloat16),
            pltpu.VMEM((local // 16, tenants * 16, rank2), jnp.bfloat16),
            pltpu.VMEM((tenants, tokens + BLK, rank2), jnp.float32),
            pltpu.VMEM((tokens + BLK, HD), jnp.float32),
            pltpu.SMEM((2, devices), jnp.int32),
            pltpu.SemaphoreType.DMA((chunks, 2)),
            pltpu.SemaphoreType.DMA((d_chunks + 2,)),
            pltpu.SemaphoreType.DMA((4,)),
        ],
        compiler_params=pltpu.CompilerParams(vmem_limit_bytes=PROJECT_VMEM),
        name="project",
    )(
        *(
            pltpu.with_memory_space_constraint(x, pltpu.HBM)
            for x in (
                tenant, tenant_page_table, request_block_count, placement,
                hidden, key_value_weight, adapter_down_weight, up_by_page,
            )
        )
    )
    arrived = lax.all_to_all(outgoing, "tensor", split_axis=0, concat_axis=0, tiled=True)

    query = decode_step_query.reshape(steps, dec_rows, HEADS, HD)
    query = query.transpose(0, 2, 1, 3).reshape(steps * HEADS * dec_rows, HD)
    steps_kv = step_key_value.reshape(steps, dec_rows, heads2, HD)
    steps_kv = steps_kv.transpose(0, 2, 1, 3).reshape(steps * heads2 * dec_rows, HD)
    q_rows = steps * HEADS * dec_rows
    state = jax.ShapeDtypeStruct((HD, q_rows), jnp.float32)
    line = jax.ShapeDtypeStruct((8, q_rows), jnp.float32)
    handed = pl.pallas_call(
        cached_kernel,
        out_shape=(
            jax.ShapeDtypeStruct((HD, q_rows), jnp.bfloat16),
            state,
            line,
            line,
            jax.ShapeDtypeStruct((KVH * CAPT, q_rows), jnp.float32),
        ),
        in_specs=[SMEM_SPEC] * 4 + [VMEM_SPEC] * 3,
        out_specs=(VMEM_SPEC,) * 5,
        scratch_shapes=[pltpu.VMEM((q_rows, HD), jnp.float32)] * 3,
        compiler_params=pltpu.CompilerParams(vmem_limit_bytes=ATTEND_VMEM),
        name="cached",
    )(
        context_length, request_block_count, last_block_tokens, placement,
        key_value_cache, query, steps_kv,
    )
    attended = pl.pallas_call(
        functools.partial(merge_kernel, features),
        out_shape=jax.ShapeDtypeStruct((q_rows, HD), jnp.bfloat16),
        in_specs=[VMEM_SPEC] * 6,
        out_specs=ANY_SPEC,
        scratch_shapes=[
            pltpu.VMEM((q_rows, HD), jnp.bfloat16),
            pltpu.SemaphoreType.DMA((steps,)),
        ],
        compiler_params=pltpu.CompilerParams(vmem_limit_bytes=ATTEND_VMEM),
        name="merge",
    )(arrived, *handed)
    attended = attended.reshape(steps, HEADS, dec_rows, HD).transpose(0, 2, 1, 3)
    return attended.reshape(steps, dec_rows, HEADS * HD)


def solution(mesh):
    return jax.shard_map(
        body,
        mesh=mesh,
        in_specs=(
            P("parts", None),
            P("tensor", None),
            P("tensor", None, None),
            P("tensor", None, None),
            P("parts"),
            P(),
            P("parts"),
            P("parts"),
            P("parts"),
            P(("parts", "tensor"), None, None),
            P(("parts", "tensor")),
            P(None, ("parts", "tensor"), None),
            P(None, ("parts", "tensor"), None),
        ),
        out_specs=P(None, ("parts", "tensor"), None),
        check_vma=False,
    )
```

```python
import functools

import jax
import jax.numpy as jnp
from jax import lax
from jax.experimental import pallas as pl
from jax.experimental.pallas import tpu as pltpu
from jax.sharding import PartitionSpec as P

HEADS = 64
KVH = 8
HD = 128
BLK = 8
MOSTB = 2
CAPT = MOSTB * BLK
ADAPTER_SCALE = 0.5
NEG_LARGE = -1e30
PROJECT_VMEM = 32 * 1024 * 1024
ATTEND_VMEM = 16 * 1024 * 1024
WIRE = jnp.bfloat16

SMEM_SPEC = pl.BlockSpec(memory_space=pltpu.SMEM)
VMEM_SPEC = pl.BlockSpec(memory_space=pltpu.VMEM)
ANY_SPEC = pl.BlockSpec(memory_space=pl.ANY)


def div(x, n):
    shift = n.bit_length() - 1
    return lax.shift_right_logical(x, shift) if n == 1 << shift else x // n


def mod(x, n):
    return x & (n - 1) if n & (n - 1) == 0 else x % n


def project_kernel(
    dec_rows, d_chunks, chunks, devices, tenant_h, table_h, counts_h, placement_h, hidden, weight, down, up, out,
    tenant, table, counts, placement,
    h_s, w_s, d_s, mine_s, u_s, wide_s, part_s, base_s, dest_table, sems, d_sems, int_sems,
):
    tokens, width = hidden.shape
    features = weight.shape[0]
    local, pages, rank2 = down.shape
    tenants = table.shape[0]
    requests = tenant.shape[0]
    me = lax.axis_index("tensor")
    d_step = local // d_chunks
    step = width // chunks

    int_copies = [
        pltpu.make_async_copy(src, dst, int_sems.at[i])
        for i, (src, dst) in enumerate(
            ((table_h, table), (tenant_h, tenant), (counts_h, counts), (placement_h, placement))
        )
    ]
    for copy in int_copies:
        copy.start()
    d_copies = [
        pltpu.make_async_copy(
            down.at[pl.ds(c * d_step, d_step)], d_s.at[pl.ds(c * d_step, d_step)], d_sems.at[c])
        for c in range(d_chunks)
    ]
    h_copies = [
        pltpu.make_async_copy(hidden.at[:, pl.ds(c * step, step)], h_s.at[c], sems.at[c, 0])
        for c in range(chunks)
    ]
    w_copies = [
        pltpu.make_async_copy(weight.at[:, pl.ds(c * step, step)], w_s.at[c], sems.at[c, 1])
        for c in range(chunks)
    ]
    my_copy = pltpu.make_async_copy(
        hidden.at[:, pl.ds(pl.multiple_of(me * local, 128), local)], mine_s, d_sems.at[d_chunks]
    )
    up_copy = pltpu.make_async_copy(up, u_s, d_sems.at[d_chunks + 1])
    for copy in d_copies + [my_copy, up_copy]:
        copy.start()
    for c in range(chunks):
        h_copies[c].start()
        w_copies[c].start()

    for c in range(d_chunks):
        d_copies[c].wait()
        part = d_s[pl.ds(c * d_step, d_step)].astype(jnp.float32)
        wide_s[pl.ds(c * d_step * pages, d_step * pages), :] = part.reshape(d_step * pages, rank2)
    for copy in int_copies:
        copy.wait()
    for dest in range(devices):
        dest_table[0, dest] = 0
        dest_table[1, dest] = 0
    first = jnp.int32(0)
    for r in range(requests):
        dest = div(placement[r], dec_rows)
        dest_table[0, dest] = first * BLK
        dest_table[1, dest] = tenant[r]
        first = first + counts[r]
    my_copy.wait()
    mine = mine_s[...]
    for k in range(0, tenants, 2):
        pair = min(2, tenants - k)
        maps = jnp.concatenate(
            [
                wide_s[pl.ds(table[j], local, stride=pages), :].astype(jnp.bfloat16)
                for j in range(k, k + pair)
            ],
            axis=1,
        )
        product = jnp.dot(mine, maps, preferred_element_type=jnp.float32)
        for j in range(pair):
            part_s[k + j, :tokens] = product[:, j * rank2 : (j + 1) * rank2]
            part_s[k + j, tokens:] = jnp.zeros((BLK, rank2), jnp.float32)

    total = jnp.zeros((tokens, features), jnp.float32)
    for c in range(chunks):
        h_copies[c].wait()
        w_copies[c].wait()
        total = total + lax.dot_general(h_s[c], w_s[c], NT, preferred_element_type=jnp.float32)
    base_s[tokens:] = jnp.zeros((BLK, HD), jnp.float32)
    if features < HD:
        base_s[...] = jnp.zeros_like(base_s)
    base_s[:tokens, :features] = total
    up_copy.wait()
    for dest in range(devices):
        start = pl.multiple_of(dest_table[0, dest], BLK)
        who = dest_table[1, dest]
        out[dest, :CAPT, :] = part_s[who, pl.ds(start, CAPT), :].astype(out.dtype)
        out[dest, CAPT : 2 * CAPT, :] = base_s[pl.ds(start, CAPT), :].astype(out.dtype)
        if features < HD:
            out[dest, 2 * CAPT :, :] = jnp.zeros((out.shape[1] - 2 * CAPT, HD), out.dtype)
        out[dest, 2 * CAPT :, :features] = u_s[table[who]]


NT = (((1,), (1,)), ((), ()))


def gather_queries(query, k, group, steps, stride):
    return jnp.concatenate(
        [query[pl.ds(s * stride + k * group, group), :] for s in range(steps)], axis=0
    )


def cached_kernel(
    lengths, counts, last, placement, cache, query, steps_kv,
    query_t, acc_t, top_t, total_t, fresh_ok, acc, top_out, total_out,
):
    dec_rows, ctx, kv_width = cache.shape
    half_width = kv_width // 2
    step_rows = KVH * dec_rows
    steps = steps_kv.shape[0] // (2 * step_rows)
    group = HEADS // KVH * dec_rows
    q_rows = steps * group
    stride = HEADS * dec_rows

    row = lax.broadcasted_iota(jnp.int32, (q_rows, ctx), 0)
    col = lax.broadcasted_iota(jnp.int32, (q_rows, ctx), 1)
    row_slot = mod(row, dec_rows)
    cache_ok = [(row_slot == g) & (col < lengths[g]) for g in range(dec_rows)]
    row = lax.broadcasted_iota(jnp.int32, (q_rows, steps * step_rows), 0)
    col = lax.broadcasted_iota(jnp.int32, (q_rows, steps * step_rows), 1)
    step_ok = (mod(row, dec_rows) == mod(col, dec_rows)) & (div(col, step_rows) <= div(row, group))
    step_head = div(mod(col, step_rows), dec_rows)
    step_keys, step_values = (
        jnp.concatenate(
            [steps_kv[pl.ds((2 * s + half) * step_rows, step_rows), :] for s in range(steps)], axis=0
        )
        for half in range(2)
    )

    scale = HD ** (-0.5)
    for k in range(KVH):
        lanes = pl.ds(k * HD, HD)
        vlanes = pl.ds(half_width + k * HD, HD)
        q = gather_queries(query, k, group, steps, stride)
        keys = [cache[g, :, lanes] for g in range(dec_rows)] + [step_keys]
        values = [cache[g, :, vlanes] for g in range(dec_rows)] + [step_values]
        scores = [
            jnp.where(
                ok,
                lax.dot_general(q, key, NT, preferred_element_type=jnp.float32) * scale,
                NEG_LARGE,
            )
            for ok, key in zip(cache_ok + [step_ok & (step_head == k)], keys)
        ]
        top = functools.reduce(jnp.maximum, [jnp.max(s, axis=1, keepdims=True) for s in scores])
        weights = [jnp.exp(s - top) for s in scores]
        total = sum(jnp.sum(w, axis=1, keepdims=True) for w in weights)
        mixed = sum(
            jnp.dot(w.astype(jnp.bfloat16), v, preferred_element_type=jnp.float32)
            for w, v in zip(weights, values)
        )
        for s in range(steps):
            here = pl.ds(s * stride + k * group, group)
            part = slice(s * group, (s + 1) * group)
            acc[here, :] = mixed[part]
            top_out[here, :] = jnp.broadcast_to(top[part], (group, HD))
            total_out[here, :] = jnp.broadcast_to(total[part], (group, HD))

    my_slot = jnp.int32(-1)
    my_length = jnp.int32(0)
    for r in range(placement.shape[0]):
        hit = div(placement[r], dec_rows) == lax.axis_index("tensor")
        my_slot = jnp.where(hit, mod(placement[r], dec_rows), my_slot)
        my_length = jnp.where(hit, (counts[r] - 1) * BLK + last[r], my_length)
    col = lax.broadcasted_iota(jnp.int32, fresh_ok.shape, 0)
    row = lax.broadcasted_iota(jnp.int32, fresh_ok.shape, 1)
    ok = (
        (mod(div(row, group), KVH) == div(col, CAPT))
        & (mod(row, dec_rows) == my_slot)
        & (mod(col, CAPT) < my_length)
    )
    fresh_ok[...] = jnp.where(ok, jnp.float32(1), jnp.float32(0))
    query_t[...] = query[...].T
    acc_t[...] = acc[...].T
    top_t[...] = top_out[...].T[: top_t.shape[0]]
    total_t[...] = total_out[...].T[: total_t.shape[0]]


def merge_kernel(features, box, query_t, acc_t, top_t, total_t, fresh_ok, out, result, sems):
    devices = box.shape[0]
    rank = box.shape[1] - 2 * CAPT
    terms = [box[i, :CAPT].astype(jnp.float32) for i in range(devices)]
    while len(terms) > 1:
        pairs = [a + b for a, b in zip(terms[::2], terms[1::2])]
        terms = pairs + terms[2 * len(pairs) :]
    shrunk = terms[0].astype(jnp.bfloat16)
    halves = (shrunk[:, :rank], shrunk[:, rank:])
    pieces = HD // features

    def rows(i, first, count):
        parts = [box[i * pieces + p, first : first + count, :features] for p in range(pieces)]
        return parts[0] if pieces == 1 else jnp.concatenate(parts, axis=1)

    def fresh(first):
        made = []
        for i in range(first, first + KVH, 2):
            ups = jnp.concatenate([rows(i + j, 2 * CAPT, rank) for j in range(2)], axis=1)
            delta = jnp.dot(halves[first // KVH], ups, preferred_element_type=jnp.float32)
            for j in range(2):
                base = rows(i + j, CAPT, CAPT).astype(jnp.float32)
                both = base + ADAPTER_SCALE * delta[:, j * HD : (j + 1) * HD]
                made.append(both.astype(jnp.bfloat16))
        return jnp.concatenate(made, axis=0)

    keys = fresh(0)
    values_t = fresh(KVH).T
    scale = HD ** (-0.5)
    part = out.shape[0] // sems.shape[0]
    copies = []
    for c in range(sems.shape[0]):
        here = pl.ds(c * part, part)
        s = jnp.dot(keys, query_t[:, here], preferred_element_type=jnp.float32)
        s = jnp.where(fresh_ok[:, here] > 0, s * scale, NEG_LARGE)
        old = top_t[:1, here]
        top = jnp.maximum(old, jnp.max(s, axis=0, keepdims=True))
        fade = jnp.exp(old - top)
        w = jnp.exp(s - top)
        total = total_t[:1, here] * fade + jnp.sum(w, axis=0, keepdims=True)
        mixed = acc_t[:, here] * fade + jnp.dot(
            values_t, w.astype(jnp.bfloat16), preferred_element_type=jnp.float32
        )
        result[here, :] = (mixed / total).T.astype(jnp.bfloat16)
        copies.append(pltpu.make_async_copy(result.at[here, :], out.at[here, :], sems.at[c]))
        copies[c].start()
    for copy in copies:
        copy.wait()


def body(
    hidden,
    key_value_weight,
    adapter_down_weight,
    adapter_up_weight,
    tenant,
    tenant_page_table,
    request_block_count,
    last_block_tokens,
    placement,
    key_value_cache,
    context_length,
    decode_step_query,
    step_key_value,
):
    devices = lax.axis_size("tensor")
    tokens, width = hidden.shape
    features = key_value_weight.shape[0]
    local, pages, rank2 = adapter_down_weight.shape
    rank = adapter_up_weight.shape[2]
    tenants = tenant_page_table.shape[0]
    dec_rows, ctx, kv_width = key_value_cache.shape
    steps = step_key_value.shape[0]
    heads2 = kv_width // HD
    d_chunks, chunks = 4, 2
    up_by_page = jnp.transpose(adapter_up_weight, (1, 2, 0))
    rows = 2 * CAPT + rank
    outgoing = pl.pallas_call(
        functools.partial(project_kernel, dec_rows, d_chunks, chunks, devices),
        out_shape=pltpu.VMEM((devices, rows, HD), WIRE),
        in_specs=[ANY_SPEC] * 8,
        out_specs=VMEM_SPEC,
        scratch_shapes=[
            pltpu.SMEM(tenant.shape, jnp.int32),
            pltpu.SMEM(tenant_page_table.shape, jnp.int32),
            pltpu.SMEM(request_block_count.shape, jnp.int32),
            pltpu.SMEM(placement.shape, jnp.int32),
            pltpu.VMEM((chunks, tokens, width // chunks), jnp.bfloat16),
            pltpu.VMEM((chunks, features, width // chunks), jnp.bfloat16),
            pltpu.VMEM((local, pages, rank2), jnp.bfloat16),
            pltpu.VMEM((tokens, local), jnp.bfloat16),
            pltpu.VMEM((pages, rank, features), jnp.bfloat16),
            pltpu.VMEM((local * pages, rank2), jnp.float32),
            pltpu.VMEM((tenants, tokens + BLK, rank2), jnp.float32),
            pltpu.VMEM((tokens + BLK, HD), jnp.float32),
            pltpu.SMEM((2, devices), jnp.int32),
            pltpu.SemaphoreType.DMA((chunks, 2)),
            pltpu.SemaphoreType.DMA((d_chunks + 2,)),
            pltpu.SemaphoreType.DMA((4,)),
        ],
        compiler_params=pltpu.CompilerParams(vmem_limit_bytes=PROJECT_VMEM),
        name="project",
    )(
        *(
            pltpu.with_memory_space_constraint(x, pltpu.HBM)
            for x in (
                tenant, tenant_page_table, request_block_count, placement,
                hidden, key_value_weight, adapter_down_weight, up_by_page,
            )
        )
    )
    arrived = lax.all_to_all(outgoing, "tensor", split_axis=0, concat_axis=0, tiled=True)

    query = decode_step_query.reshape(steps, dec_rows, HEADS, HD)
    query = query.transpose(0, 2, 1, 3).reshape(steps * HEADS * dec_rows, HD)
    steps_kv = step_key_value.reshape(steps, dec_rows, heads2, HD)
    steps_kv = steps_kv.transpose(0, 2, 1, 3).reshape(steps * heads2 * dec_rows, HD)
    q_rows = steps * HEADS * dec_rows
    state = jax.ShapeDtypeStruct((HD, q_rows), jnp.float32)
    line = jax.ShapeDtypeStruct((8, q_rows), jnp.float32)
    handed = pl.pallas_call(
        cached_kernel,
        out_shape=(
            jax.ShapeDtypeStruct((HD, q_rows), jnp.bfloat16),
            state,
            line,
            line,
            jax.ShapeDtypeStruct((KVH * CAPT, q_rows), jnp.float32),
        ),
        in_specs=[SMEM_SPEC] * 4 + [VMEM_SPEC] * 3,
        out_specs=(VMEM_SPEC,) * 5,
        scratch_shapes=[pltpu.VMEM((q_rows, HD), jnp.float32)] * 3,
        compiler_params=pltpu.CompilerParams(vmem_limit_bytes=ATTEND_VMEM),
        name="cached",
    )(
        context_length, request_block_count, last_block_tokens, placement,
        key_value_cache, query, steps_kv,
    )
    attended = pl.pallas_call(
        functools.partial(merge_kernel, features),
        out_shape=jax.ShapeDtypeStruct((q_rows, HD), jnp.bfloat16),
        in_specs=[VMEM_SPEC] * 6,
        out_specs=ANY_SPEC,
        scratch_shapes=[
            pltpu.VMEM((q_rows, HD), jnp.bfloat16),
            pltpu.SemaphoreType.DMA((steps,)),
        ],
        compiler_params=pltpu.CompilerParams(vmem_limit_bytes=ATTEND_VMEM),
        name="merge",
    )(arrived, *handed)
    attended = attended.reshape(steps, HEADS, dec_rows, HD).transpose(0, 2, 1, 3)
    return attended.reshape(steps, dec_rows, HEADS * HD)


def solution(mesh):
    return jax.shard_map(
        body,
        mesh=mesh,
        in_specs=(
            P("parts", None),
            P("tensor", None),
            P("tensor", None, None),
            P("tensor", None, None),
            P("parts"),
            P(),
            P("parts"),
            P("parts"),
            P("parts"),
            P(("parts", "tensor"), None, None),
            P(("parts", "tensor")),
            P(None, ("parts", "tensor"), None),
            P(None, ("parts", "tensor"), None),
        ),
        out_specs=P(None, ("parts", "tensor"), None),
        check_vma=False,
    )
```

```python
import functools

import jax
import jax.numpy as jnp
from jax import lax
from jax.experimental import pallas as pl
from jax.experimental.pallas import tpu as pltpu
from jax.sharding import PartitionSpec as P

HEADS = 64
KVH = 8
HD = 128
BLK = 8
MOSTB = 2
CAPT = MOSTB * BLK
ADAPTER_SCALE = 0.5
NEG_LARGE = -1e30
PROJECT_VMEM = 32 * 1024 * 1024
ATTEND_VMEM = 16 * 1024 * 1024
WIRE = jnp.bfloat16

SMEM_SPEC = pl.BlockSpec(memory_space=pltpu.SMEM)
VMEM_SPEC = pl.BlockSpec(memory_space=pltpu.VMEM)
ANY_SPEC = pl.BlockSpec(memory_space=pl.ANY)


def div(x, n):
    shift = n.bit_length() - 1
    return lax.shift_right_logical(x, shift) if n == 1 << shift else x // n


def mod(x, n):
    return x & (n - 1) if n & (n - 1) == 0 else x % n


def project_kernel(
    dec_rows, d_chunks, chunks, devices, tenant_h, table_h, counts_h, placement_h, hidden, weight, down, up, out,
    tenant, table, counts, placement,
    h_s, w_s, d_s, mine_s, u_s, sel_s, part_s, base_s, dest_table, sems, d_sems, int_sems,
):
    tokens, width = hidden.shape
    features = weight.shape[0]
    local, pages, rank2 = down.shape
    tenants = table.shape[0]
    requests = tenant.shape[0]
    me = lax.axis_index("tensor")
    d_step = local // d_chunks
    wide = min(4, d_step // 16)
    step = width // chunks

    int_copies = [
        pltpu.make_async_copy(src, dst, int_sems.at[i])
        for i, (src, dst) in enumerate(
            ((table_h, table), (tenant_h, tenant), (counts_h, counts), (placement_h, placement))
        )
    ]
    for copy in int_copies:
        copy.start()
    d_copies = [
        pltpu.make_async_copy(
            down.at[pl.ds(c * d_step, d_step)], d_s.at[pl.ds(c * d_step, d_step)], d_sems.at[c])
        for c in range(d_chunks)
    ]
    h_copies = [
        pltpu.make_async_copy(hidden.at[:, pl.ds(c * step, step)], h_s.at[c], sems.at[c, 0])
        for c in range(chunks)
    ]
    w_copies = [
        pltpu.make_async_copy(weight.at[:, pl.ds(c * step, step)], w_s.at[c], sems.at[c, 1])
        for c in range(chunks)
    ]
    my_copy = pltpu.make_async_copy(
        hidden.at[:, pl.ds(pl.multiple_of(me * local, 128), local)], mine_s, d_sems.at[d_chunks]
    )
    up_copy = pltpu.make_async_copy(up, u_s, d_sems.at[d_chunks + 1])
    for copy in d_copies + [my_copy, up_copy]:
        copy.start()
    for c in range(chunks):
        h_copies[c].start()
        w_copies[c].start()

    int_copies[0].wait()
    rows = lax.broadcasted_iota(jnp.int32, (tenants * 16, 16 * pages), 0)
    cols = lax.broadcasted_iota(jnp.int32, (tenants * 16, 16 * pages), 1)
    page_of_row = jnp.zeros_like(rows)
    for k in range(tenants):
        page_of_row = jnp.where(div(rows, 16) == k, table[k], page_of_row)
    pick = (mod(rows, 16) == div(cols, pages)) & (mod(cols, pages) == page_of_row)
    pick = jnp.where(pick, jnp.float32(1), jnp.float32(0)).astype(jnp.bfloat16)

    for c in range(d_chunks):
        d_copies[c].wait()
        for b in range(c * d_step // 16, (c + 1) * d_step // 16, wide):
            block = jnp.concatenate(
                [
                    d_s[pl.ds((b + i) * 16, 16)].reshape(16 * pages, rank2)
                    for i in range(wide)
                ],
                axis=1,
            )
            chosen = jnp.dot(pick, block, preferred_element_type=jnp.float32)
            for i in range(wide):
                sel_s[b + i] = chosen[:, i * rank2 : (i + 1) * rank2].astype(jnp.bfloat16)
    for copy in int_copies[1:]:
        copy.wait()
    for dest in range(devices):
        dest_table[0, dest] = 0
        dest_table[1, dest] = 0
    first = jnp.int32(0)
    for r in range(requests):
        dest = div(placement[r], dec_rows)
        dest_table[0, dest] = first * BLK
        dest_table[1, dest] = tenant[r]
        first = first + counts[r]
    my_copy.wait()
    mine = mine_s[...]
    for k in range(0, tenants, 4):
        pair = min(4, tenants - k)
        maps = jnp.concatenate(
            [sel_s[:, j * 16 : (j + 1) * 16, :].reshape(local, rank2) for j in range(k, k + pair)],
            axis=1,
        )
        product = jnp.dot(mine, maps, preferred_element_type=jnp.float32)
        for j in range(pair):
            part_s[k + j, :tokens] = product[:, j * rank2 : (j + 1) * rank2]
            part_s[k + j, tokens:] = jnp.zeros((BLK, rank2), jnp.float32)

    total = jnp.zeros((tokens, features), jnp.float32)
    for c in range(chunks):
        h_copies[c].wait()
        w_copies[c].wait()
        total = total + lax.dot_general(h_s[c], w_s[c], NT, preferred_element_type=jnp.float32)
    base_s[tokens:] = jnp.zeros((BLK, HD), jnp.float32)
    if features < HD:
        base_s[...] = jnp.zeros_like(base_s)
    base_s[:tokens, :features] = total
    up_copy.wait()
    for dest in range(devices):
        start = pl.multiple_of(dest_table[0, dest], BLK)
        who = dest_table[1, dest]
        out[dest, :CAPT, :] = part_s[who, pl.ds(start, CAPT), :].astype(out.dtype)
        out[dest, CAPT : 2 * CAPT, :] = base_s[pl.ds(start, CAPT), :].astype(out.dtype)
        if features < HD:
            out[dest, 2 * CAPT :, :] = jnp.zeros((out.shape[1] - 2 * CAPT, HD), out.dtype)
        out[dest, 2 * CAPT :, :features] = u_s[table[who]]


NT = (((1,), (1,)), ((), ()))


def gather_queries(query, k, group, steps, stride):
    return jnp.concatenate(
        [query[pl.ds(s * stride + k * group, group), :] for s in range(steps)], axis=0
    )


def cached_kernel(
    lengths, counts, last, placement, cache, query, steps_kv,
    query_t, acc_t, top_t, total_t, fresh_ok, acc, top_out, total_out,
):
    dec_rows, ctx, kv_width = cache.shape
    half_width = kv_width // 2
    step_rows = KVH * dec_rows
    steps = steps_kv.shape[0] // (2 * step_rows)
    group = HEADS // KVH * dec_rows
    q_rows = steps * group
    stride = HEADS * dec_rows

    row = lax.broadcasted_iota(jnp.int32, (q_rows, ctx), 0)
    col = lax.broadcasted_iota(jnp.int32, (q_rows, ctx), 1)
    row_slot = mod(row, dec_rows)
    cache_ok = [(row_slot == g) & (col < lengths[g]) for g in range(dec_rows)]
    row = lax.broadcasted_iota(jnp.int32, (q_rows, steps * step_rows), 0)
    col = lax.broadcasted_iota(jnp.int32, (q_rows, steps * step_rows), 1)
    step_ok = (mod(row, dec_rows) == mod(col, dec_rows)) & (div(col, step_rows) <= div(row, group))
    step_head = div(mod(col, step_rows), dec_rows)
    step_keys, step_values = (
        jnp.concatenate(
            [steps_kv[pl.ds((2 * s + half) * step_rows, step_rows), :] for s in range(steps)], axis=0
        )
        for half in range(2)
    )

    scale = HD ** (-0.5)
    for k in range(KVH):
        lanes = pl.ds(k * HD, HD)
        vlanes = pl.ds(half_width + k * HD, HD)
        q = gather_queries(query, k, group, steps, stride)
        keys = [cache[g, :, lanes] for g in range(dec_rows)] + [step_keys]
        values = [cache[g, :, vlanes] for g in range(dec_rows)] + [step_values]
        scores = [
            jnp.where(
                ok,
                lax.dot_general(q, key, NT, preferred_element_type=jnp.float32) * scale,
                NEG_LARGE,
            )
            for ok, key in zip(cache_ok + [step_ok & (step_head == k)], keys)
        ]
        top = functools.reduce(jnp.maximum, [jnp.max(s, axis=1, keepdims=True) for s in scores])
        weights = [jnp.exp(s - top) for s in scores]
        total = sum(jnp.sum(w, axis=1, keepdims=True) for w in weights)
        mixed = sum(
            jnp.dot(w.astype(jnp.bfloat16), v, preferred_element_type=jnp.float32)
            for w, v in zip(weights, values)
        )
        for s in range(steps):
            here = pl.ds(s * stride + k * group, group)
            part = slice(s * group, (s + 1) * group)
            acc[here, :] = mixed[part]
            top_out[here, :] = jnp.broadcast_to(top[part], (group, HD))
            total_out[here, :] = jnp.broadcast_to(total[part], (group, HD))

    my_slot = jnp.int32(-1)
    my_length = jnp.int32(0)
    for r in range(placement.shape[0]):
        hit = div(placement[r], dec_rows) == lax.axis_index("tensor")
        my_slot = jnp.where(hit, mod(placement[r], dec_rows), my_slot)
        my_length = jnp.where(hit, (counts[r] - 1) * BLK + last[r], my_length)
    col = lax.broadcasted_iota(jnp.int32, fresh_ok.shape, 0)
    row = lax.broadcasted_iota(jnp.int32, fresh_ok.shape, 1)
    ok = (
        (mod(div(row, group), KVH) == div(col, CAPT))
        & (mod(row, dec_rows) == my_slot)
        & (mod(col, CAPT) < my_length)
    )
    fresh_ok[...] = jnp.where(ok, jnp.float32(1), jnp.float32(0))
    query_t[...] = query[...].T
    acc_t[...] = acc[...].T
    top_t[...] = top_out[...].T[: top_t.shape[0]]
    total_t[...] = total_out[...].T[: total_t.shape[0]]


def merge_kernel(features, box, query_t, acc_t, top_t, total_t, fresh_ok, out, result, sems):
    devices = box.shape[0]
    rank = box.shape[1] - 2 * CAPT
    terms = [box[i, :CAPT].astype(jnp.float32) for i in range(devices)]
    while len(terms) > 1:
        pairs = [a + b for a, b in zip(terms[::2], terms[1::2])]
        terms = pairs + terms[2 * len(pairs) :]
    shrunk = terms[0].astype(jnp.bfloat16)
    halves = (shrunk[:, :rank], shrunk[:, rank:])
    pieces = HD // features

    def rows(i, first, count):
        parts = [box[i * pieces + p, first : first + count, :features] for p in range(pieces)]
        return parts[0] if pieces == 1 else jnp.concatenate(parts, axis=1)

    def fresh(first):
        made = []
        for i in range(first, first + KVH, 4):
            ups = jnp.concatenate([rows(i + j, 2 * CAPT, rank) for j in range(4)], axis=1)
            delta = jnp.dot(halves[first // KVH], ups, preferred_element_type=jnp.float32)
            for j in range(4):
                base = rows(i + j, CAPT, CAPT).astype(jnp.float32)
                both = base + ADAPTER_SCALE * delta[:, j * HD : (j + 1) * HD]
                made.append(both.astype(jnp.bfloat16))
        return jnp.concatenate(made, axis=0)

    keys = fresh(0)
    values_t = fresh(KVH).T
    scale = HD ** (-0.5)
    part = out.shape[0] // sems.shape[0]
    copies = []
    for c in range(sems.shape[0]):
        here = pl.ds(c * part, part)
        s = jnp.dot(keys, query_t[:, here], preferred_element_type=jnp.float32)
        s = jnp.where(fresh_ok[:, here] > 0, s * scale, NEG_LARGE)
        old = top_t[:1, here]
        top = jnp.maximum(old, jnp.max(s, axis=0, keepdims=True))
        fade = jnp.exp(old - top)
        w = jnp.exp(s - top)
        total = total_t[:1, here] * fade + jnp.sum(w, axis=0, keepdims=True)
        mixed = acc_t[:, here] * fade + jnp.dot(
            values_t, w.astype(jnp.bfloat16), preferred_element_type=jnp.float32
        )
        result[here, :] = (mixed / total).T.astype(jnp.bfloat16)
        copies.append(pltpu.make_async_copy(result.at[here, :], out.at[here, :], sems.at[c]))
        copies[c].start()
    for copy in copies:
        copy.wait()


def body(
    hidden,
    key_value_weight,
    adapter_down_weight,
    adapter_up_weight,
    tenant,
    tenant_page_table,
    request_block_count,
    last_block_tokens,
    placement,
    key_value_cache,
    context_length,
    decode_step_query,
    step_key_value,
):
    devices = lax.axis_size("tensor")
    tokens, width = hidden.shape
    features = key_value_weight.shape[0]
    local, pages, rank2 = adapter_down_weight.shape
    rank = adapter_up_weight.shape[2]
    tenants = tenant_page_table.shape[0]
    dec_rows, ctx, kv_width = key_value_cache.shape
    steps = step_key_value.shape[0]
    heads2 = kv_width // HD
    d_chunks, chunks = 4, 2
    up_by_page = jnp.transpose(adapter_up_weight, (1, 2, 0))
    rows = 2 * CAPT + rank
    outgoing = pl.pallas_call(
        functools.partial(project_kernel, dec_rows, d_chunks, chunks, devices),
        out_shape=pltpu.VMEM((devices, rows, HD), WIRE),
        in_specs=[ANY_SPEC] * 8,
        out_specs=VMEM_SPEC,
        scratch_shapes=[
            pltpu.SMEM(tenant.shape, jnp.int32),
            pltpu.SMEM(tenant_page_table.shape, jnp.int32),
            pltpu.SMEM(request_block_count.shape, jnp.int32),
            pltpu.SMEM(placement.shape, jnp.int32),
            pltpu.VMEM((chunks, tokens, width // chunks), jnp.bfloat16),
            pltpu.VMEM((chunks, features, width // chunks), jnp.bfloat16),
            pltpu.VMEM((local, pages, rank2), jnp.bfloat16),
            pltpu.VMEM((tokens, local), jnp.bfloat16),
            pltpu.VMEM((pages, rank, features), jnp.bfloat16),
            pltpu.VMEM((local // 16, tenants * 16, rank2), jnp.bfloat16),
            pltpu.VMEM((tenants, tokens + BLK, rank2), jnp.float32),
            pltpu.VMEM((tokens + BLK, HD), jnp.float32),
            pltpu.SMEM((2, devices), jnp.int32),
            pltpu.SemaphoreType.DMA((chunks, 2)),
            pltpu.SemaphoreType.DMA((d_chunks + 2,)),
            pltpu.SemaphoreType.DMA((4,)),
        ],
        compiler_params=pltpu.CompilerParams(vmem_limit_bytes=PROJECT_VMEM),
        name="project",
    )(
        *(
            pltpu.with_memory_space_constraint(x, pltpu.HBM)
            for x in (
                tenant, tenant_page_table, request_block_count, placement,
                hidden, key_value_weight, adapter_down_weight, up_by_page,
            )
        )
    )
    arrived = lax.all_to_all(outgoing, "tensor", split_axis=0, concat_axis=0, tiled=True)

    query = decode_step_query.reshape(steps, dec_rows, HEADS, HD)
    query = query.transpose(0, 2, 1, 3).reshape(steps * HEADS * dec_rows, HD)
    steps_kv = step_key_value.reshape(steps, dec_rows, heads2, HD)
    steps_kv = steps_kv.transpose(0, 2, 1, 3).reshape(steps * heads2 * dec_rows, HD)
    q_rows = steps * HEADS * dec_rows
    state = jax.ShapeDtypeStruct((HD, q_rows), jnp.float32)
    line = jax.ShapeDtypeStruct((8, q_rows), jnp.float32)
    handed = pl.pallas_call(
        cached_kernel,
        out_shape=(
            jax.ShapeDtypeStruct((HD, q_rows), jnp.bfloat16),
            state,
            line,
            line,
            jax.ShapeDtypeStruct((KVH * CAPT, q_rows), jnp.float32),
        ),
        in_specs=[SMEM_SPEC] * 4 + [VMEM_SPEC] * 3,
        out_specs=(VMEM_SPEC,) * 5,
        scratch_shapes=[pltpu.VMEM((q_rows, HD), jnp.float32)] * 3,
        compiler_params=pltpu.CompilerParams(vmem_limit_bytes=ATTEND_VMEM),
        name="cached",
    )(
        context_length, request_block_count, last_block_tokens, placement,
        key_value_cache, query, steps_kv,
    )
    attended = pl.pallas_call(
        functools.partial(merge_kernel, features),
        out_shape=jax.ShapeDtypeStruct((q_rows, HD), jnp.bfloat16),
        in_specs=[VMEM_SPEC] * 6,
        out_specs=ANY_SPEC,
        scratch_shapes=[
            pltpu.VMEM((q_rows, HD), jnp.bfloat16),
            pltpu.SemaphoreType.DMA((2,)),
        ],
        compiler_params=pltpu.CompilerParams(vmem_limit_bytes=ATTEND_VMEM),
        name="merge",
    )(arrived, *handed)
    attended = attended.reshape(steps, HEADS, dec_rows, HD).transpose(0, 2, 1, 3)
    return attended.reshape(steps, dec_rows, HEADS * HD)


def solution(mesh):
    return jax.shard_map(
        body,
        mesh=mesh,
        in_specs=(
            P("parts", None),
            P("tensor", None),
            P("tensor", None, None),
            P("tensor", None, None),
            P("parts"),
            P(),
            P("parts"),
            P("parts"),
            P("parts"),
            P(("parts", "tensor"), None, None),
            P(("parts", "tensor")),
            P(None, ("parts", "tensor"), None),
            P(None, ("parts", "tensor"), None),
        ),
        out_specs=P(None, ("parts", "tensor"), None),
        check_vma=False,
    )
```

```python
import functools

import jax
import jax.numpy as jnp
from jax import lax
from jax.experimental import pallas as pl
from jax.experimental.pallas import tpu as pltpu
from jax.sharding import PartitionSpec as P

HEADS = 64
KVH = 8
HD = 128
BLK = 8
MOSTB = 2
CAPT = MOSTB * BLK
ADAPTER_SCALE = 0.5
NEG_LARGE = -1e30
PROJECT_VMEM = 32 * 1024 * 1024
ATTEND_VMEM = 16 * 1024 * 1024
WIRE = jnp.bfloat16

SMEM_SPEC = pl.BlockSpec(memory_space=pltpu.SMEM)
VMEM_SPEC = pl.BlockSpec(memory_space=pltpu.VMEM)
ANY_SPEC = pl.BlockSpec(memory_space=pl.ANY)


def div(x, n):
    shift = n.bit_length() - 1
    return lax.shift_right_logical(x, shift) if n == 1 << shift else x // n


def mod(x, n):
    return x & (n - 1) if n & (n - 1) == 0 else x % n


def project_kernel(
    dec_rows, d_chunks, chunks, devices, tenant_h, table_h, counts_h, placement_h, hidden, weight, down, up, out,
    tenant, table, counts, placement,
    h_s, w_s, d_s, mine_s, u_s, sel_s, part_s, base_s, dest_table, sems, d_sems, int_sems,
):
    tokens, width = hidden.shape
    features = weight.shape[0]
    local, pages, rank2 = down.shape
    tenants = table.shape[0]
    requests = tenant.shape[0]
    me = lax.axis_index("tensor")
    d_step = local // d_chunks
    step = width // chunks

    int_copies = [
        pltpu.make_async_copy(src, dst, int_sems.at[i])
        for i, (src, dst) in enumerate(
            ((table_h, table), (tenant_h, tenant), (counts_h, counts), (placement_h, placement))
        )
    ]
    for copy in int_copies:
        copy.start()
    d_copies = [
        pltpu.make_async_copy(
            down.at[pl.ds(c * d_step, d_step)], d_s.at[pl.ds(c * d_step, d_step)], d_sems.at[c])
        for c in range(d_chunks)
    ]
    h_copies = [
        pltpu.make_async_copy(hidden.at[:, pl.ds(c * step, step)], h_s.at[c], sems.at[c, 0])
        for c in range(chunks)
    ]
    w_copies = [
        pltpu.make_async_copy(weight.at[:, pl.ds(c * step, step)], w_s.at[c], sems.at[c, 1])
        for c in range(chunks)
    ]
    my_copy = pltpu.make_async_copy(
        hidden.at[:, pl.ds(pl.multiple_of(me * local, 128), local)], mine_s, d_sems.at[d_chunks]
    )
    up_copy = pltpu.make_async_copy(up, u_s, d_sems.at[d_chunks + 1])
    for copy in d_copies + [my_copy, up_copy]:
        copy.start()
    for c in range(chunks):
        h_copies[c].start()
        w_copies[c].start()

    int_copies[0].wait()
    rows = lax.broadcasted_iota(jnp.int32, (tenants * 16, 16 * pages), 0)
    cols = lax.broadcasted_iota(jnp.int32, (tenants * 16, 16 * pages), 1)
    page_of_row = jnp.zeros_like(rows)
    for k in range(tenants):
        page_of_row = jnp.where(div(rows, 16) == k, table[k], page_of_row)
    pick = (mod(rows, 16) == div(cols, pages)) & (mod(cols, pages) == page_of_row)
    pick = jnp.where(pick, jnp.float32(1), jnp.float32(0)).astype(jnp.bfloat16)

    for c in range(d_chunks):
        d_copies[c].wait()
        for b in range(c * d_step // 16, (c + 1) * d_step // 16, 2):
            block = jnp.concatenate(
                [d_s[pl.ds((b + i) * 16, 16)].reshape(16 * pages, rank2) for i in range(2)], axis=1
            )
            chosen = jnp.dot(pick, block, preferred_element_type=jnp.float32)
            for i in range(2):
                sel_s[b + i] = chosen[:, i * rank2 : (i + 1) * rank2].astype(jnp.bfloat16)
    for copy in int_copies[1:]:
        copy.wait()
    for dest in range(devices):
        dest_table[0, dest] = 0
        dest_table[1, dest] = 0
    first = jnp.int32(0)
    for r in range(requests):
        dest = div(placement[r], dec_rows)
        dest_table[0, dest] = first * BLK
        dest_table[1, dest] = tenant[r]
        first = first + counts[r]
    my_copy.wait()
    h_copies[0].wait()
    w_copies[0].wait()
    mine = mine_s[...]
    for k in range(0, tenants, 2):
        pair = min(2, tenants - k)
        maps = jnp.concatenate(
            [sel_s[:, j * 16 : (j + 1) * 16, :].reshape(local, rank2) for j in range(k, k + pair)],
            axis=1,
        )
        product = jnp.dot(mine, maps, preferred_element_type=jnp.float32)
        for j in range(pair):
            part_s[k + j, :tokens] = product[:, j * rank2 : (j + 1) * rank2]
            part_s[k + j, tokens:] = jnp.zeros((BLK, rank2), jnp.float32)

    total = jnp.zeros((tokens, features), jnp.float32)
    for c in range(chunks):
        if c > 0:
            h_copies[c].wait()
            w_copies[c].wait()
        total = total + lax.dot_general(h_s[c], w_s[c], NT, preferred_element_type=jnp.float32)
    base_s[tokens:] = jnp.zeros((BLK, HD), jnp.float32)
    if features < HD:
        base_s[...] = jnp.zeros_like(base_s)
    base_s[:tokens, :features] = total
    up_copy.wait()
    for dest in range(devices):
        start = pl.multiple_of(dest_table[0, dest], BLK)
        who = dest_table[1, dest]
        out[dest, :CAPT, :] = part_s[who, pl.ds(start, CAPT), :].astype(out.dtype)
        out[dest, CAPT : 2 * CAPT, :] = base_s[pl.ds(start, CAPT), :].astype(out.dtype)
        if features < HD:
            out[dest, 2 * CAPT :, :] = jnp.zeros((out.shape[1] - 2 * CAPT, HD), out.dtype)
        out[dest, 2 * CAPT :, :features] = u_s[table[who]]


NT = (((1,), (1,)), ((), ()))


def gather_queries(query, k, group, steps, stride):
    return jnp.concatenate(
        [query[pl.ds(s * stride + k * group, group), :] for s in range(steps)], axis=0
    )


def cached_kernel(
    lengths, counts, last, placement, cache, query, steps_kv,
    query_t, acc_t, top_t, total_t, fresh_ok, acc, top_out, total_out,
):
    dec_rows, ctx, kv_width = cache.shape
    half_width = kv_width // 2
    step_rows = KVH * dec_rows
    steps = steps_kv.shape[0] // (2 * step_rows)
    group = HEADS // KVH * dec_rows
    q_rows = steps * group
    stride = HEADS * dec_rows

    row = lax.broadcasted_iota(jnp.int32, (q_rows, ctx), 0)
    col = lax.broadcasted_iota(jnp.int32, (q_rows, ctx), 1)
    row_slot = mod(row, dec_rows)
    cache_ok = [(row_slot == g) & (col < lengths[g]) for g in range(dec_rows)]
    row = lax.broadcasted_iota(jnp.int32, (q_rows, steps * step_rows), 0)
    col = lax.broadcasted_iota(jnp.int32, (q_rows, steps * step_rows), 1)
    step_ok = (mod(row, dec_rows) == mod(col, dec_rows)) & (div(col, step_rows) <= div(row, group))
    step_head = div(mod(col, step_rows), dec_rows)
    step_keys, step_values = (
        jnp.concatenate(
            [steps_kv[pl.ds((2 * s + half) * step_rows, step_rows), :] for s in range(steps)], axis=0
        )
        for half in range(2)
    )

    scale = HD ** (-0.5)
    for k in range(KVH):
        lanes = pl.ds(k * HD, HD)
        vlanes = pl.ds(half_width + k * HD, HD)
        q = gather_queries(query, k, group, steps, stride)
        keys = [cache[g, :, lanes] for g in range(dec_rows)] + [step_keys]
        values = [cache[g, :, vlanes] for g in range(dec_rows)] + [step_values]
        scores = [
            jnp.where(
                ok,
                lax.dot_general(q, key, NT, preferred_element_type=jnp.float32) * scale,
                NEG_LARGE,
            )
            for ok, key in zip(cache_ok + [step_ok & (step_head == k)], keys)
        ]
        top = functools.reduce(jnp.maximum, [jnp.max(s, axis=1, keepdims=True) for s in scores])
        weights = [jnp.exp(s - top) for s in scores]
        total = sum(jnp.sum(w, axis=1, keepdims=True) for w in weights)
        mixed = sum(
            jnp.dot(w.astype(jnp.bfloat16), v, preferred_element_type=jnp.float32)
            for w, v in zip(weights, values)
        )
        for s in range(steps):
            here = pl.ds(s * stride + k * group, group)
            part = slice(s * group, (s + 1) * group)
            acc[here, :] = mixed[part]
            top_out[here, :] = jnp.broadcast_to(top[part], (group, HD))
            total_out[here, :] = jnp.broadcast_to(total[part], (group, HD))

    my_slot = jnp.int32(-1)
    my_length = jnp.int32(0)
    for r in range(placement.shape[0]):
        hit = div(placement[r], dec_rows) == lax.axis_index("tensor")
        my_slot = jnp.where(hit, mod(placement[r], dec_rows), my_slot)
        my_length = jnp.where(hit, (counts[r] - 1) * BLK + last[r], my_length)
    col = lax.broadcasted_iota(jnp.int32, fresh_ok.shape, 0)
    row = lax.broadcasted_iota(jnp.int32, fresh_ok.shape, 1)
    ok = (
        (mod(div(row, group), KVH) == div(col, CAPT))
        & (mod(row, dec_rows) == my_slot)
        & (mod(col, CAPT) < my_length)
    )
    fresh_ok[...] = jnp.where(ok, jnp.float32(1), jnp.float32(0))
    query_t[...] = query[...].T
    acc_t[...] = acc[...].T
    top_t[...] = top_out[...].T[: top_t.shape[0]]
    total_t[...] = total_out[...].T[: total_t.shape[0]]


def merge_kernel(features, box, query_t, acc_t, top_t, total_t, fresh_ok, out, result, sems):
    devices = box.shape[0]
    rank = box.shape[1] - 2 * CAPT
    terms = [box[i, :CAPT].astype(jnp.float32) for i in range(devices)]
    while len(terms) > 1:
        pairs = [a + b for a, b in zip(terms[::2], terms[1::2])]
        terms = pairs + terms[2 * len(pairs) :]
    shrunk = terms[0].astype(jnp.bfloat16)
    halves = (shrunk[:, :rank], shrunk[:, rank:])
    pieces = HD // features

    def rows(i, first, count):
        parts = [box[i * pieces + p, first : first + count, :features] for p in range(pieces)]
        return parts[0] if pieces == 1 else jnp.concatenate(parts, axis=1)

    def fresh(first):
        made = []
        for i in range(first, first + KVH, 2):
            ups = jnp.concatenate([rows(i + j, 2 * CAPT, rank) for j in range(2)], axis=1)
            delta = jnp.dot(halves[first // KVH], ups, preferred_element_type=jnp.float32)
            for j in range(2):
                base = rows(i + j, CAPT, CAPT).astype(jnp.float32)
                both = base + ADAPTER_SCALE * delta[:, j * HD : (j + 1) * HD]
                made.append(both.astype(jnp.bfloat16))
        return jnp.concatenate(made, axis=0)

    keys = fresh(0)
    values_t = fresh(KVH).T
    scale = HD ** (-0.5)
    part = out.shape[0] // sems.shape[0]
    copies = []
    for c in range(sems.shape[0]):
        here = pl.ds(c * part, part)
        s = jnp.dot(keys, query_t[:, here], preferred_element_type=jnp.float32)
        s = jnp.where(fresh_ok[:, here] > 0, s * scale, NEG_LARGE)
        old = top_t[:1, here]
        top = jnp.maximum(old, jnp.max(s, axis=0, keepdims=True))
        fade = jnp.exp(old - top)
        w = jnp.exp(s - top)
        total = total_t[:1, here] * fade + jnp.sum(w, axis=0, keepdims=True)
        mixed = acc_t[:, here] * fade + jnp.dot(
            values_t, w.astype(jnp.bfloat16), preferred_element_type=jnp.float32
        )
        result[here, :] = (mixed / total).T.astype(jnp.bfloat16)
        copies.append(pltpu.make_async_copy(result.at[here, :], out.at[here, :], sems.at[c]))
        copies[c].start()
    for copy in copies:
        copy.wait()


def body(
    hidden,
    key_value_weight,
    adapter_down_weight,
    adapter_up_weight,
    tenant,
    tenant_page_table,
    request_block_count,
    last_block_tokens,
    placement,
    key_value_cache,
    context_length,
    decode_step_query,
    step_key_value,
):
    devices = lax.axis_size("tensor")
    tokens, width = hidden.shape
    features = key_value_weight.shape[0]
    local, pages, rank2 = adapter_down_weight.shape
    rank = adapter_up_weight.shape[2]
    tenants = tenant_page_table.shape[0]
    dec_rows, ctx, kv_width = key_value_cache.shape
    steps = step_key_value.shape[0]
    heads2 = kv_width // HD
    d_chunks, chunks = 4, 2
    up_by_page = jnp.transpose(adapter_up_weight, (1, 2, 0))
    rows = 2 * CAPT + rank
    outgoing = pl.pallas_call(
        functools.partial(project_kernel, dec_rows, d_chunks, chunks, devices),
        out_shape=pltpu.VMEM((devices, rows, HD), WIRE),
        in_specs=[ANY_SPEC] * 8,
        out_specs=VMEM_SPEC,
        scratch_shapes=[
            pltpu.SMEM(tenant.shape, jnp.int32),
            pltpu.SMEM(tenant_page_table.shape, jnp.int32),
            pltpu.SMEM(request_block_count.shape, jnp.int32),
            pltpu.SMEM(placement.shape, jnp.int32),
            pltpu.VMEM((chunks, tokens, width // chunks), jnp.bfloat16),
            pltpu.VMEM((chunks, features, width // chunks), jnp.bfloat16),
            pltpu.VMEM((local, pages, rank2), jnp.bfloat16),
            pltpu.VMEM((tokens, local), jnp.bfloat16),
            pltpu.VMEM((pages, rank, features), jnp.bfloat16),
            pltpu.VMEM((local // 16, tenants * 16, rank2), jnp.bfloat16),
            pltpu.VMEM((tenants, tokens + BLK, rank2), jnp.float32),
            pltpu.VMEM((tokens + BLK, HD), jnp.float32),
            pltpu.SMEM((2, devices), jnp.int32),
            pltpu.SemaphoreType.DMA((chunks, 2)),
            pltpu.SemaphoreType.DMA((d_chunks + 2,)),
            pltpu.SemaphoreType.DMA((4,)),
        ],
        compiler_params=pltpu.CompilerParams(vmem_limit_bytes=PROJECT_VMEM),
        name="project",
    )(
        *(
            pltpu.with_memory_space_constraint(x, pltpu.HBM)
            for x in (
                tenant, tenant_page_table, request_block_count, placement,
                hidden, key_value_weight, adapter_down_weight, up_by_page,
            )
        )
    )
    arrived = lax.all_to_all(outgoing, "tensor", split_axis=0, concat_axis=0, tiled=True)

    query = decode_step_query.reshape(steps, dec_rows, HEADS, HD)
    query = query.transpose(0, 2, 1, 3).reshape(steps * HEADS * dec_rows, HD)
    steps_kv = step_key_value.reshape(steps, dec_rows, heads2, HD)
    steps_kv = steps_kv.transpose(0, 2, 1, 3).reshape(steps * heads2 * dec_rows, HD)
    q_rows = steps * HEADS * dec_rows
    state = jax.ShapeDtypeStruct((HD, q_rows), jnp.float32)
    line = jax.ShapeDtypeStruct((8, q_rows), jnp.float32)
    handed = pl.pallas_call(
        cached_kernel,
        out_shape=(
            jax.ShapeDtypeStruct((HD, q_rows), jnp.bfloat16),
            state,
            line,
            line,
            jax.ShapeDtypeStruct((KVH * CAPT, q_rows), jnp.float32),
        ),
        in_specs=[SMEM_SPEC] * 4 + [VMEM_SPEC] * 3,
        out_specs=(VMEM_SPEC,) * 5,
        scratch_shapes=[pltpu.VMEM((q_rows, HD), jnp.float32)] * 3,
        compiler_params=pltpu.CompilerParams(vmem_limit_bytes=ATTEND_VMEM),
        name="cached",
    )(
        context_length, request_block_count, last_block_tokens, placement,
        key_value_cache, query, steps_kv,
    )
    attended = pl.pallas_call(
        functools.partial(merge_kernel, features),
        out_shape=jax.ShapeDtypeStruct((q_rows, HD), jnp.bfloat16),
        in_specs=[VMEM_SPEC] * 6,
        out_specs=ANY_SPEC,
        scratch_shapes=[
            pltpu.VMEM((q_rows, HD), jnp.bfloat16),
            pltpu.SemaphoreType.DMA((steps,)),
        ],
        compiler_params=pltpu.CompilerParams(vmem_limit_bytes=ATTEND_VMEM),
        name="merge",
    )(arrived, *handed)
    attended = attended.reshape(steps, HEADS, dec_rows, HD).transpose(0, 2, 1, 3)
    return attended.reshape(steps, dec_rows, HEADS * HD)


def solution(mesh):
    return jax.shard_map(
        body,
        mesh=mesh,
        in_specs=(
            P("parts", None),
            P("tensor", None),
            P("tensor", None, None),
            P("tensor", None, None),
            P("parts"),
            P(),
            P("parts"),
            P("parts"),
            P("parts"),
            P(("parts", "tensor"), None, None),
            P(("parts", "tensor")),
            P(None, ("parts", "tensor"), None),
            P(None, ("parts", "tensor"), None),
        ),
        out_specs=P(None, ("parts", "tensor"), None),
        check_vma=False,
    )
```

```python
import functools

import jax
import jax.numpy as jnp
from jax import lax
from jax.experimental import pallas as pl
from jax.experimental.pallas import tpu as pltpu
from jax.sharding import PartitionSpec as P

HEADS = 64
KVH = 8
HD = 128
BLK = 8
MOSTB = 2
CAPT = MOSTB * BLK
ADAPTER_SCALE = 0.5
NEG_LARGE = -1e30
PROJECT_VMEM = 32 * 1024 * 1024
ATTEND_VMEM = 16 * 1024 * 1024
WIRE = jnp.bfloat16

SMEM_SPEC = pl.BlockSpec(memory_space=pltpu.SMEM)
VMEM_SPEC = pl.BlockSpec(memory_space=pltpu.VMEM)
ANY_SPEC = pl.BlockSpec(memory_space=pl.ANY)


def div(x, n):
    shift = n.bit_length() - 1
    return lax.shift_right_logical(x, shift) if n == 1 << shift else x // n


def mod(x, n):
    return x & (n - 1) if n & (n - 1) == 0 else x % n


def project_kernel(
    dec_rows, d_chunks, chunks, devices, tenant_h, table_h, counts_h, placement_h, hidden, weight, down, up, out,
    tenant, table, counts, placement,
    h_s, w_s, d_s, mine_s, u_s, sel_s, part_s, base_s, dest_table, sems, d_sems, int_sems,
):
    tokens, width = hidden.shape
    features = weight.shape[0]
    local, pages, rank2 = down.shape
    tenants = table.shape[0]
    requests = tenant.shape[0]
    me = lax.axis_index("tensor")
    d_step = local // d_chunks
    step = width // chunks

    int_copies = [
        pltpu.make_async_copy(src, dst, int_sems.at[i])
        for i, (src, dst) in enumerate(
            ((table_h, table), (tenant_h, tenant), (counts_h, counts), (placement_h, placement))
        )
    ]
    for copy in int_copies:
        copy.start()
    def d_copy(c):
        rows = pl.ds(c * d_step, d_step)
        return pltpu.make_async_copy(down.at[rows], d_s.at[rows], d_sems.at[c])

    h_copies = [
        pltpu.make_async_copy(hidden.at[:, pl.ds(c * step, step)], h_s.at[c], sems.at[c, 0])
        for c in range(chunks)
    ]
    w_copies = [
        pltpu.make_async_copy(weight.at[:, pl.ds(c * step, step)], w_s.at[c], sems.at[c, 1])
        for c in range(chunks)
    ]
    my_copy = pltpu.make_async_copy(
        hidden.at[:, pl.ds(pl.multiple_of(me * local, 128), local)], mine_s, d_sems.at[d_chunks]
    )
    up_copy = pltpu.make_async_copy(up, u_s, d_sems.at[d_chunks + 1])
    for copy in [d_copy(c) for c in range(d_chunks)] + [my_copy, up_copy]:
        copy.start()
    for c in range(chunks):
        h_copies[c].start()
        w_copies[c].start()

    int_copies[0].wait()
    rows = lax.broadcasted_iota(jnp.int32, (tenants * 16, 16 * pages), 0)
    cols = lax.broadcasted_iota(jnp.int32, (tenants * 16, 16 * pages), 1)
    page_of_row = jnp.zeros_like(rows)
    for k in range(tenants):
        page_of_row = jnp.where(div(rows, 16) == k, table[k], page_of_row)
    pick = (mod(rows, 16) == div(cols, pages)) & (mod(cols, pages) == page_of_row)
    pick = jnp.where(pick, jnp.float32(1), jnp.float32(0)).astype(jnp.bfloat16)

    blocks = d_step // 16

    def select(c, carry):
        d_copy(c).wait()
        for b in range(0, blocks, 2):
            block = jnp.concatenate(
                [
                    d_s[pl.ds(c * d_step + (b + i) * 16, 16)].reshape(16 * pages, rank2)
                    for i in range(2)
                ],
                axis=1,
            )
            chosen = jnp.dot(pick, block, preferred_element_type=jnp.float32)
            for i in range(2):
                sel_s[c * blocks + b + i] = chosen[:, i * rank2 : (i + 1) * rank2].astype(
                    jnp.bfloat16
                )
        return carry

    lax.fori_loop(0, d_chunks, select, 0)
    for copy in int_copies[1:]:
        copy.wait()
    for dest in range(devices):
        dest_table[0, dest] = 0
        dest_table[1, dest] = 0
    first = jnp.int32(0)
    for r in range(requests):
        dest = div(placement[r], dec_rows)
        dest_table[0, dest] = first * BLK
        dest_table[1, dest] = tenant[r]
        first = first + counts[r]
    my_copy.wait()
    mine = mine_s[...]
    for k in range(0, tenants, 2):
        pair = min(2, tenants - k)
        maps = jnp.concatenate(
            [sel_s[:, j * 16 : (j + 1) * 16, :].reshape(local, rank2) for j in range(k, k + pair)],
            axis=1,
        )
        product = jnp.dot(mine, maps, preferred_element_type=jnp.float32)
        for j in range(pair):
            part_s[k + j, :tokens] = product[:, j * rank2 : (j + 1) * rank2]
            part_s[k + j, tokens:] = jnp.zeros((BLK, rank2), jnp.float32)

    total = jnp.zeros((tokens, features), jnp.float32)
    for c in range(chunks):
        h_copies[c].wait()
        w_copies[c].wait()
        total = total + lax.dot_general(h_s[c], w_s[c], NT, preferred_element_type=jnp.float32)
    base_s[tokens:] = jnp.zeros((BLK, HD), jnp.float32)
    if features < HD:
        base_s[...] = jnp.zeros_like(base_s)
    base_s[:tokens, :features] = total
    up_copy.wait()

    def lay_out(first, carry):
        for i in range(4):
            dest = first * 4 + i
            start = pl.multiple_of(dest_table[0, dest], BLK)
            who = dest_table[1, dest]
            out[dest, :CAPT, :] = part_s[who, pl.ds(start, CAPT), :].astype(out.dtype)
            out[dest, CAPT : 2 * CAPT, :] = base_s[pl.ds(start, CAPT), :].astype(out.dtype)
            if features < HD:
                out[dest, 2 * CAPT :, :] = jnp.zeros((out.shape[1] - 2 * CAPT, HD), out.dtype)
            out[dest, 2 * CAPT :, :features] = u_s[table[who]]
        return carry

    lax.fori_loop(0, devices // 4, lay_out, 0)


NT = (((1,), (1,)), ((), ()))


def gather_queries(query, k, group, steps, stride):
    return jnp.concatenate(
        [query[pl.ds(s * stride + k * group, group), :] for s in range(steps)], axis=0
    )


def cached_kernel(
    lengths, counts, last, placement, cache, query, steps_kv,
    query_t, acc_t, top_t, total_t, fresh_ok, acc, top_out, total_out,
):
    dec_rows, ctx, kv_width = cache.shape
    half_width = kv_width // 2
    step_rows = KVH * dec_rows
    steps = steps_kv.shape[0] // (2 * step_rows)
    group = HEADS // KVH * dec_rows
    q_rows = steps * group
    stride = HEADS * dec_rows

    row = lax.broadcasted_iota(jnp.int32, (q_rows, ctx), 0)
    col = lax.broadcasted_iota(jnp.int32, (q_rows, ctx), 1)
    row_slot = mod(row, dec_rows)
    cache_ok = [(row_slot == g) & (col < lengths[g]) for g in range(dec_rows)]
    row = lax.broadcasted_iota(jnp.int32, (q_rows, steps * step_rows), 0)
    col = lax.broadcasted_iota(jnp.int32, (q_rows, steps * step_rows), 1)
    step_ok = (mod(row, dec_rows) == mod(col, dec_rows)) & (div(col, step_rows) <= div(row, group))
    step_head = div(mod(col, step_rows), dec_rows)
    step_keys, step_values = (
        jnp.concatenate(
            [steps_kv[pl.ds((2 * s + half) * step_rows, step_rows), :] for s in range(steps)], axis=0
        )
        for half in range(2)
    )

    scale = HD ** (-0.5)
    for k in range(KVH):
        lanes = pl.ds(k * HD, HD)
        vlanes = pl.ds(half_width + k * HD, HD)
        q = gather_queries(query, k, group, steps, stride)
        keys = [cache[g, :, lanes] for g in range(dec_rows)] + [step_keys]
        values = [cache[g, :, vlanes] for g in range(dec_rows)] + [step_values]
        scores = [
            jnp.where(
                ok,
                lax.dot_general(q, key, NT, preferred_element_type=jnp.float32) * scale,
                NEG_LARGE,
            )
            for ok, key in zip(cache_ok + [step_ok & (step_head == k)], keys)
        ]
        top = functools.reduce(jnp.maximum, [jnp.max(s, axis=1, keepdims=True) for s in scores])
        weights = [jnp.exp(s - top) for s in scores]
        total = sum(jnp.sum(w, axis=1, keepdims=True) for w in weights)
        mixed = sum(
            jnp.dot(w.astype(jnp.bfloat16), v, preferred_element_type=jnp.float32)
            for w, v in zip(weights, values)
        )
        for s in range(steps):
            here = pl.ds(s * stride + k * group, group)
            part = slice(s * group, (s + 1) * group)
            acc[here, :] = mixed[part]
            top_out[here, :] = jnp.broadcast_to(top[part], (group, HD))
            total_out[here, :] = jnp.broadcast_to(total[part], (group, HD))

    my_slot = jnp.int32(-1)
    my_length = jnp.int32(0)
    for r in range(placement.shape[0]):
        hit = div(placement[r], dec_rows) == lax.axis_index("tensor")
        my_slot = jnp.where(hit, mod(placement[r], dec_rows), my_slot)
        my_length = jnp.where(hit, (counts[r] - 1) * BLK + last[r], my_length)
    col = lax.broadcasted_iota(jnp.int32, fresh_ok.shape, 0)
    row = lax.broadcasted_iota(jnp.int32, fresh_ok.shape, 1)
    ok = (
        (mod(div(row, group), KVH) == div(col, CAPT))
        & (mod(row, dec_rows) == my_slot)
        & (mod(col, CAPT) < my_length)
    )
    fresh_ok[...] = jnp.where(ok, jnp.float32(1), jnp.float32(0))
    query_t[...] = query[...].T
    acc_t[...] = acc[...].T
    top_t[...] = top_out[...].T[: top_t.shape[0]]
    total_t[...] = total_out[...].T[: total_t.shape[0]]


def merge_kernel(features, box, query_t, acc_t, top_t, total_t, fresh_ok, out, result, sems):
    devices = box.shape[0]
    rank = box.shape[1] - 2 * CAPT
    terms = [box[i, :CAPT].astype(jnp.float32) for i in range(devices)]
    while len(terms) > 1:
        pairs = [a + b for a, b in zip(terms[::2], terms[1::2])]
        terms = pairs + terms[2 * len(pairs) :]
    shrunk = terms[0].astype(jnp.bfloat16)
    halves = (shrunk[:, :rank], shrunk[:, rank:])
    pieces = HD // features

    def rows(i, first, count):
        parts = [box[i * pieces + p, first : first + count, :features] for p in range(pieces)]
        return parts[0] if pieces == 1 else jnp.concatenate(parts, axis=1)

    def fresh(first):
        made = []
        for i in range(first, first + KVH, 2):
            ups = jnp.concatenate([rows(i + j, 2 * CAPT, rank) for j in range(2)], axis=1)
            delta = jnp.dot(halves[first // KVH], ups, preferred_element_type=jnp.float32)
            for j in range(2):
                base = rows(i + j, CAPT, CAPT).astype(jnp.float32)
                both = base + ADAPTER_SCALE * delta[:, j * HD : (j + 1) * HD]
                made.append(both.astype(jnp.bfloat16))
        return jnp.concatenate(made, axis=0)

    keys = fresh(0)
    values_t = fresh(KVH).T
    scale = HD ** (-0.5)
    part = out.shape[0] // sems.shape[0]
    copies = []
    for c in range(sems.shape[0]):
        here = pl.ds(c * part, part)
        s = jnp.dot(keys, query_t[:, here], preferred_element_type=jnp.float32)
        s = jnp.where(fresh_ok[:, here] > 0, s * scale, NEG_LARGE)
        old = top_t[:1, here]
        top = jnp.maximum(old, jnp.max(s, axis=0, keepdims=True))
        fade = jnp.exp(old - top)
        w = jnp.exp(s - top)
        total = total_t[:1, here] * fade + jnp.sum(w, axis=0, keepdims=True)
        mixed = acc_t[:, here] * fade + jnp.dot(
            values_t, w.astype(jnp.bfloat16), preferred_element_type=jnp.float32
        )
        result[here, :] = (mixed / total).T.astype(jnp.bfloat16)
        copies.append(pltpu.make_async_copy(result.at[here, :], out.at[here, :], sems.at[c]))
        copies[c].start()
    for copy in copies:
        copy.wait()


def body(
    hidden,
    key_value_weight,
    adapter_down_weight,
    adapter_up_weight,
    tenant,
    tenant_page_table,
    request_block_count,
    last_block_tokens,
    placement,
    key_value_cache,
    context_length,
    decode_step_query,
    step_key_value,
):
    devices = lax.axis_size("tensor")
    tokens, width = hidden.shape
    features = key_value_weight.shape[0]
    local, pages, rank2 = adapter_down_weight.shape
    rank = adapter_up_weight.shape[2]
    tenants = tenant_page_table.shape[0]
    dec_rows, ctx, kv_width = key_value_cache.shape
    steps = step_key_value.shape[0]
    heads2 = kv_width // HD
    d_chunks, chunks = 4, 2
    up_by_page = jnp.transpose(adapter_up_weight, (1, 2, 0))
    rows = 2 * CAPT + rank
    outgoing = pl.pallas_call(
        functools.partial(project_kernel, dec_rows, d_chunks, chunks, devices),
        out_shape=pltpu.VMEM((devices, rows, HD), WIRE),
        in_specs=[ANY_SPEC] * 8,
        out_specs=VMEM_SPEC,
        scratch_shapes=[
            pltpu.SMEM(tenant.shape, jnp.int32),
            pltpu.SMEM(tenant_page_table.shape, jnp.int32),
            pltpu.SMEM(request_block_count.shape, jnp.int32),
            pltpu.SMEM(placement.shape, jnp.int32),
            pltpu.VMEM((chunks, tokens, width // chunks), jnp.bfloat16),
            pltpu.VMEM((chunks, features, width // chunks), jnp.bfloat16),
            pltpu.VMEM((local, pages, rank2), jnp.bfloat16),
            pltpu.VMEM((tokens, local), jnp.bfloat16),
            pltpu.VMEM((pages, rank, features), jnp.bfloat16),
            pltpu.VMEM((local // 16, tenants * 16, rank2), jnp.bfloat16),
            pltpu.VMEM((tenants, tokens + BLK, rank2), jnp.float32),
            pltpu.VMEM((tokens + BLK, HD), jnp.float32),
            pltpu.SMEM((2, devices), jnp.int32),
            pltpu.SemaphoreType.DMA((chunks, 2)),
            pltpu.SemaphoreType.DMA((d_chunks + 2,)),
            pltpu.SemaphoreType.DMA((4,)),
        ],
        compiler_params=pltpu.CompilerParams(vmem_limit_bytes=PROJECT_VMEM),
        name="project",
    )(
        *(
            pltpu.with_memory_space_constraint(x, pltpu.HBM)
            for x in (
                tenant, tenant_page_table, request_block_count, placement,
                hidden, key_value_weight, adapter_down_weight, up_by_page,
            )
        )
    )
    arrived = lax.all_to_all(outgoing, "tensor", split_axis=0, concat_axis=0, tiled=True)

    query = decode_step_query.reshape(steps, dec_rows, HEADS, HD)
    query = query.transpose(0, 2, 1, 3).reshape(steps * HEADS * dec_rows, HD)
    steps_kv = step_key_value.reshape(steps, dec_rows, heads2, HD)
    steps_kv = steps_kv.transpose(0, 2, 1, 3).reshape(steps * heads2 * dec_rows, HD)
    q_rows = steps * HEADS * dec_rows
    state = jax.ShapeDtypeStruct((HD, q_rows), jnp.float32)
    line = jax.ShapeDtypeStruct((8, q_rows), jnp.float32)
    handed = pl.pallas_call(
        cached_kernel,
        out_shape=(
            jax.ShapeDtypeStruct((HD, q_rows), jnp.bfloat16),
            state,
            line,
            line,
            jax.ShapeDtypeStruct((KVH * CAPT, q_rows), jnp.float32),
        ),
        in_specs=[SMEM_SPEC] * 4 + [VMEM_SPEC] * 3,
        out_specs=(VMEM_SPEC,) * 5,
        scratch_shapes=[pltpu.VMEM((q_rows, HD), jnp.float32)] * 3,
        compiler_params=pltpu.CompilerParams(vmem_limit_bytes=ATTEND_VMEM),
        name="cached",
    )(
        context_length, request_block_count, last_block_tokens, placement,
        key_value_cache, query, steps_kv,
    )
    attended = pl.pallas_call(
        functools.partial(merge_kernel, features),
        out_shape=jax.ShapeDtypeStruct((q_rows, HD), jnp.bfloat16),
        in_specs=[VMEM_SPEC] * 6,
        out_specs=ANY_SPEC,
        scratch_shapes=[
            pltpu.VMEM((q_rows, HD), jnp.bfloat16),
            pltpu.SemaphoreType.DMA((steps,)),
        ],
        compiler_params=pltpu.CompilerParams(vmem_limit_bytes=ATTEND_VMEM),
        name="merge",
    )(arrived, *handed)
    attended = attended.reshape(steps, HEADS, dec_rows, HD).transpose(0, 2, 1, 3)
    return attended.reshape(steps, dec_rows, HEADS * HD)


def solution(mesh):
    return jax.shard_map(
        body,
        mesh=mesh,
        in_specs=(
            P("parts", None),
            P("tensor", None),
            P("tensor", None, None),
            P("tensor", None, None),
            P("parts"),
            P(),
            P("parts"),
            P("parts"),
            P("parts"),
            P(("parts", "tensor"), None, None),
            P(("parts", "tensor")),
            P(None, ("parts", "tensor"), None),
            P(None, ("parts", "tensor"), None),
        ),
        out_specs=P(None, ("parts", "tensor"), None),
        check_vma=False,
    )
```

```python
import functools

import jax
import jax.numpy as jnp
from jax import lax
from jax.experimental import pallas as pl
from jax.experimental.pallas import tpu as pltpu
from jax.sharding import PartitionSpec as P

HEADS = 64
KVH = 8
HD = 128
BLK = 8
MOSTB = 2
CAPT = MOSTB * BLK
ADAPTER_SCALE = 0.5
NEG_LARGE = -1e30
PROJECT_VMEM = 32 * 1024 * 1024
ATTEND_VMEM = 16 * 1024 * 1024
WIRE = jnp.bfloat16

SMEM_SPEC = pl.BlockSpec(memory_space=pltpu.SMEM)
VMEM_SPEC = pl.BlockSpec(memory_space=pltpu.VMEM)
ANY_SPEC = pl.BlockSpec(memory_space=pl.ANY)


def div(x, n):
    shift = n.bit_length() - 1
    return lax.shift_right_logical(x, shift) if n == 1 << shift else x // n


def mod(x, n):
    return x & (n - 1) if n & (n - 1) == 0 else x % n


def project_kernel(
    dec_rows, d_chunks, chunks, devices, tenant_h, table_h, counts_h, placement_h, hidden, weight, down, up, out,
    tenant, table, counts, placement,
    h_s, w_s, d_s, mine_s, u_s, sel_s, part_s, base_s, dest_table, sems, d_sems, int_sems,
):
    tokens, width = hidden.shape
    features = weight.shape[0]
    local, pages, rank2 = down.shape
    tenants = table.shape[0]
    requests = tenant.shape[0]
    me = lax.axis_index("tensor")
    d_step = local // d_chunks
    step = width // chunks

    int_copies = [
        pltpu.make_async_copy(src, dst, int_sems.at[i])
        for i, (src, dst) in enumerate(
            ((table_h, table), (tenant_h, tenant), (counts_h, counts), (placement_h, placement))
        )
    ]
    for copy in int_copies:
        copy.start()
    def d_copy(c):
        rows = pl.ds(c * d_step, d_step)
        return pltpu.make_async_copy(down.at[rows], d_s.at[rows], d_sems.at[c])

    h_copies = [
        pltpu.make_async_copy(hidden.at[:, pl.ds(c * step, step)], h_s.at[c], sems.at[c, 0])
        for c in range(chunks)
    ]
    w_copies = [
        pltpu.make_async_copy(weight.at[:, pl.ds(c * step, step)], w_s.at[c], sems.at[c, 1])
        for c in range(chunks)
    ]
    my_copy = pltpu.make_async_copy(
        hidden.at[:, pl.ds(pl.multiple_of(me * local, 128), local)], mine_s, d_sems.at[d_chunks]
    )
    up_copy = pltpu.make_async_copy(up, u_s, d_sems.at[d_chunks + 1])
    for copy in [d_copy(c) for c in range(d_chunks)] + [my_copy, up_copy]:
        copy.start()
    for c in range(chunks):
        h_copies[c].start()
        w_copies[c].start()

    int_copies[0].wait()
    rows = lax.broadcasted_iota(jnp.int32, (tenants * 16, 16 * pages), 0)
    cols = lax.broadcasted_iota(jnp.int32, (tenants * 16, 16 * pages), 1)
    page_of_row = jnp.zeros_like(rows)
    for k in range(tenants):
        page_of_row = jnp.where(div(rows, 16) == k, table[k], page_of_row)
    pick = (mod(rows, 16) == div(cols, pages)) & (mod(cols, pages) == page_of_row)
    pick = jnp.where(pick, jnp.float32(1), jnp.float32(0)).astype(jnp.bfloat16)

    blocks = d_step // 16

    def select(c, carry):
        d_copy(c).wait()
        for b in range(0, blocks, 2):
            block = jnp.concatenate(
                [
                    d_s[pl.ds(c * d_step + (b + i) * 16, 16)].reshape(16 * pages, rank2)
                    for i in range(2)
                ],
                axis=1,
            )
            chosen = jnp.dot(pick, block, preferred_element_type=jnp.float32)
            for i in range(2):
                sel_s[c * blocks + b + i] = chosen[:, i * rank2 : (i + 1) * rank2].astype(
                    jnp.bfloat16
                )
        return carry

    lax.fori_loop(0, d_chunks, select, 0)
    for copy in int_copies[1:]:
        copy.wait()
    for dest in range(devices):
        dest_table[0, dest] = 0
        dest_table[1, dest] = 0
    first = jnp.int32(0)
    for r in range(requests):
        dest = div(placement[r], dec_rows)
        dest_table[0, dest] = first * BLK
        dest_table[1, dest] = tenant[r]
        first = first + counts[r]
    my_copy.wait()
    mine = mine_s[...]
    for k in range(0, tenants, 2):
        pair = min(2, tenants - k)
        maps = jnp.concatenate(
            [sel_s[:, j * 16 : (j + 1) * 16, :].reshape(local, rank2) for j in range(k, k + pair)],
            axis=1,
        )
        product = jnp.dot(mine, maps, preferred_element_type=jnp.float32)
        for j in range(pair):
            part_s[k + j, :tokens] = product[:, j * rank2 : (j + 1) * rank2]
            part_s[k + j, tokens:] = jnp.zeros((BLK, rank2), jnp.float32)

    total = jnp.zeros((tokens, features), jnp.float32)
    for c in range(chunks):
        h_copies[c].wait()
        w_copies[c].wait()
        total = total + lax.dot_general(h_s[c], w_s[c], NT, preferred_element_type=jnp.float32)
    base_s[tokens:] = jnp.zeros((BLK, HD), jnp.float32)
    if features < HD:
        base_s[...] = jnp.zeros_like(base_s)
    base_s[:tokens, :features] = total
    up_copy.wait()

    def lay_out(first, carry):
        for i in range(4):
            dest = first * 4 + i
            start = pl.multiple_of(dest_table[0, dest], BLK)
            who = dest_table[1, dest]
            out[dest, :CAPT, :] = part_s[who, pl.ds(start, CAPT), :].astype(out.dtype)
            out[dest, CAPT : 2 * CAPT, :] = base_s[pl.ds(start, CAPT), :].astype(out.dtype)
            if features < HD:
                out[dest, 2 * CAPT :, :] = jnp.zeros((out.shape[1] - 2 * CAPT, HD), out.dtype)
            out[dest, 2 * CAPT :, :features] = u_s[table[who]]
        return carry

    lax.fori_loop(0, devices // 4, lay_out, 0)


NT = (((1,), (1,)), ((), ()))


def gather_queries(query, k, group, steps, stride):
    return jnp.concatenate(
        [query[pl.ds(s * stride + k * group, group), :] for s in range(steps)], axis=0
    )


def cached_kernel(
    lengths, counts, last, placement, cache, query, steps_kv,
    query_t, acc_t, top_t, total_t, fresh_ok, acc, top_out, total_out,
):
    dec_rows, ctx, kv_width = cache.shape
    half_width = kv_width // 2
    step_rows = KVH * dec_rows
    steps = steps_kv.shape[0] // (2 * step_rows)
    group = HEADS // KVH * dec_rows
    q_rows = steps * group
    stride = HEADS * dec_rows

    row = lax.broadcasted_iota(jnp.int32, (q_rows, ctx), 0)
    col = lax.broadcasted_iota(jnp.int32, (q_rows, ctx), 1)
    row_slot = mod(row, dec_rows)
    cache_ok = [(row_slot == g) & (col < lengths[g]) for g in range(dec_rows)]
    row = lax.broadcasted_iota(jnp.int32, (q_rows, steps * step_rows), 0)
    col = lax.broadcasted_iota(jnp.int32, (q_rows, steps * step_rows), 1)
    step_ok = (mod(row, dec_rows) == mod(col, dec_rows)) & (div(col, step_rows) <= div(row, group))
    step_head = div(mod(col, step_rows), dec_rows)
    step_keys, step_values = (
        jnp.concatenate(
            [steps_kv[pl.ds((2 * s + half) * step_rows, step_rows), :] for s in range(steps)], axis=0
        )
        for half in range(2)
    )

    scale = HD ** (-0.5)
    for k in range(KVH):
        lanes = pl.ds(k * HD, HD)
        vlanes = pl.ds(half_width + k * HD, HD)
        q = gather_queries(query, k, group, steps, stride)
        keys = [cache[g, :, lanes] for g in range(dec_rows)] + [step_keys]
        values = [cache[g, :, vlanes] for g in range(dec_rows)] + [step_values]
        scores = [
            jnp.where(
                ok,
                lax.dot_general(q, key, NT, preferred_element_type=jnp.float32) * scale,
                NEG_LARGE,
            )
            for ok, key in zip(cache_ok + [step_ok & (step_head == k)], keys)
        ]
        top = functools.reduce(jnp.maximum, [jnp.max(s, axis=1, keepdims=True) for s in scores])
        weights = [jnp.exp(s - top) for s in scores]
        total = sum(jnp.sum(w, axis=1, keepdims=True) for w in weights)
        mixed = sum(
            jnp.dot(w.astype(jnp.bfloat16), v, preferred_element_type=jnp.float32)
            for w, v in zip(weights, values)
        )
        for s in range(steps):
            here = pl.ds(s * stride + k * group, group)
            part = slice(s * group, (s + 1) * group)
            acc[here, :] = mixed[part]
            top_out[here, :] = jnp.broadcast_to(top[part], (group, HD))
            total_out[here, :] = jnp.broadcast_to(total[part], (group, HD))

    my_slot = jnp.int32(-1)
    my_length = jnp.int32(0)
    for r in range(placement.shape[0]):
        hit = div(placement[r], dec_rows) == lax.axis_index("tensor")
        my_slot = jnp.where(hit, mod(placement[r], dec_rows), my_slot)
        my_length = jnp.where(hit, (counts[r] - 1) * BLK + last[r], my_length)
    col = lax.broadcasted_iota(jnp.int32, fresh_ok.shape, 0)
    row = lax.broadcasted_iota(jnp.int32, fresh_ok.shape, 1)
    ok = (
        (mod(div(row, group), KVH) == div(col, CAPT))
        & (mod(row, dec_rows) == my_slot)
        & (mod(col, CAPT) < my_length)
    )
    fresh_ok[...] = jnp.where(ok, jnp.float32(1), jnp.float32(0))
    query_t[...] = query[...].T
    acc_t[...] = acc[...].T
    top_t[...] = top_out[...].T[: top_t.shape[0]]
    total_t[...] = total_out[...].T[: total_t.shape[0]]


def merge_kernel(
    features, kept, swapped, query_t, acc_t, top_t, total_t, fresh_ok, out, box, result, sems
):
    devices, size = box.shape[:2]
    rank = size - 2 * CAPT
    core = mod(lax.axis_index("tensor"), 2)
    mine = pl.ds(pl.multiple_of(core * size, 16), size)
    for chip in range(devices // 2):
        box[2 * chip + core] = kept[chip, mine, :]
        box[2 * chip + 1 - core] = swapped[chip, mine, :]
    terms = [box[i, :CAPT].astype(jnp.float32) for i in range(devices)]
    while len(terms) > 1:
        pairs = [a + b for a, b in zip(terms[::2], terms[1::2])]
        terms = pairs + terms[2 * len(pairs) :]
    shrunk = terms[0].astype(jnp.bfloat16)
    halves = (shrunk[:, :rank], shrunk[:, rank:])
    pieces = HD // features

    def rows(i, first, count):
        parts = [box[i * pieces + p, first : first + count, :features] for p in range(pieces)]
        return parts[0] if pieces == 1 else jnp.concatenate(parts, axis=1)

    def fresh(first):
        made = []
        for i in range(first, first + KVH, 2):
            ups = jnp.concatenate([rows(i + j, 2 * CAPT, rank) for j in range(2)], axis=1)
            delta = jnp.dot(halves[first // KVH], ups, preferred_element_type=jnp.float32)
            for j in range(2):
                base = rows(i + j, CAPT, CAPT).astype(jnp.float32)
                both = base + ADAPTER_SCALE * delta[:, j * HD : (j + 1) * HD]
                made.append(both.astype(jnp.bfloat16))
        return jnp.concatenate(made, axis=0)

    keys = fresh(0)
    values_t = fresh(KVH).T
    scale = HD ** (-0.5)
    part = out.shape[0] // sems.shape[0]
    copies = []
    for c in range(sems.shape[0]):
        here = pl.ds(c * part, part)
        s = jnp.dot(keys, query_t[:, here], preferred_element_type=jnp.float32)
        s = jnp.where(fresh_ok[:, here] > 0, s * scale, NEG_LARGE)
        old = top_t[:1, here]
        top = jnp.maximum(old, jnp.max(s, axis=0, keepdims=True))
        fade = jnp.exp(old - top)
        w = jnp.exp(s - top)
        total = total_t[:1, here] * fade + jnp.sum(w, axis=0, keepdims=True)
        mixed = acc_t[:, here] * fade + jnp.dot(
            values_t, w.astype(jnp.bfloat16), preferred_element_type=jnp.float32
        )
        result[here, :] = (mixed / total).T.astype(jnp.bfloat16)
        copies.append(pltpu.make_async_copy(result.at[here, :], out.at[here, :], sems.at[c]))
        copies[c].start()
    for copy in copies:
        copy.wait()


def body(
    hidden,
    key_value_weight,
    adapter_down_weight,
    adapter_up_weight,
    tenant,
    tenant_page_table,
    request_block_count,
    last_block_tokens,
    placement,
    key_value_cache,
    context_length,
    decode_step_query,
    step_key_value,
):
    devices = lax.axis_size("tensor")
    tokens, width = hidden.shape
    features = key_value_weight.shape[0]
    local, pages, rank2 = adapter_down_weight.shape
    rank = adapter_up_weight.shape[2]
    tenants = tenant_page_table.shape[0]
    dec_rows, ctx, kv_width = key_value_cache.shape
    steps = step_key_value.shape[0]
    heads2 = kv_width // HD
    d_chunks, chunks = 4, 2
    up_by_page = jnp.transpose(adapter_up_weight, (1, 2, 0))
    rows = 2 * CAPT + rank
    outgoing = pl.pallas_call(
        functools.partial(project_kernel, dec_rows, d_chunks, chunks, devices),
        out_shape=pltpu.VMEM((devices, rows, HD), WIRE),
        in_specs=[ANY_SPEC] * 8,
        out_specs=VMEM_SPEC,
        scratch_shapes=[
            pltpu.SMEM(tenant.shape, jnp.int32),
            pltpu.SMEM(tenant_page_table.shape, jnp.int32),
            pltpu.SMEM(request_block_count.shape, jnp.int32),
            pltpu.SMEM(placement.shape, jnp.int32),
            pltpu.VMEM((chunks, tokens, width // chunks), jnp.bfloat16),
            pltpu.VMEM((chunks, features, width // chunks), jnp.bfloat16),
            pltpu.VMEM((local, pages, rank2), jnp.bfloat16),
            pltpu.VMEM((tokens, local), jnp.bfloat16),
            pltpu.VMEM((pages, rank, features), jnp.bfloat16),
            pltpu.VMEM((local // 16, tenants * 16, rank2), jnp.bfloat16),
            pltpu.VMEM((tenants, tokens + BLK, rank2), jnp.float32),
            pltpu.VMEM((tokens + BLK, HD), jnp.float32),
            pltpu.SMEM((2, devices), jnp.int32),
            pltpu.SemaphoreType.DMA((chunks, 2)),
            pltpu.SemaphoreType.DMA((d_chunks + 2,)),
            pltpu.SemaphoreType.DMA((4,)),
        ],
        compiler_params=pltpu.CompilerParams(vmem_limit_bytes=PROJECT_VMEM),
        name="project",
    )(
        *(
            pltpu.with_memory_space_constraint(x, pltpu.HBM)
            for x in (
                tenant, tenant_page_table, request_block_count, placement,
                hidden, key_value_weight, adapter_down_weight, up_by_page,
            )
        )
    )
    chips = devices // 2
    same_core = [[2 * chip + core for chip in range(chips)] for core in range(2)]
    kept = lax.all_to_all(
        outgoing.reshape(chips, 2 * rows, HD), "tensor", split_axis=0, concat_axis=0,
        axis_index_groups=same_core, tiled=True,
    )
    swapped = lax.ppermute(kept, "tensor", [(i, i ^ 1) for i in range(devices)])

    query = decode_step_query.reshape(steps, dec_rows, HEADS, HD)
    query = query.transpose(0, 2, 1, 3).reshape(steps * HEADS * dec_rows, HD)
    steps_kv = step_key_value.reshape(steps, dec_rows, heads2, HD)
    steps_kv = steps_kv.transpose(0, 2, 1, 3).reshape(steps * heads2 * dec_rows, HD)
    q_rows = steps * HEADS * dec_rows
    state = jax.ShapeDtypeStruct((HD, q_rows), jnp.float32)
    line = jax.ShapeDtypeStruct((8, q_rows), jnp.float32)
    handed = pl.pallas_call(
        cached_kernel,
        out_shape=(
            jax.ShapeDtypeStruct((HD, q_rows), jnp.bfloat16),
            state,
            line,
            line,
            jax.ShapeDtypeStruct((KVH * CAPT, q_rows), jnp.float32),
        ),
        in_specs=[SMEM_SPEC] * 4 + [VMEM_SPEC] * 3,
        out_specs=(VMEM_SPEC,) * 5,
        scratch_shapes=[pltpu.VMEM((q_rows, HD), jnp.float32)] * 3,
        compiler_params=pltpu.CompilerParams(vmem_limit_bytes=ATTEND_VMEM),
        name="cached",
    )(
        context_length, request_block_count, last_block_tokens, placement,
        key_value_cache, query, steps_kv,
    )
    attended = pl.pallas_call(
        functools.partial(merge_kernel, features),
        out_shape=jax.ShapeDtypeStruct((q_rows, HD), jnp.bfloat16),
        in_specs=[VMEM_SPEC] * 7,
        out_specs=ANY_SPEC,
        scratch_shapes=[
            pltpu.VMEM((devices, rows, HD), WIRE),
            pltpu.VMEM((q_rows, HD), jnp.bfloat16),
            pltpu.SemaphoreType.DMA((steps,)),
        ],
        compiler_params=pltpu.CompilerParams(vmem_limit_bytes=ATTEND_VMEM),
        name="merge",
    )(kept, swapped, *handed)
    attended = attended.reshape(steps, HEADS, dec_rows, HD).transpose(0, 2, 1, 3)
    return attended.reshape(steps, dec_rows, HEADS * HD)


def solution(mesh):
    return jax.shard_map(
        body,
        mesh=mesh,
        in_specs=(
            P("parts", None),
            P("tensor", None),
            P("tensor", None, None),
            P("tensor", None, None),
            P("parts"),
            P(),
            P("parts"),
            P("parts"),
            P("parts"),
            P(("parts", "tensor"), None, None),
            P(("parts", "tensor")),
            P(None, ("parts", "tensor"), None),
            P(None, ("parts", "tensor"), None),
        ),
        out_specs=P(None, ("parts", "tensor"), None),
        check_vma=False,
    )
```

```python
import functools

import jax
import jax.numpy as jnp
from jax import lax
from jax.experimental import pallas as pl
from jax.experimental.pallas import tpu as pltpu
from jax.sharding import PartitionSpec as P

HEADS = 64
KVH = 8
HD = 128
BLK = 8
MOSTB = 2
CAPT = MOSTB * BLK
ADAPTER_SCALE = 0.5
NEG_LARGE = -1e30
PROJECT_VMEM = 32 * 1024 * 1024
ATTEND_VMEM = 16 * 1024 * 1024
WIRE = jnp.bfloat16

SMEM_SPEC = pl.BlockSpec(memory_space=pltpu.SMEM)
VMEM_SPEC = pl.BlockSpec(memory_space=pltpu.VMEM)
ANY_SPEC = pl.BlockSpec(memory_space=pl.ANY)


def div(x, n):
    shift = n.bit_length() - 1
    return lax.shift_right_logical(x, shift) if n == 1 << shift else x // n


def mod(x, n):
    return x & (n - 1) if n & (n - 1) == 0 else x % n


def project_kernel(
    dec_rows, d_chunks, chunks, devices, tenant_h, table_h, counts_h, placement_h, hidden, weight, down, up, out,
    tenant, table, counts, placement,
    h_s, w_s, d_s, mine_s, u_s, sel_s, part_s, base_s, out_s, dest_table, sems, d_sems, int_sems,
    out_sems,
):
    tokens, width = hidden.shape
    features = weight.shape[0]
    local, pages, rank2 = down.shape
    tenants = table.shape[0]
    rank = up.shape[1]
    requests = tenant.shape[0]
    me = lax.axis_index("tensor")
    d_step = local // d_chunks
    step = width // chunks

    int_copies = [
        pltpu.make_async_copy(src, dst, int_sems.at[i])
        for i, (src, dst) in enumerate(
            ((table_h, table), (tenant_h, tenant), (counts_h, counts), (placement_h, placement))
        )
    ]
    for copy in int_copies:
        copy.start()
    def d_copy(c):
        rows = pl.ds(c * d_step, d_step)
        return pltpu.make_async_copy(down.at[rows], d_s.at[rows], d_sems.at[c])

    h_copies = [
        pltpu.make_async_copy(hidden.at[:, pl.ds(c * step, step)], h_s.at[c], sems.at[c, 0])
        for c in range(chunks)
    ]
    w_copies = [
        pltpu.make_async_copy(weight.at[:, pl.ds(c * step, step)], w_s.at[c], sems.at[c, 1])
        for c in range(chunks)
    ]
    my_copy = pltpu.make_async_copy(
        hidden.at[:, pl.ds(pl.multiple_of(me * local, 128), local)], mine_s, d_sems.at[d_chunks]
    )
    up_copy = pltpu.make_async_copy(up, u_s, d_sems.at[d_chunks + 1])
    for copy in [d_copy(c) for c in range(d_chunks)] + [my_copy, up_copy]:
        copy.start()
    for c in range(chunks):
        h_copies[c].start()
        w_copies[c].start()

    int_copies[0].wait()
    rows = lax.broadcasted_iota(jnp.int32, (tenants * 16, 16 * pages), 0)
    cols = lax.broadcasted_iota(jnp.int32, (tenants * 16, 16 * pages), 1)
    page_of_row = jnp.zeros_like(rows)
    for k in range(tenants):
        page_of_row = jnp.where(div(rows, 16) == k, table[k], page_of_row)
    pick = (mod(rows, 16) == div(cols, pages)) & (mod(cols, pages) == page_of_row)
    pick = jnp.where(pick, jnp.float32(1), jnp.float32(0)).astype(jnp.bfloat16)

    blocks = d_step // 16

    def select(c, carry):
        d_copy(c).wait()
        for b in range(0, blocks, 2):
            block = jnp.concatenate(
                [
                    d_s[pl.ds(c * d_step + (b + i) * 16, 16)].reshape(16 * pages, rank2)
                    for i in range(2)
                ],
                axis=1,
            )
            chosen = jnp.dot(pick, block, preferred_element_type=jnp.float32)
            for i in range(2):
                sel_s[c * blocks + b + i] = chosen[:, i * rank2 : (i + 1) * rank2].astype(
                    jnp.bfloat16
                )
        return carry

    lax.fori_loop(0, d_chunks, select, 0)
    for copy in int_copies[1:]:
        copy.wait()
    for dest in range(devices):
        dest_table[0, dest] = 0
        dest_table[1, dest] = 0
    first = jnp.int32(0)
    for r in range(requests):
        dest = div(placement[r], dec_rows)
        dest_table[0, dest] = first * BLK
        dest_table[1, dest] = tenant[r]
        first = first + counts[r]
    up_copy.wait()
    whole = features == HD
    sent = []
    if whole:
        for dest in range(devices):
            page = table[dest_table[1, dest]]
            sent.append(pltpu.make_async_copy(
                u_s.at[page], out.at[dest, pl.ds(2 * CAPT, rank), :], out_sems.at[dest]))
            sent[-1].start()
    my_copy.wait()
    mine = mine_s[...]
    for k in range(0, tenants, 2):
        pair = min(2, tenants - k)
        maps = jnp.concatenate(
            [sel_s[:, j * 16 : (j + 1) * 16, :].reshape(local, rank2) for j in range(k, k + pair)],
            axis=1,
        )
        product = jnp.dot(mine, maps, preferred_element_type=jnp.float32)
        for j in range(pair):
            part_s[k + j, :tokens] = product[:, j * rank2 : (j + 1) * rank2]
            part_s[k + j, tokens:] = jnp.zeros((BLK, rank2), jnp.float32)

    for dest in range(devices):
        start = pl.multiple_of(dest_table[0, dest], BLK)
        rows = part_s[dest_table[1, dest], pl.ds(start, CAPT), :]
        out_s[dest, :CAPT, :] = rows.astype(out.dtype)
    if whole:
        lines = pl.ds(0, CAPT)
        sent.append(pltpu.make_async_copy(
            out_s.at[:, lines, :], out.at[:, lines, :], out_sems.at[devices]))
        sent[-1].start()

    total = jnp.zeros((tokens, features), jnp.float32)
    for c in range(chunks):
        h_copies[c].wait()
        w_copies[c].wait()
        total = total + lax.dot_general(h_s[c], w_s[c], NT, preferred_element_type=jnp.float32)
    base_s[tokens:] = jnp.zeros((BLK, HD), jnp.float32)
    if features < HD:
        base_s[...] = jnp.zeros_like(base_s)
    base_s[:tokens, :features] = total
    for dest in range(devices):
        start = pl.multiple_of(dest_table[0, dest], BLK)
        out_s[dest, CAPT : 2 * CAPT, :] = base_s[pl.ds(start, CAPT), :].astype(out.dtype)
        if not whole:
            out_s[dest, 2 * CAPT :, :] = jnp.zeros((rank, HD), out.dtype)
            out_s[dest, 2 * CAPT :, :features] = u_s[table[dest_table[1, dest]]]
    lines = pl.ds(CAPT, CAPT) if whole else pl.ds(0, out.shape[1])
    sent.append(pltpu.make_async_copy(
        out_s.at[:, lines, :], out.at[:, lines, :], out_sems.at[devices + 1]))
    sent[-1].start()
    for copy in sent:
        copy.wait()


NT = (((1,), (1,)), ((), ()))


def gather_queries(query, k, group, steps, stride):
    return jnp.concatenate(
        [query[pl.ds(s * stride + k * group, group), :] for s in range(steps)], axis=0
    )


def cached_kernel(
    lengths, counts, last, placement, cache, query, steps_kv,
    query_t, acc_t, top_t, total_t, fresh_ok, acc, top_out, total_out,
):
    dec_rows, ctx, kv_width = cache.shape
    half_width = kv_width // 2
    step_rows = KVH * dec_rows
    steps = steps_kv.shape[0] // (2 * step_rows)
    group = HEADS // KVH * dec_rows
    q_rows = steps * group
    stride = HEADS * dec_rows

    row = lax.broadcasted_iota(jnp.int32, (q_rows, ctx), 0)
    col = lax.broadcasted_iota(jnp.int32, (q_rows, ctx), 1)
    row_slot = mod(row, dec_rows)
    cache_ok = [(row_slot == g) & (col < lengths[g]) for g in range(dec_rows)]
    row = lax.broadcasted_iota(jnp.int32, (q_rows, steps * step_rows), 0)
    col = lax.broadcasted_iota(jnp.int32, (q_rows, steps * step_rows), 1)
    step_ok = (mod(row, dec_rows) == mod(col, dec_rows)) & (div(col, step_rows) <= div(row, group))
    step_head = div(mod(col, step_rows), dec_rows)
    step_keys, step_values = (
        jnp.concatenate(
            [steps_kv[pl.ds((2 * s + half) * step_rows, step_rows), :] for s in range(steps)], axis=0
        )
        for half in range(2)
    )

    scale = HD ** (-0.5)
    for k in range(KVH):
        lanes = pl.ds(k * HD, HD)
        vlanes = pl.ds(half_width + k * HD, HD)
        q = gather_queries(query, k, group, steps, stride)
        keys = [cache[g, :, lanes] for g in range(dec_rows)] + [step_keys]
        values = [cache[g, :, vlanes] for g in range(dec_rows)] + [step_values]
        scores = [
            jnp.where(
                ok,
                lax.dot_general(q, key, NT, preferred_element_type=jnp.float32) * scale,
                NEG_LARGE,
            )
            for ok, key in zip(cache_ok + [step_ok & (step_head == k)], keys)
        ]
        top = functools.reduce(jnp.maximum, [jnp.max(s, axis=1, keepdims=True) for s in scores])
        weights = [jnp.exp(s - top) for s in scores]
        total = sum(jnp.sum(w, axis=1, keepdims=True) for w in weights)
        mixed = sum(
            jnp.dot(w.astype(jnp.bfloat16), v, preferred_element_type=jnp.float32)
            for w, v in zip(weights, values)
        )
        for s in range(steps):
            here = pl.ds(s * stride + k * group, group)
            part = slice(s * group, (s + 1) * group)
            acc[here, :] = mixed[part]
            top_out[here, :] = jnp.broadcast_to(top[part], (group, HD))
            total_out[here, :] = jnp.broadcast_to(total[part], (group, HD))

    my_slot = jnp.int32(-1)
    my_length = jnp.int32(0)
    for r in range(placement.shape[0]):
        hit = div(placement[r], dec_rows) == lax.axis_index("tensor")
        my_slot = jnp.where(hit, mod(placement[r], dec_rows), my_slot)
        my_length = jnp.where(hit, (counts[r] - 1) * BLK + last[r], my_length)
    col = lax.broadcasted_iota(jnp.int32, fresh_ok.shape, 0)
    row = lax.broadcasted_iota(jnp.int32, fresh_ok.shape, 1)
    ok = (
        (mod(div(row, group), KVH) == div(col, CAPT))
        & (mod(row, dec_rows) == my_slot)
        & (mod(col, CAPT) < my_length)
    )
    fresh_ok[...] = jnp.where(ok, jnp.float32(1), jnp.float32(0))
    query_t[...] = query[...].T
    acc_t[...] = acc[...].T
    top_t[...] = top_out[...].T[: top_t.shape[0]]
    total_t[...] = total_out[...].T[: total_t.shape[0]]


def merge_kernel(features, box, query_t, acc_t, top_t, total_t, fresh_ok, out, result, sems):
    devices = box.shape[0]
    rank = box.shape[1] - 2 * CAPT
    terms = [box[i, :CAPT].astype(jnp.float32) for i in range(devices)]
    while len(terms) > 1:
        pairs = [a + b for a, b in zip(terms[::2], terms[1::2])]
        terms = pairs + terms[2 * len(pairs) :]
    shrunk = terms[0].astype(jnp.bfloat16)
    halves = (shrunk[:, :rank], shrunk[:, rank:])
    pieces = HD // features

    def rows(i, first, count):
        parts = [box[i * pieces + p, first : first + count, :features] for p in range(pieces)]
        return parts[0] if pieces == 1 else jnp.concatenate(parts, axis=1)

    def fresh(first):
        made = []
        for i in range(first, first + KVH, 2):
            ups = jnp.concatenate([rows(i + j, 2 * CAPT, rank) for j in range(2)], axis=1)
            delta = jnp.dot(halves[first // KVH], ups, preferred_element_type=jnp.float32)
            for j in range(2):
                base = rows(i + j, CAPT, CAPT).astype(jnp.float32)
                both = base + ADAPTER_SCALE * delta[:, j * HD : (j + 1) * HD]
                made.append(both.astype(jnp.bfloat16))
        return jnp.concatenate(made, axis=0)

    keys = fresh(0)
    values_t = fresh(KVH).T
    scale = HD ** (-0.5)
    part = out.shape[0] // sems.shape[0]
    copies = []
    for c in range(sems.shape[0]):
        here = pl.ds(c * part, part)
        s = jnp.dot(keys, query_t[:, here], preferred_element_type=jnp.float32)
        s = jnp.where(fresh_ok[:, here] > 0, s * scale, NEG_LARGE)
        old = top_t[:1, here]
        top = jnp.maximum(old, jnp.max(s, axis=0, keepdims=True))
        fade = jnp.exp(old - top)
        w = jnp.exp(s - top)
        total = total_t[:1, here] * fade + jnp.sum(w, axis=0, keepdims=True)
        mixed = acc_t[:, here] * fade + jnp.dot(
            values_t, w.astype(jnp.bfloat16), preferred_element_type=jnp.float32
        )
        result[here, :] = (mixed / total).T.astype(jnp.bfloat16)
        copies.append(pltpu.make_async_copy(result.at[here, :], out.at[here, :], sems.at[c]))
        copies[c].start()
    for copy in copies:
        copy.wait()


def body(
    hidden,
    key_value_weight,
    adapter_down_weight,
    adapter_up_weight,
    tenant,
    tenant_page_table,
    request_block_count,
    last_block_tokens,
    placement,
    key_value_cache,
    context_length,
    decode_step_query,
    step_key_value,
):
    devices = lax.axis_size("tensor")
    tokens, width = hidden.shape
    features = key_value_weight.shape[0]
    local, pages, rank2 = adapter_down_weight.shape
    rank = adapter_up_weight.shape[2]
    tenants = tenant_page_table.shape[0]
    dec_rows, ctx, kv_width = key_value_cache.shape
    steps = step_key_value.shape[0]
    heads2 = kv_width // HD
    d_chunks, chunks = 4, 2
    up_by_page = jnp.transpose(adapter_up_weight, (1, 2, 0))
    rows = 2 * CAPT + rank
    outgoing = pl.pallas_call(
        functools.partial(project_kernel, dec_rows, d_chunks, chunks, devices),
        out_shape=jax.ShapeDtypeStruct((devices, rows, HD), WIRE),
        in_specs=[ANY_SPEC] * 8,
        out_specs=ANY_SPEC,
        scratch_shapes=[
            pltpu.SMEM(tenant.shape, jnp.int32),
            pltpu.SMEM(tenant_page_table.shape, jnp.int32),
            pltpu.SMEM(request_block_count.shape, jnp.int32),
            pltpu.SMEM(placement.shape, jnp.int32),
            pltpu.VMEM((chunks, tokens, width // chunks), jnp.bfloat16),
            pltpu.VMEM((chunks, features, width // chunks), jnp.bfloat16),
            pltpu.VMEM((local, pages, rank2), jnp.bfloat16),
            pltpu.VMEM((tokens, local), jnp.bfloat16),
            pltpu.VMEM((pages, rank, features), jnp.bfloat16),
            pltpu.VMEM((local // 16, tenants * 16, rank2), jnp.bfloat16),
            pltpu.VMEM((tenants, tokens + BLK, rank2), jnp.float32),
            pltpu.VMEM((tokens + BLK, HD), jnp.float32),
            pltpu.VMEM((devices, rows, HD), WIRE),
            pltpu.SMEM((2, devices), jnp.int32),
            pltpu.SemaphoreType.DMA((chunks, 2)),
            pltpu.SemaphoreType.DMA((d_chunks + 2,)),
            pltpu.SemaphoreType.DMA((4,)),
            pltpu.SemaphoreType.DMA((devices + 2,)),
        ],
        compiler_params=pltpu.CompilerParams(vmem_limit_bytes=PROJECT_VMEM),
        name="project",
    )(
        *(
            pltpu.with_memory_space_constraint(x, pltpu.HBM)
            for x in (
                tenant, tenant_page_table, request_block_count, placement,
                hidden, key_value_weight, adapter_down_weight, up_by_page,
            )
        )
    )
    arrived = lax.all_to_all(outgoing, "tensor", split_axis=0, concat_axis=0, tiled=True)

    query = decode_step_query.reshape(steps, dec_rows, HEADS, HD)
    query = query.transpose(0, 2, 1, 3).reshape(steps * HEADS * dec_rows, HD)
    steps_kv = step_key_value.reshape(steps, dec_rows, heads2, HD)
    steps_kv = steps_kv.transpose(0, 2, 1, 3).reshape(steps * heads2 * dec_rows, HD)
    q_rows = steps * HEADS * dec_rows
    state = jax.ShapeDtypeStruct((HD, q_rows), jnp.float32)
    line = jax.ShapeDtypeStruct((8, q_rows), jnp.float32)
    handed = pl.pallas_call(
        cached_kernel,
        out_shape=(
            jax.ShapeDtypeStruct((HD, q_rows), jnp.bfloat16),
            state,
            line,
            line,
            jax.ShapeDtypeStruct((KVH * CAPT, q_rows), jnp.float32),
        ),
        in_specs=[SMEM_SPEC] * 4 + [VMEM_SPEC] * 3,
        out_specs=(VMEM_SPEC,) * 5,
        scratch_shapes=[pltpu.VMEM((q_rows, HD), jnp.float32)] * 3,
        compiler_params=pltpu.CompilerParams(vmem_limit_bytes=ATTEND_VMEM),
        name="cached",
    )(
        context_length, request_block_count, last_block_tokens, placement,
        key_value_cache, query, steps_kv,
    )
    attended = pl.pallas_call(
        functools.partial(merge_kernel, features),
        out_shape=jax.ShapeDtypeStruct((q_rows, HD), jnp.bfloat16),
        in_specs=[VMEM_SPEC] * 6,
        out_specs=ANY_SPEC,
        scratch_shapes=[
            pltpu.VMEM((q_rows, HD), jnp.bfloat16),
            pltpu.SemaphoreType.DMA((steps,)),
        ],
        compiler_params=pltpu.CompilerParams(vmem_limit_bytes=ATTEND_VMEM),
        name="merge",
    )(arrived, *handed)
    attended = attended.reshape(steps, HEADS, dec_rows, HD).transpose(0, 2, 1, 3)
    return attended.reshape(steps, dec_rows, HEADS * HD)


def solution(mesh):
    return jax.shard_map(
        body,
        mesh=mesh,
        in_specs=(
            P("parts", None),
            P("tensor", None),
            P("tensor", None, None),
            P("tensor", None, None),
            P("parts"),
            P(),
            P("parts"),
            P("parts"),
            P("parts"),
            P(("parts", "tensor"), None, None),
            P(("parts", "tensor")),
            P(None, ("parts", "tensor"), None),
            P(None, ("parts", "tensor"), None),
        ),
        out_specs=P(None, ("parts", "tensor"), None),
        check_vma=False,
    )
```

```python
import functools

import jax
import jax.numpy as jnp
from jax import lax
from jax.experimental import pallas as pl
from jax.experimental.pallas import tpu as pltpu
from jax.sharding import PartitionSpec as P

HEADS = 64
KVH = 8
HD = 128
BLK = 8
MOSTB = 2
CAPT = MOSTB * BLK
ADAPTER_SCALE = 0.5
NEG_LARGE = -1e30
PROJECT_VMEM = 32 * 1024 * 1024
ATTEND_VMEM = 16 * 1024 * 1024
WIRE = jnp.bfloat16

SMEM_SPEC = pl.BlockSpec(memory_space=pltpu.SMEM)
VMEM_SPEC = pl.BlockSpec(memory_space=pltpu.VMEM)
ANY_SPEC = pl.BlockSpec(memory_space=pl.ANY)


def div(x, n):
    shift = n.bit_length() - 1
    return lax.shift_right_logical(x, shift) if n == 1 << shift else x // n


def mod(x, n):
    return x & (n - 1) if n & (n - 1) == 0 else x % n


def front_kernel(
    dec_rows, d_chunks, chunks, devices,
    tenant_h, table_h, counts_h, placement_h, lengths_h, last_h,
    hidden, weight, down, up, cache_h, query_h, steps_h,
    out, query_t, acc_t, top_t, total_t, fresh_ok,
    tenant, table, counts, placement, lengths, last,
    h_s, w_s, d_s, mine_s, u_s, sel_s, part_s, base_s, dest_table, sems, d_sems, int_sems,
    cache, query, steps_kv, acc, top_out, total_out, c_sems,
):
    tokens, width = hidden.shape
    features = weight.shape[0]
    local, pages, rank2 = down.shape
    tenants = table.shape[0]
    requests = tenant.shape[0]
    me = lax.axis_index("tensor")
    d_step = local // d_chunks
    step = width // chunks

    int_copies = [
        pltpu.make_async_copy(src, dst, int_sems.at[i])
        for i, (src, dst) in enumerate(
            (
                (table_h, table), (tenant_h, tenant), (counts_h, counts), (placement_h, placement),
                (lengths_h, lengths), (last_h, last),
            )
        )
    ]
    for copy in int_copies:
        copy.start()
    def d_copy(c):
        rows = pl.ds(c * d_step, d_step)
        return pltpu.make_async_copy(down.at[rows], d_s.at[rows], d_sems.at[c])

    h_copies = [
        pltpu.make_async_copy(hidden.at[:, pl.ds(c * step, step)], h_s.at[c], sems.at[c, 0])
        for c in range(chunks)
    ]
    w_copies = [
        pltpu.make_async_copy(weight.at[:, pl.ds(c * step, step)], w_s.at[c], sems.at[c, 1])
        for c in range(chunks)
    ]
    my_copy = pltpu.make_async_copy(
        hidden.at[:, pl.ds(pl.multiple_of(me * local, 128), local)], mine_s, d_sems.at[d_chunks]
    )
    up_copy = pltpu.make_async_copy(up, u_s, d_sems.at[d_chunks + 1])
    c_copies = [
        pltpu.make_async_copy(src, dst, c_sems.at[i])
        for i, (src, dst) in enumerate(((query_h, query), (steps_h, steps_kv), (cache_h, cache)))
    ]
    for copy in [d_copy(c) for c in range(d_chunks)] + [my_copy] + c_copies + [up_copy]:
        copy.start()
    for c in range(chunks):
        h_copies[c].start()
        w_copies[c].start()

    int_copies[0].wait()
    rows = lax.broadcasted_iota(jnp.int32, (tenants * 16, 16 * pages), 0)
    cols = lax.broadcasted_iota(jnp.int32, (tenants * 16, 16 * pages), 1)
    page_of_row = jnp.zeros_like(rows)
    for k in range(tenants):
        page_of_row = jnp.where(div(rows, 16) == k, table[k], page_of_row)
    pick = (mod(rows, 16) == div(cols, pages)) & (mod(cols, pages) == page_of_row)
    pick = jnp.where(pick, jnp.float32(1), jnp.float32(0)).astype(jnp.bfloat16)

    blocks = d_step // 16

    def select(c, carry):
        d_copy(c).wait()
        for b in range(0, blocks, 2):
            block = jnp.concatenate(
                [
                    d_s[pl.ds(c * d_step + (b + i) * 16, 16)].reshape(16 * pages, rank2)
                    for i in range(2)
                ],
                axis=1,
            )
            chosen = jnp.dot(pick, block, preferred_element_type=jnp.float32)
            for i in range(2):
                sel_s[c * blocks + b + i] = chosen[:, i * rank2 : (i + 1) * rank2].astype(
                    jnp.bfloat16
                )
        return carry

    lax.fori_loop(0, d_chunks, select, 0)
    for copy in int_copies[1:]:
        copy.wait()
    for dest in range(devices):
        dest_table[0, dest] = 0
        dest_table[1, dest] = 0
    first = jnp.int32(0)
    for r in range(requests):
        dest = div(placement[r], dec_rows)
        dest_table[0, dest] = first * BLK
        dest_table[1, dest] = tenant[r]
        first = first + counts[r]
    my_copy.wait()
    for copy in c_copies:
        copy.wait()
    head, finish = cached_parts(
        lengths, counts, last, placement, cache, query, steps_kv,
        query_t, acc_t, top_t, total_t, fresh_ok, acc, top_out, total_out,
    )
    mine = mine_s[...]
    for k in range(KVH // 2):
        head(k)
    for k in range(0, tenants, 2):
        pair = min(2, tenants - k)
        maps = jnp.concatenate(
            [sel_s[:, j * 16 : (j + 1) * 16, :].reshape(local, rank2) for j in range(k, k + pair)],
            axis=1,
        )
        product = jnp.dot(mine, maps, preferred_element_type=jnp.float32)
        for j in range(pair):
            part_s[k + j, :tokens] = product[:, j * rank2 : (j + 1) * rank2]
            part_s[k + j, tokens:] = jnp.zeros((BLK, rank2), jnp.float32)

    total = jnp.zeros((tokens, features), jnp.float32)
    for c in range(chunks):
        h_copies[c].wait()
        w_copies[c].wait()
        total = total + lax.dot_general(h_s[c], w_s[c], NT, preferred_element_type=jnp.float32)
        if c == 0:
            for k in range(KVH // 2, KVH):
                head(k)
        if c == chunks - 1:
            finish()
    base_s[tokens:] = jnp.zeros((BLK, HD), jnp.float32)
    if features < HD:
        base_s[...] = jnp.zeros_like(base_s)
    base_s[:tokens, :features] = total
    up_copy.wait()

    def lay_out(first, carry):
        for i in range(4):
            dest = first * 4 + i
            start = pl.multiple_of(dest_table[0, dest], BLK)
            who = dest_table[1, dest]
            out[dest, :CAPT, :] = part_s[who, pl.ds(start, CAPT), :].astype(out.dtype)
            out[dest, CAPT : 2 * CAPT, :] = base_s[pl.ds(start, CAPT), :].astype(out.dtype)
            if features < HD:
                out[dest, 2 * CAPT :, :] = jnp.zeros((out.shape[1] - 2 * CAPT, HD), out.dtype)
            out[dest, 2 * CAPT :, :features] = u_s[table[who]]
        return carry

    lax.fori_loop(0, devices // 4, lay_out, 0)


NT = (((1,), (1,)), ((), ()))


def gather_queries(query, k, group, steps, stride):
    return jnp.concatenate(
        [query[pl.ds(s * stride + k * group, group), :] for s in range(steps)], axis=0
    )


def cached_parts(
    lengths, counts, last, placement, cache, query, steps_kv,
    query_t, acc_t, top_t, total_t, fresh_ok, acc, top_out, total_out,
):
    dec_rows, ctx, kv_width = cache.shape
    half_width = kv_width // 2
    step_rows = KVH * dec_rows
    steps = steps_kv.shape[0] // (2 * step_rows)
    group = HEADS // KVH * dec_rows
    q_rows = steps * group
    stride = HEADS * dec_rows

    row = lax.broadcasted_iota(jnp.int32, (q_rows, ctx), 0)
    col = lax.broadcasted_iota(jnp.int32, (q_rows, ctx), 1)
    row_slot = mod(row, dec_rows)
    cache_ok = [(row_slot == g) & (col < lengths[g]) for g in range(dec_rows)]
    row = lax.broadcasted_iota(jnp.int32, (q_rows, steps * step_rows), 0)
    col = lax.broadcasted_iota(jnp.int32, (q_rows, steps * step_rows), 1)
    step_ok = (mod(row, dec_rows) == mod(col, dec_rows)) & (div(col, step_rows) <= div(row, group))
    step_head = div(mod(col, step_rows), dec_rows)
    step_keys, step_values = (
        jnp.concatenate(
            [steps_kv[pl.ds((2 * s + half) * step_rows, step_rows), :] for s in range(steps)], axis=0
        )
        for half in range(2)
    )

    scale = HD ** (-0.5)
    def head(k):
        lanes = pl.ds(k * HD, HD)
        vlanes = pl.ds(half_width + k * HD, HD)
        q = gather_queries(query, k, group, steps, stride)
        keys = [cache[g, :, lanes] for g in range(dec_rows)] + [step_keys]
        values = [cache[g, :, vlanes] for g in range(dec_rows)] + [step_values]
        scores = [
            jnp.where(
                ok,
                lax.dot_general(q, key, NT, preferred_element_type=jnp.float32) * scale,
                NEG_LARGE,
            )
            for ok, key in zip(cache_ok + [step_ok & (step_head == k)], keys)
        ]
        top = functools.reduce(jnp.maximum, [jnp.max(s, axis=1, keepdims=True) for s in scores])
        weights = [jnp.exp(s - top) for s in scores]
        total = sum(jnp.sum(w, axis=1, keepdims=True) for w in weights)
        mixed = sum(
            jnp.dot(w.astype(jnp.bfloat16), v, preferred_element_type=jnp.float32)
            for w, v in zip(weights, values)
        )
        for s in range(steps):
            here = pl.ds(s * stride + k * group, group)
            part = slice(s * group, (s + 1) * group)
            acc[here, :] = mixed[part]
            top_out[here, :] = jnp.broadcast_to(top[part], (group, HD))
            total_out[here, :] = jnp.broadcast_to(total[part], (group, HD))

    def finish():
        my_slot = jnp.int32(-1)
        my_length = jnp.int32(0)
        for r in range(placement.shape[0]):
            hit = div(placement[r], dec_rows) == lax.axis_index("tensor")
            my_slot = jnp.where(hit, mod(placement[r], dec_rows), my_slot)
            my_length = jnp.where(hit, (counts[r] - 1) * BLK + last[r], my_length)
        col = lax.broadcasted_iota(jnp.int32, fresh_ok.shape, 0)
        row = lax.broadcasted_iota(jnp.int32, fresh_ok.shape, 1)
        ok = (
            (mod(div(row, group), KVH) == div(col, CAPT))
            & (mod(row, dec_rows) == my_slot)
            & (mod(col, CAPT) < my_length)
        )
        fresh_ok[...] = jnp.where(ok, jnp.float32(1), jnp.float32(0))
        query_t[...] = query[...].T
        acc_t[...] = acc[...].T
        top_t[...] = top_out[...].T[: top_t.shape[0]]
        total_t[...] = total_out[...].T[: total_t.shape[0]]

    return head, finish


def merge_kernel(features, box, query_t, acc_t, top_t, total_t, fresh_ok, out, result, sems):
    devices = box.shape[0]
    rank = box.shape[1] - 2 * CAPT
    terms = [box[i, :CAPT].astype(jnp.float32) for i in range(devices)]
    while len(terms) > 1:
        pairs = [a + b for a, b in zip(terms[::2], terms[1::2])]
        terms = pairs + terms[2 * len(pairs) :]
    shrunk = terms[0].astype(jnp.bfloat16)
    halves = (shrunk[:, :rank], shrunk[:, rank:])
    pieces = HD // features

    def rows(i, first, count):
        parts = [box[i * pieces + p, first : first + count, :features] for p in range(pieces)]
        return parts[0] if pieces == 1 else jnp.concatenate(parts, axis=1)

    def fresh(first):
        made = []
        for i in range(first, first + KVH, 2):
            ups = jnp.concatenate([rows(i + j, 2 * CAPT, rank) for j in range(2)], axis=1)
            delta = jnp.dot(halves[first // KVH], ups, preferred_element_type=jnp.float32)
            for j in range(2):
                base = rows(i + j, CAPT, CAPT).astype(jnp.float32)
                both = base + ADAPTER_SCALE * delta[:, j * HD : (j + 1) * HD]
                made.append(both.astype(jnp.bfloat16))
        return jnp.concatenate(made, axis=0)

    keys = fresh(0)
    values_t = fresh(KVH).T
    scale = HD ** (-0.5)
    part = out.shape[0] // sems.shape[0]
    copies = []
    for c in range(sems.shape[0]):
        here = pl.ds(c * part, part)
        s = jnp.dot(keys, query_t[:, here], preferred_element_type=jnp.float32)
        s = jnp.where(fresh_ok[:, here] > 0, s * scale, NEG_LARGE)
        old = top_t[:1, here]
        top = jnp.maximum(old, jnp.max(s, axis=0, keepdims=True))
        fade = jnp.exp(old - top)
        w = jnp.exp(s - top)
        total = total_t[:1, here] * fade + jnp.sum(w, axis=0, keepdims=True)
        mixed = acc_t[:, here] * fade + jnp.dot(
            values_t, w.astype(jnp.bfloat16), preferred_element_type=jnp.float32
        )
        result[here, :] = (mixed / total).T.astype(jnp.bfloat16)
        copies.append(pltpu.make_async_copy(result.at[here, :], out.at[here, :], sems.at[c]))
        copies[c].start()
    for copy in copies:
        copy.wait()


def body(
    hidden,
    key_value_weight,
    adapter_down_weight,
    adapter_up_weight,
    tenant,
    tenant_page_table,
    request_block_count,
    last_block_tokens,
    placement,
    key_value_cache,
    context_length,
    decode_step_query,
    step_key_value,
):
    devices = lax.axis_size("tensor")
    tokens, width = hidden.shape
    features = key_value_weight.shape[0]
    local, pages, rank2 = adapter_down_weight.shape
    rank = adapter_up_weight.shape[2]
    tenants = tenant_page_table.shape[0]
    dec_rows, ctx, kv_width = key_value_cache.shape
    steps = step_key_value.shape[0]
    heads2 = kv_width // HD
    d_chunks, chunks = 4, 2
    up_by_page = jnp.transpose(adapter_up_weight, (1, 2, 0))
    rows = 2 * CAPT + rank
    query = decode_step_query.reshape(steps, dec_rows, HEADS, HD)
    query = query.transpose(0, 2, 1, 3).reshape(steps * HEADS * dec_rows, HD)
    steps_kv = step_key_value.reshape(steps, dec_rows, heads2, HD)
    steps_kv = steps_kv.transpose(0, 2, 1, 3).reshape(steps * heads2 * dec_rows, HD)
    q_rows = steps * HEADS * dec_rows
    outgoing, *handed = pl.pallas_call(
        functools.partial(front_kernel, dec_rows, d_chunks, chunks, devices),
        out_shape=(
            pltpu.VMEM((devices, rows, HD), WIRE),
            pltpu.VMEM((HD, q_rows), jnp.bfloat16),
            pltpu.VMEM((HD, q_rows), jnp.float32),
            pltpu.VMEM((8, q_rows), jnp.float32),
            pltpu.VMEM((8, q_rows), jnp.float32),
            pltpu.VMEM((KVH * CAPT, q_rows), jnp.float32),
        ),
        in_specs=[ANY_SPEC] * 13,
        out_specs=(VMEM_SPEC,) * 6,
        scratch_shapes=[
            pltpu.SMEM(tenant.shape, jnp.int32),
            pltpu.SMEM(tenant_page_table.shape, jnp.int32),
            pltpu.SMEM(request_block_count.shape, jnp.int32),
            pltpu.SMEM(placement.shape, jnp.int32),
            pltpu.SMEM(context_length.shape, jnp.int32),
            pltpu.SMEM(last_block_tokens.shape, jnp.int32),
            pltpu.VMEM((chunks, tokens, width // chunks), jnp.bfloat16),
            pltpu.VMEM((chunks, features, width // chunks), jnp.bfloat16),
            pltpu.VMEM((local, pages, rank2), jnp.bfloat16),
            pltpu.VMEM((tokens, local), jnp.bfloat16),
            pltpu.VMEM((pages, rank, features), jnp.bfloat16),
            pltpu.VMEM((local // 16, tenants * 16, rank2), jnp.bfloat16),
            pltpu.VMEM((tenants, tokens + BLK, rank2), jnp.float32),
            pltpu.VMEM((tokens + BLK, HD), jnp.float32),
            pltpu.SMEM((2, devices), jnp.int32),
            pltpu.SemaphoreType.DMA((chunks, 2)),
            pltpu.SemaphoreType.DMA((d_chunks + 2,)),
            pltpu.SemaphoreType.DMA((6,)),
            pltpu.VMEM(key_value_cache.shape, jnp.bfloat16),
            pltpu.VMEM(query.shape, jnp.bfloat16),
            pltpu.VMEM(steps_kv.shape, jnp.bfloat16),
            pltpu.VMEM((q_rows, HD), jnp.float32),
            pltpu.VMEM((q_rows, HD), jnp.float32),
            pltpu.VMEM((q_rows, HD), jnp.float32),
            pltpu.SemaphoreType.DMA((3,)),
        ],
        compiler_params=pltpu.CompilerParams(vmem_limit_bytes=PROJECT_VMEM),
        name="front",
    )(
        *(
            pltpu.with_memory_space_constraint(x, pltpu.HBM)
            for x in (
                tenant, tenant_page_table, request_block_count, placement,
                context_length, last_block_tokens,
                hidden, key_value_weight, adapter_down_weight, up_by_page,
                key_value_cache, query, steps_kv,
            )
        )
    )
    arrived = lax.all_to_all(
        outgoing, "tensor", split_axis=0, concat_axis=0,
        axis_index_groups=[list(range(devices))], tiled=True,
    )
    attended = pl.pallas_call(
        functools.partial(merge_kernel, features),
        out_shape=jax.ShapeDtypeStruct((q_rows, HD), jnp.bfloat16),
        in_specs=[VMEM_SPEC] * 6,
        out_specs=ANY_SPEC,
        scratch_shapes=[
            pltpu.VMEM((q_rows, HD), jnp.bfloat16),
            pltpu.SemaphoreType.DMA((steps,)),
        ],
        compiler_params=pltpu.CompilerParams(vmem_limit_bytes=ATTEND_VMEM),
        name="merge",
    )(arrived, *handed)
    attended = attended.reshape(steps, HEADS, dec_rows, HD).transpose(0, 2, 1, 3)
    return attended.reshape(steps, dec_rows, HEADS * HD)


def solution(mesh):
    return jax.shard_map(
        body,
        mesh=mesh,
        in_specs=(
            P("parts", None),
            P("tensor", None),
            P("tensor", None, None),
            P("tensor", None, None),
            P("parts"),
            P(),
            P("parts"),
            P("parts"),
            P("parts"),
            P(("parts", "tensor"), None, None),
            P(("parts", "tensor")),
            P(None, ("parts", "tensor"), None),
            P(None, ("parts", "tensor"), None),
        ),
        out_specs=P(None, ("parts", "tensor"), None),
        check_vma=False,
    )
```

```python
import functools

import jax
import jax.numpy as jnp
from jax import lax
from jax.experimental import pallas as pl
from jax.experimental.pallas import tpu as pltpu
from jax.sharding import PartitionSpec as P

HEADS = 64
KVH = 8
HD = 128
BLK = 8
MOSTB = 2
CAPT = MOSTB * BLK
ADAPTER_SCALE = 0.5
NEG_LARGE = -1e30
PROJECT_VMEM = 32 * 1024 * 1024
ATTEND_VMEM = 16 * 1024 * 1024
WIRE = jnp.bfloat16

SMEM_SPEC = pl.BlockSpec(memory_space=pltpu.SMEM)
VMEM_SPEC = pl.BlockSpec(memory_space=pltpu.VMEM)
ANY_SPEC = pl.BlockSpec(memory_space=pl.ANY)


def div(x, n):
    shift = n.bit_length() - 1
    return lax.shift_right_logical(x, shift) if n == 1 << shift else x // n


def mod(x, n):
    return x & (n - 1) if n & (n - 1) == 0 else x % n


def project_kernel(
    dec_rows, d_chunks, chunks, devices, tenant_h, table_h, counts_h, placement_h, hidden, weight, down, up, out,
    tenant, table, counts, placement,
    h_s, w_s, d_s, mine_s, u_s, sel_s, part_s, base_s, out_s, dest_table, sems, d_sems, int_sems,
    out_sems,
):
    tokens, width = hidden.shape
    features = weight.shape[0]
    local, pages, rank2 = down.shape
    tenants = table.shape[0]
    rank = up.shape[1]
    requests = tenant.shape[0]
    me = lax.axis_index("tensor")
    d_step = local // d_chunks
    step = width // chunks

    int_copies = [
        pltpu.make_async_copy(src, dst, int_sems.at[i])
        for i, (src, dst) in enumerate(
            ((table_h, table), (tenant_h, tenant), (counts_h, counts), (placement_h, placement))
        )
    ]
    for copy in int_copies:
        copy.start()
    def d_copy(c):
        rows = pl.ds(c * d_step, d_step)
        return pltpu.make_async_copy(down.at[rows], d_s.at[rows], d_sems.at[c])

    h_copies = [
        pltpu.make_async_copy(hidden.at[:, pl.ds(c * step, step)], h_s.at[c], sems.at[c, 0])
        for c in range(chunks)
    ]
    w_copies = [
        pltpu.make_async_copy(weight.at[:, pl.ds(c * step, step)], w_s.at[c], sems.at[c, 1])
        for c in range(chunks)
    ]
    my_copy = pltpu.make_async_copy(
        hidden.at[:, pl.ds(pl.multiple_of(me * local, 128), local)], mine_s, d_sems.at[d_chunks]
    )
    up_copy = pltpu.make_async_copy(up, u_s, d_sems.at[d_chunks + 1])
    for copy in [d_copy(c) for c in range(d_chunks)] + [my_copy, up_copy]:
        copy.start()
    for c in range(chunks):
        h_copies[c].start()
        w_copies[c].start()

    int_copies[0].wait()
    rows = lax.broadcasted_iota(jnp.int32, (tenants * 16, 16 * pages), 0)
    cols = lax.broadcasted_iota(jnp.int32, (tenants * 16, 16 * pages), 1)
    page_of_row = jnp.zeros_like(rows)
    for k in range(tenants):
        page_of_row = jnp.where(div(rows, 16) == k, table[k], page_of_row)
    pick = (mod(rows, 16) == div(cols, pages)) & (mod(cols, pages) == page_of_row)
    pick = jnp.where(pick, jnp.float32(1), jnp.float32(0)).astype(jnp.bfloat16)

    blocks = d_step // 16

    def select(c, carry):
        d_copy(c).wait()
        for b in range(0, blocks, 2):
            block = jnp.concatenate(
                [
                    d_s[pl.ds(c * d_step + (b + i) * 16, 16)].reshape(16 * pages, rank2)
                    for i in range(2)
                ],
                axis=1,
            )
            chosen = jnp.dot(pick, block, preferred_element_type=jnp.float32)
            for i in range(2):
                sel_s[c * blocks + b + i] = chosen[:, i * rank2 : (i + 1) * rank2].astype(
                    jnp.bfloat16
                )
        return carry

    lax.fori_loop(0, d_chunks, select, 0)
    for copy in int_copies[1:]:
        copy.wait()
    for dest in range(devices):
        dest_table[0, dest] = 0
        dest_table[1, dest] = 0
    first = jnp.int32(0)
    for r in range(requests):
        dest = div(placement[r], dec_rows)
        dest_table[0, dest] = first * BLK
        dest_table[1, dest] = tenant[r]
        first = first + counts[r]
    up_copy.wait()
    whole = features == HD
    sent = []
    my_copy.wait()
    mine = mine_s[...]
    for k in range(0, tenants, 2):
        pair = min(2, tenants - k)
        maps = jnp.concatenate(
            [sel_s[:, j * 16 : (j + 1) * 16, :].reshape(local, rank2) for j in range(k, k + pair)],
            axis=1,
        )
        product = jnp.dot(mine, maps, preferred_element_type=jnp.float32)
        for j in range(pair):
            part_s[k + j, :tokens] = product[:, j * rank2 : (j + 1) * rank2]
            part_s[k + j, tokens:] = jnp.zeros((BLK, rank2), jnp.float32)

    for dest in range(devices):
        start = pl.multiple_of(dest_table[0, dest], BLK)
        who = dest_table[1, dest]
        out_s[dest, :CAPT, :] = part_s[who, pl.ds(start, CAPT), :].astype(out.dtype)
        if not whole:
            out_s[dest, 2 * CAPT :, :] = jnp.zeros((rank, HD), out.dtype)
        out_s[dest, 2 * CAPT :, :features] = u_s[table[who]]
    for i, lines in enumerate((pl.ds(0, CAPT), pl.ds(2 * CAPT, rank))):
        sent.append(pltpu.make_async_copy(
            out_s.at[:, lines, :], out.at[:, lines, :], out_sems.at[i]))
        sent[-1].start()

    total = jnp.zeros((tokens, features), jnp.float32)
    for c in range(chunks):
        h_copies[c].wait()
        w_copies[c].wait()
        total = total + lax.dot_general(h_s[c], w_s[c], NT, preferred_element_type=jnp.float32)
    base_s[tokens:] = jnp.zeros((BLK, HD), jnp.float32)
    if features < HD:
        base_s[...] = jnp.zeros_like(base_s)
    base_s[:tokens, :features] = total
    for dest in range(devices):
        start = pl.multiple_of(dest_table[0, dest], BLK)
        out_s[dest, CAPT : 2 * CAPT, :] = base_s[pl.ds(start, CAPT), :].astype(out.dtype)
    lines = pl.ds(CAPT, CAPT)
    sent.append(pltpu.make_async_copy(
        out_s.at[:, lines, :], out.at[:, lines, :], out_sems.at[2]))
    sent[-1].start()
    for copy in sent:
        copy.wait()


NT = (((1,), (1,)), ((), ()))


def gather_queries(query, k, group, steps, stride):
    return jnp.concatenate(
        [query[pl.ds(s * stride + k * group, group), :] for s in range(steps)], axis=0
    )


def cached_kernel(
    lengths, counts, last, placement, cache, query, steps_kv,
    query_t, acc_t, top_t, total_t, fresh_ok, acc, top_out, total_out,
):
    dec_rows, ctx, kv_width = cache.shape
    half_width = kv_width // 2
    step_rows = KVH * dec_rows
    steps = steps_kv.shape[0] // (2 * step_rows)
    group = HEADS // KVH * dec_rows
    q_rows = steps * group
    stride = HEADS * dec_rows

    row = lax.broadcasted_iota(jnp.int32, (q_rows, ctx), 0)
    col = lax.broadcasted_iota(jnp.int32, (q_rows, ctx), 1)
    row_slot = mod(row, dec_rows)
    cache_ok = [(row_slot == g) & (col < lengths[g]) for g in range(dec_rows)]
    row = lax.broadcasted_iota(jnp.int32, (q_rows, steps * step_rows), 0)
    col = lax.broadcasted_iota(jnp.int32, (q_rows, steps * step_rows), 1)
    step_ok = (mod(row, dec_rows) == mod(col, dec_rows)) & (div(col, step_rows) <= div(row, group))
    step_head = div(mod(col, step_rows), dec_rows)
    step_keys, step_values = (
        jnp.concatenate(
            [steps_kv[pl.ds((2 * s + half) * step_rows, step_rows), :] for s in range(steps)], axis=0
        )
        for half in range(2)
    )

    scale = HD ** (-0.5)
    for k in range(KVH):
        lanes = pl.ds(k * HD, HD)
        vlanes = pl.ds(half_width + k * HD, HD)
        q = gather_queries(query, k, group, steps, stride)
        keys = [cache[g, :, lanes] for g in range(dec_rows)] + [step_keys]
        values = [cache[g, :, vlanes] for g in range(dec_rows)] + [step_values]
        scores = [
            jnp.where(
                ok,
                lax.dot_general(q, key, NT, preferred_element_type=jnp.float32) * scale,
                NEG_LARGE,
            )
            for ok, key in zip(cache_ok + [step_ok & (step_head == k)], keys)
        ]
        top = functools.reduce(jnp.maximum, [jnp.max(s, axis=1, keepdims=True) for s in scores])
        weights = [jnp.exp(s - top) for s in scores]
        total = sum(jnp.sum(w, axis=1, keepdims=True) for w in weights)
        mixed = sum(
            jnp.dot(w.astype(jnp.bfloat16), v, preferred_element_type=jnp.float32)
            for w, v in zip(weights, values)
        )
        for s in range(steps):
            here = pl.ds(s * stride + k * group, group)
            part = slice(s * group, (s + 1) * group)
            acc[here, :] = mixed[part]
            top_out[here, :] = jnp.broadcast_to(top[part], (group, HD))
            total_out[here, :] = jnp.broadcast_to(total[part], (group, HD))

    my_slot = jnp.int32(-1)
    my_length = jnp.int32(0)
    for r in range(placement.shape[0]):
        hit = div(placement[r], dec_rows) == lax.axis_index("tensor")
        my_slot = jnp.where(hit, mod(placement[r], dec_rows), my_slot)
        my_length = jnp.where(hit, (counts[r] - 1) * BLK + last[r], my_length)
    col = lax.broadcasted_iota(jnp.int32, fresh_ok.shape, 0)
    row = lax.broadcasted_iota(jnp.int32, fresh_ok.shape, 1)
    ok = (
        (mod(div(row, group), KVH) == div(col, CAPT))
        & (mod(row, dec_rows) == my_slot)
        & (mod(col, CAPT) < my_length)
    )
    fresh_ok[...] = jnp.where(ok, jnp.float32(1), jnp.float32(0))
    query_t[...] = query[...].T
    acc_t[...] = acc[...].T
    top_t[...] = top_out[...].T[: top_t.shape[0]]
    total_t[...] = total_out[...].T[: total_t.shape[0]]


def merge_kernel(features, box, query_t, acc_t, top_t, total_t, fresh_ok, out, result, sems):
    devices = box.shape[0]
    rank = box.shape[1] - 2 * CAPT
    terms = [box[i, :CAPT].astype(jnp.float32) for i in range(devices)]
    while len(terms) > 1:
        pairs = [a + b for a, b in zip(terms[::2], terms[1::2])]
        terms = pairs + terms[2 * len(pairs) :]
    shrunk = terms[0].astype(jnp.bfloat16)
    halves = (shrunk[:, :rank], shrunk[:, rank:])
    pieces = HD // features

    def rows(i, first, count):
        parts = [box[i * pieces + p, first : first + count, :features] for p in range(pieces)]
        return parts[0] if pieces == 1 else jnp.concatenate(parts, axis=1)

    def fresh(first):
        made = []
        for i in range(first, first + KVH, 2):
            ups = jnp.concatenate([rows(i + j, 2 * CAPT, rank) for j in range(2)], axis=1)
            delta = jnp.dot(halves[first // KVH], ups, preferred_element_type=jnp.float32)
            for j in range(2):
                base = rows(i + j, CAPT, CAPT).astype(jnp.float32)
                both = base + ADAPTER_SCALE * delta[:, j * HD : (j + 1) * HD]
                made.append(both.astype(jnp.bfloat16))
        return jnp.concatenate(made, axis=0)

    keys = fresh(0)
    values_t = fresh(KVH).T
    scale = HD ** (-0.5)
    part = out.shape[0] // sems.shape[0]
    copies = []
    for c in range(sems.shape[0]):
        here = pl.ds(c * part, part)
        s = jnp.dot(keys, query_t[:, here], preferred_element_type=jnp.float32)
        s = jnp.where(fresh_ok[:, here] > 0, s * scale, NEG_LARGE)
        old = top_t[:1, here]
        top = jnp.maximum(old, jnp.max(s, axis=0, keepdims=True))
        fade = jnp.exp(old - top)
        w = jnp.exp(s - top)
        total = total_t[:1, here] * fade + jnp.sum(w, axis=0, keepdims=True)
        mixed = acc_t[:, here] * fade + jnp.dot(
            values_t, w.astype(jnp.bfloat16), preferred_element_type=jnp.float32
        )
        result[here, :] = (mixed / total).T.astype(jnp.bfloat16)
        copies.append(pltpu.make_async_copy(result.at[here, :], out.at[here, :], sems.at[c]))
        copies[c].start()
    for copy in copies:
        copy.wait()


def body(
    hidden,
    key_value_weight,
    adapter_down_weight,
    adapter_up_weight,
    tenant,
    tenant_page_table,
    request_block_count,
    last_block_tokens,
    placement,
    key_value_cache,
    context_length,
    decode_step_query,
    step_key_value,
):
    devices = lax.axis_size("tensor")
    tokens, width = hidden.shape
    features = key_value_weight.shape[0]
    local, pages, rank2 = adapter_down_weight.shape
    rank = adapter_up_weight.shape[2]
    tenants = tenant_page_table.shape[0]
    dec_rows, ctx, kv_width = key_value_cache.shape
    steps = step_key_value.shape[0]
    heads2 = kv_width // HD
    d_chunks, chunks = 4, 2
    up_by_page = jnp.transpose(adapter_up_weight, (1, 2, 0))
    rows = 2 * CAPT + rank
    outgoing = pl.pallas_call(
        functools.partial(project_kernel, dec_rows, d_chunks, chunks, devices),
        out_shape=jax.ShapeDtypeStruct((devices, rows, HD), WIRE),
        in_specs=[ANY_SPEC] * 8,
        out_specs=ANY_SPEC,
        scratch_shapes=[
            pltpu.SMEM(tenant.shape, jnp.int32),
            pltpu.SMEM(tenant_page_table.shape, jnp.int32),
            pltpu.SMEM(request_block_count.shape, jnp.int32),
            pltpu.SMEM(placement.shape, jnp.int32),
            pltpu.VMEM((chunks, tokens, width // chunks), jnp.bfloat16),
            pltpu.VMEM((chunks, features, width // chunks), jnp.bfloat16),
            pltpu.VMEM((local, pages, rank2), jnp.bfloat16),
            pltpu.VMEM((tokens, local), jnp.bfloat16),
            pltpu.VMEM((pages, rank, features), jnp.bfloat16),
            pltpu.VMEM((local // 16, tenants * 16, rank2), jnp.bfloat16),
            pltpu.VMEM((tenants, tokens + BLK, rank2), jnp.float32),
            pltpu.VMEM((tokens + BLK, HD), jnp.float32),
            pltpu.VMEM((devices, rows, HD), WIRE),
            pltpu.SMEM((2, devices), jnp.int32),
            pltpu.SemaphoreType.DMA((chunks, 2)),
            pltpu.SemaphoreType.DMA((d_chunks + 2,)),
            pltpu.SemaphoreType.DMA((4,)),
            pltpu.SemaphoreType.DMA((3,)),
        ],
        compiler_params=pltpu.CompilerParams(vmem_limit_bytes=PROJECT_VMEM),
        name="project",
    )(
        *(
            pltpu.with_memory_space_constraint(x, pltpu.HBM)
            for x in (
                tenant, tenant_page_table, request_block_count, placement,
                hidden, key_value_weight, adapter_down_weight, up_by_page,
            )
        )
    )
    arrived = lax.all_to_all(outgoing, "tensor", split_axis=0, concat_axis=0, tiled=True)

    query = decode_step_query.reshape(steps, dec_rows, HEADS, HD)
    query = query.transpose(0, 2, 1, 3).reshape(steps * HEADS * dec_rows, HD)
    steps_kv = step_key_value.reshape(steps, dec_rows, heads2, HD)
    steps_kv = steps_kv.transpose(0, 2, 1, 3).reshape(steps * heads2 * dec_rows, HD)
    q_rows = steps * HEADS * dec_rows
    state = jax.ShapeDtypeStruct((HD, q_rows), jnp.float32)
    line = jax.ShapeDtypeStruct((8, q_rows), jnp.float32)
    handed = pl.pallas_call(
        cached_kernel,
        out_shape=(
            jax.ShapeDtypeStruct((HD, q_rows), jnp.bfloat16),
            state,
            line,
            line,
            jax.ShapeDtypeStruct((KVH * CAPT, q_rows), jnp.float32),
        ),
        in_specs=[SMEM_SPEC] * 4 + [VMEM_SPEC] * 3,
        out_specs=(VMEM_SPEC,) * 5,
        scratch_shapes=[pltpu.VMEM((q_rows, HD), jnp.float32)] * 3,
        compiler_params=pltpu.CompilerParams(vmem_limit_bytes=ATTEND_VMEM),
        name="cached",
    )(
        context_length, request_block_count, last_block_tokens, placement,
        key_value_cache, query, steps_kv,
    )
    attended = pl.pallas_call(
        functools.partial(merge_kernel, features),
        out_shape=jax.ShapeDtypeStruct((q_rows, HD), jnp.bfloat16),
        in_specs=[VMEM_SPEC] * 6,
        out_specs=ANY_SPEC,
        scratch_shapes=[
            pltpu.VMEM((q_rows, HD), jnp.bfloat16),
            pltpu.SemaphoreType.DMA((steps,)),
        ],
        compiler_params=pltpu.CompilerParams(vmem_limit_bytes=ATTEND_VMEM),
        name="merge",
    )(arrived, *handed)
    attended = attended.reshape(steps, HEADS, dec_rows, HD).transpose(0, 2, 1, 3)
    return attended.reshape(steps, dec_rows, HEADS * HD)


def solution(mesh):
    return jax.shard_map(
        body,
        mesh=mesh,
        in_specs=(
            P("parts", None),
            P("tensor", None),
            P("tensor", None, None),
            P("tensor", None, None),
            P("parts"),
            P(),
            P("parts"),
            P("parts"),
            P("parts"),
            P(("parts", "tensor"), None, None),
            P(("parts", "tensor")),
            P(None, ("parts", "tensor"), None),
            P(None, ("parts", "tensor"), None),
        ),
        out_specs=P(None, ("parts", "tensor"), None),
        check_vma=False,
    )
```

```python
import functools

import jax
import jax.numpy as jnp
from jax import lax
from jax.experimental import pallas as pl
from jax.experimental.pallas import tpu as pltpu
from jax.sharding import PartitionSpec as P

HEADS = 64
KVH = 8
HD = 128
BLK = 8
MOSTB = 2
CAPT = MOSTB * BLK
ADAPTER_SCALE = 0.5
NEG_LARGE = -1e30
PROJECT_VMEM = 32 * 1024 * 1024
ATTEND_VMEM = 16 * 1024 * 1024
WIRE = jnp.bfloat16

SMEM_SPEC = pl.BlockSpec(memory_space=pltpu.SMEM)
VMEM_SPEC = pl.BlockSpec(memory_space=pltpu.VMEM)
ANY_SPEC = pl.BlockSpec(memory_space=pl.ANY)


def div(x, n):
    shift = n.bit_length() - 1
    return lax.shift_right_logical(x, shift) if n == 1 << shift else x // n


def mod(x, n):
    return x & (n - 1) if n & (n - 1) == 0 else x % n


def project_kernel(
    dec_rows, d_chunks, chunks, devices, tenant_h, table_h, counts_h, placement_h, hidden, weight, down, up, out,
    tenant, table, counts, placement,
    h_s, w_s, d_s, mine_s, u_s, sel_s, part_s, base_s, dest_table, sems, d_sems, int_sems,
):
    tokens, width = hidden.shape
    features = weight.shape[0]
    local, pages, rank2 = down.shape
    tenants = table.shape[0]
    requests = tenant.shape[0]
    me = lax.axis_index("tensor")
    d_step = local // d_chunks
    step = width // chunks

    int_copies = [
        pltpu.make_async_copy(src, dst, int_sems.at[i])
        for i, (src, dst) in enumerate(
            ((table_h, table), (tenant_h, tenant), (counts_h, counts), (placement_h, placement))
        )
    ]
    for copy in int_copies:
        copy.start()
    def d_copy(c):
        rows = pl.ds(c * d_step, d_step)
        return pltpu.make_async_copy(down.at[rows], d_s.at[rows], d_sems.at[c])

    h_copies = [
        pltpu.make_async_copy(hidden.at[:, pl.ds(c * step, step)], h_s.at[c], sems.at[c, 0])
        for c in range(chunks)
    ]
    w_copies = [
        pltpu.make_async_copy(weight.at[:, pl.ds(c * step, step)], w_s.at[c], sems.at[c, 1])
        for c in range(chunks)
    ]
    my_copy = pltpu.make_async_copy(
        hidden.at[:, pl.ds(pl.multiple_of(me * local, 128), local)], mine_s, d_sems.at[d_chunks]
    )
    up_copy = pltpu.make_async_copy(up, u_s, d_sems.at[d_chunks + 1])
    for copy in [d_copy(c) for c in range(d_chunks)] + [my_copy, up_copy]:
        copy.start()

    int_copies[0].wait()
    rows = lax.broadcasted_iota(jnp.int32, (tenants * 16, 16 * pages), 0)
    cols = lax.broadcasted_iota(jnp.int32, (tenants * 16, 16 * pages), 1)
    page_of_row = jnp.zeros_like(rows)
    for k in range(tenants):
        page_of_row = jnp.where(div(rows, 16) == k, table[k], page_of_row)
    pick = (mod(rows, 16) == div(cols, pages)) & (mod(cols, pages) == page_of_row)
    pick = jnp.where(pick, jnp.float32(1), jnp.float32(0)).astype(jnp.bfloat16)

    blocks = d_step // 16

    def select(c, carry):
        for b in range(0, blocks, 2):
            block = jnp.concatenate(
                [
                    d_s[pl.ds(c * d_step + (b + i) * 16, 16)].reshape(16 * pages, rank2)
                    for i in range(2)
                ],
                axis=1,
            )
            chosen = jnp.dot(pick, block, preferred_element_type=jnp.float32)
            for i in range(2):
                sel_s[c * blocks + b + i] = chosen[:, i * rank2 : (i + 1) * rank2].astype(
                    jnp.bfloat16
                )
        return carry

    for c in range(d_chunks):
        d_copy(c).wait()
        if c == 0:
            for h_copy, w_copy in zip(h_copies, w_copies):
                h_copy.start()
                w_copy.start()
        select(c, 0)
    for copy in int_copies[1:]:
        copy.wait()
    for dest in range(devices):
        dest_table[0, dest] = 0
        dest_table[1, dest] = 0
    first = jnp.int32(0)
    for r in range(requests):
        dest = div(placement[r], dec_rows)
        dest_table[0, dest] = first * BLK
        dest_table[1, dest] = tenant[r]
        first = first + counts[r]
    my_copy.wait()
    mine = mine_s[...]
    for k in range(0, tenants, 2):
        pair = min(2, tenants - k)
        maps = jnp.concatenate(
            [sel_s[:, j * 16 : (j + 1) * 16, :].reshape(local, rank2) for j in range(k, k + pair)],
            axis=1,
        )
        product = jnp.dot(mine, maps, preferred_element_type=jnp.float32)
        for j in range(pair):
            part_s[k + j, :tokens] = product[:, j * rank2 : (j + 1) * rank2]
            part_s[k + j, tokens:] = jnp.zeros((BLK, rank2), jnp.float32)

    total = jnp.zeros((tokens, features), jnp.float32)
    for c in range(chunks):
        h_copies[c].wait()
        w_copies[c].wait()
        total = total + lax.dot_general(h_s[c], w_s[c], NT, preferred_element_type=jnp.float32)
    base_s[tokens:] = jnp.zeros((BLK, HD), jnp.float32)
    if features < HD:
        base_s[...] = jnp.zeros_like(base_s)
    base_s[:tokens, :features] = total
    up_copy.wait()

    def lay_out(first, carry):
        for i in range(4):
            dest = first * 4 + i
            start = pl.multiple_of(dest_table[0, dest], BLK)
            who = dest_table[1, dest]
            out[dest, :CAPT, :] = part_s[who, pl.ds(start, CAPT), :].astype(out.dtype)
            out[dest, CAPT : 2 * CAPT, :] = base_s[pl.ds(start, CAPT), :].astype(out.dtype)
            if features < HD:
                out[dest, 2 * CAPT :, :] = jnp.zeros((out.shape[1] - 2 * CAPT, HD), out.dtype)
            out[dest, 2 * CAPT :, :features] = u_s[table[who]]
        return carry

    lax.fori_loop(0, devices // 4, lay_out, 0)


NT = (((1,), (1,)), ((), ()))


def gather_queries(query, k, group, steps, stride):
    return jnp.concatenate(
        [query[pl.ds(s * stride + k * group, group), :] for s in range(steps)], axis=0
    )


def cached_kernel(
    lengths, counts, last, placement, cache, query, steps_kv,
    query_t, acc_t, top_t, total_t, fresh_ok, acc, top_out, total_out,
):
    dec_rows, ctx, kv_width = cache.shape
    half_width = kv_width // 2
    step_rows = KVH * dec_rows
    steps = steps_kv.shape[0] // (2 * step_rows)
    group = HEADS // KVH * dec_rows
    q_rows = steps * group
    stride = HEADS * dec_rows

    row = lax.broadcasted_iota(jnp.int32, (q_rows, ctx), 0)
    col = lax.broadcasted_iota(jnp.int32, (q_rows, ctx), 1)
    row_slot = mod(row, dec_rows)
    cache_ok = [(row_slot == g) & (col < lengths[g]) for g in range(dec_rows)]
    row = lax.broadcasted_iota(jnp.int32, (q_rows, steps * step_rows), 0)
    col = lax.broadcasted_iota(jnp.int32, (q_rows, steps * step_rows), 1)
    step_ok = (mod(row, dec_rows) == mod(col, dec_rows)) & (div(col, step_rows) <= div(row, group))
    step_head = div(mod(col, step_rows), dec_rows)
    step_keys, step_values = (
        jnp.concatenate(
            [steps_kv[pl.ds((2 * s + half) * step_rows, step_rows), :] for s in range(steps)], axis=0
        )
        for half in range(2)
    )

    scale = HD ** (-0.5)
    for k in range(KVH):
        lanes = pl.ds(k * HD, HD)
        vlanes = pl.ds(half_width + k * HD, HD)
        q = gather_queries(query, k, group, steps, stride)
        keys = [cache[g, :, lanes] for g in range(dec_rows)] + [step_keys]
        values = [cache[g, :, vlanes] for g in range(dec_rows)] + [step_values]
        scores = [
            jnp.where(
                ok,
                lax.dot_general(q, key, NT, preferred_element_type=jnp.float32) * scale,
                NEG_LARGE,
            )
            for ok, key in zip(cache_ok + [step_ok & (step_head == k)], keys)
        ]
        top = functools.reduce(jnp.maximum, [jnp.max(s, axis=1, keepdims=True) for s in scores])
        weights = [jnp.exp(s - top) for s in scores]
        total = sum(jnp.sum(w, axis=1, keepdims=True) for w in weights)
        mixed = sum(
            jnp.dot(w.astype(jnp.bfloat16), v, preferred_element_type=jnp.float32)
            for w, v in zip(weights, values)
        )
        for s in range(steps):
            here = pl.ds(s * stride + k * group, group)
            part = slice(s * group, (s + 1) * group)
            acc[here, :] = mixed[part]
            top_out[here, :] = jnp.broadcast_to(top[part], (group, HD))
            total_out[here, :] = jnp.broadcast_to(total[part], (group, HD))

    my_slot = jnp.int32(-1)
    my_length = jnp.int32(0)
    for r in range(placement.shape[0]):
        hit = div(placement[r], dec_rows) == lax.axis_index("tensor")
        my_slot = jnp.where(hit, mod(placement[r], dec_rows), my_slot)
        my_length = jnp.where(hit, (counts[r] - 1) * BLK + last[r], my_length)
    col = lax.broadcasted_iota(jnp.int32, fresh_ok.shape, 0)
    row = lax.broadcasted_iota(jnp.int32, fresh_ok.shape, 1)
    ok = (
        (mod(div(row, group), KVH) == div(col, CAPT))
        & (mod(row, dec_rows) == my_slot)
        & (mod(col, CAPT) < my_length)
    )
    fresh_ok[...] = jnp.where(ok, jnp.float32(1), jnp.float32(0))
    query_t[...] = query[...].T
    acc_t[...] = acc[...].T
    top_t[...] = top_out[...].T[: top_t.shape[0]]
    total_t[...] = total_out[...].T[: total_t.shape[0]]


def merge_kernel(features, box, query_t, acc_t, top_t, total_t, fresh_ok, out, result, sems):
    devices = box.shape[0]
    rank = box.shape[1] - 2 * CAPT
    terms = [box[i, :CAPT].astype(jnp.float32) for i in range(devices)]
    while len(terms) > 1:
        pairs = [a + b for a, b in zip(terms[::2], terms[1::2])]
        terms = pairs + terms[2 * len(pairs) :]
    shrunk = terms[0].astype(jnp.bfloat16)
    halves = (shrunk[:, :rank], shrunk[:, rank:])
    pieces = HD // features

    def rows(i, first, count):
        parts = [box[i * pieces + p, first : first + count, :features] for p in range(pieces)]
        return parts[0] if pieces == 1 else jnp.concatenate(parts, axis=1)

    def fresh(first):
        made = []
        for i in range(first, first + KVH, 2):
            ups = jnp.concatenate([rows(i + j, 2 * CAPT, rank) for j in range(2)], axis=1)
            delta = jnp.dot(halves[first // KVH], ups, preferred_element_type=jnp.float32)
            for j in range(2):
                base = rows(i + j, CAPT, CAPT).astype(jnp.float32)
                both = base + ADAPTER_SCALE * delta[:, j * HD : (j + 1) * HD]
                made.append(both.astype(jnp.bfloat16))
        return jnp.concatenate(made, axis=0)

    keys = fresh(0)
    values_t = fresh(KVH).T
    scale = HD ** (-0.5)
    part = out.shape[0] // sems.shape[0]
    copies = []
    for c in range(sems.shape[0]):
        here = pl.ds(c * part, part)
        s = jnp.dot(keys, query_t[:, here], preferred_element_type=jnp.float32)
        s = jnp.where(fresh_ok[:, here] > 0, s * scale, NEG_LARGE)
        old = top_t[:1, here]
        top = jnp.maximum(old, jnp.max(s, axis=0, keepdims=True))
        fade = jnp.exp(old - top)
        w = jnp.exp(s - top)
        total = total_t[:1, here] * fade + jnp.sum(w, axis=0, keepdims=True)
        mixed = acc_t[:, here] * fade + jnp.dot(
            values_t, w.astype(jnp.bfloat16), preferred_element_type=jnp.float32
        )
        result[here, :] = (mixed / total).T.astype(jnp.bfloat16)
        copies.append(pltpu.make_async_copy(result.at[here, :], out.at[here, :], sems.at[c]))
        copies[c].start()
    for copy in copies:
        copy.wait()


def body(
    hidden,
    key_value_weight,
    adapter_down_weight,
    adapter_up_weight,
    tenant,
    tenant_page_table,
    request_block_count,
    last_block_tokens,
    placement,
    key_value_cache,
    context_length,
    decode_step_query,
    step_key_value,
):
    devices = lax.axis_size("tensor")
    tokens, width = hidden.shape
    features = key_value_weight.shape[0]
    local, pages, rank2 = adapter_down_weight.shape
    rank = adapter_up_weight.shape[2]
    tenants = tenant_page_table.shape[0]
    dec_rows, ctx, kv_width = key_value_cache.shape
    steps = step_key_value.shape[0]
    heads2 = kv_width // HD
    d_chunks, chunks = 4, 2
    up_by_page = jnp.transpose(adapter_up_weight, (1, 2, 0))
    rows = 2 * CAPT + rank
    outgoing = pl.pallas_call(
        functools.partial(project_kernel, dec_rows, d_chunks, chunks, devices),
        out_shape=pltpu.VMEM((devices, rows, HD), WIRE),
        in_specs=[ANY_SPEC] * 8,
        out_specs=VMEM_SPEC,
        scratch_shapes=[
            pltpu.SMEM(tenant.shape, jnp.int32),
            pltpu.SMEM(tenant_page_table.shape, jnp.int32),
            pltpu.SMEM(request_block_count.shape, jnp.int32),
            pltpu.SMEM(placement.shape, jnp.int32),
            pltpu.VMEM((chunks, tokens, width // chunks), jnp.bfloat16),
            pltpu.VMEM((chunks, features, width // chunks), jnp.bfloat16),
            pltpu.VMEM((local, pages, rank2), jnp.bfloat16),
            pltpu.VMEM((tokens, local), jnp.bfloat16),
            pltpu.VMEM((pages, rank, features), jnp.bfloat16),
            pltpu.VMEM((local // 16, tenants * 16, rank2), jnp.bfloat16),
            pltpu.VMEM((tenants, tokens + BLK, rank2), jnp.float32),
            pltpu.VMEM((tokens + BLK, HD), jnp.float32),
            pltpu.SMEM((2, devices), jnp.int32),
            pltpu.SemaphoreType.DMA((chunks, 2)),
            pltpu.SemaphoreType.DMA((d_chunks + 2,)),
            pltpu.SemaphoreType.DMA((4,)),
        ],
        compiler_params=pltpu.CompilerParams(vmem_limit_bytes=PROJECT_VMEM),
        name="project",
    )(
        *(
            pltpu.with_memory_space_constraint(x, pltpu.HBM)
            for x in (
                tenant, tenant_page_table, request_block_count, placement,
                hidden, key_value_weight, adapter_down_weight, up_by_page,
            )
        )
    )
    arrived = lax.all_to_all(outgoing, "tensor", split_axis=0, concat_axis=0, tiled=True)

    query = decode_step_query.reshape(steps, dec_rows, HEADS, HD)
    query = query.transpose(0, 2, 1, 3).reshape(steps * HEADS * dec_rows, HD)
    steps_kv = step_key_value.reshape(steps, dec_rows, heads2, HD)
    steps_kv = steps_kv.transpose(0, 2, 1, 3).reshape(steps * heads2 * dec_rows, HD)
    q_rows = steps * HEADS * dec_rows
    state = jax.ShapeDtypeStruct((HD, q_rows), jnp.float32)
    line = jax.ShapeDtypeStruct((8, q_rows), jnp.float32)
    handed = pl.pallas_call(
        cached_kernel,
        out_shape=(
            jax.ShapeDtypeStruct((HD, q_rows), jnp.bfloat16),
            state,
            line,
            line,
            jax.ShapeDtypeStruct((KVH * CAPT, q_rows), jnp.float32),
        ),
        in_specs=[SMEM_SPEC] * 4 + [VMEM_SPEC] * 3,
        out_specs=(VMEM_SPEC,) * 5,
        scratch_shapes=[pltpu.VMEM((q_rows, HD), jnp.float32)] * 3,
        compiler_params=pltpu.CompilerParams(vmem_limit_bytes=ATTEND_VMEM),
        name="cached",
    )(
        context_length, request_block_count, last_block_tokens, placement,
        key_value_cache, query, steps_kv,
    )
    attended = pl.pallas_call(
        functools.partial(merge_kernel, features),
        out_shape=jax.ShapeDtypeStruct((q_rows, HD), jnp.bfloat16),
        in_specs=[VMEM_SPEC] * 6,
        out_specs=ANY_SPEC,
        scratch_shapes=[
            pltpu.VMEM((q_rows, HD), jnp.bfloat16),
            pltpu.SemaphoreType.DMA((steps,)),
        ],
        compiler_params=pltpu.CompilerParams(vmem_limit_bytes=ATTEND_VMEM),
        name="merge",
    )(arrived, *handed)
    attended = attended.reshape(steps, HEADS, dec_rows, HD).transpose(0, 2, 1, 3)
    return attended.reshape(steps, dec_rows, HEADS * HD)


def solution(mesh):
    return jax.shard_map(
        body,
        mesh=mesh,
        in_specs=(
            P("parts", None),
            P("tensor", None),
            P("tensor", None, None),
            P("tensor", None, None),
            P("parts"),
            P(),
            P("parts"),
            P("parts"),
            P("parts"),
            P(("parts", "tensor"), None, None),
            P(("parts", "tensor")),
            P(None, ("parts", "tensor"), None),
            P(None, ("parts", "tensor"), None),
        ),
        out_specs=P(None, ("parts", "tensor"), None),
        check_vma=False,
    )
```

```python
import functools

import jax
import jax.numpy as jnp
from jax import lax
from jax.experimental import pallas as pl
from jax.experimental.pallas import tpu as pltpu
from jax.sharding import PartitionSpec as P

HEADS = 64
KVH = 8
HD = 128
BLK = 8
MOSTB = 2
CAPT = MOSTB * BLK
ADAPTER_SCALE = 0.5
NEG_LARGE = -1e30
PROJECT_VMEM = 32 * 1024 * 1024
ATTEND_VMEM = 16 * 1024 * 1024
WIRE = jnp.bfloat16

SMEM_SPEC = pl.BlockSpec(memory_space=pltpu.SMEM)
VMEM_SPEC = pl.BlockSpec(memory_space=pltpu.VMEM)
ANY_SPEC = pl.BlockSpec(memory_space=pl.ANY)


def div(x, n):
    shift = n.bit_length() - 1
    return lax.shift_right_logical(x, shift) if n == 1 << shift else x // n


def mod(x, n):
    return x & (n - 1) if n & (n - 1) == 0 else x % n


def project_kernel(
    dec_rows, d_chunks, chunks, devices, tenant_h, table_h, counts_h, placement_h, hidden, weight, down, up, out,
    tenant, table, counts, placement,
    h_s, w_s, d_s, mine_s, u_s, sel_s, part_s, base_s, out_s, dest_table, sems, d_sems, int_sems,
    out_sems,
):
    tokens, width = hidden.shape
    features = weight.shape[0]
    local, pages, rank2 = down.shape
    tenants = table.shape[0]
    rank = up.shape[1]
    requests = tenant.shape[0]
    me = lax.axis_index("tensor")
    d_step = local // d_chunks
    step = width // chunks

    int_copies = [
        pltpu.make_async_copy(src, dst, int_sems.at[i])
        for i, (src, dst) in enumerate(
            ((table_h, table), (tenant_h, tenant), (counts_h, counts), (placement_h, placement))
        )
    ]
    for copy in int_copies:
        copy.start()
    def d_copy(c):
        rows = pl.ds(c * d_step, d_step)
        return pltpu.make_async_copy(down.at[rows], d_s.at[rows], d_sems.at[c])

    h_copies = [
        pltpu.make_async_copy(hidden.at[:, pl.ds(c * step, step)], h_s.at[c], sems.at[c, 0])
        for c in range(chunks)
    ]
    w_copies = [
        pltpu.make_async_copy(weight.at[:, pl.ds(c * step, step)], w_s.at[c], sems.at[c, 1])
        for c in range(chunks)
    ]
    my_copy = pltpu.make_async_copy(
        hidden.at[:, pl.ds(pl.multiple_of(me * local, 128), local)], mine_s, d_sems.at[d_chunks]
    )
    up_copy = pltpu.make_async_copy(up, u_s, d_sems.at[d_chunks + 1])
    for copy in [d_copy(c) for c in range(d_chunks)] + [my_copy, up_copy]:
        copy.start()
    for c in range(chunks):
        h_copies[c].start()
        w_copies[c].start()

    int_copies[0].wait()
    rows = lax.broadcasted_iota(jnp.int32, (tenants * 16, 16 * pages), 0)
    cols = lax.broadcasted_iota(jnp.int32, (tenants * 16, 16 * pages), 1)
    page_of_row = jnp.zeros_like(rows)
    for k in range(tenants):
        page_of_row = jnp.where(div(rows, 16) == k, table[k], page_of_row)
    pick = (mod(rows, 16) == div(cols, pages)) & (mod(cols, pages) == page_of_row)
    pick = jnp.where(pick, jnp.float32(1), jnp.float32(0)).astype(jnp.bfloat16)

    blocks = d_step // 16

    def select(c, carry):
        d_copy(c).wait()
        for b in range(0, blocks, 2):
            block = jnp.concatenate(
                [
                    d_s[pl.ds(c * d_step + (b + i) * 16, 16)].reshape(16 * pages, rank2)
                    for i in range(2)
                ],
                axis=1,
            )
            chosen = jnp.dot(pick, block, preferred_element_type=jnp.float32)
            for i in range(2):
                sel_s[c * blocks + b + i] = chosen[:, i * rank2 : (i + 1) * rank2].astype(
                    jnp.bfloat16
                )
        return carry

    lax.fori_loop(0, d_chunks, select, 0)
    for copy in int_copies[1:]:
        copy.wait()
    for dest in range(devices):
        dest_table[0, dest] = 0
        dest_table[1, dest] = 0
    first = jnp.int32(0)
    for r in range(requests):
        dest = div(placement[r], dec_rows)
        dest_table[0, dest] = first * BLK
        dest_table[1, dest] = tenant[r]
        first = first + counts[r]
    up_copy.wait()
    whole = features == HD
    sent = []
    my_copy.wait()
    h_copies[0].wait()
    w_copies[0].wait()
    mine = mine_s[...]
    for k in range(0, tenants, 2):
        pair = min(2, tenants - k)
        maps = jnp.concatenate(
            [sel_s[:, j * 16 : (j + 1) * 16, :].reshape(local, rank2) for j in range(k, k + pair)],
            axis=1,
        )
        product = jnp.dot(mine, maps, preferred_element_type=jnp.float32)
        for j in range(pair):
            part_s[k + j, :tokens] = product[:, j * rank2 : (j + 1) * rank2]
            part_s[k + j, tokens:] = jnp.zeros((BLK, rank2), jnp.float32)

    for dest in range(devices):
        start = pl.multiple_of(dest_table[0, dest], BLK)
        who = dest_table[1, dest]
        out_s[dest, :CAPT, :] = part_s[who, pl.ds(start, CAPT), :].astype(out.dtype)
        if not whole:
            out_s[dest, 2 * CAPT :, :] = jnp.zeros((rank, HD), out.dtype)
        out_s[dest, 2 * CAPT :, :features] = u_s[table[who]]
    for i, lines in enumerate((pl.ds(0, CAPT), pl.ds(2 * CAPT, rank))):
        sent.append(pltpu.make_async_copy(
            out_s.at[:, lines, :], out.at[:, lines, :], out_sems.at[i]))
        sent[-1].start()

    total = jnp.zeros((tokens, features), jnp.float32)
    for c in range(chunks):
        if c > 0:
            h_copies[c].wait()
            w_copies[c].wait()
        total = total + lax.dot_general(h_s[c], w_s[c], NT, preferred_element_type=jnp.float32)
    base_s[tokens:] = jnp.zeros((BLK, HD), jnp.float32)
    if features < HD:
        base_s[...] = jnp.zeros_like(base_s)
    base_s[:tokens, :features] = total
    for dest in range(devices):
        start = pl.multiple_of(dest_table[0, dest], BLK)
        out_s[dest, CAPT : 2 * CAPT, :] = base_s[pl.ds(start, CAPT), :].astype(out.dtype)
    lines = pl.ds(CAPT, CAPT)
    sent.append(pltpu.make_async_copy(
        out_s.at[:, lines, :], out.at[:, lines, :], out_sems.at[2]))
    sent[-1].start()
    for copy in sent:
        copy.wait()


NT = (((1,), (1,)), ((), ()))


def gather_queries(query, k, group, steps, stride):
    return jnp.concatenate(
        [query[pl.ds(s * stride + k * group, group), :] for s in range(steps)], axis=0
    )


def cached_kernel(
    lengths, counts, last, placement, cache, query, steps_kv,
    query_t, acc_t, top_t, total_t, fresh_ok, acc, top_out, total_out,
):
    dec_rows, ctx, kv_width = cache.shape
    half_width = kv_width // 2
    step_rows = KVH * dec_rows
    steps = steps_kv.shape[0] // (2 * step_rows)
    group = HEADS // KVH * dec_rows
    q_rows = steps * group
    stride = HEADS * dec_rows

    row = lax.broadcasted_iota(jnp.int32, (q_rows, ctx), 0)
    col = lax.broadcasted_iota(jnp.int32, (q_rows, ctx), 1)
    row_slot = mod(row, dec_rows)
    cache_ok = [(row_slot == g) & (col < lengths[g]) for g in range(dec_rows)]
    row = lax.broadcasted_iota(jnp.int32, (q_rows, steps * step_rows), 0)
    col = lax.broadcasted_iota(jnp.int32, (q_rows, steps * step_rows), 1)
    step_ok = (mod(row, dec_rows) == mod(col, dec_rows)) & (div(col, step_rows) <= div(row, group))
    step_head = div(mod(col, step_rows), dec_rows)
    step_keys, step_values = (
        jnp.concatenate(
            [steps_kv[pl.ds((2 * s + half) * step_rows, step_rows), :] for s in range(steps)], axis=0
        )
        for half in range(2)
    )

    scale = HD ** (-0.5)
    for k in range(KVH):
        lanes = pl.ds(k * HD, HD)
        vlanes = pl.ds(half_width + k * HD, HD)
        q = gather_queries(query, k, group, steps, stride)
        keys = [cache[g, :, lanes] for g in range(dec_rows)] + [step_keys]
        values = [cache[g, :, vlanes] for g in range(dec_rows)] + [step_values]
        scores = [
            jnp.where(
                ok,
                lax.dot_general(q, key, NT, preferred_element_type=jnp.float32) * scale,
                NEG_LARGE,
            )
            for ok, key in zip(cache_ok + [step_ok & (step_head == k)], keys)
        ]
        top = functools.reduce(jnp.maximum, [jnp.max(s, axis=1, keepdims=True) for s in scores])
        weights = [jnp.exp(s - top) for s in scores]
        total = sum(jnp.sum(w, axis=1, keepdims=True) for w in weights)
        mixed = sum(
            jnp.dot(w.astype(jnp.bfloat16), v, preferred_element_type=jnp.float32)
            for w, v in zip(weights, values)
        )
        for s in range(steps):
            here = pl.ds(s * stride + k * group, group)
            part = slice(s * group, (s + 1) * group)
            acc[here, :] = mixed[part]
            top_out[here, :] = jnp.broadcast_to(top[part], (group, HD))
            total_out[here, :] = jnp.broadcast_to(total[part], (group, HD))

    my_slot = jnp.int32(-1)
    my_length = jnp.int32(0)
    for r in range(placement.shape[0]):
        hit = div(placement[r], dec_rows) == lax.axis_index("tensor")
        my_slot = jnp.where(hit, mod(placement[r], dec_rows), my_slot)
        my_length = jnp.where(hit, (counts[r] - 1) * BLK + last[r], my_length)
    col = lax.broadcasted_iota(jnp.int32, fresh_ok.shape, 0)
    row = lax.broadcasted_iota(jnp.int32, fresh_ok.shape, 1)
    ok = (
        (mod(div(row, group), KVH) == div(col, CAPT))
        & (mod(row, dec_rows) == my_slot)
        & (mod(col, CAPT) < my_length)
    )
    fresh_ok[...] = jnp.where(ok, jnp.float32(1), jnp.float32(0))
    query_t[...] = query[...].T
    acc_t[...] = acc[...].T
    top_t[...] = top_out[...].T[: top_t.shape[0]]
    total_t[...] = total_out[...].T[: total_t.shape[0]]


def merge_kernel(features, box, query_t, acc_t, top_t, total_t, fresh_ok, out, result, sems):
    devices = box.shape[0]
    rank = box.shape[1] - 2 * CAPT
    terms = [box[i, :CAPT].astype(jnp.float32) for i in range(devices)]
    while len(terms) > 1:
        pairs = [a + b for a, b in zip(terms[::2], terms[1::2])]
        terms = pairs + terms[2 * len(pairs) :]
    shrunk = terms[0].astype(jnp.bfloat16)
    halves = (shrunk[:, :rank], shrunk[:, rank:])
    pieces = HD // features

    def rows(i, first, count):
        parts = [box[i * pieces + p, first : first + count, :features] for p in range(pieces)]
        return parts[0] if pieces == 1 else jnp.concatenate(parts, axis=1)

    def fresh(first):
        made = []
        for i in range(first, first + KVH, 2):
            ups = jnp.concatenate([rows(i + j, 2 * CAPT, rank) for j in range(2)], axis=1)
            delta = jnp.dot(halves[first // KVH], ups, preferred_element_type=jnp.float32)
            for j in range(2):
                base = rows(i + j, CAPT, CAPT).astype(jnp.float32)
                both = base + ADAPTER_SCALE * delta[:, j * HD : (j + 1) * HD]
                made.append(both.astype(jnp.bfloat16))
        return jnp.concatenate(made, axis=0)

    keys = fresh(0)
    values_t = fresh(KVH).T
    scale = HD ** (-0.5)
    part = out.shape[0] // sems.shape[0]
    copies = []
    for c in range(sems.shape[0]):
        here = pl.ds(c * part, part)
        s = jnp.dot(keys, query_t[:, here], preferred_element_type=jnp.float32)
        s = jnp.where(fresh_ok[:, here] > 0, s * scale, NEG_LARGE)
        old = top_t[:1, here]
        top = jnp.maximum(old, jnp.max(s, axis=0, keepdims=True))
        fade = jnp.exp(old - top)
        w = jnp.exp(s - top)
        total = total_t[:1, here] * fade + jnp.sum(w, axis=0, keepdims=True)
        mixed = acc_t[:, here] * fade + jnp.dot(
            values_t, w.astype(jnp.bfloat16), preferred_element_type=jnp.float32
        )
        result[here, :] = (mixed / total).T.astype(jnp.bfloat16)
        copies.append(pltpu.make_async_copy(result.at[here, :], out.at[here, :], sems.at[c]))
        copies[c].start()
    for copy in copies:
        copy.wait()


def body(
    hidden,
    key_value_weight,
    adapter_down_weight,
    adapter_up_weight,
    tenant,
    tenant_page_table,
    request_block_count,
    last_block_tokens,
    placement,
    key_value_cache,
    context_length,
    decode_step_query,
    step_key_value,
):
    devices = lax.axis_size("tensor")
    tokens, width = hidden.shape
    features = key_value_weight.shape[0]
    local, pages, rank2 = adapter_down_weight.shape
    rank = adapter_up_weight.shape[2]
    tenants = tenant_page_table.shape[0]
    dec_rows, ctx, kv_width = key_value_cache.shape
    steps = step_key_value.shape[0]
    heads2 = kv_width // HD
    d_chunks, chunks = 4, 2
    up_by_page = jnp.transpose(adapter_up_weight, (1, 2, 0))
    rows = 2 * CAPT + rank
    outgoing = pl.pallas_call(
        functools.partial(project_kernel, dec_rows, d_chunks, chunks, devices),
        out_shape=jax.ShapeDtypeStruct((devices, rows, HD), WIRE),
        in_specs=[ANY_SPEC] * 8,
        out_specs=ANY_SPEC,
        scratch_shapes=[
            pltpu.SMEM(tenant.shape, jnp.int32),
            pltpu.SMEM(tenant_page_table.shape, jnp.int32),
            pltpu.SMEM(request_block_count.shape, jnp.int32),
            pltpu.SMEM(placement.shape, jnp.int32),
            pltpu.VMEM((chunks, tokens, width // chunks), jnp.bfloat16),
            pltpu.VMEM((chunks, features, width // chunks), jnp.bfloat16),
            pltpu.VMEM((local, pages, rank2), jnp.bfloat16),
            pltpu.VMEM((tokens, local), jnp.bfloat16),
            pltpu.VMEM((pages, rank, features), jnp.bfloat16),
            pltpu.VMEM((local // 16, tenants * 16, rank2), jnp.bfloat16),
            pltpu.VMEM((tenants, tokens + BLK, rank2), jnp.float32),
            pltpu.VMEM((tokens + BLK, HD), jnp.float32),
            pltpu.VMEM((devices, rows, HD), WIRE),
            pltpu.SMEM((2, devices), jnp.int32),
            pltpu.SemaphoreType.DMA((chunks, 2)),
            pltpu.SemaphoreType.DMA((d_chunks + 2,)),
            pltpu.SemaphoreType.DMA((4,)),
            pltpu.SemaphoreType.DMA((3,)),
        ],
        compiler_params=pltpu.CompilerParams(vmem_limit_bytes=PROJECT_VMEM),
        name="project",
    )(
        *(
            pltpu.with_memory_space_constraint(x, pltpu.HBM)
            for x in (
                tenant, tenant_page_table, request_block_count, placement,
                hidden, key_value_weight, adapter_down_weight, up_by_page,
            )
        )
    )
    arrived = lax.all_to_all(outgoing, "tensor", split_axis=0, concat_axis=0, tiled=True)

    query = decode_step_query.reshape(steps, dec_rows, HEADS, HD)
    query = query.transpose(0, 2, 1, 3).reshape(steps * HEADS * dec_rows, HD)
    steps_kv = step_key_value.reshape(steps, dec_rows, heads2, HD)
    steps_kv = steps_kv.transpose(0, 2, 1, 3).reshape(steps * heads2 * dec_rows, HD)
    q_rows = steps * HEADS * dec_rows
    state = jax.ShapeDtypeStruct((HD, q_rows), jnp.float32)
    line = jax.ShapeDtypeStruct((8, q_rows), jnp.float32)
    handed = pl.pallas_call(
        cached_kernel,
        out_shape=(
            jax.ShapeDtypeStruct((HD, q_rows), jnp.bfloat16),
            state,
            line,
            line,
            jax.ShapeDtypeStruct((KVH * CAPT, q_rows), jnp.float32),
        ),
        in_specs=[SMEM_SPEC] * 4 + [VMEM_SPEC] * 3,
        out_specs=(VMEM_SPEC,) * 5,
        scratch_shapes=[pltpu.VMEM((q_rows, HD), jnp.float32)] * 3,
        compiler_params=pltpu.CompilerParams(vmem_limit_bytes=ATTEND_VMEM),
        name="cached",
    )(
        context_length, request_block_count, last_block_tokens, placement,
        key_value_cache, query, steps_kv,
    )
    attended = pl.pallas_call(
        functools.partial(merge_kernel, features),
        out_shape=jax.ShapeDtypeStruct((q_rows, HD), jnp.bfloat16),
        in_specs=[VMEM_SPEC] * 6,
        out_specs=ANY_SPEC,
        scratch_shapes=[
            pltpu.VMEM((q_rows, HD), jnp.bfloat16),
            pltpu.SemaphoreType.DMA((steps,)),
        ],
        compiler_params=pltpu.CompilerParams(vmem_limit_bytes=ATTEND_VMEM),
        name="merge",
    )(arrived, *handed)
    attended = attended.reshape(steps, HEADS, dec_rows, HD).transpose(0, 2, 1, 3)
    return attended.reshape(steps, dec_rows, HEADS * HD)


def solution(mesh):
    return jax.shard_map(
        body,
        mesh=mesh,
        in_specs=(
            P("parts", None),
            P("tensor", None),
            P("tensor", None, None),
            P("tensor", None, None),
            P("parts"),
            P(),
            P("parts"),
            P("parts"),
            P("parts"),
            P(("parts", "tensor"), None, None),
            P(("parts", "tensor")),
            P(None, ("parts", "tensor"), None),
            P(None, ("parts", "tensor"), None),
        ),
        out_specs=P(None, ("parts", "tensor"), None),
        check_vma=False,
    )
```

```python
import functools

import jax
import jax.numpy as jnp
from jax import lax
from jax.experimental import pallas as pl
from jax.experimental.pallas import tpu as pltpu
from jax.sharding import PartitionSpec as P

HEADS = 64
KVH = 8
HD = 128
BLK = 8
MOSTB = 2
CAPT = MOSTB * BLK
ADAPTER_SCALE = 0.5
NEG_LARGE = -1e30
PROJECT_VMEM = 32 * 1024 * 1024
ATTEND_VMEM = 16 * 1024 * 1024
WIRE = jnp.bfloat16

SMEM_SPEC = pl.BlockSpec(memory_space=pltpu.SMEM)
VMEM_SPEC = pl.BlockSpec(memory_space=pltpu.VMEM)
ANY_SPEC = pl.BlockSpec(memory_space=pl.ANY)


def div(x, n):
    shift = n.bit_length() - 1
    return lax.shift_right_logical(x, shift) if n == 1 << shift else x // n


def mod(x, n):
    return x & (n - 1) if n & (n - 1) == 0 else x % n


def project_kernel(
    dec_rows, d_chunks, chunks, devices, tenant_h, table_h, counts_h, placement_h, hidden, weight, down, up, out,
    tenant, table, counts, placement,
    h_s, w_s, d_s, mine_s, u_s, sel_s, part_s, base_s, dest_table, sems, d_sems, int_sems,
):
    tokens, width = hidden.shape
    features = weight.shape[0]
    local, pages, rank2 = down.shape
    tenants = table.shape[0]
    requests = tenant.shape[0]
    me = lax.axis_index("tensor")
    d_step = local // d_chunks
    step = width // chunks

    int_copies = [
        pltpu.make_async_copy(src, dst, int_sems.at[i])
        for i, (src, dst) in enumerate(
            ((table_h, table), (tenant_h, tenant), (counts_h, counts), (placement_h, placement))
        )
    ]
    for copy in int_copies:
        copy.start()
    def d_copy(c):
        rows = pl.ds(c * d_step, d_step)
        return pltpu.make_async_copy(down.at[rows], d_s.at[rows], d_sems.at[c])

    h_copies = [
        pltpu.make_async_copy(hidden.at[:, pl.ds(c * step, step)], h_s.at[c], sems.at[c, 0])
        for c in range(chunks)
    ]
    w_copies = [
        pltpu.make_async_copy(weight.at[:, pl.ds(c * step, step)], w_s.at[c], sems.at[c, 1])
        for c in range(chunks)
    ]
    my_copy = pltpu.make_async_copy(
        hidden.at[:, pl.ds(pl.multiple_of(me * local, 128), local)], mine_s, d_sems.at[d_chunks]
    )
    up_copy = pltpu.make_async_copy(up, u_s, d_sems.at[d_chunks + 1])
    for copy in [d_copy(c) for c in range(d_chunks)] + [my_copy]:
        copy.start()
    for c in range(chunks):
        h_copies[c].start()
        w_copies[c].start()
    up_copy.start()

    int_copies[0].wait()
    rows = lax.broadcasted_iota(jnp.int32, (tenants * 16, 16 * pages), 0)
    cols = lax.broadcasted_iota(jnp.int32, (tenants * 16, 16 * pages), 1)
    page_of_row = jnp.zeros_like(rows)
    for k in range(tenants):
        page_of_row = jnp.where(div(rows, 16) == k, table[k], page_of_row)
    pick = (mod(rows, 16) == div(cols, pages)) & (mod(cols, pages) == page_of_row)
    pick = jnp.where(pick, jnp.float32(1), jnp.float32(0)).astype(jnp.bfloat16)

    blocks = d_step // 16

    def select(c, carry):
        d_copy(c).wait()
        for b in range(0, blocks, 2):
            block = jnp.concatenate(
                [
                    d_s[pl.ds(c * d_step + (b + i) * 16, 16)].reshape(16 * pages, rank2)
                    for i in range(2)
                ],
                axis=1,
            )
            chosen = jnp.dot(pick, block, preferred_element_type=jnp.float32)
            for i in range(2):
                sel_s[c * blocks + b + i] = chosen[:, i * rank2 : (i + 1) * rank2].astype(
                    jnp.bfloat16
                )
        return carry

    lax.fori_loop(0, d_chunks, select, 0)
    for copy in int_copies[1:]:
        copy.wait()
    for dest in range(devices):
        dest_table[0, dest] = 0
        dest_table[1, dest] = 0
    first = jnp.int32(0)
    for r in range(requests):
        dest = div(placement[r], dec_rows)
        dest_table[0, dest] = first * BLK
        dest_table[1, dest] = tenant[r]
        first = first + counts[r]
    my_copy.wait()
    mine = mine_s[...]
    for k in range(0, tenants, 2):
        pair = min(2, tenants - k)
        maps = jnp.concatenate(
            [sel_s[:, j * 16 : (j + 1) * 16, :].reshape(local, rank2) for j in range(k, k + pair)],
            axis=1,
        )
        product = jnp.dot(mine, maps, preferred_element_type=jnp.float32)
        for j in range(pair):
            part_s[k + j, :tokens] = product[:, j * rank2 : (j + 1) * rank2]
            part_s[k + j, tokens:] = jnp.zeros((BLK, rank2), jnp.float32)

    total = jnp.zeros((tokens, features), jnp.float32)
    for c in range(chunks):
        h_copies[c].wait()
        w_copies[c].wait()
        total = total + lax.dot_general(h_s[c], w_s[c], NT, preferred_element_type=jnp.float32)
    base_s[tokens:] = jnp.zeros((BLK, HD), jnp.float32)
    if features < HD:
        base_s[...] = jnp.zeros_like(base_s)
    base_s[:tokens, :features] = total
    up_copy.wait()

    def lay_out(first, carry):
        for i in range(4):
            dest = first * 4 + i
            start = pl.multiple_of(dest_table[0, dest], BLK)
            who = dest_table[1, dest]
            out[dest, :CAPT, :] = part_s[who, pl.ds(start, CAPT), :].astype(out.dtype)
            out[dest, CAPT : 2 * CAPT, :] = base_s[pl.ds(start, CAPT), :].astype(out.dtype)
            if features < HD:
                out[dest, 2 * CAPT :, :] = jnp.zeros((out.shape[1] - 2 * CAPT, HD), out.dtype)
            out[dest, 2 * CAPT :, :features] = u_s[table[who]]
        return carry

    lax.fori_loop(0, devices // 4, lay_out, 0)


NT = (((1,), (1,)), ((), ()))


def gather_queries(query, k, group, steps, stride):
    return jnp.concatenate(
        [query[pl.ds(s * stride + k * group, group), :] for s in range(steps)], axis=0
    )


def cached_kernel(
    lengths, counts, last, placement, cache, query, steps_kv,
    query_t, acc_t, top_t, total_t, fresh_ok, acc, top_out, total_out,
):
    dec_rows, ctx, kv_width = cache.shape
    half_width = kv_width // 2
    step_rows = KVH * dec_rows
    steps = steps_kv.shape[0] // (2 * step_rows)
    group = HEADS // KVH * dec_rows
    q_rows = steps * group
    stride = HEADS * dec_rows

    row = lax.broadcasted_iota(jnp.int32, (q_rows, ctx), 0)
    col = lax.broadcasted_iota(jnp.int32, (q_rows, ctx), 1)
    row_slot = mod(row, dec_rows)
    cache_ok = [(row_slot == g) & (col < lengths[g]) for g in range(dec_rows)]
    row = lax.broadcasted_iota(jnp.int32, (q_rows, steps * step_rows), 0)
    col = lax.broadcasted_iota(jnp.int32, (q_rows, steps * step_rows), 1)
    step_ok = (mod(row, dec_rows) == mod(col, dec_rows)) & (div(col, step_rows) <= div(row, group))
    step_head = div(mod(col, step_rows), dec_rows)
    step_keys, step_values = (
        jnp.concatenate(
            [steps_kv[pl.ds((2 * s + half) * step_rows, step_rows), :] for s in range(steps)], axis=0
        )
        for half in range(2)
    )

    scale = HD ** (-0.5)
    for k in range(KVH):
        lanes = pl.ds(k * HD, HD)
        vlanes = pl.ds(half_width + k * HD, HD)
        q = gather_queries(query, k, group, steps, stride)
        keys = [cache[g, :, lanes] for g in range(dec_rows)] + [step_keys]
        values = [cache[g, :, vlanes] for g in range(dec_rows)] + [step_values]
        scores = [
            jnp.where(
                ok,
                lax.dot_general(q, key, NT, preferred_element_type=jnp.float32) * scale,
                NEG_LARGE,
            )
            for ok, key in zip(cache_ok + [step_ok & (step_head == k)], keys)
        ]
        top = functools.reduce(jnp.maximum, [jnp.max(s, axis=1, keepdims=True) for s in scores])
        weights = [jnp.exp(s - top) for s in scores]
        total = sum(jnp.sum(w, axis=1, keepdims=True) for w in weights)
        mixed = sum(
            jnp.dot(w.astype(jnp.bfloat16), v, preferred_element_type=jnp.float32)
            for w, v in zip(weights, values)
        )
        for s in range(steps):
            here = pl.ds(s * stride + k * group, group)
            part = slice(s * group, (s + 1) * group)
            acc[here, :] = mixed[part]
            top_out[here, :] = jnp.broadcast_to(top[part], (group, HD))
            total_out[here, :] = jnp.broadcast_to(total[part], (group, HD))

    my_slot = jnp.int32(-1)
    my_length = jnp.int32(0)
    for r in range(placement.shape[0]):
        hit = div(placement[r], dec_rows) == lax.axis_index("tensor")
        my_slot = jnp.where(hit, mod(placement[r], dec_rows), my_slot)
        my_length = jnp.where(hit, (counts[r] - 1) * BLK + last[r], my_length)
    col = lax.broadcasted_iota(jnp.int32, fresh_ok.shape, 0)
    row = lax.broadcasted_iota(jnp.int32, fresh_ok.shape, 1)
    ok = (
        (mod(div(row, group), KVH) == div(col, CAPT))
        & (mod(row, dec_rows) == my_slot)
        & (mod(col, CAPT) < my_length)
    )
    fresh_ok[...] = jnp.where(ok, jnp.float32(1), jnp.float32(0))
    query_t[...] = query[...].T
    acc_t[...] = acc[...].T
    top_t[...] = top_out[...].T[: top_t.shape[0]]
    total_t[...] = total_out[...].T[: total_t.shape[0]]


def merge_kernel(features, box, query_t, acc_t, top_t, total_t, fresh_ok, out, result, sems):
    devices = box.shape[0]
    rank = box.shape[1] - 2 * CAPT
    terms = [box[i, :CAPT].astype(jnp.float32) for i in range(devices)]
    while len(terms) > 1:
        pairs = [a + b for a, b in zip(terms[::2], terms[1::2])]
        terms = pairs + terms[2 * len(pairs) :]
    shrunk = terms[0].astype(jnp.bfloat16)
    halves = (shrunk[:, :rank], shrunk[:, rank:])
    pieces = HD // features

    def rows(i, first, count):
        parts = [box[i * pieces + p, first : first + count, :features] for p in range(pieces)]
        return parts[0] if pieces == 1 else jnp.concatenate(parts, axis=1)

    def fresh(first):
        made = []
        for i in range(first, first + KVH, 2):
            ups = jnp.concatenate([rows(i + j, 2 * CAPT, rank) for j in range(2)], axis=1)
            delta = jnp.dot(halves[first // KVH], ups, preferred_element_type=jnp.float32)
            for j in range(2):
                base = rows(i + j, CAPT, CAPT).astype(jnp.float32)
                both = base + ADAPTER_SCALE * delta[:, j * HD : (j + 1) * HD]
                made.append(both.astype(jnp.bfloat16))
        return jnp.concatenate(made, axis=0)

    keys = fresh(0)
    values_t = fresh(KVH).T
    scale = HD ** (-0.5)
    part = out.shape[0] // sems.shape[0]
    copies = []
    for c in range(sems.shape[0]):
        here = pl.ds(c * part, part)
        s = jnp.dot(keys, query_t[:, here], preferred_element_type=jnp.float32)
        s = jnp.where(fresh_ok[:, here] > 0, s * scale, NEG_LARGE)
        old = top_t[:1, here]
        top = jnp.maximum(old, jnp.max(s, axis=0, keepdims=True))
        fade = jnp.exp(old - top)
        w = jnp.exp(s - top)
        total = total_t[:1, here] * fade + jnp.sum(w, axis=0, keepdims=True)
        mixed = acc_t[:, here] * fade + jnp.dot(
            values_t, w.astype(jnp.bfloat16), preferred_element_type=jnp.float32
        )
        result[here, :] = (mixed / total).T.astype(jnp.bfloat16)
        copies.append(pltpu.make_async_copy(result.at[here, :], out.at[here, :], sems.at[c]))
        copies[c].start()
    for copy in copies:
        copy.wait()


def body(
    hidden,
    key_value_weight,
    adapter_down_weight,
    adapter_up_weight,
    tenant,
    tenant_page_table,
    request_block_count,
    last_block_tokens,
    placement,
    key_value_cache,
    context_length,
    decode_step_query,
    step_key_value,
):
    devices = lax.axis_size("tensor")
    tokens, width = hidden.shape
    features = key_value_weight.shape[0]
    local, pages, rank2 = adapter_down_weight.shape
    rank = adapter_up_weight.shape[2]
    tenants = tenant_page_table.shape[0]
    dec_rows, ctx, kv_width = key_value_cache.shape
    steps = step_key_value.shape[0]
    heads2 = kv_width // HD
    d_chunks, chunks = 4, 2
    up_by_page = jnp.transpose(adapter_up_weight, (1, 2, 0))
    rows = 2 * CAPT + rank
    outgoing = pl.pallas_call(
        functools.partial(project_kernel, dec_rows, d_chunks, chunks, devices),
        out_shape=pltpu.VMEM((devices, rows, HD), WIRE),
        in_specs=[ANY_SPEC] * 8,
        out_specs=VMEM_SPEC,
        scratch_shapes=[
            pltpu.SMEM(tenant.shape, jnp.int32),
            pltpu.SMEM(tenant_page_table.shape, jnp.int32),
            pltpu.SMEM(request_block_count.shape, jnp.int32),
            pltpu.SMEM(placement.shape, jnp.int32),
            pltpu.VMEM((chunks, tokens, width // chunks), jnp.bfloat16),
            pltpu.VMEM((chunks, features, width // chunks), jnp.bfloat16),
            pltpu.VMEM((local, pages, rank2), jnp.bfloat16),
            pltpu.VMEM((tokens, local), jnp.bfloat16),
            pltpu.VMEM((pages, rank, features), jnp.bfloat16),
            pltpu.VMEM((local // 16, tenants * 16, rank2), jnp.bfloat16),
            pltpu.VMEM((tenants, tokens + BLK, rank2), jnp.float32),
            pltpu.VMEM((tokens + BLK, HD), jnp.float32),
            pltpu.SMEM((2, devices), jnp.int32),
            pltpu.SemaphoreType.DMA((chunks, 2)),
            pltpu.SemaphoreType.DMA((d_chunks + 2,)),
            pltpu.SemaphoreType.DMA((4,)),
        ],
        compiler_params=pltpu.CompilerParams(vmem_limit_bytes=PROJECT_VMEM),
        name="project",
    )(
        *(
            pltpu.with_memory_space_constraint(x, pltpu.HBM)
            for x in (
                tenant, tenant_page_table, request_block_count, placement,
                hidden, key_value_weight, adapter_down_weight, up_by_page,
            )
        )
    )
    arrived = lax.all_to_all(outgoing, "tensor", split_axis=0, concat_axis=0, tiled=True)

    query = decode_step_query.reshape(steps, dec_rows, HEADS, HD)
    query = query.transpose(0, 2, 1, 3).reshape(steps * HEADS * dec_rows, HD)
    steps_kv = step_key_value.reshape(steps, dec_rows, heads2, HD)
    steps_kv = steps_kv.transpose(0, 2, 1, 3).reshape(steps * heads2 * dec_rows, HD)
    q_rows = steps * HEADS * dec_rows
    state = jax.ShapeDtypeStruct((HD, q_rows), jnp.float32)
    line = jax.ShapeDtypeStruct((8, q_rows), jnp.float32)
    handed = pl.pallas_call(
        cached_kernel,
        out_shape=(
            jax.ShapeDtypeStruct((HD, q_rows), jnp.bfloat16),
            state,
            line,
            line,
            jax.ShapeDtypeStruct((KVH * CAPT, q_rows), jnp.float32),
        ),
        in_specs=[SMEM_SPEC] * 4 + [VMEM_SPEC] * 3,
        out_specs=(VMEM_SPEC,) * 5,
        scratch_shapes=[pltpu.VMEM((q_rows, HD), jnp.float32)] * 3,
        compiler_params=pltpu.CompilerParams(vmem_limit_bytes=ATTEND_VMEM),
        name="cached",
    )(
        context_length, request_block_count, last_block_tokens, placement,
        key_value_cache, query, steps_kv,
    )
    attended = pl.pallas_call(
        functools.partial(merge_kernel, features),
        out_shape=jax.ShapeDtypeStruct((q_rows, HD), jnp.bfloat16),
        in_specs=[VMEM_SPEC] * 6,
        out_specs=ANY_SPEC,
        scratch_shapes=[
            pltpu.VMEM((q_rows, HD), jnp.bfloat16),
            pltpu.SemaphoreType.DMA((steps,)),
        ],
        compiler_params=pltpu.CompilerParams(vmem_limit_bytes=ATTEND_VMEM),
        name="merge",
    )(arrived, *handed)
    attended = attended.reshape(steps, HEADS, dec_rows, HD).transpose(0, 2, 1, 3)
    return attended.reshape(steps, dec_rows, HEADS * HD)


def solution(mesh):
    return jax.shard_map(
        body,
        mesh=mesh,
        in_specs=(
            P("parts", None),
            P("tensor", None),
            P("tensor", None, None),
            P("tensor", None, None),
            P("parts"),
            P(),
            P("parts"),
            P("parts"),
            P("parts"),
            P(("parts", "tensor"), None, None),
            P(("parts", "tensor")),
            P(None, ("parts", "tensor"), None),
            P(None, ("parts", "tensor"), None),
        ),
        out_specs=P(None, ("parts", "tensor"), None),
        check_vma=False,
    )
```
